32 devices in a mesh: res: 8 (over z, x), hid: 4 (over y, core).
Axes of the slice: x: 2, y: 2, z: 4, core: 2. Of those that a mesh axis runs over, the one named last changes fastest.
Arguments:
- node_in: bfloat16 [2048, 512], P(('res', 'hid')), may hold values from -6 to 6
- edge_in: bfloat16 [2048, 60, 192], P(('res', 'hid')), may hold values from -6 to 6
- neighbours: int32 [2048, 60], P(('res', 'hid')), may hold values from 0 to 2047, as said below
- live_counts: int32 [2048], P(('res', 'hid')), may hold values from 30 to 60
- message_first: bfloat16 [1216, 512], replicated, may hold values from -0.15625 to 0.15625
- message_first_bias: float32 [512], replicated, may hold values from -3 to 3
- message_second: bfloat16 [512, 512], replicated, may hold values from -0.25 to 0.25
- message_second_bias: float32 [512], replicated, may hold values from -3 to 3
- message_third: bfloat16 [512, 512], replicated, may hold values from -1 to 1
- message_third_bias: float32 [512], replicated, may hold values from -3 to 3
- norm_one: float32 [512], replicated, may hold values from 0.5 to 1.5
- feed_first: bfloat16 [512, 2048], P(None, 'hid'), may hold values from -0.25 to 0.25
- feed_first_bias: float32 [2048], P('hid'), may hold values from -3 to 3
- feed_second: bfloat16 [2048, 512], P('hid'), may hold values from -0.125 to 0.125
- feed_second_bias: float32 [512], replicated, may hold values from -3 to 3
- norm_two: float32 [512], replicated, may hold values from 0.5 to 1.5
- edge_first: bfloat16 [1216, 192], replicated, may hold values from -0.15625 to 0.15625
- edge_first_bias: float32 [192], replicated, may hold values from -3 to 3
- edge_second: bfloat16 [192, 192], replicated, may hold values from -0.4375 to 0.4375
- edge_second_bias: float32 [192], replicated, may hold values from -3 to 3
- edge_third: bfloat16 [192, 192], replicated, may hold values from -0.4375 to 0.4375
- edge_third_bias: float32 [192], replicated, may hold values from -3 to 3
- norm_three: float32 [192], replicated, may hold values from 0.5 to 1.5
- node_cotangent: bfloat16 [2048, 512], P(('res', 'hid')), may hold values from -6 to 6
- edge_cotangent: bfloat16 [2048, 60, 192], P(('res', 'hid')), may hold values from -6 to 6
Outputs:
- node_out: bfloat16 [2048, 512], P(('res', 'hid'))
- edge_out: bfloat16 [2048, 60, 192], P(('res', 'hid'))
- node_gradient: float32 [2048, 512], P(('res', 'hid'))
- edge_gradient: float32 [2048, 60, 192], P(('res', 'hid'))
- message_first_gradient: float32 [1216, 512], replicated
- message_first_bias_gradient: float32 [512], replicated
- message_second_gradient: float32 [512, 512], replicated
- message_second_bias_gradient: float32 [512], replicated
- message_third_gradient: float32 [512, 512], replicated
- message_third_bias_gradient: float32 [512], replicated
- norm_one_gradient: float32 [512], replicated
- feed_first_gradient: float32 [512, 2048], P(None, 'hid')
- feed_first_bias_gradient: float32 [2048], P('hid')
- feed_second_gradient: float32 [2048, 512], P('hid')
- feed_second_bias_gradient: float32 [512], replicated
- norm_two_gradient: float32 [512], replicated
- edge_first_gradient: float32 [1216, 192], replicated
- edge_first_bias_gradient: float32 [192], replicated
- edge_second_gradient: float32 [192, 192], replicated
- edge_second_bias_gradient: float32 [192], replicated
- edge_third_gradient: float32 [192, 192], replicated
- edge_third_bias_gradient: float32 [192], replicated
- norm_three_gradient: float32 [192], replicated
The draws below stay inside these ranges and needn't reach their ends.
Inputs may be any that keep to these rules, and one draw needn't show every extreme that they name: `neighbours`: in each block of 64 consecutive residues, the table's 64 x 60 entries name residues of each aligned group of 256 residues exactly 480 times, repeats counted.
All inputs are finite; a program needn't handle non-finite values.
Results may differ from the reference program's by a relative error of at most 0.018.
Values may be sent and summed in bfloat16 or wider, within the bound.
No kernel may reach another device: no remote copies, remote signals or barrier semaphores. Data moves between devices by JAX's collectives and lax.ppermute only.
A program may use at most 256 MiB of HBM per device.

```python
import jax
import jax.numpy as jnp
from jax import lax

D = 512
E = 192
FF = 2048
SLOTS = 60
RES_DEV = 64
GROUP = 256
CAP = 480
RESIDUES = 2048


def draw_neighbours(key, part):
    key = jax.random.fold_in(key, 11)
    key_order, key_local = jax.random.split(key)
    blocks = RESIDUES // RES_DEV
    entries = RES_DEV * SLOTS
    scores = jax.random.randint(key_order, (blocks, entries), 0, 2 ** 17) * entries
    scores = scores + jnp.arange(entries, dtype=jnp.int32)[None, :]
    placing = jnp.argsort(scores, axis=1).astype(jnp.int32)
    owners = placing // CAP
    local = jax.random.randint(key_local, (blocks, entries), 0, GROUP)
    return (owners * GROUP + local).reshape(RESIDUES, SLOTS).astype(jnp.int32)


def plant(result, stream_key, low, top_value):
    longest = result.shape.index(max(result.shape))
    spots = []
    for shift in (0, 1):
        where = [jax.random.randint(jax.random.fold_in(stream_key, axis), (), 0, length) for axis, length in enumerate(result.shape)]
        where[longest] = (where[longest] + shift) % result.shape[longest]
        spots.append(tuple(where))
    return result.at[spots[0]].set(low).at[spots[1]].set(top_value)


def block_scale(stream_key, dims, cuts, smallest, top_value):
    loudness, own = 1.0, jax.random.fold_in(stream_key, 6)
    for position, shards_of in cuts:
        steps = jnp.exp(jax.random.uniform(jax.random.fold_in(own, position), (shards_of,), jnp.float32, smallest / len(cuts), top_value / len(cuts)))
        loudness = loudness * jnp.repeat(steps, dims[position] // shards_of).reshape([-1 if axis == position else 1 for axis in range(len(dims))])
    return loudness


def centred(rng, extent, width, limit, cuts=(), kind=jnp.bfloat16):
    values = jax.random.normal(rng, extent, jnp.float32) * width
    if len(cuts) > 0:
        values = block_scale(rng, extent, cuts, -0.22, 0.18) * values
    return jnp.clip(values, min=-limit, max=limit).astype(kind)


def setup_inputs(seed: int = 0) -> dict:
    key_list = jax.random.split(jax.random.key(seed), 26)
    node_in = centred(key_list[0], (RESIDUES, D), 1.0, 6.0, ((0, 32),))
    edge_in = centred(key_list[1], (RESIDUES, SLOTS, E), 1.0, 6.0, ((0, 32),))
    neighbours = draw_neighbours(jax.random.fold_in(key_list[25], 71), 0)
    live_counts = plant(jax.random.randint(key_list[3], (RESIDUES,), SLOTS // 2, SLOTS + 1), jax.random.fold_in(key_list[3], 1), SLOTS // 2, SLOTS).astype(jnp.int32)
    message_first = centred(key_list[4], (2 * D + E, D), (2 * D + E) ** -0.5, 0.15625)
    message_first_bias = centred(key_list[5], (D,), 0.5, 3.0, (), jnp.float32)
    message_second = centred(key_list[6], (D, D), D ** -0.5, 0.25)
    message_second_bias = centred(key_list[7], (D,), 0.5, 3.0, (), jnp.float32)
    message_third = centred(key_list[8], (D, D), (D // 16) ** -0.5, 1.0)
    message_third_bias = centred(key_list[9], (D,), 0.5, 3.0, (), jnp.float32)
    norm_one = jnp.clip(1.0 + 0.1 * jax.random.normal(key_list[10], (D,), jnp.float32), 0.5, 1.5)
    feed_first = centred(key_list[11], (D, FF), D ** -0.5, 0.25, ((1, 4),))
    feed_first_bias = centred(key_list[12], (FF,), 0.5, 3.0, ((0, 4),), jnp.float32)
    feed_second = centred(key_list[13], (FF, D), FF ** -0.5, 0.125, ((0, 4),))
    feed_second_bias = centred(key_list[14], (D,), 0.5, 3.0, (), jnp.float32)
    norm_two = jnp.clip(1.0 + 0.1 * jax.random.normal(key_list[15], (D,), jnp.float32), 0.5, 1.5)
    edge_first = centred(key_list[16], (2 * D + E, E), (2 * D + E) ** -0.5, 0.15625)
    edge_first_bias = centred(key_list[17], (E,), 0.5, 3.0, (), jnp.float32)
    edge_second = centred(key_list[18], (E, E), E ** -0.5, 0.4375)
    edge_second_bias = centred(key_list[19], (E,), 0.5, 3.0, (), jnp.float32)
    edge_third = centred(key_list[20], (E, E), E ** -0.5, 0.4375)
    edge_third_bias = centred(key_list[21], (E,), 0.5, 3.0, (), jnp.float32)
    norm_three = jnp.clip(1.0 + 0.1 * jax.random.normal(key_list[22], (E,), jnp.float32), 0.5, 1.5)
    node_cotangent = centred(key_list[23], (RESIDUES, D), 1.0, 6.0, ((0, 32),))
    edge_cotangent = centred(key_list[24], (RESIDUES, SLOTS, E), 1.0, 6.0, ((0, 32),))
    return {"node_in": node_in, "edge_in": edge_in, "neighbours": neighbours, "live_counts": live_counts, "message_first": message_first, "message_first_bias": message_first_bias, "message_second": message_second, "message_second_bias": message_second_bias, "message_third": message_third, "message_third_bias": message_third_bias, "norm_one": norm_one, "feed_first": feed_first, "feed_first_bias": feed_first_bias, "feed_second": feed_second, "feed_second_bias": feed_second_bias, "norm_two": norm_two, "edge_first": edge_first, "edge_first_bias": edge_first_bias, "edge_second": edge_second, "edge_second_bias": edge_second_bias, "edge_third": edge_third, "edge_third_bias": edge_third_bias, "norm_three": norm_three, "node_cotangent": node_cotangent, "edge_cotangent": edge_cotangent}


EPS = 1e-05

@jax.custom_vjp
def low(v):
    return lax.optimization_barrier(v.astype(jnp.bfloat16)).astype(jnp.float32)

@jax.custom_vjp
def low_back(v):
    return v

def low_keep(v):
    return (low(v), None)

def low_pass(kept, grad):
    return (grad,)

def back_keep(v):
    return (v, None)

def back_low(kept, grad):
    return (low(grad),)
low.defvjp(low_keep, low_pass)
low_back.defvjp(back_keep, back_low)

def matmul(left, right):
    return jnp.dot(left, right, precision=lax.Precision.HIGHEST)

def layer_norm(value, gain):
    centre = value - lax.optimization_barrier(jnp.mean(value, -1, keepdims=True))
    variance = lax.optimization_barrier(jnp.mean(centre * centre, -1, keepdims=True))
    return centre * lax.rsqrt(variance + EPS) * gain

def first_layer(own, edge_rows, far, weights, bias):
    spread = jnp.broadcast_to(own[:, None, :], (own.shape[0], far.shape[1], own.shape[1]))
    joined = jnp.concatenate([spread, edge_rows, far], axis=-1)
    return matmul(joined, weights) + bias

def forward(node, edge, neighbours, live, share, params):
    m_one, mb_one, m_two, mb_two, m_three, mb_three, gain_one, f_one, fb_one, f_two, fb_two, gain_two, e_one, eb_one, e_two, eb_two, e_three, eb_three, gain_three = params
    blocks = RESIDUES // GROUP

    def message_block(piece):
        own, edge_rows, index_rows, share_rows = piece
        far = node[index_rows]
        z_one = low_back(first_layer(own, edge_rows, far, m_one, mb_one))
        act_one = low(jax.nn.gelu(z_one))
        z_two = low_back(matmul(act_one, m_two) + mb_two)
        act_two = low(jax.nn.gelu(z_two))
        message = low_back(matmul(act_two, m_three) + mb_three)
        return lax.optimization_barrier(jnp.sum(share_rows[:, :, None] * message, axis=1))
    update = lax.map(jax.checkpoint(message_block), (node.reshape(blocks, GROUP, D), edge.reshape(blocks, GROUP, SLOTS, E), neighbours.reshape(blocks, GROUP, SLOTS), share.reshape(blocks, GROUP, SLOTS))).reshape(RESIDUES, D)
    hidden_one = layer_norm(node + update, gain_one)
    low_one = low(hidden_one)
    pre_feed = low_back(matmul(low_one, f_one) + fb_one)
    act_feed = low(jax.nn.gelu(pre_feed))
    feed_out = low_back(matmul(act_feed, f_two) + fb_two)
    hidden_two = layer_norm(hidden_one + feed_out, gain_two)
    low_two = low(hidden_two)

    def edge_block(piece):
        own, edge_rows, index_rows, live_rows = piece
        far = low_two[index_rows]
        w_one = low_back(first_layer(own, edge_rows, far, e_one, eb_one))
        act_one = low(jax.nn.gelu(w_one))
        w_two = low_back(matmul(act_one, e_two) + eb_two)
        act_two = low(jax.nn.gelu(w_two))
        w_three = low_back(matmul(act_two, e_three) + eb_three)
        return layer_norm(edge_rows + w_three, gain_three) * live_rows[:, :, None]
    edge_out = lax.map(jax.checkpoint(edge_block), (low_two.reshape(blocks, GROUP, D), edge.reshape(blocks, GROUP, SLOTS, E), neighbours.reshape(blocks, GROUP, SLOTS), live.reshape(blocks, GROUP, SLOTS))).reshape(RESIDUES, SLOTS, E)
    return (hidden_two, edge_out)

def reference(node_in, edge_in, neighbours, live_counts, message_first, message_first_bias, message_second, message_second_bias, message_third, message_third_bias, norm_one, feed_first, feed_first_bias, feed_second, feed_second_bias, norm_two, edge_first, edge_first_bias, edge_second, edge_second_bias, edge_third, edge_third_bias, norm_three, node_cotangent, edge_cotangent):
    slot_ids = jnp.arange(SLOTS, dtype=jnp.int32)
    live = (slot_ids[None, :] < live_counts[:, None]).astype(jnp.float32)
    share = live / live_counts.astype(jnp.float32)[:, None]
    params = tuple((p.astype(jnp.float32) for p in (message_first, message_first_bias, message_second, message_second_bias, message_third, message_third_bias, norm_one, feed_first, feed_first_bias, feed_second, feed_second_bias, norm_two, edge_first, edge_first_bias, edge_second, edge_second_bias, edge_third, edge_third_bias, norm_three)))

    def run(node, edge, weights):
        return forward(node, edge, neighbours, live, share, weights)
    outputs, pullback = jax.vjp(run, node_in.astype(jnp.float32), edge_in.astype(jnp.float32), params)
    node_grad, edge_grad, grads = pullback((node_cotangent.astype(jnp.float32), edge_cotangent.astype(jnp.float32)))
    g_m1, g_mb1, g_m2, g_mb2, g_m3, g_mb3, g_n1, g_f1, g_fb1, g_f2, g_fb2, g_n2, g_e1, g_eb1, g_e2, g_eb2, g_e3, g_eb3, g_n3 = grads
    return (outputs[0].astype(jnp.bfloat16), outputs[1].astype(jnp.bfloat16), node_grad, edge_grad, g_m1, g_mb1, g_m2, g_mb2, g_m3, g_mb3, g_n1, g_f1, g_fb1, g_f2, g_fb2, g_n2, g_e1, g_eb1, g_e2, g_eb2, g_e3, g_eb3, g_n3)
```

```python
import functools

import jax
import jax.numpy as jnp
from jax import lax
from jax.experimental import pallas as pl
from jax.experimental.pallas import tpu as pltpu
from jax.sharding import PartitionSpec as P

EPS = 1e-05
AXES = ("res", "hid")
F32 = jnp.float32
BF16 = jnp.bfloat16
TANH_SCALE = 0.7978845608028654
TANH_CUBE = 0.044715
LANES = 128
CHUNK = 2048
MIB = 1024 * 1024


def dot(left, right):
    return lax.dot_general(left, right, (((1,), (0,)), ((), ())), preferred_element_type=F32)


def dot_rows(left, right):
    return lax.dot_general(left, right, (((0,), (0,)), ((), ())), preferred_element_type=F32)


def dot_back(left, right):
    return lax.dot_general(left, right, (((1,), (1,)), ((), ())), preferred_element_type=F32)


def halves(value):
    high = value.astype(BF16)
    return high, (value - high.astype(F32)).astype(BF16)


def fine(product, value, weights):
    high, low = halves(value)
    return product(high, weights) + product(low, weights)


def gelu_parts(x):
    square = x * x
    t = jnp.tanh(x * (TANH_SCALE + (TANH_SCALE * TANH_CUBE) * square))
    gate = 0.5 + 0.5 * t
    act = x * gate
    slope = gate + act * (1.0 - gate) * (2 * TANH_SCALE + (6 * TANH_SCALE * TANH_CUBE) * square)
    return act, slope


def one_hot_columns(idx, start, count):
    lane = lax.broadcasted_iota(jnp.int32, idx.shape, 1)
    parts = [
        jnp.where(idx == lane + (start + first), 1.0, 0.0).astype(BF16)
        for first in range(0, count, LANES)
    ]
    return jnp.concatenate(parts, axis=1)


def pick_rows(idx, table_refs):
    total, start = None, 0
    for ref in table_refs:
        rows = ref.shape[0]
        step = min(rows, CHUNK)
        for first in range(0, rows, step):
            part = dot(one_hot_columns(idx, start + first, step), ref[first : first + step, :])
            total = part if total is None else total + part
        start += rows
    return total


def one_hot_rows(idx_row, start, count):
    row = lax.broadcasted_iota(jnp.int32, (count, idx_row.shape[1]), 0) + start
    return jnp.where(jnp.broadcast_to(idx_row, row.shape) == row, 1.0, 0.0).astype(BF16)


def spread(column, width):
    return jnp.concatenate([column] * (width // LANES), axis=1)


def norm(value):
    centre = value - jnp.mean(value, -1, keepdims=True)
    scale = lax.rsqrt(jnp.mean(centre * centre, -1, keepdims=True) + EPS)
    return centre * scale, scale


def norm_back(inner, normed, scale):
    mean_first = jnp.mean(inner, -1, keepdims=True)
    mean_second = jnp.mean(inner * normed, -1, keepdims=True)
    return scale * (inner - mean_first - normed * mean_second)


def column_sum(value):
    return jnp.sum(value, axis=0, keepdims=True)


def whole(*_):
    return (0, 0)


def const_spec(shape):
    return pl.BlockSpec(shape, lambda *_: (0,) * len(shape), pipeline_mode=pl.Buffered(1))


def slot_block(slots):
    for size in (12, 10, 8, 6, 5, 4, 3, 2):
        if slots % size == 0:
            return size
    return 1


def message_forward_kernel(
    sb, node_lo, node_hi, node_own, edge, idx, live_col, m1, b1, m2, b2,
    a1_out, s1_out, s2_out, sum_out, far_lo, far_hi, own_part,
):
    step = pl.program_id(0)
    width = node_own.shape[1]
    edge_width = edge.shape[2]
    rows = edge.shape[1]

    @pl.when(step == 0)
    def _():
        own_part[...] = dot(node_own[...], m1[:width, :]) + b1[...]
        tile = min(512, node_lo.shape[0])
        for source, target in ((node_lo, far_lo), (node_hi, far_hi)):
            def body(i, carry, source=source, target=target):
                at = pl.ds(pl.multiple_of(i * tile, tile), tile)
                target[at, :] = dot(source[at, :], m1[width + edge_width :, :]).astype(BF16)
                return carry
            lax.fori_loop(0, source.shape[0] // tile, body, 0)
        sum_out[...] = jnp.zeros_like(sum_out)

    flat = edge[...].reshape(sb * rows, edge_width)
    mixed = pick_rows(idx[...], (far_lo, far_hi)) + dot(flat, m1[width : width + edge_width, :])
    z_one = (mixed.reshape(sb, rows, width) + own_part[...][None]).reshape(sb * rows, width)
    act, slope = gelu_parts(z_one)
    act = act.astype(BF16)
    a1_out[...] = act
    s1_out[...] = slope.astype(BF16)
    act, slope = gelu_parts(dot(act, m2[...]) + b2[...])
    s2_out[...] = slope.astype(BF16)
    act = act.astype(BF16).astype(F32).reshape(sb, rows, width)
    count = live_col[...]
    inverse = 1.0 / count.astype(F32)
    total = sum_out[...]
    for s in range(sb):
        share = jnp.where(count > step * sb + s, inverse, 0.0)
        total = total + act[s] * spread(share, width)
    sum_out[...] = total


def message_forward(node_lo, node_hi, node_own, edge, idx, live_col, m1, b1, m2, b2):
    slots, rows, edge_width = edge.shape
    width = node_own.shape[1]
    sb = slot_block(slots)
    edges = slots * rows
    block = sb * rows
    return pl.pallas_call(
        functools.partial(message_forward_kernel, sb),
        grid=(slots // sb,),
        in_specs=[
            const_spec(node_lo.shape),
            const_spec(node_hi.shape),
            const_spec(node_own.shape),
            pl.BlockSpec((sb, rows, edge_width), lambda i: (i, 0, 0)),
            pl.BlockSpec((block, LANES), lambda i: (i, 0)),
            const_spec(live_col.shape),
            const_spec(m1.shape),
            const_spec(b1.shape),
            const_spec(m2.shape),
            const_spec(b2.shape),
        ],
        out_specs=[
            pl.BlockSpec((block, width), lambda i: (i, 0)),
            pl.BlockSpec((block, width), lambda i: (i, 0)),
            pl.BlockSpec((block, width), lambda i: (i, 0)),
            pl.BlockSpec((rows, width), lambda i: (0, 0)),
        ],
        out_shape=[
            jax.ShapeDtypeStruct((edges, width), BF16),
            jax.ShapeDtypeStruct((edges, width), BF16),
            jax.ShapeDtypeStruct((edges, width), BF16),
            jax.ShapeDtypeStruct((rows, width), F32),
        ],
        scratch_shapes=[
            pltpu.VMEM(node_lo.shape, BF16),
            pltpu.VMEM(node_hi.shape, BF16),
            pltpu.VMEM((rows, width), F32),
        ],
        compiler_params=pltpu.CompilerParams(vmem_limit_bytes=56 * MIB),
        name="message_forward",
        cost_estimate=pl.CostEstimate(
            flops=2 * edges * width * (2 * node_lo.shape[0] + edge_width + width),
            bytes_accessed=edges * width * 6 + edges * edge_width * 2 + edges * LANES * 4,
            transcendentals=2 * edges * width,
        ),
    )(node_lo, node_hi, node_own, edge, idx, live_col, m1, b1, m2, b2)


def residue_forward_kernel(
    parts, node, total, m3, b3, g1, fb1, fb2, g2, e_own, e_far, eb, *refs
):
    f1, f2, fb1_parts = refs[:parts], refs[parts : 2 * parts], fb1
    h1b_out, n1_out, sc1_out, n2_out, sc2_out, slope_out, h2b_out, far_out, own_out = refs[2 * parts :]
    hidden = f1[0].shape[1]
    u1 = node[...].astype(F32) + fine(dot, total[...], m3[...]) + b3[...]
    n1, sc1 = norm(u1)
    h1 = n1 * g1[...]
    h1b = h1.astype(BF16)
    h1b_out[...] = h1b
    n1_out[...] = n1
    sc1_out[...] = jnp.broadcast_to(sc1, sc1_out.shape)
    y2 = None
    for p in range(parts):
        act, slope = gelu_parts(dot(h1b, f1[p][...]) + fb1_parts[p : p + 1, :])
        slope_out[:, p * hidden : (p + 1) * hidden] = slope
        part = dot(act.astype(BF16), f2[p][...])
        y2 = part if y2 is None else y2 + part
    n2, sc2 = norm(h1 + (y2 + fb2[...]))
    h2b = (n2 * g2[...]).astype(BF16)
    n2_out[...] = n2
    sc2_out[...] = jnp.broadcast_to(sc2, sc2_out.shape)
    h2b_out[...] = h2b
    far_out[...] = dot_back(h2b, e_far[...]).astype(BF16)
    own_out[...] = dot_back(h2b, e_own[...]) + eb[...]


def residue_forward(node, total, m3, b3, g1, fb1, fb2, g2, e_own, e_far, eb, f1, f2):
    rows, width = node.shape
    edge_width = e_own.shape[0]
    hidden = len(f1) * f1[0].shape[1]
    shapes = [
        ((rows, width), BF16),
        ((rows, width), F32),
        ((rows, LANES), F32),
        ((rows, width), F32),
        ((rows, LANES), F32),
        ((rows, hidden), F32),
        ((rows, width), BF16),
        ((rows, edge_width), BF16),
        ((rows, edge_width), F32),
    ]
    args = (node, total, m3, b3, g1, fb1, fb2, g2, e_own, e_far, eb, *f1, *f2)
    return pl.pallas_call(
        functools.partial(residue_forward_kernel, len(f1)),
        in_specs=[pl.BlockSpec(memory_space=pltpu.VMEM)] * len(args),
        out_specs=[pl.BlockSpec(memory_space=pltpu.VMEM)] * len(shapes),
        out_shape=[jax.ShapeDtypeStruct(*s) for s in shapes],
        compiler_params=pltpu.CompilerParams(vmem_limit_bytes=24 * MIB),
        name="residue_forward",
        cost_estimate=pl.CostEstimate(
            flops=4 * rows * width * hidden, bytes_accessed=5 * MIB, transcendentals=rows * hidden
        ),
    )(*args)


def edge_kernel(
    sb, blocks, hi_chunks, far_lo, far_hi, own, edge, cot, idx, idx_row, live_col,
    e1, e2, eb2, e3, eb3, g3,
    edge_out, part_out, hi_out, lo_out, own_out, e1g, e2g, e3g, bias_out,
    low_first, b1s, b2s, b3s, gs,
):
    step = pl.program_id(0)
    rows, width = own.shape

    @pl.when(step == 0)
    def _():
        for ref in (own_out, e1g, e2g, e3g, b2s, b3s, gs):
            ref[...] = jnp.zeros_like(ref)

    @pl.when(step < blocks)
    def _():
        block = sb * rows
        flat = edge[...].reshape(block, width)
        mixed = pick_rows(idx[...], (far_lo, far_hi)) + dot_back(flat, e1[...])
        w_one = (mixed.reshape(sb, rows, width) + own[...][None]).reshape(block, width)
        act_one, slope_one = gelu_parts(w_one)
        act_one = act_one.astype(BF16)
        act_two, slope_two = gelu_parts(dot(act_one, e2[...]) + eb2[...])
        act_two = act_two.astype(BF16)
        w_three = dot(act_two, e3[...]) + eb3[...]
        normed, scale = norm(flat.astype(F32) + w_three)
        count = live_col[...]
        live = jnp.concatenate(
            [jnp.where(count > step * sb + s, 1.0, 0.0)[:, :1] for s in range(sb)], axis=0
        )
        edge_out[...] = (normed * g3[...] * live).astype(BF16).reshape(sb, rows, width)
        grad = cot[...].reshape(block, width).astype(F32) * live
        gs[...] += jnp.sum((grad * normed).reshape(sb, rows, width), axis=0)
        grad_sum = norm_back(grad * g3[...], normed, scale)
        low_three = grad_sum.astype(BF16)
        e3g[...] += dot_rows(act_two, low_three)
        b3s[...] += jnp.sum(low_three.astype(F32).reshape(sb, rows, width), axis=0)
        low_two = (dot_back(low_three, e3[...]) * slope_two).astype(BF16)
        e2g[...] += dot_rows(act_one, low_two)
        b2s[...] += jnp.sum(low_two.astype(F32).reshape(sb, rows, width), axis=0)
        low_one = (dot_back(low_two, e2[...]) * slope_one).astype(BF16)
        e1g[...] += dot_rows(low_one, flat)
        own_out[...] += jnp.sum(low_one.astype(F32).reshape(sb, rows, width), axis=0)
        part_out[...] = (grad_sum + dot(low_one, e1[...])).reshape(sb, rows, width)
        low_first[pl.ds(pl.multiple_of(step * block, block), block), :] = low_one

    chunk = hi_out.shape[0]

    @pl.when((step >= blocks) & (step < blocks + hi_chunks))
    def _():
        start = (step - blocks + hi_chunks) * chunk
        hi_out[...] = dot(one_hot_rows(idx_row[...], start, chunk), low_first[...]).astype(BF16)

    @pl.when(step >= blocks + hi_chunks)
    def _():
        start = (step - blocks - hi_chunks) * chunk
        lo_out[...] = dot(one_hot_rows(idx_row[...], start, chunk), low_first[...])

    @pl.when(step == blocks + 2 * hi_chunks - 1)
    def _():
        bias_out[...] = jnp.concatenate(
            [
                column_sum(own_out[...]),
                column_sum(b2s[...]),
                column_sum(b3s[...]),
                column_sum(gs[...]),
                jnp.zeros((4, width), F32),
            ],
            axis=0,
        )


def edge_branch(far_lo, far_hi, own, edge, cot, idx, idx_row, live_col, e1, e2, eb2, e3, eb3, g3):
    slots, rows, width = edge.shape
    sb = slot_block(slots)
    edges = slots * rows
    block = sb * rows
    blocks = slots // sb
    half = far_lo.shape[0]
    chunk = min(512, half)
    hi_chunks = half // chunk
    blk = lambda i: jnp.minimum(i, blocks - 1)
    hi_at = lambda i: (jnp.clip(i - blocks, 0, hi_chunks - 1), 0)
    lo_at = lambda i: (jnp.clip(i - blocks - hi_chunks, 0, hi_chunks - 1), 0)
    slot_spec = pl.BlockSpec((sb, rows, width), lambda i: (blk(i), 0, 0))
    return pl.pallas_call(
        functools.partial(edge_kernel, sb, blocks, hi_chunks),
        grid=(blocks + 2 * hi_chunks,),
        in_specs=[
            const_spec(far_lo.shape),
            const_spec(far_hi.shape),
            const_spec(own.shape),
            slot_spec,
            slot_spec,
            pl.BlockSpec((block, LANES), lambda i: (blk(i), 0)),
            const_spec(idx_row.shape),
            const_spec(live_col.shape),
            const_spec(e1.shape),
            const_spec(e2.shape),
            const_spec(eb2.shape),
            const_spec(e3.shape),
            const_spec(eb3.shape),
            const_spec(g3.shape),
        ],
        out_specs=[
            slot_spec,
            slot_spec,
            pl.BlockSpec((chunk, width), hi_at),
            pl.BlockSpec((chunk, width), lo_at),
            pl.BlockSpec((rows, width), whole),
            pl.BlockSpec((width, width), whole),
            pl.BlockSpec((width, width), whole),
            pl.BlockSpec((width, width), whole),
            pl.BlockSpec((8, width), whole),
        ],
        out_shape=[
            jax.ShapeDtypeStruct((slots, rows, width), BF16),
            jax.ShapeDtypeStruct((slots, rows, width), F32),
            jax.ShapeDtypeStruct((half, width), BF16),
            jax.ShapeDtypeStruct((half, width), F32),
            jax.ShapeDtypeStruct((rows, width), F32),
            jax.ShapeDtypeStruct((width, width), F32),
            jax.ShapeDtypeStruct((width, width), F32),
            jax.ShapeDtypeStruct((width, width), F32),
            jax.ShapeDtypeStruct((8, width), F32),
        ],
        scratch_shapes=[pltpu.VMEM((edges, width), BF16)] + [pltpu.VMEM((rows, width), F32)] * 4,
        compiler_params=pltpu.CompilerParams(vmem_limit_bytes=56 * MIB),
        name="edge_branch",
        cost_estimate=pl.CostEstimate(
            flops=2 * edges * width * (4 * half + 9 * width),
            bytes_accessed=edges * width * 10 + edges * LANES * 4,
            transcendentals=2 * edges * width,
        ),
    )(far_lo, far_hi, own, edge, cot, idx, idx_row, live_col, e1, e2, eb2, e3, eb3, g3)


def residue_backward_kernel(
    parts, pieces, node_cot, own_sum, e_own, e_far, h2b, n1, sc1, n2, sc2, slope, g1, g2, m3, total,
    *refs,
):
    far = refs[:pieces]
    f1 = refs[pieces : pieces + parts]
    f2 = refs[pieces + parts : pieces + 2 * parts]
    gu1_out, v_out, gy2_out, e1own_out, e1far_out, m3g_out, bias_out = refs[pieces + 2 * parts :]
    hidden = f1[0].shape[1]
    far_sum = far[0][...]
    for ref in far[1:]:
        far_sum = far_sum + ref[...].astype(F32)
    own = own_sum[...]
    g_h2 = (
        node_cot[...].astype(F32) + fine(dot, own, e_own[...]) + fine(dot, far_sum, e_far[...])
    )
    e1own_out[...] = dot_rows(own.astype(BF16), h2b[...]).astype(BF16)
    e1far_out[...] = dot_rows(far_sum.astype(BF16), h2b[...]).astype(BF16)
    gain_two = column_sum(g_h2 * n2[...])
    g_u2 = norm_back(g_h2 * g2[...], n2[...], sc2[:, :1])
    gy2 = g_u2.astype(BF16)
    gy2_out[...] = gy2
    g_h1 = g_u2
    for p in range(parts):
        gy1 = dot_back(gy2, f2[p][...]) * slope[:, p * hidden : (p + 1) * hidden]
        g_h1 = g_h1 + dot_back(gy1.astype(BF16), f1[p][...])
    gain_one = column_sum(g_h1 * n1[...])
    g_u1 = norm_back(g_h1 * g1[...], n1[...], sc1[:, :1])
    gu1_out[...] = g_u1
    v_out[...] = fine(dot_back, g_u1, m3[...])
    m3g_out[...] = dot_rows(total[...].astype(BF16), g_u1.astype(BF16)).astype(BF16)
    bias_out[...] = jnp.concatenate(
        [
            gain_one,
            gain_two,
            column_sum(gy2.astype(F32)),
            column_sum(g_u1),
            jnp.zeros((4, g_u1.shape[1]), F32),
        ],
        axis=0,
    )


def residue_backward(
    node_cot, own_sum, e_own, e_far, h2b, n1, sc1, n2, sc2, slope, g1, g2, m3, total, far, f1, f2
):
    rows, width = h2b.shape
    edge_width = e_own.shape[0]
    shapes = [
        ((rows, width), F32),
        ((rows, width), F32),
        ((rows, width), BF16),
        ((edge_width, width), BF16),
        ((edge_width, width), BF16),
        ((width, width), BF16),
        ((8, width), F32),
    ]
    args = (
        node_cot, own_sum, e_own, e_far, h2b, n1, sc1, n2, sc2, slope, g1, g2, m3, total,
        *far, *f1, *f2,
    )
    return pl.pallas_call(
        functools.partial(residue_backward_kernel, len(f1), len(far)),
        in_specs=[pl.BlockSpec(memory_space=pltpu.VMEM)] * len(args),
        out_specs=[pl.BlockSpec(memory_space=pltpu.VMEM)] * len(shapes),
        out_shape=[jax.ShapeDtypeStruct(*s) for s in shapes],
        compiler_params=pltpu.CompilerParams(vmem_limit_bytes=24 * MIB),
        name="residue_backward",
        cost_estimate=pl.CostEstimate(
            flops=4 * rows * width * slope.shape[1], bytes_accessed=6 * MIB, transcendentals=0
        ),
    )(*args)


def feed_kernel(h1b, gy2, f1, fb1, f2, f1g, f2g, fb1g):
    act, slope = gelu_parts(dot(h1b[...], f1[...]) + fb1[...])
    f2g[...] = dot_rows(act.astype(BF16), gy2[...]).astype(BF16)
    gy1 = (dot_back(gy2[...], f2[...]) * slope).astype(BF16)
    f1g[...] = dot_rows(h1b[...], gy1).astype(BF16)
    fb1g[...] = jnp.broadcast_to(column_sum(gy1.astype(F32)), fb1g.shape)


def feed_gradients(h1b, gy2, f1, fb1, f2):
    args = (h1b, gy2, f1, fb1, f2)
    return pl.pallas_call(
        feed_kernel,
        in_specs=[pl.BlockSpec(memory_space=pltpu.VMEM)] * len(args),
        out_specs=[pl.BlockSpec(memory_space=pltpu.VMEM)] * 3,
        out_shape=[
            jax.ShapeDtypeStruct(f1.shape, BF16),
            jax.ShapeDtypeStruct(f2.shape, BF16),
            jax.ShapeDtypeStruct((8, f1.shape[1]), F32),
        ],
        compiler_params=pltpu.CompilerParams(vmem_limit_bytes=24 * MIB),
        name="feed_gradients",
        cost_estimate=pl.CostEstimate(
            flops=8 * h1b.shape[0] * f1.shape[0] * f1.shape[1],
            bytes_accessed=3 * MIB,
            transcendentals=h1b.shape[0] * f1.shape[1],
        ),
    )(*args)


def message_backward_kernel(
    sb, blocks, hi_chunks, v, a1, s1, s2, edge, part, idx_row, live_col, m1e, m2,
    node_lo, node_hi,
    edge_grad, hi_out, lo_out, own_out, m2g, m1eg, m1fg, bias_out,
    low_first, b2s,
):
    step = pl.program_id(0)
    rows, width = v.shape
    edge_width = edge.shape[2]

    @pl.when(step == 0)
    def _():
        for ref in (own_out, m2g, m1eg, m1fg, b2s):
            ref[...] = jnp.zeros_like(ref)

    @pl.when(step < blocks)
    def _():
        block = sb * rows
        count = live_col[...]
        inverse = 1.0 / count.astype(F32)
        grads = [
            v[...] * spread(jnp.where(count > step * sb + s, inverse, 0.0), width)
            for s in range(sb)
        ]
        low_two = (jnp.concatenate(grads, axis=0) * s2[...].astype(F32)).astype(BF16)
        m2g[...] += dot_rows(a1[...], low_two)
        b2s[...] += jnp.sum(low_two.astype(F32).reshape(sb, rows, width), axis=0)
        low_one = (dot_back(low_two, m2[...]) * s1[...].astype(F32)).astype(BF16)
        flat = edge[...].reshape(block, edge_width)
        m1eg[...] += dot_rows(flat, low_one)
        own_out[...] += jnp.sum(low_one.astype(F32).reshape(sb, rows, width), axis=0)
        grad = part[...].reshape(block, edge_width) + dot_back(low_one, m1e[...])
        edge_grad[...] = grad.reshape(sb, rows, edge_width)
        low_first[pl.ds(pl.multiple_of(step * block, block), block), :] = low_one

    chunk = hi_out.shape[0]

    @pl.when((step >= blocks) & (step < blocks + hi_chunks))
    def _():
        at = step - blocks
        start = (at + hi_chunks) * chunk
        sums = dot(one_hot_rows(idx_row[...], start, chunk), low_first[...]).astype(BF16)
        hi_out[...] = sums
        m1fg[...] += dot_rows(node_hi[pl.ds(pl.multiple_of(at * chunk, chunk), chunk), :], sums)

    @pl.when(step >= blocks + hi_chunks)
    def _():
        at = step - blocks - hi_chunks
        start = at * chunk
        sums = dot(one_hot_rows(idx_row[...], start, chunk), low_first[...])
        lo_out[...] = sums
        m1fg[...] += dot_rows(
            node_lo[pl.ds(pl.multiple_of(at * chunk, chunk), chunk), :], sums.astype(BF16)
        )

    @pl.when(step == blocks + 2 * hi_chunks - 1)
    def _():
        bias_out[...] = jnp.concatenate(
            [column_sum(own_out[...]), column_sum(b2s[...]), jnp.zeros((6, width), F32)], axis=0
        )


def message_backward(v, a1, s1, s2, edge, part, idx_row, live_col, m1e, m2, node_lo, node_hi):
    slots, rows, edge_width = edge.shape
    width = v.shape[1]
    sb = slot_block(slots)
    edges = slots * rows
    block = sb * rows
    blocks = slots // sb
    half = node_lo.shape[0]
    chunk = min(512, half)
    hi_chunks = half // chunk
    blk = lambda i: jnp.minimum(i, blocks - 1)
    hi_at = lambda i: (jnp.clip(i - blocks, 0, hi_chunks - 1), 0)
    lo_at = lambda i: (jnp.clip(i - blocks - hi_chunks, 0, hi_chunks - 1), 0)
    slot_spec = pl.BlockSpec((sb, rows, edge_width), lambda i: (blk(i), 0, 0))
    row_spec = pl.BlockSpec((block, width), lambda i: (blk(i), 0))
    return pl.pallas_call(
        functools.partial(message_backward_kernel, sb, blocks, hi_chunks),
        grid=(blocks + 2 * hi_chunks,),
        in_specs=[
            const_spec(v.shape),
            row_spec,
            row_spec,
            row_spec,
            slot_spec,
            slot_spec,
            const_spec(idx_row.shape),
            const_spec(live_col.shape),
            const_spec(m1e.shape),
            const_spec(m2.shape),
            const_spec(node_lo.shape),
            const_spec(node_hi.shape),
        ],
        out_specs=[
            slot_spec,
            pl.BlockSpec((chunk, width), hi_at),
            pl.BlockSpec((chunk, width), lo_at),
            pl.BlockSpec((rows, width), whole),
            pl.BlockSpec((width, width), whole),
            pl.BlockSpec((edge_width, width), whole),
            pl.BlockSpec((width, width), whole),
            pl.BlockSpec((8, width), whole),
        ],
        out_shape=[
            jax.ShapeDtypeStruct((slots, rows, edge_width), F32),
            jax.ShapeDtypeStruct((half, width), BF16),
            jax.ShapeDtypeStruct((half, width), F32),
            jax.ShapeDtypeStruct((rows, width), F32),
            jax.ShapeDtypeStruct((width, width), F32),
            jax.ShapeDtypeStruct((edge_width, width), F32),
            jax.ShapeDtypeStruct((width, width), F32),
            jax.ShapeDtypeStruct((8, width), F32),
        ],
        scratch_shapes=[pltpu.VMEM((edges, width), BF16), pltpu.VMEM((rows, width), F32)],
        compiler_params=pltpu.CompilerParams(vmem_limit_bytes=58 * MIB),
        name="message_backward",
        cost_estimate=pl.CostEstimate(
            flops=2 * edges * width * (2 * half + 2 * width + 2 * edge_width),
            bytes_accessed=edges * width * 6 + edges * edge_width * 10,
            transcendentals=0,
        ),
    )(v, a1, s1, s2, edge, part, idx_row, live_col, m1e, m2, node_lo, node_hi)


def node_kernel(pieces, g_u1, own, node, m1, *refs):
    far = refs[:pieces]
    grad_out, m1og_out = refs[pieces:]
    width = own.shape[1]
    far_sum = far[0][...]
    for ref in far[1:]:
        far_sum = far_sum + ref[...].astype(F32)
    far_first = m1.shape[0] - width
    grad_out[...] = (
        g_u1[...]
        + fine(dot_back, own[...], m1[:width, :])
        + fine(dot_back, far_sum, m1[far_first:, :])
    )
    m1og_out[...] = dot_rows(node[...], own[...].astype(BF16))


def node_last(g_u1, own, node, m1, far):
    args = (g_u1, own, node, m1, *far)
    return pl.pallas_call(
        functools.partial(node_kernel, len(far)),
        in_specs=[pl.BlockSpec(memory_space=pltpu.VMEM)] * len(args),
        out_specs=[pl.BlockSpec(memory_space=pltpu.VMEM)] * 2,
        out_shape=[
            jax.ShapeDtypeStruct(own.shape, F32),
            jax.ShapeDtypeStruct((own.shape[1], own.shape[1]), F32),
        ],
        compiler_params=pltpu.CompilerParams(vmem_limit_bytes=16 * MIB),
        name="node_last",
    )(*args)


def exchange(value, mask, devices):
    return lax.ppermute(value, AXES, [(d, d ^ mask) for d in range(devices)])


def mask_groups(bits):
    masks = [1 << b for b in range(bits - 1, 0, -1)]
    return [masks[i : i + 2] for i in range(0, len(masks), 2)] + [[1]]


def combined(group, code):
    mask = 0
    for bit, part in enumerate(group):
        if code >> bit & 1:
            mask |= part
    return mask


def gather_pieces(value, groups, devices):
    for at, group in enumerate(groups):
        pieces = [value]
        for code in range(1, 1 << len(group)):
            pieces.append(exchange(value, combined(group, code), devices))
        if at + 1 == len(groups):
            return pieces
        value = jnp.concatenate(pieces, axis=0)


def scatter_sums(keep, send, groups, devices):
    received = [exchange(send, 1, devices)]
    for group in reversed(groups[:-1]):
        total = keep
        for part in received:
            total = total + part.astype(F32)
        parts = 1 << len(group)
        rows = total.shape[0] // parts
        keep = total[:rows]
        received = [
            exchange(
                total[code * rows : (code + 1) * rows].astype(BF16), combined(group, code), devices
            )
            for code in range(1, parts)
        ]
    return [keep] + received


def per_device(
    node_in,
    edge_in,
    neighbours,
    live_counts,
    message_first,
    message_first_bias,
    message_second,
    message_second_bias,
    message_third,
    message_third_bias,
    norm_one,
    feed_first,
    feed_first_bias,
    feed_second,
    feed_second_bias,
    norm_two,
    edge_first,
    edge_first_bias,
    edge_second,
    edge_second_bias,
    edge_third,
    edge_third_bias,
    norm_three,
    node_cotangent,
    edge_cotangent,
):
    rows, slots = neighbours.shape
    width = node_in.shape[1]
    edge_width = edge_in.shape[2]
    edges = rows * slots
    hid_count = lax.axis_size("hid")
    devices = lax.axis_size("res") * hid_count
    bits = devices.bit_length() - 1
    groups = mask_groups(bits)
    order = [mask for group in groups for mask in group]
    hid_groups = [g for g in ([m for m in group if m < hid_count] for group in groups) if g]
    me = lax.axis_index("res") * hid_count + lax.axis_index("hid")

    row = lambda vector: vector.reshape(1, -1)

    node_lo, node_hi = gather_pieces(node_in, groups, devices)

    feed_pieces = [feed_first, feed_second, row(feed_first_bias)]
    f1, f2, fb1 = [
        [p] for p in feed_pieces
    ]
    for group in reversed(hid_groups):
        new = []
        for held in (f1, f2, fb1):
            got = list(held)
            for code in range(1, 1 << len(group)):
                got += [exchange(p, combined(group, code), devices) for p in held]
            new.append(got)
        f1, f2, fb1 = new
    fb1 = jnp.concatenate(fb1, axis=0)

    names = neighbours.T.reshape(edges)
    apart = (names // rows) ^ me
    place = jnp.zeros_like(names)
    for bit, mask in enumerate(order):
        place = place | jnp.where((apart & mask) != 0, 1 << bit, 0)
    place = place * rows + names % rows
    idx_row = place.reshape(1, edges)
    idx = jnp.broadcast_to(place[:, None], (edges, LANES))
    live_col = jnp.broadcast_to(live_counts[:, None], (rows, LANES))
    edge = edge_in.transpose(1, 0, 2)
    cot = edge_cotangent.transpose(1, 0, 2)
    first_t = edge_first.T
    e_own, e_mid, e_far = (
        first_t[:, :width],
        first_t[:, width : width + edge_width],
        first_t[:, width + edge_width :],
    )

    a1, s1, s2, total = message_forward(
        node_lo, node_hi, node_in, edge, idx, live_col,
        message_first, row(message_first_bias), message_second, row(message_second_bias),
    )
    h1b, n1, sc1, n2, sc2, slope, h2b, far_part, own_part = residue_forward(
        node_in, total, message_third, row(message_third_bias), row(norm_one), fb1,
        row(feed_second_bias), row(norm_two), e_own, e_far, row(edge_first_bias), f1, f2,
    )
    q_lo, q_hi = gather_pieces(far_part, groups, devices)
    h1b_group = h1b
    for group in hid_groups:
        h1b_group = jnp.concatenate(
            [h1b_group]
            + [exchange(h1b_group, combined(group, c), devices) for c in range(1, 1 << len(group))],
            axis=0,
        )
    edge_out, part, hi, lo, own_sum, e1g, e2g, e3g, edge_bias = edge_branch(
        q_lo, q_hi, own_part, edge, cot, idx, idx_row, live_col, e_mid,
        edge_second, row(edge_second_bias), edge_third, row(edge_third_bias), row(norm_three),
    )
    far_terms = scatter_sums(lo, hi, groups, devices)
    g_u1, v, gy2, e1og, e1fg, m3g, res_bias = residue_backward(
        node_cotangent, own_sum, e_own, e_far, h2b, n1, sc1, n2, sc2, slope,
        row(norm_one), row(norm_two), message_third, total, far_terms, f1, f2,
    )
    gy2_group = gy2
    for group in hid_groups:
        gy2_group = jnp.concatenate(
            [gy2_group]
            + [exchange(gy2_group, combined(group, c), devices) for c in range(1, 1 << len(group))],
            axis=0,
        )
    early = lax.psum(
        (
            e1og,
            e1g.astype(BF16),
            e1fg,
            e2g.astype(BF16),
            e3g.astype(BF16),
            m3g,
            edge_bias,
            res_bias,
        ),
        AXES,
    )
    f1g, f2g, fb1g = feed_gradients(
        h1b_group, gy2_group, feed_first, row(feed_first_bias), feed_second
    )
    feed = lax.psum((f1g, f2g, fb1g), "res")

    edge_grad, hi, lo, own, m2g, m1eg, m1fg, message_bias = message_backward(
        v, a1, s1, s2, edge, part, idx_row, live_col,
        message_first[width : width + edge_width], message_second, node_lo, node_hi,
    )
    far_terms = scatter_sums(lo, hi, groups, devices)
    node_gradient, m1og = node_last(g_u1, own, node_in, message_first, far_terms)
    late = lax.psum(
        (
            jnp.concatenate([m1og, m1eg, m1fg], axis=0).astype(BF16),
            m2g.astype(BF16),
            message_bias,
        ),
        AXES,
    )
    e1og, e1g, e1fg, e2g, e3g, m3g, edge_bias, res_bias = early
    first_grad = jnp.concatenate([e1og, e1g, e1fg], axis=1).T.astype(F32)
    m1g, m2g, message_bias = late
    return (
        h2b,
        edge_out.transpose(1, 0, 2),
        node_gradient,
        edge_grad.transpose(1, 0, 2),
        m1g.astype(F32),
        message_bias[0],
        m2g.astype(F32),
        message_bias[1],
        m3g.astype(F32),
        res_bias[3],
        res_bias[0],
        feed[0].astype(F32),
        feed[2][0],
        feed[1].astype(F32),
        res_bias[2],
        res_bias[1],
        first_grad,
        edge_bias[0],
        e2g.astype(F32),
        edge_bias[1],
        e3g.astype(F32),
        edge_bias[2],
        edge_bias[3],
    )


def solution(mesh):
    nodes, edges, shared = P(AXES, None), P(AXES, None, None), P()
    return jax.shard_map(
        per_device,
        mesh=mesh,
        in_specs=(nodes, edges, nodes, P(AXES))
        + (shared,) * 7
        + (P(None, "hid"), P("hid"), P("hid", None))
        + (shared,) * 9
        + (nodes, edges),
        out_specs=(nodes, edges, nodes, edges)
        + (shared,) * 7
        + (P(None, "hid"), P("hid"), P("hid", None))
        + (shared,) * 9,
        check_vma=False,
    )
```

```python
import functools

import jax
import jax.numpy as jnp
from jax import lax
from jax.experimental import pallas as pl
from jax.experimental.pallas import tpu as pltpu
from jax.sharding import PartitionSpec as P

EPS = 1e-05
AXES = ("res", "hid")
F32 = jnp.float32
BF16 = jnp.bfloat16
TANH_SCALE = 0.7978845608028654
TANH_CUBE = 0.044715
LANES = 128
CHUNK = 2048
MIB = 1024 * 1024


def dot(left, right):
    return lax.dot_general(left, right, (((1,), (0,)), ((), ())), preferred_element_type=F32)


def dot_rows(left, right):
    return lax.dot_general(left, right, (((0,), (0,)), ((), ())), preferred_element_type=F32)


def dot_back(left, right):
    return lax.dot_general(left, right, (((1,), (1,)), ((), ())), preferred_element_type=F32)


def halves(value):
    high = value.astype(BF16)
    return high, (value - high.astype(F32)).astype(BF16)


def fine(product, value, weights):
    high, low = halves(value)
    return product(high, weights) + product(low, weights)


def gelu_parts(x):
    square = x * x
    t = jnp.tanh(x * (TANH_SCALE + (TANH_SCALE * TANH_CUBE) * square))
    gate = 0.5 + 0.5 * t
    act = x * gate
    slope = gate + act * (1.0 - gate) * (2 * TANH_SCALE + (6 * TANH_SCALE * TANH_CUBE) * square)
    return act, slope


def one_hot_columns(idx, start, count):
    lane = lax.broadcasted_iota(jnp.int32, idx.shape, 1)
    parts = [
        jnp.where(idx == lane + (start + first), 1.0, 0.0).astype(BF16)
        for first in range(0, count, LANES)
    ]
    return jnp.concatenate(parts, axis=1)


def pick_rows(idx, table_refs):
    total, start = None, 0
    for ref in table_refs:
        rows = ref.shape[0]
        step = min(rows, CHUNK)
        for first in range(0, rows, step):
            part = dot(one_hot_columns(idx, start + first, step), ref[first : first + step, :])
            total = part if total is None else total + part
        start += rows
    return total


def one_hot_rows(idx_row, start, count):
    row = lax.broadcasted_iota(jnp.int32, (count, idx_row.shape[1]), 0) + start
    return jnp.where(jnp.broadcast_to(idx_row, row.shape) == row, 1.0, 0.0).astype(BF16)


def spread(column, width):
    return jnp.concatenate([column] * (width // LANES), axis=1)


def norm(value):
    centre = value - jnp.mean(value, -1, keepdims=True)
    scale = lax.rsqrt(jnp.mean(centre * centre, -1, keepdims=True) + EPS)
    return centre * scale, scale


def norm_back(inner, normed, scale):
    mean_first = jnp.mean(inner, -1, keepdims=True)
    mean_second = jnp.mean(inner * normed, -1, keepdims=True)
    return scale * (inner - mean_first - normed * mean_second)


def column_sum(value):
    return jnp.sum(value, axis=0, keepdims=True)


def whole(*_):
    return (0, 0)


def const_spec(shape):
    return pl.BlockSpec(shape, lambda *_: (0,) * len(shape), pipeline_mode=pl.Buffered(1))


def small_call(kernel, args, shapes, name, vmem, scratch=(), flops=0, moved=0, exps=0, scalars=0):
    return pl.pallas_call(
        kernel,
        grid=(1,),
        in_specs=[pl.BlockSpec(memory_space=pltpu.SMEM)] * scalars
        + [const_spec(a.shape) for a in args[scalars:]],
        out_specs=[pl.BlockSpec(s, lambda *_, n=len(s): (0,) * n) for s, _ in shapes],
        out_shape=[jax.ShapeDtypeStruct(*s) for s in shapes],
        scratch_shapes=list(scratch),
        compiler_params=pltpu.CompilerParams(vmem_limit_bytes=vmem * MIB),
        name=name,
        cost_estimate=pl.CostEstimate(flops=flops, bytes_accessed=moved, transcendentals=exps),
    )(*args)


def tile_count(shape):
    return pl.cdiv(shape[0], 16) * pl.cdiv(shape[1], LANES)


def slab_tiles(shapes, chunks):
    return pl.cdiv(sum(tile_count(s) for s in shapes), chunks) * chunks


def pack(slab, values):
    at = 0
    for value in values:
        rows, columns = value.shape
        count = rows // 16
        for first in range(0, columns, LANES):
            take = min(LANES, columns - first)
            tile = value[:, first : first + take].astype(BF16).reshape(count, 16, take)
            slab[at : at + count, :, :take] = tile
            at += count


def unpack(slab, at, rows, columns):
    count = rows // 16
    parts = [
        slab[at + i * count : at + (i + 1) * count].reshape(rows, LANES).astype(F32)
        for i in range(pl.cdiv(columns, LANES))
    ]
    return jnp.concatenate(parts, axis=1)


def order_out(slab, base, codes, keep, send):
    size = slab.shape[0] // len(codes)
    half = len(codes) // 2
    for place, code in enumerate(codes):
        out = keep if place < half else send
        at = (place % half) * size
        out[at : at + size] = slab[pl.ds((base ^ code) * size, size)]


def order_in(slab, base, codes, first, second):
    size = slab.shape[0] // len(codes)
    half = len(codes) // 2
    for place, code in enumerate(codes):
        source = first if place < half else second
        at = (place % half) * size
        slab[pl.ds((base ^ code) * size, size)] = source[at : at + size]


def half_shapes(tiles):
    return [((tiles // 2, 16, LANES), BF16)] * 2


def slab_scratch(tiles):
    return pltpu.VMEM((tiles, 16, LANES), BF16)


def padded_rows(parts, width):
    return jnp.concatenate(parts + [jnp.zeros((16 - len(parts), width), F32)], axis=0)


def slot_block(slots):
    for size in (10, 12, 8, 6, 5, 4, 3, 2):
        if slots % size == 0:
            return size
    return 1


def message_forward_kernel(sb, first_block, blocks, fresh, node_own, edge, idx, live_col, m1, b1, m2, b2, *refs):
    if fresh:
        node_lo, node_hi = refs[:2]
        a1_out, s1_out, s2_out, sum_out, own_part, lo_out, hi_out, far_lo, far_hi, sems = refs[2:]
    else:
        far_lo, far_hi, own_part, sum_in = refs[:4]
        a1_out, s1_out, s2_out, sum_out = refs[4:]
    step = pl.program_id(0)
    width = node_own.shape[1]
    edge_width = edge.shape[2]
    rows = edge.shape[1]

    @pl.when(step == 0)
    def _():
        if not fresh:
            sum_out[...] = sum_in[...]
            return
        sum_out[...] = jnp.zeros_like(sum_out)
        own_part[...] = dot(node_own[...], m1[:width, :]) + b1[...]
        tile = min(512, node_lo.shape[0])
        for source, target in ((node_lo, far_lo), (node_hi, far_hi)):
            def body(i, carry, source=source, target=target):
                at = pl.ds(pl.multiple_of(i * tile, tile), tile)
                target[at, :] = dot(source[at, :], m1[width + edge_width :, :]).astype(BF16)
                return carry
            lax.fori_loop(0, source.shape[0] // tile, body, 0)
        pltpu.make_async_copy(far_lo, lo_out, sems.at[0]).start()
        pltpu.make_async_copy(far_hi, hi_out, sems.at[1]).start()

    flat = edge[...].reshape(sb * rows, edge_width)
    mixed = pick_rows(idx[...], (far_lo, far_hi)) + dot(flat, m1[width : width + edge_width, :])
    z_one = (mixed.reshape(sb, rows, width) + own_part[...][None]).reshape(sb * rows, width)
    act, slope = gelu_parts(z_one)
    act = act.astype(BF16)
    a1_out[...] = act
    s1_out[...] = slope.astype(BF16)
    act, slope = gelu_parts(dot(act, m2[...]) + b2[...])
    s2_out[...] = slope.astype(BF16)
    act = act.astype(BF16).astype(F32).reshape(sb, rows, width)
    count = live_col[...]
    inverse = 1.0 / count.astype(F32)
    total = sum_out[...]
    for s in range(sb):
        share = jnp.where(count > (step + first_block) * sb + s, inverse, 0.0)
        total = total + act[s] * spread(share, width)
    sum_out[...] = total

    if fresh:
        @pl.when(step == blocks - 1)
        def _():
            pltpu.make_async_copy(far_lo, lo_out, sems.at[0]).wait()
            pltpu.make_async_copy(far_hi, hi_out, sems.at[1]).wait()


def message_forward(first_block, blocks, node_own, edge, idx, live_col, m1, b1, m2, b2, more):
    slots, rows, edge_width = edge.shape
    width = node_own.shape[1]
    sb = slot_block(slots)
    block = sb * rows
    edges = blocks * block
    fresh = len(more) == 2
    half = more[0].shape
    out_specs = [pl.BlockSpec((block, width), lambda i: (i, 0))] * 3 + [pl.BlockSpec((rows, width), whole)]
    out_shape = [jax.ShapeDtypeStruct((edges, width), BF16)] * 3 + [
        jax.ShapeDtypeStruct((rows, width), F32)
    ]
    scratch = []
    if fresh:
        out_specs += [pl.BlockSpec((rows, width), whole)] + [pl.BlockSpec(memory_space=pl.ANY)] * 2
        out_shape += [jax.ShapeDtypeStruct((rows, width), F32)] + [jax.ShapeDtypeStruct(half, BF16)] * 2
        scratch = [pltpu.VMEM(half, BF16), pltpu.VMEM(half, BF16), pltpu.SemaphoreType.DMA((2,))]
    return pl.pallas_call(
        functools.partial(message_forward_kernel, sb, first_block, blocks, fresh),
        grid=(blocks,),
        in_specs=[
            const_spec(node_own.shape),
            pl.BlockSpec((sb, rows, edge_width), lambda i: (i + first_block, 0, 0)),
            pl.BlockSpec((block, LANES), lambda i: (i + first_block, 0)),
            const_spec(live_col.shape),
            const_spec(m1.shape),
            const_spec(b1.shape),
            const_spec(m2.shape),
            const_spec(b2.shape),
        ]
        + [const_spec(a.shape) for a in more],
        out_specs=out_specs,
        out_shape=out_shape,
        scratch_shapes=scratch,
        compiler_params=pltpu.CompilerParams(vmem_limit_bytes=56 * MIB),
        name="message_forward",
        cost_estimate=pl.CostEstimate(
            flops=2 * edges * width * (2 * half[0] + edge_width + width),
            bytes_accessed=edges * width * 6 + edges * edge_width * 2 + edges * LANES * 4,
            transcendentals=2 * edges * width,
        ),
    )(node_own, edge, idx, live_col, m1, b1, m2, b2, *more)


def residue_forward_kernel(parts, node, total, m3, b3, g1, fb2, g2, e_own, e_far, eb, *refs):
    f1, f2 = refs[:parts], refs[parts : 2 * parts]
    h1b_out, n1_out, sc1_out, n2_out, sc2_out, slope_out, h2b_out, far_out, own_out = refs[2 * parts :]
    width, hidden = node.shape[1], f1[0].shape[1]
    u1 = node[...].astype(F32) + fine(dot, total[...], m3[...]) + b3[...]
    n1, sc1 = norm(u1)
    h1 = n1 * g1[...]
    h1b = h1.astype(BF16)
    h1b_out[...] = h1b
    n1_out[...] = n1
    sc1_out[...] = jnp.broadcast_to(sc1, sc1_out.shape)
    y2 = None
    for p in range(parts):
        bias = f1[p][width : width + 16, :].astype(F32)
        bias = bias[0:1] + bias[1:2] + bias[2:3]
        act, slope = gelu_parts(dot(h1b, f1[p][:width, :]) + bias)
        slope_out[:, p * hidden : (p + 1) * hidden] = slope
        part = dot(act.astype(BF16), f2[p][...])
        y2 = part if y2 is None else y2 + part
    n2, sc2 = norm(h1 + (y2 + fb2[...]))
    h2b = (n2 * g2[...]).astype(BF16)
    n2_out[...] = n2
    sc2_out[...] = jnp.broadcast_to(sc2, sc2_out.shape)
    h2b_out[...] = h2b
    far_out[...] = dot_back(h2b, e_far[...]).astype(BF16)
    own_out[...] = dot_back(h2b, e_own[...]) + eb[...]


def residue_forward(node, total, m3, b3, g1, fb2, g2, e_own, e_far, eb, f1, f2):
    rows, width = node.shape
    edge_width = e_own.shape[0]
    hidden = len(f1) * f1[0].shape[1]
    shapes = [
        ((rows, width), BF16),
        ((rows, width), F32),
        ((rows, LANES), F32),
        ((rows, width), F32),
        ((rows, LANES), F32),
        ((rows, hidden), F32),
        ((rows, width), BF16),
        ((rows, edge_width), BF16),
        ((rows, edge_width), F32),
    ]
    return small_call(
        functools.partial(residue_forward_kernel, len(f1)),
        (node, total, m3, b3, g1, fb2, g2, e_own, e_far, eb, *f1, *f2),
        shapes, "residue_forward", 24, flops=4 * rows * width * hidden, moved=5 * MIB,
        exps=rows * hidden,
    )


def edge_kernel(
    sb, blocks, hi_chunks, far_lo, far_hi, own, edge, cot, idx, idx_row, live_col,
    e1, e2, eb2, e3, eb3, g3,
    edge_out, part_out, hi_out, lo_out, own_out, e1g, e2g, e3g, bias_out,
    low_first, b1s, b2s, b3s, gs,
):
    step = pl.program_id(0)
    rows, width = own.shape

    @pl.when(step == 0)
    def _():
        for ref in (own_out, e1g, e2g, e3g, b2s, b3s, gs):
            ref[...] = jnp.zeros_like(ref)

    @pl.when(step < blocks)
    def _():
        block = sb * rows
        flat = edge[...].reshape(block, width)
        mixed = pick_rows(idx[...], (far_lo, far_hi)) + dot_back(flat, e1[...])
        w_one = (mixed.reshape(sb, rows, width) + own[...][None]).reshape(block, width)
        act_one, slope_one = gelu_parts(w_one)
        act_one = act_one.astype(BF16)
        act_two, slope_two = gelu_parts(dot(act_one, e2[...]) + eb2[...])
        act_two = act_two.astype(BF16)
        w_three = dot(act_two, e3[...]) + eb3[...]
        normed, scale = norm(flat.astype(F32) + w_three)
        count = live_col[...]
        count = spread(count, pl.cdiv(width, LANES) * LANES)[:, :width]
        live = jnp.concatenate(
            [jnp.where(count > step * sb + s, 1.0, 0.0) for s in range(sb)], axis=0
        )
        edge_out[...] = (normed * g3[...] * live).astype(BF16).reshape(sb, rows, width)
        grad = cot[...].reshape(block, width).astype(F32) * live
        gs[...] += jnp.sum((grad * normed).reshape(sb, rows, width), axis=0)
        grad_sum = norm_back(grad * g3[...], normed, scale)
        low_three = grad_sum.astype(BF16)
        e3g[...] += dot_rows(act_two, low_three)
        b3s[...] += jnp.sum(low_three.astype(F32).reshape(sb, rows, width), axis=0)
        low_two = (dot_back(low_three, e3[...]) * slope_two).astype(BF16)
        e2g[...] += dot_rows(act_one, low_two)
        b2s[...] += jnp.sum(low_two.astype(F32).reshape(sb, rows, width), axis=0)
        low_one = (dot_back(low_two, e2[...]) * slope_one).astype(BF16)
        e1g[...] += dot_rows(low_one, flat)
        own_out[...] += jnp.sum(low_one.astype(F32).reshape(sb, rows, width), axis=0)
        part_out[...] = (grad_sum + dot(low_one, e1[...])).reshape(sb, rows, width)
        low_first[pl.ds(pl.multiple_of(step * block, block), block), :] = low_one

    chunk = hi_out.shape[0]

    @pl.when((step >= blocks) & (step < blocks + hi_chunks))
    def _():
        start = (step - blocks + hi_chunks) * chunk
        hi_out[...] = dot(one_hot_rows(idx_row[...], start, chunk), low_first[...]).astype(BF16)

    @pl.when(step >= blocks + hi_chunks)
    def _():
        start = (step - blocks - hi_chunks) * chunk
        lo_out[...] = dot(one_hot_rows(idx_row[...], start, chunk), low_first[...])

    @pl.when(step == blocks + 2 * hi_chunks - 1)
    def _():
        bias_out[...] = jnp.concatenate(
            [
                column_sum(own_out[...]),
                column_sum(b2s[...]),
                column_sum(b3s[...]),
                column_sum(gs[...]),
                jnp.zeros((4, width), F32),
            ],
            axis=0,
        )


def edge_branch(far_lo, far_hi, own, edge, cot, idx, idx_row, live_col, e1, e2, eb2, e3, eb3, g3):
    slots, rows, width = edge.shape
    sb = slot_block(slots)
    edges = slots * rows
    block = sb * rows
    blocks = slots // sb
    half = far_lo.shape[0]
    chunk = min(512, half)
    hi_chunks = half // chunk
    blk = lambda i: jnp.minimum(i, blocks - 1)
    hi_at = lambda i: (jnp.clip(i - blocks, 0, hi_chunks - 1), 0)
    lo_at = lambda i: (jnp.clip(i - blocks - hi_chunks, 0, hi_chunks - 1), 0)
    slot_spec = pl.BlockSpec((sb, rows, width), lambda i: (blk(i), 0, 0))
    return pl.pallas_call(
        functools.partial(edge_kernel, sb, blocks, hi_chunks),
        grid=(blocks + 2 * hi_chunks,),
        in_specs=[
            const_spec(far_lo.shape),
            const_spec(far_hi.shape),
            const_spec(own.shape),
            slot_spec,
            slot_spec,
            pl.BlockSpec((block, LANES), lambda i: (blk(i), 0)),
            const_spec(idx_row.shape),
            const_spec(live_col.shape),
            const_spec(e1.shape),
            const_spec(e2.shape),
            const_spec(eb2.shape),
            const_spec(e3.shape),
            const_spec(eb3.shape),
            const_spec(g3.shape),
        ],
        out_specs=[
            slot_spec,
            slot_spec,
            pl.BlockSpec((chunk, width), hi_at),
            pl.BlockSpec((chunk, width), lo_at),
            pl.BlockSpec((rows, width), whole),
            pl.BlockSpec((width, width), whole),
            pl.BlockSpec((width, width), whole),
            pl.BlockSpec((width, width), whole),
            pl.BlockSpec((8, width), whole),
        ],
        out_shape=[
            jax.ShapeDtypeStruct((slots, rows, width), BF16),
            jax.ShapeDtypeStruct((slots, rows, width), F32),
            jax.ShapeDtypeStruct((half, width), BF16),
            jax.ShapeDtypeStruct((half, width), F32),
            jax.ShapeDtypeStruct((rows, width), F32),
            jax.ShapeDtypeStruct((width, width), F32),
            jax.ShapeDtypeStruct((width, width), F32),
            jax.ShapeDtypeStruct((width, width), F32),
            jax.ShapeDtypeStruct((8, width), F32),
        ],
        scratch_shapes=[pltpu.VMEM((edges, width), BF16)] + [pltpu.VMEM((rows, width), F32)] * 4,
        compiler_params=pltpu.CompilerParams(vmem_limit_bytes=56 * MIB),
        name="edge_branch",
        cost_estimate=pl.CostEstimate(
            flops=2 * edges * width * (4 * half + 9 * width),
            bytes_accessed=edges * width * 10 + edges * LANES * 4,
            transcendentals=2 * edges * width,
        ),
    )(far_lo, far_hi, own, edge, cot, idx, idx_row, live_col, e1, e2, eb2, e3, eb3, g3)


def early_shapes(width, edge_width):
    return [
        (width, width),
        (edge_width, width),
        (edge_width, edge_width),
        (edge_width, width),
        (edge_width, edge_width),
        (edge_width, edge_width),
        (16, width),
        (16, edge_width),
    ]


def residue_backward_kernel(
    parts, pieces, codes, base, node_cot, own_sum, e_own, e_far, h2b, n1, sc1, n2, sc2, slope, g1, g2, m3,
    total, e1g, e2g, e3g, edge_bias, *refs,
):
    far = refs[:pieces]
    f1 = refs[pieces : pieces + parts]
    f2 = refs[pieces + parts : pieces + 2 * parts]
    gu1_out, v_out, gy2_out, keep, send, slab = refs[pieces + 2 * parts :]
    width, hidden = h2b.shape[1], f1[0].shape[1]
    far_sum = far[0][...]
    for ref in far[1:]:
        far_sum = far_sum + ref[...].astype(F32)
    own = own_sum[...]
    g_h2 = (
        node_cot[...].astype(F32) + fine(dot, own, e_own[...]) + fine(dot, far_sum, e_far[...])
    )
    gain_two = column_sum(g_h2 * n2[...])
    g_u2 = norm_back(g_h2 * g2[...], n2[...], sc2[:, :1])
    gy2 = g_u2.astype(BF16)
    gy2_out[...] = gy2
    g_h1 = g_u2
    for p in range(parts):
        gy1 = dot_back(gy2, f2[p][...]) * slope[:, p * hidden : (p + 1) * hidden]
        g_h1 = g_h1 + dot_back(gy1.astype(BF16), f1[p][:width, :])
    gain_one = column_sum(g_h1 * n1[...])
    g_u1 = norm_back(g_h1 * g1[...], n1[...], sc1[:, :1])
    gu1_out[...] = g_u1
    v_out[...] = fine(dot_back, g_u1, m3[...])
    bias = [gain_one, gain_two, column_sum(gy2.astype(F32)), column_sum(g_u1)]
    slab[...] = jnp.zeros_like(slab)
    pack(
        slab,
        [
            dot_rows(total[...].astype(BF16), g_u1.astype(BF16)),
            dot_rows(own.astype(BF16), h2b[...]),
            e1g[...],
            dot_rows(far_sum.astype(BF16), h2b[...]),
            e2g[...],
            e3g[...],
            padded_rows(bias, width),
            jnp.concatenate([edge_bias[...], jnp.zeros_like(edge_bias[...])], axis=0),
        ],
    )
    order_out(slab, base[0], codes, keep, send)


def residue_backward(codes, base, args, far, f1, f2):
    node_cot, e_own, slope = args[0], args[2], args[9]
    rows, width = node_cot.shape
    tiles = slab_tiles(early_shapes(width, e_own.shape[0]), len(codes))
    shapes = [((rows, width), F32), ((rows, width), F32), ((rows, width), BF16)] + half_shapes(tiles)
    return small_call(
        functools.partial(residue_backward_kernel, len(f1), len(far), codes),
        (base, *args, *far, *f1, *f2),
        shapes, "residue_backward", 32, [slab_scratch(tiles)],
        flops=4 * rows * width * slope.shape[1], moved=8 * MIB, scalars=1,
    )


def early_out_kernel(codes, base, first, second, m3g, e1g, e2g, e3g, b3, g1, g2, fb2, eb1, eb2, eb3, g3, slab):
    order_in(slab, base[0], codes, first, second)
    width, edge_width = m3g.shape[0], e2g.shape[0]
    starts, at = [], 0
    for shape in early_shapes(width, edge_width):
        starts.append(at)
        at += tile_count(shape)
    m3g[...] = unpack(slab, starts[0], width, width)
    e1g[:, :width] = unpack(slab, starts[1], edge_width, width)
    middle = unpack(slab, starts[2], edge_width, edge_width)
    far = unpack(slab, starts[3], edge_width, width)
    over = edge_width % LANES
    base_col = width + edge_width - over
    e1g[:, width:base_col] = middle[:, : edge_width - over]
    far = pltpu.roll(jnp.concatenate([far, jnp.zeros((edge_width, LANES), F32)], axis=1), over, 1)
    lane = lax.broadcasted_iota(jnp.int32, (edge_width, LANES), 1)
    e1g[:, base_col : base_col + LANES] = jnp.where(
        lane < over, middle[:, edge_width - over : edge_width - over + LANES], far[:, :LANES]
    )
    rest = e1g.shape[1] - base_col - LANES
    e1g[:, base_col + LANES :] = far[:, LANES : LANES + rest]
    e2g[...] = unpack(slab, starts[4], edge_width, edge_width)[:, :edge_width]
    e3g[...] = unpack(slab, starts[5], edge_width, edge_width)[:, :edge_width]
    bias = unpack(slab, starts[6], 16, width)
    for row, out in enumerate((g1, g2, fb2, b3)):
        out[...] = bias[row : row + 1]
    bias = unpack(slab, starts[7], 16, edge_width)
    for row, out in enumerate((eb1, eb2, eb3, g3)):
        out[...] = bias[row : row + 1, :edge_width]


def early_out(codes, base, halves_in, width, edge_width):
    shapes = [(width, width), (edge_width, 2 * width + edge_width), (edge_width, edge_width)]
    shapes += [(edge_width, edge_width)] + [(1, width)] * 4 + [(1, edge_width)] * 4
    tiles = slab_tiles(early_shapes(width, edge_width), len(codes))
    return small_call(
        functools.partial(early_out_kernel, codes),
        (base, *halves_in), [(s, F32) for s in shapes], "early_gradients", 24,
        [slab_scratch(tiles)], moved=4 * MIB, scalars=1,
    )


def feed_shapes(width, hidden):
    return [(width, hidden), (hidden, width), (16, hidden)]


def feed_kernel(count, codes, base, f1, fb1, f2, *refs):
    keep, send, slab = refs[2 * count :]
    h1b = jnp.concatenate([r[...] for r in refs[:count]], axis=0)
    gy2 = jnp.concatenate([r[...] for r in refs[count : 2 * count]], axis=0)
    act, slope = gelu_parts(dot(h1b, f1[...]) + fb1[...])
    gy1 = (dot_back(gy2, f2[...]) * slope).astype(BF16)
    slab[...] = jnp.zeros_like(slab)
    pack(
        slab,
        [
            dot_rows(h1b, gy1),
            dot_rows(act.astype(BF16), gy2),
            padded_rows([column_sum(gy1.astype(F32))], f1.shape[1]),
        ],
    )
    order_out(slab, base[0], codes, keep, send)


def feed_gradients(codes, base, f1, fb1, f2, h1b, gy2):
    width, hidden = f1.shape
    tiles = slab_tiles(feed_shapes(width, hidden), len(codes))
    rows = len(h1b) * h1b[0].shape[0]
    return small_call(
        functools.partial(feed_kernel, len(h1b), codes),
        (base, f1, fb1, f2, *h1b, *gy2), half_shapes(tiles), "feed_gradients", 24,
        [slab_scratch(tiles)], flops=8 * rows * width * hidden, moved=3 * MIB, exps=rows * hidden,
        scalars=1,
    )


def feed_out_kernel(codes, base, first, second, f1g, f2g, fb1g, slab):
    order_in(slab, base[0], codes, first, second)
    (width, hidden), at = f1g.shape, 0
    f1g[...] = unpack(slab, at, width, hidden)
    at += tile_count((width, hidden))
    f2g[...] = unpack(slab, at, hidden, width)
    at += tile_count((hidden, width))
    fb1g[...] = unpack(slab, at, 16, hidden)[:1]


def feed_out(codes, base, halves_in, width, hidden):
    tiles = slab_tiles(feed_shapes(width, hidden), len(codes))
    return small_call(
        functools.partial(feed_out_kernel, codes),
        (base, *halves_in), [((width, hidden), F32), ((hidden, width), F32), ((1, hidden), F32)],
        "feed_weight_gradients", 24, [slab_scratch(tiles)], moved=4 * MIB, scalars=1,
    )


def late_shapes(width, edge_width):
    return [(width, width), (width, width), (edge_width, width), (16, width)]


def message_backward_kernel(sb, first_block, blocks, codes, *refs):
    last = codes is not None
    if last:
        base, refs = refs[0], refs[1:]
    v, a1, s1, s2, edge, live_col, m1e, m2 = refs[:8]
    refs = refs[8:]
    if last:
        node, own_in, m2g_in, m1eg_in, b2_in, low_out, own, keep, send, m2g, m1eg, b2s, slab = refs
    else:
        low_out, own, m2g, m1eg, b2s = refs
    step = pl.program_id(0)
    rows, width = v.shape
    edge_width = edge.shape[2]
    block = sb * rows

    @pl.when(step == 0)
    def _():
        if last:
            own[...] = own_in[...]
            m2g[...] = m2g_in[...]
            m1eg[...] = m1eg_in[...]
            b2s[...] = b2_in[...]
        else:
            for ref in (own, m2g, m1eg, b2s):
                ref[...] = jnp.zeros_like(ref)

    count = live_col[...]
    inverse = 1.0 / count.astype(F32)
    grads = [
        v[...] * spread(jnp.where(count > (step + first_block) * sb + s, inverse, 0.0), width)
        for s in range(sb)
    ]
    low_two = (jnp.concatenate(grads, axis=0) * s2[...].astype(F32)).astype(BF16)
    m2g[...] += dot_rows(a1[...], low_two)
    b2s[...] += jnp.sum(low_two.astype(F32).reshape(sb, rows, width), axis=0)
    low_one = (dot_back(low_two, m2[...]) * s1[...].astype(F32)).astype(BF16)
    low_out[...] = low_one
    m1eg[...] += dot_rows(edge[...].reshape(block, edge_width), low_one)
    own[...] += jnp.sum(low_one.astype(F32).reshape(sb, rows, width), axis=0)

    if last:
        @pl.when(step == blocks - 1)
        def _():
            slab[...] = jnp.zeros_like(slab)
            bias = [column_sum(own[...]), column_sum(b2s[...])]
            pack(
                slab,
                [
                    dot_rows(node[...], own[...].astype(BF16)),
                    m2g[...],
                    m1eg[...],
                    padded_rows(bias, width),
                ],
            )
            order_out(slab, base[0], codes, keep, send)


def message_backward(first_block, blocks, v, a1, s1, s2, edge, live_col, m1e, m2, more=()):
    slots, rows, edge_width = edge.shape
    width = v.shape[1]
    sb = slot_block(slots)
    block = sb * rows
    edges = blocks * block
    row_spec = pl.BlockSpec((block, width), lambda i: (i, 0))
    sums = [(rows, width), (width, width), (edge_width, width), (rows, width)]
    in_specs = [
        const_spec(v.shape),
        row_spec,
        row_spec,
        row_spec,
        pl.BlockSpec((sb, rows, edge_width), lambda i: (i + first_block, 0, 0)),
        const_spec(live_col.shape),
        const_spec(m1e.shape),
        const_spec(m2.shape),
    ]
    args = [v, a1, s1, s2, edge, live_col, m1e, m2]
    codes, scratch = None, []
    outs = [(s, F32) for s in sums]
    if more:
        codes, base, *rest = more
        args = [base] + args + rest
        in_specs = [pl.BlockSpec(memory_space=pltpu.SMEM)] + in_specs + [const_spec(a.shape) for a in rest]
        tiles = slab_tiles(late_shapes(width, edge_width), len(codes))
        outs = [(sums[0], F32)] + half_shapes(tiles)
        scratch = [pltpu.VMEM(s, F32) for s in sums[1:]] + [slab_scratch(tiles)]
    return pl.pallas_call(
        functools.partial(message_backward_kernel, sb, first_block, blocks, codes),
        grid=(blocks,),
        in_specs=in_specs,
        out_specs=[row_spec]
        + [pl.BlockSpec(s, lambda i, n=len(s): (0,) * n) for s, _ in outs],
        out_shape=[jax.ShapeDtypeStruct((edges, width), BF16)]
        + [jax.ShapeDtypeStruct(*s) for s in outs],
        scratch_shapes=scratch,
        compiler_params=pltpu.CompilerParams(vmem_limit_bytes=48 * MIB),
        name="message_backward",
        cost_estimate=pl.CostEstimate(
            flops=2 * edges * width * (2 * width + 2 * edge_width),
            bytes_accessed=edges * width * 8 + edges * edge_width * 2,
            transcendentals=0,
        ),
    )(*args)


def far_sums_kernel(start, steps, codes, *refs):
    last = codes is not None
    if last:
        base, idx_row, low_a, low_b, node, m1fg_in, out, keep, send, m1fg, slab = refs
    else:
        idx_row, low_a, low_b, node, out, m1fg = refs
    step = pl.program_id(0)
    chunk = out.shape[0]
    cut = low_a.shape[0]

    @pl.when(step == 0)
    def _():
        m1fg[...] = m1fg_in[...] if last else jnp.zeros_like(m1fg)

    first = start + step * chunk
    sums = dot(one_hot_rows(idx_row[:, :cut], first, chunk), low_a[...]) + dot(
        one_hot_rows(idx_row[:, cut:], first, chunk), low_b[...]
    )
    out[...] = sums.astype(out.dtype)
    m1fg[...] += dot_rows(node[...], sums.astype(BF16))

    if last:
        @pl.when(step == steps - 1)
        def _():
            if slab.shape[0] * 16 * LANES > m1fg.size:
                slab[...] = jnp.zeros_like(slab)
            pack(slab, [m1fg[...]])
            order_out(slab, base[0], codes, keep, send)


def far_sums(start, idx_row, low_a, low_b, node, dtype, more=()):
    rows, width = node.shape
    chunk = min(512, rows)
    steps = rows // chunk
    args = [idx_row, low_a, low_b, node]
    in_specs = [const_spec(a.shape) for a in args[:3]] + [pl.BlockSpec((chunk, width), lambda i: (i, 0))]
    outs, codes, scratch = [((width, width), F32)], None, []
    if more:
        codes, base, m1fg = more
        args = [base] + args + [m1fg]
        in_specs = [pl.BlockSpec(memory_space=pltpu.SMEM)] + in_specs + [const_spec(m1fg.shape)]
        tiles = slab_tiles([(width, width)], len(codes))
        outs = half_shapes(tiles)
        scratch = [pltpu.VMEM((width, width), F32), slab_scratch(tiles)]
    edges = idx_row.shape[1]
    return pl.pallas_call(
        functools.partial(far_sums_kernel, start, steps, codes),
        grid=(steps,),
        in_specs=in_specs,
        out_specs=[pl.BlockSpec((chunk, width), lambda i: (i, 0))]
        + [pl.BlockSpec(s, lambda i, n=len(s): (0,) * n) for s, _ in outs],
        out_shape=[jax.ShapeDtypeStruct((rows, width), dtype)]
        + [jax.ShapeDtypeStruct(*s) for s in outs],
        scratch_shapes=scratch,
        compiler_params=pltpu.CompilerParams(vmem_limit_bytes=48 * MIB),
        name="far_sums",
        cost_estimate=pl.CostEstimate(
            flops=2 * width * rows * (edges + width),
            bytes_accessed=edges * width * 2 + rows * width * 5,
            transcendentals=0,
        ),
    )(*args)


def edge_gradient_kernel(sb, cut, part, low_a, low_b, m1e, out):
    step = pl.program_id(0)
    shape = part.shape
    for low, use in ((low_a, step < cut), (low_b, step >= cut)):
        @pl.when(use)
        def _(low=low):
            out[...] = part[...] + dot_back(low[...], m1e[...]).reshape(shape)


def edge_gradient(part, low_a, low_b, m1e):
    slots, rows, edge_width = part.shape
    width = low_a.shape[1]
    sb = slot_block(slots)
    block = sb * rows
    cut = low_a.shape[0] // block
    spec = pl.BlockSpec((sb, rows, edge_width), lambda i: (i, 0, 0))
    return pl.pallas_call(
        functools.partial(edge_gradient_kernel, sb, cut),
        grid=(slots // sb,),
        in_specs=[
            spec,
            pl.BlockSpec((block, width), lambda i: (jnp.minimum(i, cut - 1), 0)),
            pl.BlockSpec((block, width), lambda i: (jnp.maximum(i - cut, 0), 0)),
            const_spec(m1e.shape),
        ],
        out_specs=spec,
        out_shape=jax.ShapeDtypeStruct(part.shape, F32),
        compiler_params=pltpu.CompilerParams(vmem_limit_bytes=32 * MIB),
        name="edge_gradient",
        cost_estimate=pl.CostEstimate(
            flops=2 * slots * rows * width * edge_width,
            bytes_accessed=slots * rows * (width * 2 + 2048),
            transcendentals=0,
        ),
    )(part, low_a, low_b, m1e)


def node_kernel(pieces, g_u1, own, m1, *refs):
    far, grad_out = refs[:pieces], refs[pieces]
    width = own.shape[1]
    far_sum = far[0][...]
    for ref in far[1:]:
        far_sum = far_sum + ref[...].astype(F32)
    far_first = m1.shape[0] - width
    grad_out[...] = (
        g_u1[...]
        + fine(dot_back, own[...], m1[:width, :])
        + fine(dot_back, far_sum, m1[far_first:, :])
    )


def node_last(g_u1, own, m1, far):
    return small_call(
        functools.partial(node_kernel, len(far)),
        (g_u1, own, m1, *far), [(own.shape, F32)], "node_gradient", 16,
        flops=8 * own.size * own.shape[1], moved=2 * MIB,
    )[0]


def late_out_kernel(codes, base, first, second, far_first, far_second, m1g, m2g, b1, b2, slab, far_slab):
    order_in(slab, base[0], codes, first, second)
    order_in(far_slab, base[0], codes, far_first, far_second)
    width = m2g.shape[0]
    edge_width = m1g.shape[0] - 2 * width
    starts, at = [], 0
    for shape in late_shapes(width, edge_width):
        starts.append(at)
        at += tile_count(shape)
    m1g[:width, :] = unpack(slab, starts[0], width, width)
    m2g[...] = unpack(slab, starts[1], width, width)
    m1g[width : width + edge_width, :] = unpack(slab, starts[2], edge_width, width)
    m1g[width + edge_width :, :] = unpack(far_slab, 0, width, width)
    bias = unpack(slab, starts[3], 16, width)
    b1[...] = bias[0:1]
    b2[...] = bias[1:2]


def late_out(codes, base, slab_halves, far_halves, width, edge_width):
    shapes = [(2 * width + edge_width, width), (width, width), (1, width), (1, width)]
    tiles = slab_tiles(late_shapes(width, edge_width), len(codes))
    far_tiles = slab_tiles([(width, width)], len(codes))
    return small_call(
        functools.partial(late_out_kernel, codes),
        (base, *slab_halves, *far_halves), [(s, F32) for s in shapes], "late_gradients", 24,
        [slab_scratch(tiles), slab_scratch(far_tiles)], moved=6 * MIB, scalars=1,
    )


def exchange(value, mask, devices):
    return lax.ppermute(value, AXES, [(d, d ^ mask) for d in range(devices)])


def mask_groups(masks):
    return [masks[i : min(i + 2, len(masks) - 1)] for i in range(0, len(masks) - 1, 2)] + [masks[-1:]]


def order_codes(groups):
    masks = [mask for group in groups for mask in group]
    return [
        sum(mask for bit, mask in enumerate(masks) if place >> bit & 1)
        for place in range(1 << len(masks))
    ]


def combined(group, code):
    return sum(mask for bit, mask in enumerate(group) if code >> bit & 1)


def gather_pieces(value, groups, devices, hooks=()):
    for at, group in enumerate(groups):
        pieces = [value]
        for code in range(1, 1 << len(group)):
            pieces.append(exchange(value, combined(group, code), devices))
        if at + 1 == len(groups):
            return pieces
        value = jnp.concatenate(pieces, axis=0)
        if at < len(hooks):
            value = hooks[at](value)


def scatter_sums(keep, send, groups, devices):
    received = [exchange(send, groups[-1][0], devices)]
    for group in reversed(groups[:-1]):
        total = keep.astype(F32)
        for part in received:
            total = total + part.astype(F32)
        parts = 1 << len(group)
        rows = total.shape[0] // parts
        keep = total[:rows]
        received = [
            exchange(
                total[code * rows : (code + 1) * rows].astype(BF16), combined(group, code), devices
            )
            for code in range(1, parts)
        ]
    return [keep] + received


def slab_all_reduce(keep, send, groups, extra, devices):
    total = None
    for part in scatter_sums(keep, send, groups, devices):
        total = part.astype(F32) if total is None else total + part.astype(F32)
    for mask in extra:
        total = total + exchange(total.astype(BF16), mask, devices).astype(F32)
    return gather_pieces(total.astype(BF16), groups, devices)


def split_three(value):
    rows = []
    for _ in range(3):
        high = lax.reduce_precision(value, 8, 7)
        rows.append(high.astype(BF16))
        value = value - high
    return jnp.concatenate(rows + [jnp.zeros((13, value.shape[1]), BF16)], axis=0)


def per_device(
    node_in,
    edge_in,
    neighbours,
    live_counts,
    message_first,
    message_first_bias,
    message_second,
    message_second_bias,
    message_third,
    message_third_bias,
    norm_one,
    feed_first,
    feed_first_bias,
    feed_second,
    feed_second_bias,
    norm_two,
    edge_first,
    edge_first_bias,
    edge_second,
    edge_second_bias,
    edge_third,
    edge_third_bias,
    norm_three,
    node_cotangent,
    edge_cotangent,
):
    rows, slots = neighbours.shape
    width = node_in.shape[1]
    edge_width = edge_in.shape[2]
    edges = rows * slots
    hid_count = lax.axis_size("hid")
    res_count = lax.axis_size("res")
    devices = res_count * hid_count
    bits = devices.bit_length() - 1
    masks = [1 << b for b in range(bits - 1, -1, -1)]
    groups = mask_groups(masks)
    slab_masks = [m for m in masks if m < 32]
    slab_groups = mask_groups(slab_masks)
    slab_extra = [m for m in masks if m >= 32]
    slab_codes = order_codes(slab_groups)
    feed_groups = mask_groups([m for m in masks if m >= hid_count])
    feed_codes = [c // hid_count for c in order_codes(feed_groups)]
    me = lax.axis_index("res") * hid_count + lax.axis_index("hid")
    slab_base = (me % len(slab_codes)).reshape(1)
    feed_base = lax.axis_index("res").reshape(1)
    row = lambda vector: vector.reshape(1, -1)

    names = neighbours.T.reshape(edges)
    apart = (names // rows) ^ me
    place = jnp.zeros_like(names)
    for bit, mask in enumerate(masks):
        place = place | jnp.where((apart & mask) != 0, 1 << bit, 0)
    place = place * rows + names % rows
    idx_row = place.reshape(1, edges)
    idx = jnp.broadcast_to(place[:, None], (edges, LANES))
    live_col = jnp.broadcast_to(live_counts[:, None], (rows, LANES))
    edge = edge_in.transpose(1, 0, 2)
    cot = edge_cotangent.transpose(1, 0, 2)
    first_t = edge_first.T
    e_own, e_mid, e_far = (
        first_t[:, :width],
        first_t[:, width : width + edge_width],
        first_t[:, width + edge_width :],
    )
    m1e = message_first[width : width + edge_width]
    f1x = jnp.concatenate([feed_first, split_three(row(feed_first_bias))], axis=0)
    f2x = feed_second

    def first_hook(value):
        nonlocal idx_row, e_own, e_mid, e_far, m1e
        value, idx_row, e_own, e_mid, e_far, m1e = lax.optimization_barrier(
            (value, idx_row, e_own, e_mid, e_far, m1e)
        )
        return value

    def second_hook(value):
        nonlocal idx, live_col, f1x, f2x
        value, idx, live_col, f1x, f2x = lax.optimization_barrier((value, idx, live_col, f1x, f2x))
        return value

    node_lo, node_hi = gather_pieces(node_in, groups, devices, (first_hook, second_hook))

    f1, f2 = [f1x], [f2x]
    hid_masks = [m for m in masks if m < hid_count]
    for mask in hid_masks[:-1]:
        f1, f2 = [held + [exchange(p, mask, devices) for p in held] for held in (f1, f2)]

    sb = slot_block(slots)
    blocks = slots // sb
    cut = blocks // 2
    message_args = (
        node_in, edge, idx, live_col, message_first, row(message_first_bias), message_second,
        row(message_second_bias),
    )
    a1a, s1a, s2a, total, own_part, far_lo, far_hi = message_forward(
        0, cut, *message_args, (node_lo, node_hi)
    )
    total, f1, f2 = lax.optimization_barrier((total, f1, f2))
    f1, f2 = [held + [exchange(p, hid_masks[-1], devices) for p in held] for held in (f1, f2)]
    a1b, s1b, s2b, total = message_forward(
        cut, blocks - cut, *message_args, (far_lo, far_hi, own_part, total)
    )
    h1b, n1, sc1, n2, sc2, slope, h2b, far_part, own_part = residue_forward(
        node_in, total, message_third, row(message_third_bias), row(norm_one),
        row(feed_second_bias), row(norm_two), e_own, e_far, row(edge_first_bias), f1, f2,
    )
    q_lo, q_hi = gather_pieces(far_part, groups, devices)
    edge_out, part, hi, lo, own_sum, e1g, e2g, e3g, edge_bias = edge_branch(
        q_lo, q_hi, own_part, edge, cot, idx, idx_row, live_col, e_mid,
        edge_second, row(edge_second_bias), edge_third, row(edge_third_bias), row(norm_three),
    )
    group_pieces = lambda value: [value] + [
        exchange(value, mask, devices) for mask in range(1, hid_count)
    ]
    h1b_group = group_pieces(h1b)
    far_terms = scatter_sums(lo, hi, groups, devices)
    g_u1, v, gy2, early_keep, early_send = residue_backward(
        slab_codes, slab_base,
        (
            node_cotangent, own_sum, e_own, e_far, h2b, n1, sc1, n2, sc2, slope, row(norm_one),
            row(norm_two), message_third, total, e1g, e2g, e3g, edge_bias,
        ),
        far_terms, f1, f2,
    )
    early = slab_all_reduce(early_keep, early_send, slab_groups, slab_extra, devices)
    gy2_group = group_pieces(gy2)

    low_a, *sums = message_backward(
        0, cut, v, a1a, s1a, s2a, edge, live_col, m1e, message_second
    )
    feed_keep, feed_send = feed_gradients(
        feed_codes, feed_base, feed_first, row(feed_first_bias), feed_second, h1b_group, gy2_group
    )
    feed = slab_all_reduce(feed_keep, feed_send, feed_groups, (), devices)
    low_b, own, late_keep, late_send = message_backward(
        cut, blocks - cut, v, a1b, s1b, s2b, edge, live_col, m1e, message_second,
        (slab_codes, slab_base, node_in, *sums),
    )
    late = slab_all_reduce(late_keep, late_send, slab_groups, slab_extra, devices)
    half = node_lo.shape[0]
    hi, m1fg = far_sums(half, idx_row, low_a, low_b, node_hi, BF16)
    lo, far_keep, far_send = far_sums(
        0, idx_row, low_a, low_b, node_lo, F32, (slab_codes, slab_base, m1fg)
    )
    far_terms = scatter_sums(lo, hi, groups, devices)
    late_far = slab_all_reduce(far_keep, far_send, slab_groups, slab_extra, devices)
    edge_grad = edge_gradient(part, low_a, low_b, m1e)
    node_gradient = node_last(g_u1, own, message_first, far_terms)
    m3g, e1g, e2g, e3g, b3, g1, g2, fb2, eb1, eb2, eb3, g3 = early_out(
        slab_codes, slab_base, early, width, edge_width
    )
    f1g, f2g, fb1g = feed_out(feed_codes, feed_base, feed, width, feed_first.shape[1])
    m1g, m2g, b1, b2 = late_out(slab_codes, slab_base, late, late_far, width, edge_width)
    flat = lambda vector: vector.reshape(-1)
    return (
        h2b,
        edge_out.transpose(1, 0, 2),
        node_gradient,
        edge_grad.transpose(1, 0, 2),
        m1g,
        flat(b1),
        m2g,
        flat(b2),
        m3g,
        flat(b3),
        flat(g1),
        f1g,
        flat(fb1g),
        f2g,
        flat(fb2),
        flat(g2),
        e1g.T,
        flat(eb1),
        e2g,
        flat(eb2),
        e3g,
        flat(eb3),
        flat(g3),
    )


def solution(mesh):
    nodes, edges, shared = P(AXES, None), P(AXES, None, None), P()
    return jax.shard_map(
        per_device,
        mesh=mesh,
        in_specs=(nodes, edges, nodes, P(AXES))
        + (shared,) * 7
        + (P(None, "hid"), P("hid"), P("hid", None))
        + (shared,) * 9
        + (nodes, edges),
        out_specs=(nodes, edges, nodes, edges)
        + (shared,) * 7
        + (P(None, "hid"), P("hid"), P("hid", None))
        + (shared,) * 9,
        check_vma=False,
    )
```

```python
import functools

import jax
import jax.numpy as jnp
from jax import lax
from jax.experimental import pallas as pl
from jax.experimental.pallas import tpu as pltpu
from jax.sharding import PartitionSpec as P

EPS = 1e-05
AXES = ("res", "hid")
F32 = jnp.float32
BF16 = jnp.bfloat16
TANH_SCALE = 0.7978845608028654
TANH_CUBE = 0.044715
LANES = 128
CHUNK = 2048
MIB = 1024 * 1024
VMEM = 58 * MIB


def dot(left, right):
    return lax.dot_general(left, right, (((1,), (0,)), ((), ())), preferred_element_type=F32)


def dot_rows(left, right):
    return lax.dot_general(left, right, (((0,), (0,)), ((), ())), preferred_element_type=F32)


def dot_back(left, right):
    return lax.dot_general(left, right, (((1,), (1,)), ((), ())), preferred_element_type=F32)


def halves(value):
    high = value.astype(BF16)
    return high, (value - high.astype(F32)).astype(BF16)


def fine(product, value, weights):
    high, low = halves(value)
    return product(high, weights) + product(low, weights)


def gelu_parts(x):
    square = x * x
    t = jnp.tanh(x * (TANH_SCALE + (TANH_SCALE * TANH_CUBE) * square))
    gate = 0.5 + 0.5 * t
    act = x * gate
    slope = gate + act * (1.0 - gate) * (2 * TANH_SCALE + (6 * TANH_SCALE * TANH_CUBE) * square)
    return act, slope


def index_columns(idx_row):
    parts = [
        jnp.broadcast_to(idx_row[:, first : first + LANES], (LANES, LANES)).T
        for first in range(0, idx_row.shape[1], LANES)
    ]
    return jnp.concatenate(parts, axis=0)


def one_hot_columns(idx, start, count):
    lane = lax.broadcasted_iota(jnp.int32, idx.shape, 1)
    parts = [
        jnp.where(idx == lane + (start + first), 1.0, 0.0).astype(BF16)
        for first in range(0, count, LANES)
    ]
    return jnp.concatenate(parts, axis=1)


def pick_rows(idx, table_refs):
    total, start = None, 0
    for ref in table_refs:
        rows = ref.shape[0]
        step = min(rows, CHUNK)
        for first in range(0, rows, step):
            part = dot(one_hot_columns(idx, start + first, step), ref[first : first + step, :])
            total = part if total is None else total + part
        start += rows
    return total


def one_hot_rows(idx_row, start, count):
    row = lax.broadcasted_iota(jnp.int32, (count, idx_row.shape[1]), 0) + start
    return jnp.where(jnp.broadcast_to(idx_row, row.shape) == row, 1.0, 0.0).astype(BF16)


def spread(column, width):
    return jnp.concatenate([column] * (width // LANES), axis=1)


def norm(value):
    centre = value - jnp.mean(value, -1, keepdims=True)
    scale = lax.rsqrt(jnp.mean(centre * centre, -1, keepdims=True) + EPS)
    return centre * scale, scale


def norm_back(inner, normed, scale):
    mean_first = jnp.mean(inner, -1, keepdims=True)
    mean_second = jnp.mean(inner * normed, -1, keepdims=True)
    return scale * (inner - mean_first - normed * mean_second)


def column_sum(value):
    return jnp.sum(value, axis=0, keepdims=True)


def whole(*_):
    return (0, 0)


def const_spec(shape):
    return pl.BlockSpec(shape, lambda *_: (0,) * len(shape), pipeline_mode=pl.Buffered(1))


def small_call(kernel, args, shapes, name, scratch=(), flops=0, moved=0, exps=0, scalars=0):
    return pl.pallas_call(
        kernel,
        grid=(1,),
        in_specs=[pl.BlockSpec(memory_space=pltpu.SMEM)] * scalars
        + [const_spec(a.shape) for a in args[scalars:]],
        out_specs=[pl.BlockSpec(s, lambda *_, n=len(s): (0,) * n) for s, _ in shapes],
        out_shape=[jax.ShapeDtypeStruct(*s) for s in shapes],
        scratch_shapes=list(scratch),
        compiler_params=pltpu.CompilerParams(vmem_limit_bytes=VMEM),
        name=name,
        cost_estimate=pl.CostEstimate(flops=flops, bytes_accessed=moved, transcendentals=exps),
    )(*args)


def tile_count(shape):
    return pl.cdiv(shape[0], 16) * pl.cdiv(shape[1], LANES)


def all_tiles(shapes):
    return sum(tile_count(s) for s in shapes)


def pack(slab, values, at=0):
    for value in values:
        rows, columns = value.shape
        count = rows // 16
        for first in range(0, columns, LANES):
            take = min(LANES, columns - first)
            tile = value[:, first : first + take].astype(BF16).reshape(count, 16, take)
            slab[at : at + count, :, :take] = tile
            at += count


def unpack(slab, at, rows, columns):
    count = rows // 16
    parts = [
        slab[at + i * count : at + (i + 1) * count].reshape(rows, LANES).astype(F32)
        for i in range(pl.cdiv(columns, LANES))
    ]
    return jnp.concatenate(parts, axis=1)


def order_in(slab, base, codes, first, second):
    size = slab.shape[0] // len(codes)
    half = len(codes) // 2
    for place, code in enumerate(codes):
        source = first if place < half else second
        at = (place % half) * size
        slab[pl.ds((base ^ code) * size, size)] = source[at : at + size]


def padded_rows(parts, width):
    return jnp.concatenate(parts + [jnp.zeros((16 - len(parts), width), F32)], axis=0)


def slot_block(slots):
    for size in (10, 12, 8, 6, 5, 4, 3, 2):
        if slots % size == 0:
            return size
    return 1


def message_forward_kernel(sb, first_block, blocks, fresh, node_own, edge, idx_row, live_col, m1, b1, m2, b2, *refs):
    if fresh:
        node_lo, node_hi = refs[:2]
        a1_out, s1_out, s2_out, sum_out, own_part, lo_out, hi_out, far_lo, far_hi, sems = refs[2:]
    else:
        far_lo, far_hi, own_part, sum_in = refs[:4]
        a1_out, s1_out, s2_out, sum_out = refs[4:]
    step = pl.program_id(0)
    width = node_own.shape[1]
    edge_width = edge.shape[2]
    rows = edge.shape[1]

    @pl.when(step == 0)
    def _():
        if not fresh:
            sum_out[...] = sum_in[...]
            return
        sum_out[...] = jnp.zeros_like(sum_out)
        own_part[...] = dot(node_own[...], m1[:width, :]) + b1[...]
        tile = min(512, node_lo.shape[0])
        for source, target in ((node_lo, far_lo), (node_hi, far_hi)):
            def body(i, carry, source=source, target=target):
                at = pl.ds(pl.multiple_of(i * tile, tile), tile)
                target[at, :] = dot(source[at, :], m1[width + edge_width :, :]).astype(BF16)
                return carry
            lax.fori_loop(0, source.shape[0] // tile, body, 0)
        pltpu.make_async_copy(far_lo, lo_out, sems.at[0]).start()
        pltpu.make_async_copy(far_hi, hi_out, sems.at[1]).start()

    flat = edge[...].reshape(sb * rows, edge_width)
    mixed = pick_rows(index_columns(idx_row[...]), (far_lo, far_hi)) + dot(flat, m1[width : width + edge_width, :])
    z_one = (mixed.reshape(sb, rows, width) + own_part[...][None]).reshape(sb * rows, width)
    act, slope = gelu_parts(z_one)
    act = act.astype(BF16)
    a1_out[...] = act
    s1_out[...] = slope.astype(BF16)
    act, slope = gelu_parts(dot(act, m2[...]) + b2[...])
    s2_out[...] = slope.astype(BF16)
    act = act.astype(BF16).astype(F32).reshape(sb, rows, width)
    count = live_col[...]
    inverse = 1.0 / count.astype(F32)
    total = sum_out[...]
    for s in range(sb):
        share = jnp.where(count > (step + first_block) * sb + s, inverse, 0.0)
        total = total + act[s] * spread(share, width)
    sum_out[...] = total

    if fresh:
        @pl.when(step == blocks - 1)
        def _():
            pltpu.make_async_copy(far_lo, lo_out, sems.at[0]).wait()
            pltpu.make_async_copy(far_hi, hi_out, sems.at[1]).wait()


def message_forward(first_block, blocks, node_own, edge, idx_row, live_col, m1, b1, m2, b2, more):
    slots, rows, edge_width = edge.shape
    width = node_own.shape[1]
    sb = slot_block(slots)
    block = sb * rows
    edges = blocks * block
    fresh = len(more) == 2
    half = more[0].shape
    out_specs = [pl.BlockSpec((block, width), lambda i: (i, 0))] * 3 + [pl.BlockSpec((rows, width), whole)]
    out_shape = [jax.ShapeDtypeStruct((edges, width), BF16)] * 3 + [
        jax.ShapeDtypeStruct((rows, width), F32)
    ]
    scratch = []
    if fresh:
        out_specs += [pl.BlockSpec((rows, width), whole)] + [pl.BlockSpec(memory_space=pl.ANY)] * 2
        out_shape += [jax.ShapeDtypeStruct((rows, width), F32)] + [jax.ShapeDtypeStruct(half, BF16)] * 2
        scratch = [pltpu.VMEM(half, BF16), pltpu.VMEM(half, BF16), pltpu.SemaphoreType.DMA((2,))]
    return pl.pallas_call(
        functools.partial(message_forward_kernel, sb, first_block, blocks, fresh),
        grid=(blocks,),
        in_specs=[
            const_spec(node_own.shape),
            pl.BlockSpec((sb, rows, edge_width), lambda i: (i + first_block, 0, 0)),
            pl.BlockSpec((1, block), lambda i: (0, i + first_block)),
            const_spec(live_col.shape),
            const_spec(m1.shape),
            const_spec(b1.shape),
            const_spec(m2.shape),
            const_spec(b2.shape),
        ]
        + [const_spec(a.shape) for a in more],
        out_specs=out_specs,
        out_shape=out_shape,
        scratch_shapes=scratch,
        compiler_params=pltpu.CompilerParams(vmem_limit_bytes=VMEM),
        name="message_forward",
        cost_estimate=pl.CostEstimate(
            flops=2 * edges * width * (2 * half[0] + edge_width + width),
            bytes_accessed=edges * width * 6 + edges * edge_width * 2 + edges * LANES * 4,
            transcendentals=2 * edges * width,
        ),
    )(node_own, edge, idx_row, live_col, m1, b1, m2, b2, *more)


def residue_forward_kernel(parts, node, total, m3, b3, g1, fb2, g2, e_first, e_far, eb, *refs):
    f1, f2 = refs[:parts], refs[parts : 2 * parts]
    h1b_out, n1_out, sc1_out, n2_out, sc2_out, slope_out, h2b_out, far_out, own_out = refs[2 * parts :]
    width, hidden = node.shape[1], f1[0].shape[1]
    u1 = node[...].astype(F32) + fine(dot, total[...], m3[...]) + b3[...]
    n1, sc1 = norm(u1)
    h1 = n1 * g1[...]
    h1b = h1.astype(BF16)
    h1b_out[...] = h1b
    n1_out[...] = n1
    sc1_out[...] = jnp.broadcast_to(sc1, sc1_out.shape)
    y2 = None
    for p in range(parts):
        bias = f1[p][width : width + 16, :].astype(F32)
        bias = bias[0:1] + bias[1:2] + bias[2:3]
        act, slope = gelu_parts(dot(h1b, f1[p][:width, :]) + bias)
        slope_out[:, p * hidden : (p + 1) * hidden] = slope
        part = dot(act.astype(BF16), f2[p][...])
        y2 = part if y2 is None else y2 + part
    n2, sc2 = norm(h1 + (y2 + fb2[...]))
    h2b = (n2 * g2[...]).astype(BF16)
    n2_out[...] = n2
    sc2_out[...] = jnp.broadcast_to(sc2, sc2_out.shape)
    h2b_out[...] = h2b
    far_out[...] = dot_back(h2b, e_far[...]).astype(BF16)
    own_out[...] = dot_back(h2b, e_first[:, :width]) + eb[...]


def residue_forward(node, total, m3, b3, g1, fb2, g2, e_first, e_far, eb, f1, f2):
    rows, width = node.shape
    edge_width = e_first.shape[0]
    hidden = len(f1) * f1[0].shape[1]
    shapes = [
        ((rows, width), BF16),
        ((rows, width), F32),
        ((rows, LANES), F32),
        ((rows, width), F32),
        ((rows, LANES), F32),
        ((rows, hidden), F32),
        ((rows, width), BF16),
        ((rows, edge_width), BF16),
        ((rows, edge_width), F32),
    ]
    return small_call(
        functools.partial(residue_forward_kernel, len(f1)),
        (node, total, m3, b3, g1, fb2, g2, e_first, e_far, eb, *f1, *f2),
        shapes, "residue_forward", flops=4 * rows * width * hidden, moved=5 * MIB,
        exps=rows * hidden,
    )


def edge_kernel(
    sb, blocks, hi_chunks, far_lo, far_hi, own, edge, cot, idx, idx_row, live_col,
    e_first, e2, eb2, e3, eb3, g3,
    edge_out, act_one_out, act_two_out, low_three_out, low_two_out, low_one_out, hi_out, lo_out, own_out, gain_out,
    low_first, gs,
):
    step = pl.program_id(0)
    rows, width = own.shape
    node_width = (e_first.shape[1] - width) // 2
    e_mid = e_first.at[:, node_width : node_width + width]

    @pl.when(step == 0)
    def _():
        own_out[...] = jnp.zeros_like(own_out)
        gs[...] = jnp.zeros_like(gs)

    @pl.when(step < blocks)
    def _():
        block = sb * rows
        flat = edge[...].reshape(block, width)
        mixed = pick_rows(index_columns(idx[...]), (far_lo, far_hi)) + dot_back(flat, e_mid[...])
        w_one = (mixed.reshape(sb, rows, width) + own[...][None]).reshape(block, width)
        act_one, slope_one = gelu_parts(w_one)
        act_one = act_one.astype(BF16)
        act_one_out[...] = act_one
        act_two, slope_two = gelu_parts(dot(act_one, e2[...]) + eb2[...])
        act_two = act_two.astype(BF16)
        act_two_out[...] = act_two
        w_three = dot(act_two, e3[...]) + eb3[...]
        normed, scale = norm(flat.astype(F32) + w_three)
        count = spread(live_col[...], pl.cdiv(width, LANES) * LANES)[:, :width]
        live = jnp.concatenate(
            [jnp.where(count > step * sb + s, 1.0, 0.0) for s in range(sb)], axis=0
        )
        edge_out[...] = (normed * g3[...] * live).astype(BF16).reshape(sb, rows, width)
        grad = cot[...].reshape(block, width).astype(F32) * live
        gs[...] += jnp.sum((grad * normed).reshape(sb, rows, width), axis=0)
        low_three = norm_back(grad * g3[...], normed, scale).astype(BF16)
        low_three_out[...] = low_three
        low_two = (dot_back(low_three, e3[...]) * slope_two).astype(BF16)
        low_two_out[...] = low_two
        low_one = (dot_back(low_two, e2[...]) * slope_one).astype(BF16)
        low_one_out[...] = low_one
        own_out[...] += jnp.sum(low_one.astype(F32).reshape(sb, rows, width), axis=0)
        low_first[pl.ds(pl.multiple_of(step * block, block), block), :] = low_one

    chunk = hi_out.shape[0]

    @pl.when((step >= blocks) & (step < blocks + hi_chunks))
    def _():
        start = (step - blocks + hi_chunks) * chunk
        hi_out[...] = dot(one_hot_rows(idx_row[...], start, chunk), low_first[...]).astype(BF16)

    @pl.when(step >= blocks + hi_chunks)
    def _():
        start = (step - blocks - hi_chunks) * chunk
        lo_out[...] = dot(one_hot_rows(idx_row[...], start, chunk), low_first[...])

    @pl.when(step == blocks + 2 * hi_chunks - 1)
    def _():
        gain_out[...] = column_sum(gs[...])


def edge_branch(far_lo, far_hi, own, edge, cot, idx_row, live_col, e_first, e2, eb2, e3, eb3, g3):
    slots, rows, width = edge.shape
    sb = slot_block(slots)
    edges = slots * rows
    block = sb * rows
    blocks = slots // sb
    half = far_lo.shape[0]
    chunk = min(512, half)
    hi_chunks = half // chunk
    blk = lambda i: jnp.minimum(i, blocks - 1)
    hi_at = lambda i: (jnp.clip(i - blocks, 0, hi_chunks - 1), 0)
    lo_at = lambda i: (jnp.clip(i - blocks - hi_chunks, 0, hi_chunks - 1), 0)
    slot_spec = pl.BlockSpec((sb, rows, width), lambda i: (blk(i), 0, 0))
    row_spec = pl.BlockSpec((block, width), lambda i: (blk(i), 0))
    return pl.pallas_call(
        functools.partial(edge_kernel, sb, blocks, hi_chunks),
        grid=(blocks + 2 * hi_chunks,),
        in_specs=[
            const_spec(far_lo.shape),
            const_spec(far_hi.shape),
            const_spec(own.shape),
            slot_spec,
            slot_spec,
            pl.BlockSpec((1, block), lambda i: (0, blk(i))),
            const_spec(idx_row.shape),
            const_spec(live_col.shape),
            const_spec(e_first.shape),
            const_spec(e2.shape),
            const_spec(eb2.shape),
            const_spec(e3.shape),
            const_spec(eb3.shape),
            const_spec(g3.shape),
        ],
        out_specs=[slot_spec]
        + [row_spec] * 5
        + [
            pl.BlockSpec((chunk, width), hi_at),
            pl.BlockSpec((chunk, width), lo_at),
            pl.BlockSpec((rows, width), whole),
            pl.BlockSpec((1, width), whole),
        ],
        out_shape=[jax.ShapeDtypeStruct((slots, rows, width), BF16)]
        + [jax.ShapeDtypeStruct((edges, width), BF16)] * 5
        + [
            jax.ShapeDtypeStruct((half, width), BF16),
            jax.ShapeDtypeStruct((half, width), F32),
            jax.ShapeDtypeStruct((rows, width), F32),
            jax.ShapeDtypeStruct((1, width), F32),
        ],
        scratch_shapes=[pltpu.VMEM((edges, width), BF16), pltpu.VMEM((rows, width), F32)],
        compiler_params=pltpu.CompilerParams(vmem_limit_bytes=VMEM),
        name="edge_branch",
        cost_estimate=pl.CostEstimate(
            flops=2 * edges * width * (4 * half + 5 * width),
            bytes_accessed=edges * width * 16,
            transcendentals=2 * edges * width,
        ),
    )(far_lo, far_hi, own, edge, cot, idx_row, idx_row, live_col, e_first, e2, eb2, e3, eb3, g3)


def edge_weights_kernel(blocks, edge, act_one, act_two, low_three, low_two, low_one, e1g, e2g, e3g, bias, sums):
    step = pl.program_id(0)
    sb, rows, width = edge.shape

    @pl.when(step == 0)
    def _():
        for ref in (e1g, e2g, e3g, sums):
            ref[...] = jnp.zeros_like(ref)

    e3g[...] += dot_rows(act_two[...], low_three[...])
    e2g[...] += dot_rows(act_one[...], low_two[...])
    e1g[...] += dot_rows(low_one[...], edge[...].reshape(sb * rows, width))
    for at, low in enumerate((low_one, low_two, low_three)):
        sums[at] += jnp.sum(low[...].astype(F32).reshape(sb, rows, width), axis=0)

    @pl.when(step == blocks - 1)
    def _():
        bias[...] = jnp.concatenate(
            [column_sum(sums[at]) for at in range(3)] + [jnp.zeros((5, width), F32)], axis=0
        )


def edge_weights(edge, *arrays):
    slots, rows, width = edge.shape
    sb = slot_block(slots)
    block = sb * rows
    shapes = [(width, width)] * 3 + [(8, width)]
    return pl.pallas_call(
        functools.partial(edge_weights_kernel, slots // sb),
        grid=(slots // sb,),
        in_specs=[pl.BlockSpec((sb, rows, width), lambda i: (i, 0, 0))]
        + [pl.BlockSpec((block, width), lambda i: (i, 0))] * 5,
        out_specs=[pl.BlockSpec(s, whole) for s in shapes],
        out_shape=[jax.ShapeDtypeStruct(s, F32) for s in shapes],
        scratch_shapes=[pltpu.VMEM((3, rows, width), F32)],
        compiler_params=pltpu.CompilerParams(vmem_limit_bytes=VMEM),
        name="edge_weights",
        cost_estimate=pl.CostEstimate(
            flops=6 * slots * rows * width * width,
            bytes_accessed=slots * rows * width * 12,
            transcendentals=0,
        ),
    )(edge, *arrays)


def early_shapes(width, edge_width):
    return [
        (width, width),
        (edge_width, width),
        (edge_width, edge_width),
        (edge_width, width),
        (edge_width, edge_width),
        (edge_width, edge_width),
        (16, width),
        (16, edge_width),
    ]


def residue_backward_kernel(
    parts, pieces, node_cot, own_sum, e_first, e_far, h1b, h2b, n1, sc1, n2, sc2, slope, g1, g2, m3,
    total, e1g, e2g, e3g, edge_bias, edge_gain, *refs,
):
    far = refs[:pieces]
    f1 = refs[pieces : pieces + parts]
    f2 = refs[pieces + parts : pieces + 2 * parts]
    gu1_out, v_out, both_out, slab = refs[pieces + 2 * parts :]
    width, hidden = h2b.shape[1], f1[0].shape[1]
    far_sum = far[0][...]
    for ref in far[1:]:
        far_sum = far_sum + ref[...].astype(F32)
    own = own_sum[...]
    g_h2 = (
        node_cot[...].astype(F32)
        + fine(dot, own, e_first[:, :width])
        + fine(dot, far_sum, e_far[...])
    )
    gain_two = column_sum(g_h2 * n2[...])
    g_u2 = norm_back(g_h2 * g2[...], n2[...], sc2[:, :1])
    gy2 = g_u2.astype(BF16)
    both_out[:, :width] = h1b[...]
    both_out[:, width:] = gy2
    g_h1 = g_u2
    for p in range(parts):
        gy1 = dot_back(gy2, f2[p][...]) * slope[:, p * hidden : (p + 1) * hidden]
        g_h1 = g_h1 + dot_back(gy1.astype(BF16), f1[p][:width, :])
    gain_one = column_sum(g_h1 * n1[...])
    g_u1 = norm_back(g_h1 * g1[...], n1[...], sc1[:, :1])
    gu1_out[...] = g_u1
    v_out[...] = fine(dot_back, g_u1, m3[...])
    bias = [gain_one, gain_two, column_sum(gy2.astype(F32)), column_sum(g_u1)]
    slab[...] = jnp.zeros_like(slab)
    pack(
        slab,
        [
            dot_rows(total[...].astype(BF16), g_u1.astype(BF16)),
            dot_rows(own.astype(BF16), h2b[...]),
            e1g[...],
            dot_rows(far_sum.astype(BF16), h2b[...]),
            e2g[...],
            e3g[...],
            padded_rows(bias, width),
            padded_rows([edge_bias[0:1], edge_bias[1:2], edge_bias[2:3], edge_gain[...]], own.shape[1]),
        ],
    )


def residue_backward(args, far, f1, f2):
    node_cot, e_first, slope = args[0], args[2], args[10]
    rows, width = node_cot.shape
    tiles = all_tiles(early_shapes(width, e_first.shape[0]))
    shapes = [
        ((rows, width), F32),
        ((rows, width), F32),
        ((rows, 2 * width), BF16),
        ((tiles, 16, LANES), BF16),
    ]
    return small_call(
        functools.partial(residue_backward_kernel, len(f1), len(far)),
        (*args, *far, *f1, *f2),
        shapes, "residue_backward",
        flops=4 * rows * width * slope.shape[1], moved=8 * MIB,
    )


def feed_kernel(first, second, f1, fb1, f2, f1g, f2g, fb1g):
    width = f1.shape[0]

    @pl.when(pl.program_id(0) == 0)
    def _():
        for ref in (f1g, f2g, fb1g):
            ref[...] = jnp.zeros_like(ref)

    for both in (first, second):
        h1b, gy2 = both[:, :width], both[:, width:]
        act, slope = gelu_parts(dot(h1b, f1[...]) + fb1[...])
        gy1 = (dot_back(gy2, f2[...]) * slope).astype(BF16)
        f1g[...] += dot_rows(h1b, gy1)
        f2g[...] += dot_rows(act.astype(BF16), gy2)
        fb1g[...] += column_sum(gy1.astype(F32))


def feed_gradients(both, f1, fb1, f2):
    width, hidden = f1.shape
    half = both[0].shape[0]
    chunk = min(512, half)
    shapes = [(width, hidden), (hidden, width), (1, hidden)]
    return pl.pallas_call(
        feed_kernel,
        grid=(half // chunk,),
        in_specs=[pl.BlockSpec((chunk, 2 * width), lambda i: (i, 0))] * 2
        + [const_spec(a.shape) for a in (f1, fb1, f2)],
        out_specs=[pl.BlockSpec(s, whole) for s in shapes],
        out_shape=[jax.ShapeDtypeStruct(s, F32) for s in shapes],
        compiler_params=pltpu.CompilerParams(vmem_limit_bytes=VMEM),
        name="feed_gradients",
        cost_estimate=pl.CostEstimate(
            flops=16 * half * width * hidden,
            bytes_accessed=8 * half * width,
            transcendentals=2 * half * hidden,
        ),
    )(*both, f1, fb1, f2)


def late_shapes(width, edge_width):
    return [(width, width), (width, width), (edge_width, width), (16, width)]


def message_backward_kernel(sb, first_block, blocks, last, v, a1, s1, s2, edge, live_col, m2, *refs):
    if last:
        node, own_in, m2g_in, m1eg_in, b2_in, low_out, own, slab, m2g, m1eg, b2s = refs
    else:
        low_out, own, m2g, m1eg, b2s = refs
    step = pl.program_id(0)
    rows, width = v.shape
    edge_width = edge.shape[2]
    block = sb * rows

    @pl.when(step == 0)
    def _():
        if last:
            own[...] = own_in[...]
            m2g[...] = m2g_in[...]
            m1eg[...] = m1eg_in[...]
            b2s[...] = b2_in[...]
        else:
            for ref in (own, m2g, m1eg, b2s):
                ref[...] = jnp.zeros_like(ref)

    count = live_col[...]
    inverse = 1.0 / count.astype(F32)
    grads = [
        v[...] * spread(jnp.where(count > (step + first_block) * sb + s, inverse, 0.0), width)
        for s in range(sb)
    ]
    low_two = (jnp.concatenate(grads, axis=0) * s2[...].astype(F32)).astype(BF16)
    m2g[...] += dot_rows(a1[...], low_two)
    b2s[...] += jnp.sum(low_two.astype(F32).reshape(sb, rows, width), axis=0)
    low_one = (dot_back(low_two, m2[...]) * s1[...].astype(F32)).astype(BF16)
    low_out[...] = low_one
    m1eg[...] += dot_rows(edge[...].reshape(block, edge_width), low_one)
    own[...] += jnp.sum(low_one.astype(F32).reshape(sb, rows, width), axis=0)

    if last:
        @pl.when(step == blocks - 1)
        def _():
            slab[...] = jnp.zeros_like(slab)
            bias = [column_sum(own[...]), column_sum(b2s[...])]
            pack(
                slab,
                [
                    dot_rows(node[...], own[...].astype(BF16)),
                    m2g[...],
                    m1eg[...],
                    padded_rows(bias, width),
                ],
            )


def message_backward(first_block, blocks, v, a1, s1, s2, edge, live_col, m2, more=()):
    slots, rows, edge_width = edge.shape
    width = v.shape[1]
    sb = slot_block(slots)
    block = sb * rows
    edges = blocks * block
    row_spec = pl.BlockSpec((block, width), lambda i: (i, 0))
    sums = [(rows, width), (width, width), (edge_width, width), (rows, width)]
    in_specs = [
        const_spec(v.shape),
        row_spec,
        row_spec,
        row_spec,
        pl.BlockSpec((sb, rows, edge_width), lambda i: (i + first_block, 0, 0)),
        const_spec(live_col.shape),
        const_spec(m2.shape),
    ]
    in_specs += [const_spec(a.shape) for a in more]
    scratch = []
    outs = [(s, F32) for s in sums]
    if more:
        tiles = all_tiles(late_shapes(width, edge_width))
        outs = [(sums[0], F32), ((tiles, 16, LANES), BF16)]
        scratch = [pltpu.VMEM(s, F32) for s in sums[1:]]
    return pl.pallas_call(
        functools.partial(message_backward_kernel, sb, first_block, blocks, bool(more)),
        grid=(blocks,),
        in_specs=in_specs,
        out_specs=[row_spec]
        + [pl.BlockSpec(s, lambda i, n=len(s): (0,) * n) for s, _ in outs],
        out_shape=[jax.ShapeDtypeStruct((edges, width), BF16)]
        + [jax.ShapeDtypeStruct(*s) for s in outs],
        scratch_shapes=scratch,
        compiler_params=pltpu.CompilerParams(vmem_limit_bytes=VMEM),
        name="message_backward",
        cost_estimate=pl.CostEstimate(
            flops=2 * edges * width * (2 * width + 2 * edge_width),
            bytes_accessed=edges * width * 8 + edges * edge_width * 2,
            transcendentals=0,
        ),
    )(v, a1, s1, s2, edge, live_col, m2, *more)


def far_sums_kernel(
    steps, codes, base, idx_row, low_a, low_b, node_lo, node_hi, early, late, keep, send, m1fg, slab
):
    step = pl.program_id(0)
    cut = low_a.shape[0]
    chunk, width = node_lo.shape
    rows = node_lo.shape[0] // (len(codes) // 2 // steps)
    size = keep.shape[0] // (len(codes) // 2)
    part = slab.shape[0] // len(codes)
    height = rows // 16

    @pl.when(step == 0)
    def _():
        m1fg[...] = jnp.zeros_like(m1fg)

    for node, out, start in ((node_lo, keep, 0), (node_hi, send, steps * chunk)):
        first = start + step * chunk
        sums = dot(one_hot_rows(idx_row[:, :cut], first, chunk), low_a[...]) + dot(
            one_hot_rows(idx_row[:, cut:], first, chunk), low_b[...]
        )
        sums = sums.astype(BF16)
        m1fg[...] += dot_rows(node[...], sums)
        for place in range(chunk // rows):
            at = (step * (chunk // rows) + place) * size
            for lane in range(0, width, LANES):
                tile = sums[place * rows : (place + 1) * rows, lane : lane + LANES]
                out[pl.ds(at + lane // LANES * height, height)] = tile.reshape(height, 16, LANES)

    @pl.when(step == steps - 1)
    def _():
        count = early.shape[0]
        slab[:count] = early[...]
        slab[count : count + late.shape[0]] = late[...]
        count += late.shape[0]
        pack(slab, [m1fg[...]], count)
        count += tile_count((width, width))
        if count < slab.shape[0]:
            slab[count:] = jnp.zeros_like(slab[count:])
        half = len(codes) // 2
        for place, code in enumerate(codes):
            out = keep if place < half else send
            out[(place % half + 1) * size - part : (place % half + 1) * size] = slab[
                pl.ds((base[0] ^ code) * part, part)
            ]


def chunk_tiles(width, edge_width, chunks):
    shapes = early_shapes(width, edge_width) + late_shapes(width, edge_width) + [(width, width)]
    return pl.cdiv(all_tiles(shapes), chunks)


def far_sums(codes, base, idx_row, low_a, low_b, node_lo, node_hi, early, late, rows, edge_width):
    half, width = node_lo.shape
    chunk = min(512, half)
    steps = half // chunk
    part = chunk_tiles(width, edge_width, len(codes))
    tiles = len(codes) // 2 * (rows * width // (16 * LANES) + part)
    node_spec = pl.BlockSpec((chunk, width), lambda i: (i, 0))
    edges = idx_row.shape[1]
    return pl.pallas_call(
        functools.partial(far_sums_kernel, steps, codes),
        grid=(steps,),
        in_specs=[pl.BlockSpec(memory_space=pltpu.SMEM)]
        + [const_spec(a.shape) for a in (idx_row, low_a, low_b)]
        + [node_spec, node_spec, const_spec(early.shape), const_spec(late.shape)],
        out_specs=[
            pl.BlockSpec((tiles, 16, LANES), lambda i: (0, 0, 0), pipeline_mode=pl.Buffered(1))
        ]
        * 2,
        out_shape=[jax.ShapeDtypeStruct((tiles, 16, LANES), BF16)] * 2,
        scratch_shapes=[
            pltpu.VMEM((width, width), F32),
            pltpu.VMEM((part * len(codes), 16, LANES), BF16),
        ],
        compiler_params=pltpu.CompilerParams(vmem_limit_bytes=VMEM),
        name="far_sums",
        cost_estimate=pl.CostEstimate(
            flops=4 * width * half * (edges + width),
            bytes_accessed=edges * width * 2 + half * width * 10,
            transcendentals=0,
        ),
    )(base, idx_row, low_a, low_b, node_lo, node_hi, early, late)


def edge_gradient_kernel(sb, cut, low_three, low_edge, low_a, low_b, e_first, m1, out):
    step = pl.program_id(0)
    shape = out.shape
    edge_width, width = shape[2], low_a.shape[1]
    for low, use in ((low_a, step < cut), (low_b, step >= cut)):
        @pl.when(use)
        def _(low=low):
            total = (
                low_three[...].astype(F32)
                + dot(low_edge[...], e_first[:, width : width + edge_width])
                + dot_back(low[...], m1[width : width + edge_width, :])
            )
            out[...] = total.reshape(shape)


def edge_gradient(slots, low_three, low_edge, low_a, low_b, e_first, m1):
    edges, edge_width = low_three.shape
    rows = edges // slots
    width = low_a.shape[1]
    sb = slot_block(slots)
    block = sb * rows
    cut = low_a.shape[0] // block
    edge_spec = pl.BlockSpec((block, edge_width), lambda i: (i, 0))
    return pl.pallas_call(
        functools.partial(edge_gradient_kernel, sb, cut),
        grid=(slots // sb,),
        in_specs=[
            edge_spec,
            edge_spec,
            pl.BlockSpec((block, width), lambda i: (jnp.minimum(i, cut - 1), 0)),
            pl.BlockSpec((block, width), lambda i: (jnp.maximum(i - cut, 0), 0)),
            const_spec(e_first.shape),
            const_spec(m1.shape),
        ],
        out_specs=pl.BlockSpec((sb, rows, edge_width), lambda i: (i, 0, 0)),
        out_shape=jax.ShapeDtypeStruct((slots, rows, edge_width), F32),
        compiler_params=pltpu.CompilerParams(vmem_limit_bytes=VMEM),
        name="edge_gradient",
        cost_estimate=pl.CostEstimate(
            flops=2 * edges * edge_width * (width + edge_width),
            bytes_accessed=edges * (width * 2 + 2048),
            transcendentals=0,
        ),
    )(low_three, low_edge, low_a, low_b, e_first, m1)


def node_kernel(pieces, g_u1, own, m1, *refs):
    far, grad_out = refs[:pieces], refs[pieces]
    rows, width = own.shape
    height = rows // 16
    sums = far[0][...].astype(F32)
    for ref in far[1:]:
        sums = sums + ref[...].astype(F32)
    far_sum = jnp.concatenate(
        [sums[j * height : (j + 1) * height].reshape(rows, LANES) for j in range(width // LANES)],
        axis=1,
    )
    far_first = m1.shape[0] - width
    grad_out[...] = (
        g_u1[...]
        + fine(dot_back, own[...], m1[:width, :])
        + fine(dot_back, far_sum, m1[far_first:, :])
    )


def node_last(g_u1, own, m1, far):
    return small_call(
        functools.partial(node_kernel, len(far)),
        (g_u1, own, m1, *far), [(own.shape, F32)], "node_gradient",
        flops=8 * own.size * own.shape[1], moved=2 * MIB,
    )[0]


def weights_out_kernel(
    codes, base, first, second,
    m1g, b1, m2g, b2, m3g, e1g, e2g, e3g, b3, g1, g2, fb2, eb1, eb2, eb3, g3, slab,
):
    order_in(slab, base[0], codes, first, second)
    width, edge_width = m3g.shape[0], e2g.shape[0]
    starts, at = [], 0
    for shape in early_shapes(width, edge_width) + late_shapes(width, edge_width):
        starts.append(at)
        at += tile_count(shape)
    m3g[...] = unpack(slab, starts[0], width, width)
    e1g[:, :width] = unpack(slab, starts[1], edge_width, width)
    middle = unpack(slab, starts[2], edge_width, edge_width)
    far = unpack(slab, starts[3], edge_width, width)
    over = edge_width % LANES
    base_col = width + edge_width - over
    e1g[:, width:base_col] = middle[:, : edge_width - over]
    far = pltpu.roll(jnp.concatenate([far, jnp.zeros((edge_width, LANES), F32)], axis=1), over, 1)
    lane = lax.broadcasted_iota(jnp.int32, (edge_width, LANES), 1)
    e1g[:, base_col : base_col + LANES] = jnp.where(
        lane < over, middle[:, edge_width - over : edge_width - over + LANES], far[:, :LANES]
    )
    rest = e1g.shape[1] - base_col - LANES
    e1g[:, base_col + LANES :] = far[:, LANES : LANES + rest]
    e2g[...] = unpack(slab, starts[4], edge_width, edge_width)[:, :edge_width]
    e3g[...] = unpack(slab, starts[5], edge_width, edge_width)[:, :edge_width]
    bias = unpack(slab, starts[6], 16, width)
    for row, out in enumerate((g1, g2, fb2, b3)):
        out[...] = bias[row : row + 1]
    bias = unpack(slab, starts[7], 16, edge_width)
    for row, out in enumerate((eb1, eb2, eb3, g3)):
        out[...] = bias[row : row + 1, :edge_width]
    m1g[:width, :] = unpack(slab, starts[8], width, width)
    m2g[...] = unpack(slab, starts[9], width, width)
    m1g[width : width + edge_width, :] = unpack(slab, starts[10], edge_width, width)
    m1g[width + edge_width :, :] = unpack(slab, at, width, width)
    bias = unpack(slab, starts[11], 16, width)
    b1[...] = bias[0:1]
    b2[...] = bias[1:2]


def weights_out(codes, base, halves_in, width, edge_width):
    shapes = [(2 * width + edge_width, width), (1, width), (width, width), (1, width)]
    shapes += [(width, width), (edge_width, 2 * width + edge_width)]
    shapes += [(edge_width, edge_width)] * 2 + [(1, width)] * 4 + [(1, edge_width)] * 4
    tiles = chunk_tiles(width, edge_width, len(codes)) * len(codes)
    return small_call(
        functools.partial(weights_out_kernel, codes),
        (base, *halves_in), [(s, F32) for s in shapes], "weight_gradients",
        [pltpu.VMEM((tiles, 16, LANES), BF16)], moved=10 * MIB, scalars=1,
    )


def exchange(value, mask, devices):
    return lax.ppermute(value, AXES, [(d, d ^ mask) for d in range(devices)])


def mask_groups(masks):
    return [masks[i : min(i + 2, len(masks) - 1)] for i in range(0, len(masks) - 1, 2)] + [masks[-1:]]


def order_codes(groups):
    masks = [mask for group in groups for mask in group]
    return [
        sum(mask for bit, mask in enumerate(masks) if place >> bit & 1)
        for place in range(1 << len(masks))
    ]


def combined(group, code):
    return sum(mask for bit, mask in enumerate(group) if code >> bit & 1)


def gather_pieces(value, groups, devices, hooks=()):
    for at, group in enumerate(groups):
        pieces = [value]
        for code in range(1, 1 << len(group)):
            pieces.append(exchange(value, combined(group, code), devices))
        if at + 1 == len(groups):
            return pieces
        value = jnp.concatenate(pieces, axis=0)
        if at < len(hooks):
            value = hooks[at](value)


def scatter_sums(keep, send, groups, devices):
    received = [exchange(send, groups[-1][0], devices)]
    for group in reversed(groups[:-1]):
        total = keep.astype(F32)
        for part in received:
            total = total + part.astype(F32)
        parts = 1 << len(group)
        rows = total.shape[0] // parts
        keep = total[:rows]
        received = [
            exchange(
                total[code * rows : (code + 1) * rows].astype(BF16), combined(group, code), devices
            )
            for code in range(1, parts)
        ]
    return [keep] + received


def split_three(value):
    rows = []
    for _ in range(3):
        high = lax.reduce_precision(value, 8, 7)
        rows.append(high.astype(BF16))
        value = value - high
    return jnp.concatenate(rows + [jnp.zeros((13, value.shape[1]), BF16)], axis=0)


def per_device(
    node_in,
    edge_in,
    neighbours,
    live_counts,
    message_first,
    message_first_bias,
    message_second,
    message_second_bias,
    message_third,
    message_third_bias,
    norm_one,
    feed_first,
    feed_first_bias,
    feed_second,
    feed_second_bias,
    norm_two,
    edge_first,
    edge_first_bias,
    edge_second,
    edge_second_bias,
    edge_third,
    edge_third_bias,
    norm_three,
    node_cotangent,
    edge_cotangent,
):
    rows, slots = neighbours.shape
    width = node_in.shape[1]
    edge_width = edge_in.shape[2]
    edges = rows * slots
    hid_count = lax.axis_size("hid")
    res_count = lax.axis_size("res")
    devices = res_count * hid_count
    bits = devices.bit_length() - 1
    masks = [1 << b for b in range(bits - 1, -1, -1)]
    groups = mask_groups(masks)
    codes = order_codes(groups)
    me = lax.axis_index("res") * hid_count + lax.axis_index("hid")
    base = me.reshape(1)
    row = lambda vector: vector.reshape(1, -1)

    names = neighbours.T.reshape(edges)
    apart = (names // rows) ^ me
    place = jnp.zeros_like(names)
    for bit, mask in enumerate(masks):
        place = place | jnp.where((apart & mask) != 0, 1 << bit, 0)
    idx_row = (place * rows + names % rows).reshape(1, edges)
    live_col = jnp.broadcast_to(live_counts[:, None], (rows, LANES))
    edge = edge_in.transpose(1, 0, 2)
    cot = edge_cotangent.transpose(1, 0, 2)
    e_first = edge_first.T
    e_far = e_first[:, width + edge_width :]
    f1x = jnp.concatenate([feed_first, split_three(row(feed_first_bias))], axis=0)
    f2x = feed_second

    def first_hook(value):
        nonlocal idx_row, live_col, e_far
        value, idx_row, live_col, e_far = lax.optimization_barrier((value, idx_row, live_col, e_far))
        return value

    def second_hook(value):
        nonlocal f1x, f2x
        value, f1x, f2x = lax.optimization_barrier((value, f1x, f2x))
        return value

    node_lo, node_hi = gather_pieces(node_in, groups, devices, (first_hook, second_hook))

    f1, f2 = [f1x], [f2x]
    hid_masks = [m for m in masks if m < hid_count]
    for mask in hid_masks[:-1]:
        f1, f2 = [held + [exchange(p, mask, devices) for p in held] for held in (f1, f2)]

    sb = slot_block(slots)
    blocks = slots // sb
    cut = max(1, 2 * blocks // 3)
    message_args = (
        node_in, edge, idx_row, live_col, message_first, row(message_first_bias), message_second,
        row(message_second_bias),
    )
    a1a, s1a, s2a, total, own_part, far_lo, far_hi = message_forward(
        0, cut, *message_args, (node_lo, node_hi)
    )
    total, f1, f2 = lax.optimization_barrier((total, f1, f2))
    f1, f2 = [held + [exchange(p, hid_masks[-1], devices) for p in held] for held in (f1, f2)]
    a1b, s1b, s2b, total = message_forward(
        cut, blocks - cut, *message_args, (far_lo, far_hi, own_part, total)
    )
    h1b, n1, sc1, n2, sc2, slope, h2b, far_part, own_part = residue_forward(
        node_in, total, message_third, row(message_third_bias), row(norm_one),
        row(feed_second_bias), row(norm_two), e_first, e_far, row(edge_first_bias), f1, f2,
    )
    q_lo, q_hi = gather_pieces(far_part, groups, devices)
    edge_out, act_one, act_two, low_three, low_two, low_one, hi, lo, own_sum, edge_gain = edge_branch(
        q_lo, q_hi, own_part, edge, cot, idx_row, live_col, e_first,
        edge_second, row(edge_second_bias), edge_third, row(edge_third_bias), row(norm_three),
    )
    e1g, e2g, e3g, edge_bias = edge_weights(
        edge, act_one, act_two, low_three, low_two, low_one
    )
    far_terms = scatter_sums(lo, hi, groups, devices)
    g_u1, v, both, early = residue_backward(
        (
            node_cotangent, own_sum, e_first, e_far, h1b, h2b, n1, sc1, n2, sc2, slope,
            row(norm_one), row(norm_two), message_third, total, e1g, e2g, e3g, edge_bias, edge_gain,
        ),
        far_terms, f1, f2,
    )

    low_a, *sums = message_backward(0, cut, v, a1a, s1a, s2a, edge, live_col, message_second)
    low_b, own, late = message_backward(
        cut, blocks - cut, v, a1b, s1b, s2b, edge, live_col, message_second, (node_in, *sums)
    )
    both = gather_pieces(both, groups, devices)
    keep, send = far_sums(
        codes, base, idx_row, low_a, low_b, node_lo, node_hi, early, late, rows, edge_width
    )
    terms = scatter_sums(keep, send, groups, devices)
    f1g, f2g, fb1g = feed_gradients(both, feed_first, row(feed_first_bias), feed_second)
    edge_grad = edge_gradient(slots, low_three, low_one, low_a, low_b, e_first, message_first)
    part = terms[0].shape[0] - chunk_tiles(width, edge_width, devices)
    node_gradient = node_last(g_u1, own, message_first, [t[:part] for t in terms])
    mine = terms[0][part:].astype(F32)
    for term in terms[1:]:
        mine = mine + term[part:].astype(F32)
    m1g, b1, m2g, b2, m3g, e1g, e2g, e3g, b3, g1, g2, fb2, eb1, eb2, eb3, g3 = weights_out(
        codes, base, gather_pieces(mine.astype(BF16), groups, devices), width, edge_width
    )
    flat = lambda vector: vector.reshape(-1)
    return (
        h2b,
        edge_out.transpose(1, 0, 2),
        node_gradient,
        edge_grad.transpose(1, 0, 2),
        m1g,
        flat(b1),
        m2g,
        flat(b2),
        m3g,
        flat(b3),
        flat(g1),
        f1g,
        flat(fb1g),
        f2g,
        flat(fb2),
        flat(g2),
        e1g.T,
        flat(eb1),
        e2g,
        flat(eb2),
        e3g,
        flat(eb3),
        flat(g3),
    )


def solution(mesh):
    nodes, edges, shared = P(AXES, None), P(AXES, None, None), P()
    return jax.shard_map(
        per_device,
        mesh=mesh,
        in_specs=(nodes, edges, nodes, P(AXES))
        + (shared,) * 7
        + (P(None, "hid"), P("hid"), P("hid", None))
        + (shared,) * 9
        + (nodes, edges),
        out_specs=(nodes, edges, nodes, edges)
        + (shared,) * 7
        + (P(None, "hid"), P("hid"), P("hid", None))
        + (shared,) * 9,
        check_vma=False,
    )
```

```python
import functools

import jax
import jax.numpy as jnp
from jax import lax
from jax.experimental import pallas as pl
from jax.experimental.pallas import tpu as pltpu
from jax.sharding import PartitionSpec as P

EPS = 1e-05
AXES = ("res", "hid")
F32 = jnp.float32
BF16 = jnp.bfloat16
TANH_SCALE = 0.7978845608028654
TANH_CUBE = 0.044715
LANES = 128
CHUNK = 2048
MIB = 1024 * 1024
VMEM = 58 * MIB


def dot(left, right):
    return lax.dot_general(left, right, (((1,), (0,)), ((), ())), preferred_element_type=F32)


def dot_rows(left, right):
    return lax.dot_general(left, right, (((0,), (0,)), ((), ())), preferred_element_type=F32)


def dot_back(left, right):
    return lax.dot_general(left, right, (((1,), (1,)), ((), ())), preferred_element_type=F32)


def halves(value):
    high = value.astype(BF16)
    return high, (value - high.astype(F32)).astype(BF16)


def fine(product, value, weights):
    high, low = halves(value)
    return product(high, weights) + product(low, weights)


def gelu_parts(x):
    square = x * x
    t = jnp.tanh(x * (TANH_SCALE + (TANH_SCALE * TANH_CUBE) * square))
    gate = 0.5 + 0.5 * t
    act = x * gate
    slope = gate + act * (1.0 - gate) * (2 * TANH_SCALE + (6 * TANH_SCALE * TANH_CUBE) * square)
    return act, slope


def index_columns(idx_row):
    parts = [
        jnp.broadcast_to(idx_row[:, first : first + LANES], (LANES, LANES)).T
        for first in range(0, idx_row.shape[1], LANES)
    ]
    return jnp.concatenate(parts, axis=0)


def one_hot_columns(idx, start, count):
    lane = lax.broadcasted_iota(jnp.int32, idx.shape, 1)
    parts = [
        jnp.where(idx == lane + (start + first), 1.0, 0.0).astype(BF16)
        for first in range(0, count, LANES)
    ]
    return jnp.concatenate(parts, axis=1)


def pick_rows(idx, table_refs):
    total, start = None, 0
    for ref in table_refs:
        rows = ref.shape[0]
        step = min(rows, CHUNK)
        for first in range(0, rows, step):
            part = dot(one_hot_columns(idx, start + first, step), ref[first : first + step, :])
            total = part if total is None else total + part
        start += rows
    return total


def one_hot_rows(idx_row, start, count):
    row = lax.broadcasted_iota(jnp.int32, (count, idx_row.shape[1]), 0) + start
    return jnp.where(jnp.broadcast_to(idx_row, row.shape) == row, 1.0, 0.0).astype(BF16)


def spread(column, width):
    return jnp.concatenate([column] * (width // LANES), axis=1)


def norm(value):
    centre = value - jnp.mean(value, -1, keepdims=True)
    scale = lax.rsqrt(jnp.mean(centre * centre, -1, keepdims=True) + EPS)
    return centre * scale, scale


def norm_back(inner, normed, scale):
    mean_first = jnp.mean(inner, -1, keepdims=True)
    mean_second = jnp.mean(inner * normed, -1, keepdims=True)
    return scale * (inner - mean_first - normed * mean_second)


def column_sum(value):
    return jnp.sum(value, axis=0, keepdims=True)


def whole(*_):
    return (0, 0)


def const_spec(shape):
    return pl.BlockSpec(shape, lambda *_: (0,) * len(shape), pipeline_mode=pl.Buffered(1))


def small_call(kernel, args, shapes, name, scratch=(), flops=0, moved=0, exps=0, scalars=0):
    return pl.pallas_call(
        kernel,
        grid=(1,),
        in_specs=[pl.BlockSpec(memory_space=pltpu.SMEM)] * scalars
        + [const_spec(a.shape) for a in args[scalars:]],
        out_specs=[pl.BlockSpec(s, lambda *_, n=len(s): (0,) * n) for s, _ in shapes],
        out_shape=[jax.ShapeDtypeStruct(*s) for s in shapes],
        scratch_shapes=list(scratch),
        compiler_params=pltpu.CompilerParams(vmem_limit_bytes=VMEM),
        name=name,
        cost_estimate=pl.CostEstimate(flops=flops, bytes_accessed=moved, transcendentals=exps),
    )(*args)


def tile_count(shape):
    return pl.cdiv(shape[0], 16) * pl.cdiv(shape[1], LANES)


def all_tiles(shapes):
    return sum(tile_count(s) for s in shapes)


def pack(slab, values, at=0):
    for value in values:
        rows, columns = value.shape
        count = rows // 16
        for first in range(0, columns, LANES):
            take = min(LANES, columns - first)
            tile = value[:, first : first + take].astype(BF16).reshape(count, 16, take)
            slab[at : at + count, :, :take] = tile
            at += count


def unpack(slab, at, rows, columns):
    count = rows // 16
    parts = [
        slab[at + i * count : at + (i + 1) * count].reshape(rows, LANES).astype(F32)
        for i in range(pl.cdiv(columns, LANES))
    ]
    return jnp.concatenate(parts, axis=1)


def order_out(slab, base, codes, keep, send):
    size = slab.shape[0] // len(codes)
    half = len(codes) // 2
    for place, code in enumerate(codes):
        out = keep if place < half else send
        at = (place % half) * size
        out[at : at + size] = slab[pl.ds((base ^ code) * size, size)]


def half_shapes(tiles):
    return [((tiles // 2, 16, LANES), BF16)] * 2


def slab_scratch(tiles):
    return pltpu.VMEM((tiles, 16, LANES), BF16)


def slab_part(width, edge_width, chunks):
    return pl.cdiv(all_tiles(early_shapes(width, edge_width) + late_shapes(width, edge_width)), chunks)


def far_part_tiles(width, chunks):
    return pl.cdiv(all_tiles([(width, width)]), chunks)


def order_in(slabs, base, codes, first, second):
    sizes = [slab.shape[0] // len(codes) for slab in slabs]
    half = len(codes) // 2
    for place, code in enumerate(codes):
        source = first if place < half else second
        at = (place % half) * sum(sizes)
        for slab, size in zip(slabs, sizes):
            slab[pl.ds((base ^ code) * size, size)] = source[at : at + size]
            at += size


def padded_rows(parts, width):
    return jnp.concatenate(parts + [jnp.zeros((16 - len(parts), width), F32)], axis=0)


def slot_block(slots):
    for size in (10, 12, 8, 6, 5, 4, 3, 2):
        if slots % size == 0:
            return size
    return 1


def message_forward_kernel(sb, first_block, blocks, fresh, node_own, edge, idx_row, live_col, m1, b1, m2, b2, *refs):
    if fresh:
        node_lo, node_hi = refs[:2]
        a1_out, s1_out, s2_out, sum_out, own_part, lo_out, hi_out, far_lo, far_hi, sems = refs[2:]
    else:
        far_lo, far_hi, own_part, sum_in = refs[:4]
        a1_out, s1_out, s2_out, sum_out = refs[7:]
    step = pl.program_id(0)
    width = node_own.shape[1]
    edge_width = edge.shape[2]
    rows = edge.shape[1]

    @pl.when(step == 0)
    def _():
        if not fresh:
            sum_out[...] = sum_in[...]
            return
        sum_out[...] = jnp.zeros_like(sum_out)
        own_part[...] = dot(node_own[...], m1[:width, :]) + b1[...]
        tile = min(512, node_lo.shape[0])
        for source, target in ((node_lo, far_lo), (node_hi, far_hi)):
            def body(i, carry, source=source, target=target):
                at = pl.ds(pl.multiple_of(i * tile, tile), tile)
                target[at, :] = dot(source[at, :], m1[width + edge_width :, :]).astype(BF16)
                return carry
            lax.fori_loop(0, source.shape[0] // tile, body, 0)
        pltpu.make_async_copy(far_lo, lo_out, sems.at[0]).start()
        pltpu.make_async_copy(far_hi, hi_out, sems.at[1]).start()

    flat = edge[...].reshape(sb * rows, edge_width)
    mixed = pick_rows(index_columns(idx_row[...]), (far_lo, far_hi)) + dot(flat, m1[width : width + edge_width, :])
    z_one = (mixed.reshape(sb, rows, width) + own_part[...][None]).reshape(sb * rows, width)
    act, slope = gelu_parts(z_one)
    act = act.astype(BF16)
    a1_out[...] = act
    s1_out[...] = slope.astype(BF16)
    act, slope = gelu_parts(dot(act, m2[...]) + b2[...])
    s2_out[...] = slope.astype(BF16)
    act = act.astype(BF16).astype(F32).reshape(sb, rows, width)
    count = live_col[...]
    inverse = 1.0 / count.astype(F32)
    total = sum_out[...]
    for s in range(sb):
        share = jnp.where(count > (step + first_block) * sb + s, inverse, 0.0)
        total = total + act[s] * spread(share, width)
    sum_out[...] = total

    if fresh:
        @pl.when(step == blocks - 1)
        def _():
            pltpu.make_async_copy(far_lo, lo_out, sems.at[0]).wait()
            pltpu.make_async_copy(far_hi, hi_out, sems.at[1]).wait()


def message_forward(first_block, blocks, node_own, edge, idx_row, live_col, m1, b1, m2, b2, more):
    slots, rows, edge_width = edge.shape
    width = node_own.shape[1]
    sb = slot_block(slots)
    block = sb * rows
    edges = blocks * block
    fresh = len(more) == 2
    half = more[0].shape
    out_specs = [pl.BlockSpec((block, width), lambda i: (i + first_block, 0))] * 3
    out_specs += [pl.BlockSpec((rows, width), whole)]
    out_shape = [jax.ShapeDtypeStruct((slots * rows, width), BF16)] * 3 + [
        jax.ShapeDtypeStruct((rows, width), F32)
    ]
    scratch = []
    if fresh:
        out_specs += [pl.BlockSpec((rows, width), whole)] + [pl.BlockSpec(memory_space=pl.ANY)] * 2
        out_shape += [jax.ShapeDtypeStruct((rows, width), F32)] + [jax.ShapeDtypeStruct(half, BF16)] * 2
        scratch = [pltpu.VMEM(half, BF16), pltpu.VMEM(half, BF16), pltpu.SemaphoreType.DMA((2,))]
    return pl.pallas_call(
        functools.partial(message_forward_kernel, sb, first_block, blocks, fresh),
        grid=(blocks,),
        in_specs=[
            const_spec(node_own.shape),
            pl.BlockSpec((sb, rows, edge_width), lambda i: (i + first_block, 0, 0)),
            pl.BlockSpec((1, block), lambda i: (0, i + first_block)),
            const_spec(live_col.shape),
            const_spec(m1.shape),
            const_spec(b1.shape),
            const_spec(m2.shape),
            const_spec(b2.shape),
        ]
        + [const_spec(a.shape) for a in more[:4]]
        + [pl.BlockSpec(memory_space=pl.ANY)] * len(more[4:]),
        out_specs=out_specs,
        out_shape=out_shape,
        scratch_shapes=scratch,
        input_output_aliases={} if fresh else {12: 0, 13: 1, 14: 2},
        compiler_params=pltpu.CompilerParams(vmem_limit_bytes=VMEM),
        name="message_forward",
        cost_estimate=pl.CostEstimate(
            flops=2 * edges * width * (2 * half[0] + edge_width + width),
            bytes_accessed=edges * width * 6 + edges * edge_width * 2 + edges * LANES * 4,
            transcendentals=2 * edges * width,
        ),
    )(node_own, edge, idx_row, live_col, m1, b1, m2, b2, *more)


def residue_forward_kernel(parts, node, total, m3, b3, g1, fb2, g2, e_first, e_far, eb, *refs):
    f1, f2 = refs[:parts], refs[parts : 2 * parts]
    h1b_out, n1_out, sc1_out, n2_out, sc2_out, slope_out, h2b_out, far_out, own_out = refs[2 * parts :]
    width, hidden = node.shape[1], f1[0].shape[1]
    u1 = node[...].astype(F32) + fine(dot, total[...], m3[...]) + b3[...]
    n1, sc1 = norm(u1)
    h1 = n1 * g1[...]
    h1b = h1.astype(BF16)
    h1b_out[...] = h1b
    n1_out[...] = n1
    sc1_out[...] = jnp.broadcast_to(sc1, sc1_out.shape)
    y2 = None
    for p in range(parts):
        bias = f1[p][width : width + 16, :].astype(F32)
        bias = bias[0:1] + bias[1:2] + bias[2:3]
        act, slope = gelu_parts(dot(h1b, f1[p][:width, :]) + bias)
        slope_out[:, p * hidden : (p + 1) * hidden] = slope
        part = dot(act.astype(BF16), f2[p][...])
        y2 = part if y2 is None else y2 + part
    n2, sc2 = norm(h1 + (y2 + fb2[...]))
    h2b = (n2 * g2[...]).astype(BF16)
    n2_out[...] = n2
    sc2_out[...] = jnp.broadcast_to(sc2, sc2_out.shape)
    h2b_out[...] = h2b
    far_out[...] = dot_back(h2b, e_far[...]).astype(BF16)
    own_out[...] = dot_back(h2b, e_first[:, :width]) + eb[...]


def residue_forward(node, total, m3, b3, g1, fb2, g2, e_first, e_far, eb, f1, f2):
    rows, width = node.shape
    edge_width = e_first.shape[0]
    hidden = len(f1) * f1[0].shape[1]
    shapes = [
        ((rows, width), BF16),
        ((rows, width), F32),
        ((rows, LANES), F32),
        ((rows, width), F32),
        ((rows, LANES), F32),
        ((rows, hidden), F32),
        ((rows, width), BF16),
        ((rows, edge_width), BF16),
        ((rows, edge_width), F32),
    ]
    return small_call(
        functools.partial(residue_forward_kernel, len(f1)),
        (node, total, m3, b3, g1, fb2, g2, e_first, e_far, eb, *f1, *f2),
        shapes, "residue_forward", flops=4 * rows * width * hidden, moved=5 * MIB,
        exps=rows * hidden,
    )


def edge_kernel(
    sb, blocks, hi_chunks, far_lo, far_hi, own, edge, cot, idx, idx_row, live_col,
    e_first, e2, eb2, e3, eb3, g3,
    edge_out, act_one_out, act_two_out, low_three_out, low_two_out, low_one_out, hi_out, lo_out, own_out, gain_out,
    low_first, gs,
):
    step = pl.program_id(0)
    rows, width = own.shape
    node_width = (e_first.shape[1] - width) // 2
    e_mid = e_first.at[:, node_width : node_width + width]

    @pl.when(step == 0)
    def _():
        own_out[...] = jnp.zeros_like(own_out)
        gs[...] = jnp.zeros_like(gs)

    @pl.when(step < blocks)
    def _():
        block = sb * rows
        flat = edge[...].reshape(block, width)
        mixed = pick_rows(index_columns(idx[...]), (far_lo, far_hi)) + dot_back(flat, e_mid[...])
        w_one = (mixed.reshape(sb, rows, width) + own[...][None]).reshape(block, width)
        act_one, slope_one = gelu_parts(w_one)
        act_one = act_one.astype(BF16)
        act_one_out[...] = act_one
        act_two, slope_two = gelu_parts(dot(act_one, e2[...]) + eb2[...])
        act_two = act_two.astype(BF16)
        act_two_out[...] = act_two
        w_three = dot(act_two, e3[...]) + eb3[...]
        normed, scale = norm(flat.astype(F32) + w_three)
        count = spread(live_col[...], pl.cdiv(width, LANES) * LANES)[:, :width]
        live = jnp.concatenate(
            [jnp.where(count > step * sb + s, 1.0, 0.0) for s in range(sb)], axis=0
        )
        edge_out[...] = (normed * g3[...] * live).astype(BF16).reshape(sb, rows, width)
        grad = cot[...].reshape(block, width).astype(F32) * live
        gs[...] += jnp.sum((grad * normed).reshape(sb, rows, width), axis=0)
        low_three = norm_back(grad * g3[...], normed, scale).astype(BF16)
        low_three_out[...] = low_three
        low_two = (dot_back(low_three, e3[...]) * slope_two).astype(BF16)
        low_two_out[...] = low_two
        low_one = (dot_back(low_two, e2[...]) * slope_one).astype(BF16)
        low_one_out[...] = low_one
        own_out[...] += jnp.sum(low_one.astype(F32).reshape(sb, rows, width), axis=0)
        low_first[pl.ds(pl.multiple_of(step * block, block), block), :] = low_one

    chunk = hi_out.shape[0]

    @pl.when((step >= blocks) & (step < blocks + hi_chunks))
    def _():
        start = (step - blocks + hi_chunks) * chunk
        hi_out[...] = dot(one_hot_rows(idx_row[...], start, chunk), low_first[...]).astype(BF16)

    @pl.when(step >= blocks + hi_chunks)
    def _():
        start = (step - blocks - hi_chunks) * chunk
        lo_out[...] = dot(one_hot_rows(idx_row[...], start, chunk), low_first[...])

    @pl.when(step == blocks + 2 * hi_chunks - 1)
    def _():
        gain_out[...] = column_sum(gs[...])


def edge_branch(far_lo, far_hi, own, edge, cot, idx_row, live_col, e_first, e2, eb2, e3, eb3, g3):
    slots, rows, width = edge.shape
    sb = slot_block(slots)
    edges = slots * rows
    block = sb * rows
    blocks = slots // sb
    half = far_lo.shape[0]
    chunk = min(512, half)
    hi_chunks = half // chunk
    blk = lambda i: jnp.minimum(i, blocks - 1)
    hi_at = lambda i: (jnp.clip(i - blocks, 0, hi_chunks - 1), 0)
    lo_at = lambda i: (jnp.clip(i - blocks - hi_chunks, 0, hi_chunks - 1), 0)
    slot_spec = pl.BlockSpec((sb, rows, width), lambda i: (blk(i), 0, 0))
    row_spec = pl.BlockSpec((block, width), lambda i: (blk(i), 0))
    return pl.pallas_call(
        functools.partial(edge_kernel, sb, blocks, hi_chunks),
        grid=(blocks + 2 * hi_chunks,),
        in_specs=[
            const_spec(far_lo.shape),
            const_spec(far_hi.shape),
            const_spec(own.shape),
            slot_spec,
            slot_spec,
            pl.BlockSpec((1, block), lambda i: (0, blk(i))),
            const_spec(idx_row.shape),
            const_spec(live_col.shape),
            const_spec(e_first.shape),
            const_spec(e2.shape),
            const_spec(eb2.shape),
            const_spec(e3.shape),
            const_spec(eb3.shape),
            const_spec(g3.shape),
        ],
        out_specs=[slot_spec]
        + [row_spec] * 5
        + [
            pl.BlockSpec((chunk, width), hi_at),
            pl.BlockSpec((chunk, width), lo_at),
            pl.BlockSpec((rows, width), whole),
            pl.BlockSpec((1, width), whole),
        ],
        out_shape=[jax.ShapeDtypeStruct((slots, rows, width), BF16)]
        + [jax.ShapeDtypeStruct((edges, width), BF16)] * 5
        + [
            jax.ShapeDtypeStruct((half, width), BF16),
            jax.ShapeDtypeStruct((half, width), F32),
            jax.ShapeDtypeStruct((rows, width), F32),
            jax.ShapeDtypeStruct((1, width), F32),
        ],
        scratch_shapes=[pltpu.VMEM((edges, width), BF16), pltpu.VMEM((rows, width), F32)],
        compiler_params=pltpu.CompilerParams(vmem_limit_bytes=VMEM),
        name="edge_branch",
        cost_estimate=pl.CostEstimate(
            flops=2 * edges * width * (4 * half + 5 * width),
            bytes_accessed=edges * width * 16,
            transcendentals=2 * edges * width,
        ),
    )(far_lo, far_hi, own, edge, cot, idx_row, idx_row, live_col, e_first, e2, eb2, e3, eb3, g3)


def edge_weights_kernel(blocks, pairs, *refs):
    step = pl.program_id(0)
    lefts, rights = refs[:pairs], refs[pairs : 2 * pairs]
    grads, biases, sums = refs[2 * pairs : 3 * pairs], refs[3 * pairs : 4 * pairs], refs[-1]
    rows = sums.shape[1]

    @pl.when(step == 0)
    def _():
        for ref in (*grads, sums):
            ref[...] = jnp.zeros_like(ref)

    for at in range(pairs):
        left, right = [r[...].reshape(-1, r.shape[-1]) for r in (lefts[at], rights[at])]
        grads[at][...] += dot_rows(left, right)
        low = left if lefts[at].ndim < rights[at].ndim else right
        sums[at] += jnp.sum(low.astype(F32).reshape(-1, rows, low.shape[1]), axis=0)

    @pl.when(step == blocks - 1)
    def _():
        for at in range(pairs):
            biases[at][...] = column_sum(sums[at])


def edge_weights(lefts, rights, rows):
    pairs = len(lefts)
    edges, width = lefts[0].shape
    slots = edges // rows
    sb = slot_block(slots)

    def spec(array):
        if array.ndim == 3:
            return pl.BlockSpec((sb, rows, width), lambda i: (i, 0, 0))
        return pl.BlockSpec((sb * rows, width), lambda i: (i, 0))

    shapes = [(width, width)] * pairs + [(1, width)] * pairs
    return pl.pallas_call(
        functools.partial(edge_weights_kernel, slots // sb, pairs),
        grid=(slots // sb,),
        in_specs=[spec(array) for array in (*lefts, *rights)],
        out_specs=[pl.BlockSpec(s, whole) for s in shapes],
        out_shape=[jax.ShapeDtypeStruct(s, F32) for s in shapes],
        scratch_shapes=[pltpu.VMEM((pairs, rows, width), F32)],
        compiler_params=pltpu.CompilerParams(vmem_limit_bytes=VMEM),
        name="edge_weights",
        cost_estimate=pl.CostEstimate(
            flops=2 * pairs * edges * width * width,
            bytes_accessed=pairs * edges * width * 4,
            transcendentals=0,
        ),
    )(*lefts, *rights)


def early_shapes(width, edge_width):
    return [
        (width, width),
        (edge_width, width),
        (edge_width, edge_width),
        (edge_width, width),
        (edge_width, edge_width),
        (edge_width, edge_width),
        (16, width),
        (16, edge_width),
    ]


def residue_backward_kernel(
    parts, pieces, node_cot, own_sum, e_first, e_far, h2b, n1, sc1, n2, sc2, slope, g1, g2, m3,
    total, e1g, e2g, e3g, eb1, eb2, eb3, edge_gain, *refs,
):
    far = refs[:pieces]
    f1 = refs[pieces : pieces + parts]
    f2 = refs[pieces + parts : pieces + 2 * parts]
    gu1_out, v_out, gy2_out, slab = refs[pieces + 2 * parts :]
    width, hidden = h2b.shape[1], f1[0].shape[1]
    far_sum = far[0][...]
    for ref in far[1:]:
        far_sum = far_sum + ref[...].astype(F32)
    own = own_sum[...]
    g_h2 = (
        node_cot[...].astype(F32)
        + fine(dot, own, e_first[:, :width])
        + fine(dot, far_sum, e_far[...])
    )
    gain_two = column_sum(g_h2 * n2[...])
    g_u2 = norm_back(g_h2 * g2[...], n2[...], sc2[:, :1])
    gy2 = g_u2.astype(BF16)
    gy2_out[...] = gy2
    g_h1 = g_u2
    for p in range(parts):
        gy1 = dot_back(gy2, f2[p][...]) * slope[:, p * hidden : (p + 1) * hidden]
        g_h1 = g_h1 + dot_back(gy1.astype(BF16), f1[p][:width, :])
    gain_one = column_sum(g_h1 * n1[...])
    g_u1 = norm_back(g_h1 * g1[...], n1[...], sc1[:, :1])
    gu1_out[...] = g_u1
    v_out[...] = fine(dot_back, g_u1, m3[...])
    bias = [gain_one, gain_two, column_sum(gy2.astype(F32)), column_sum(g_u1)]
    slab[...] = jnp.zeros_like(slab)
    pack(
        slab,
        [
            dot_rows(total[...].astype(BF16), g_u1.astype(BF16)),
            dot_rows(own.astype(BF16), h2b[...]),
            e1g[...],
            dot_rows(far_sum.astype(BF16), h2b[...]),
            e2g[...],
            e3g[...],
            padded_rows(bias, width),
            padded_rows([eb1[...], eb2[...], eb3[...], edge_gain[...]], own.shape[1]),
        ],
    )


def residue_backward(args, far, f1, f2):
    node_cot, e_first, slope = args[0], args[2], args[9]
    rows, width = node_cot.shape
    tiles = all_tiles(early_shapes(width, e_first.shape[0]))
    shapes = [
        ((rows, width), F32),
        ((rows, width), F32),
        ((rows, width), BF16),
        ((tiles, 16, LANES), BF16),
    ]
    return small_call(
        functools.partial(residue_backward_kernel, len(f1), len(far)),
        (*args, *far, *f1, *f2),
        shapes, "residue_backward",
        flops=4 * rows * width * slope.shape[1], moved=8 * MIB,
    )


def feed_kernel(h_lo, h_hi, g_lo, g_hi, f1, fb1, f2, f1g, f2g, fb1g):

    @pl.when(pl.program_id(0) == 0)
    def _():
        for ref in (f1g, f2g, fb1g):
            ref[...] = jnp.zeros_like(ref)

    for h1b, gy2 in ((h_lo[...], g_lo[...]), (h_hi[...], g_hi[...])):
        act, slope = gelu_parts(dot(h1b, f1[...]) + fb1[...])
        gy1 = (dot_back(gy2, f2[...]) * slope).astype(BF16)
        f1g[...] += dot_rows(h1b, gy1)
        f2g[...] += dot_rows(act.astype(BF16), gy2)
        fb1g[...] += column_sum(gy1.astype(F32))


def feed_gradients(h1b, gy2, f1, fb1, f2):
    width, hidden = f1.shape
    half = h1b[0].shape[0]
    chunk = min(512, half)
    shapes = [(width, hidden), (hidden, width), (1, hidden)]
    return pl.pallas_call(
        feed_kernel,
        grid=(half // chunk,),
        in_specs=[pl.BlockSpec((chunk, width), lambda i: (i, 0))] * 4
        + [const_spec(a.shape) for a in (f1, fb1, f2)],
        out_specs=[pl.BlockSpec(s, whole) for s in shapes],
        out_shape=[jax.ShapeDtypeStruct(s, F32) for s in shapes],
        compiler_params=pltpu.CompilerParams(vmem_limit_bytes=VMEM),
        name="feed_gradients",
        cost_estimate=pl.CostEstimate(
            flops=16 * half * width * hidden,
            bytes_accessed=8 * half * width,
            transcendentals=2 * half * hidden,
        ),
    )(*h1b, *gy2, f1, fb1, f2)


def late_shapes(width, edge_width):
    return [(width, width), (width, width), (edge_width, width), (16, width)]


def message_backward_kernel(sb, first_block, blocks, codes, *refs):
    last = codes is not None
    if last:
        base, refs = refs[0], refs[1:]
    v, a1, s1, s2, edge, live_col, m2 = refs[:7]
    refs = refs[7:]
    if last:
        node, early, own_in, m2g_in, m1eg_in, b2_in, low_out, own, keep, send, m2g, m1eg, b2s, slab = refs
    else:
        low_out, own, m2g, m1eg, b2s = refs
    step = pl.program_id(0)
    rows, width = v.shape
    edge_width = edge.shape[2]
    block = sb * rows

    @pl.when(step == 0)
    def _():
        if last:
            own[...] = own_in[...]
            m2g[...] = m2g_in[...]
            m1eg[...] = m1eg_in[...]
            b2s[...] = b2_in[...]
        else:
            for ref in (own, m2g, m1eg, b2s):
                ref[...] = jnp.zeros_like(ref)

    count = live_col[...]
    inverse = 1.0 / count.astype(F32)
    grads = [
        v[...] * spread(jnp.where(count > (step + first_block) * sb + s, inverse, 0.0), width)
        for s in range(sb)
    ]
    low_two = (jnp.concatenate(grads, axis=0) * s2[...].astype(F32)).astype(BF16)
    m2g[...] += dot_rows(a1[...], low_two)
    b2s[...] += jnp.sum(low_two.astype(F32).reshape(sb, rows, width), axis=0)
    low_one = (dot_back(low_two, m2[...]) * s1[...].astype(F32)).astype(BF16)
    low_out[...] = low_one
    m1eg[...] += dot_rows(edge[...].reshape(block, edge_width), low_one)
    own[...] += jnp.sum(low_one.astype(F32).reshape(sb, rows, width), axis=0)

    if last:
        @pl.when(step == blocks - 1)
        def _():
            count = early.shape[0]
            slab[:count] = early[...]
            slab[count:] = jnp.zeros_like(slab[count:])
            bias = [column_sum(own[...]), column_sum(b2s[...])]
            pack(
                slab,
                [
                    dot_rows(node[...], own[...].astype(BF16)),
                    m2g[...],
                    m1eg[...],
                    padded_rows(bias, width),
                ],
                count,
            )
            order_out(slab, base[0], codes, keep, send)


def message_backward(first_block, blocks, v, a1, s1, s2, edge, live_col, m2, more=()):
    slots, rows, edge_width = edge.shape
    width = v.shape[1]
    sb = slot_block(slots)
    block = sb * rows
    edges = blocks * block
    row_spec = pl.BlockSpec((block, width), lambda i: (i + first_block, 0))
    sums = [(rows, width), (width, width), (edge_width, width), (rows, width)]
    in_specs = [
        const_spec(v.shape),
        row_spec,
        row_spec,
        row_spec,
        pl.BlockSpec((sb, rows, edge_width), lambda i: (i + first_block, 0, 0)),
        const_spec(live_col.shape),
        const_spec(m2.shape),
    ]
    args = (v, a1, s1, s2, edge, live_col, m2)
    codes, scratch = None, []
    outs = [(s, F32) for s in sums]
    if more:
        codes, base, *rest = more
        args = (base, *args, *rest)
        in_specs = [pl.BlockSpec(memory_space=pltpu.SMEM)] + in_specs
        in_specs += [const_spec(a.shape) for a in rest]
        tiles = slab_part(width, edge_width, len(codes)) * len(codes)
        outs = [(sums[0], F32)] + half_shapes(tiles)
        scratch = [pltpu.VMEM(s, F32) for s in sums[1:]] + [slab_scratch(tiles)]
    return pl.pallas_call(
        functools.partial(message_backward_kernel, sb, first_block, blocks, codes),
        grid=(blocks,),
        in_specs=in_specs,
        out_specs=[pl.BlockSpec((block, width), lambda i: (i, 0))]
        + [pl.BlockSpec(s, lambda i, n=len(s): (0,) * n) for s, _ in outs],
        out_shape=[jax.ShapeDtypeStruct((edges, width), BF16)]
        + [jax.ShapeDtypeStruct(*s) for s in outs],
        scratch_shapes=scratch,
        compiler_params=pltpu.CompilerParams(vmem_limit_bytes=VMEM),
        name="message_backward",
        cost_estimate=pl.CostEstimate(
            flops=2 * edges * width * (2 * width + 2 * edge_width),
            bytes_accessed=edges * width * 8 + edges * edge_width * 2,
            transcendentals=0,
        ),
    )(*args)


def far_sums_kernel(start, steps, rows, codes, *refs):
    last = codes is not None
    if last:
        base, idx_row, low_a, low_b, node, m1fg_in, out, keep, send, m1fg, slab = refs
    else:
        idx_row, low_a, low_b, node, out, m1fg = refs
    step = pl.program_id(0)
    cut = low_a.shape[0]
    chunk, width = node.shape
    height = rows // 16

    @pl.when(step == 0)
    def _():
        m1fg[...] = m1fg_in[...] if last else jnp.zeros_like(m1fg)

    first = start + step * chunk
    sums = dot(one_hot_rows(idx_row[:, :cut], first, chunk), low_a[...]) + dot(
        one_hot_rows(idx_row[:, cut:], first, chunk), low_b[...]
    )
    sums = sums.astype(BF16)
    m1fg[...] += dot_rows(node[...], sums)
    at = 0
    for place in range(chunk // rows):
        for lane in range(0, width, LANES):
            tile = sums[place * rows : (place + 1) * rows, lane : lane + LANES]
            out[at : at + height] = tile.reshape(height, 16, LANES)
            at += height

    if last:
        @pl.when(step == steps - 1)
        def _():
            if tile_count(m1fg.shape) < slab.shape[0]:
                slab[...] = jnp.zeros_like(slab)
            pack(slab, [m1fg[...]])
            order_out(slab, base[0], codes, keep, send)


def far_sums(start, idx_row, low_a, low_b, node, rows, more=()):
    half, width = node.shape
    chunk = min(512, half)
    steps = half // chunk
    tiles = chunk * width // (16 * LANES)
    args = [idx_row, low_a, low_b, node]
    in_specs = [const_spec(a.shape) for a in args[:3]] + [pl.BlockSpec((chunk, width), lambda i: (i, 0))]
    outs, codes, scratch = [((width, width), F32)], None, []
    if more:
        codes, base, m1fg = more
        args = [base] + args + [m1fg]
        in_specs = [pl.BlockSpec(memory_space=pltpu.SMEM)] + in_specs + [const_spec(m1fg.shape)]
        far = far_part_tiles(width, len(codes)) * len(codes)
        outs = half_shapes(far)
        scratch = [pltpu.VMEM((width, width), F32), slab_scratch(far)]
    edges = idx_row.shape[1]
    return pl.pallas_call(
        functools.partial(far_sums_kernel, start, steps, rows, codes),
        grid=(steps,),
        in_specs=in_specs,
        out_specs=[pl.BlockSpec((tiles, 16, LANES), lambda i: (i, 0, 0))]
        + [pl.BlockSpec(s, lambda i, n=len(s): (0,) * n) for s, _ in outs],
        out_shape=[jax.ShapeDtypeStruct((tiles * steps, 16, LANES), BF16)]
        + [jax.ShapeDtypeStruct(*s) for s in outs],
        scratch_shapes=scratch,
        compiler_params=pltpu.CompilerParams(vmem_limit_bytes=VMEM),
        name="far_sums",
        cost_estimate=pl.CostEstimate(
            flops=2 * width * half * (edges + width),
            bytes_accessed=edges * width * 2 + half * width * 4,
            transcendentals=0,
        ),
    )(*args)


def edge_gradient_kernel(sb, cut, low_three, low_edge, low_a, low_b, e_first, m1, out):
    step = pl.program_id(0)
    shape = out.shape
    edge_width, width = shape[2], low_a.shape[1]
    for low, use in ((low_a, step < cut), (low_b, step >= cut)):
        @pl.when(use)
        def _(low=low):
            total = (
                low_three[...].astype(F32)
                + dot(low_edge[...], e_first[:, width : width + edge_width])
                + dot_back(low[...], m1[width : width + edge_width, :])
            )
            out[...] = total.reshape(shape)


def edge_gradient(slots, low_three, low_edge, low_a, low_b, e_first, m1):
    edges, edge_width = low_three.shape
    rows = edges // slots
    width = low_a.shape[1]
    sb = slot_block(slots)
    block = sb * rows
    cut = low_a.shape[0] // block
    edge_spec = pl.BlockSpec((block, edge_width), lambda i: (i, 0))
    return pl.pallas_call(
        functools.partial(edge_gradient_kernel, sb, cut),
        grid=(slots // sb,),
        in_specs=[
            edge_spec,
            edge_spec,
            pl.BlockSpec((block, width), lambda i: (jnp.minimum(i, cut - 1), 0)),
            pl.BlockSpec((block, width), lambda i: (jnp.maximum(i - cut, 0), 0)),
            const_spec(e_first.shape),
            const_spec(m1.shape),
        ],
        out_specs=pl.BlockSpec((sb, rows, edge_width), lambda i: (i, 0, 0)),
        out_shape=jax.ShapeDtypeStruct((slots, rows, edge_width), F32),
        compiler_params=pltpu.CompilerParams(vmem_limit_bytes=VMEM),
        name="edge_gradient",
        cost_estimate=pl.CostEstimate(
            flops=2 * edges * edge_width * (width + edge_width),
            bytes_accessed=edges * (width * 2 + 2048),
            transcendentals=0,
        ),
    )(low_three, low_edge, low_a, low_b, e_first, m1)


def node_kernel(pieces, g_u1, own, m1, *refs):
    far, grad_out = refs[:pieces], refs[pieces]
    rows, width = own.shape
    height = rows // 16
    sums = far[0][...].astype(F32)
    for ref in far[1:]:
        sums = sums + ref[...].astype(F32)
    far_sum = jnp.concatenate(
        [sums[j * height : (j + 1) * height].reshape(rows, LANES) for j in range(width // LANES)],
        axis=1,
    )
    far_first = m1.shape[0] - width
    grad_out[...] = (
        g_u1[...]
        + fine(dot_back, own[...], m1[:width, :])
        + fine(dot_back, far_sum, m1[far_first:, :])
    )


def node_last(g_u1, own, m1, far):
    return small_call(
        functools.partial(node_kernel, len(far)),
        (g_u1, own, m1, *far), [(own.shape, F32)], "node_gradient",
        flops=8 * own.size * own.shape[1], moved=2 * MIB,
    )[0]


def weights_out_kernel(
    codes, base, first, second,
    m1g, b1, m2g, b2, m3g, e1g, e2g, e3g, b3, g1, g2, fb2, eb1, eb2, eb3, g3, slab, far_slab,
):
    order_in((slab, far_slab), base[0], codes, first, second)
    width, edge_width = m3g.shape[0], e2g.shape[0]
    starts, at = [], 0
    for shape in early_shapes(width, edge_width) + late_shapes(width, edge_width):
        starts.append(at)
        at += tile_count(shape)
    m3g[...] = unpack(slab, starts[0], width, width)
    e1g[:, :width] = unpack(slab, starts[1], edge_width, width)
    middle = unpack(slab, starts[2], edge_width, edge_width)
    far = unpack(slab, starts[3], edge_width, width)
    over = edge_width % LANES
    base_col = width + edge_width - over
    e1g[:, width:base_col] = middle[:, : edge_width - over]
    far = pltpu.roll(jnp.concatenate([far, jnp.zeros((edge_width, LANES), F32)], axis=1), over, 1)
    lane = lax.broadcasted_iota(jnp.int32, (edge_width, LANES), 1)
    e1g[:, base_col : base_col + LANES] = jnp.where(
        lane < over, middle[:, edge_width - over : edge_width - over + LANES], far[:, :LANES]
    )
    rest = e1g.shape[1] - base_col - LANES
    e1g[:, base_col + LANES :] = far[:, LANES : LANES + rest]
    e2g[...] = unpack(slab, starts[4], edge_width, edge_width)[:, :edge_width]
    e3g[...] = unpack(slab, starts[5], edge_width, edge_width)[:, :edge_width]
    bias = unpack(slab, starts[6], 16, width)
    for row, out in enumerate((g1, g2, fb2, b3)):
        out[...] = bias[row : row + 1]
    bias = unpack(slab, starts[7], 16, edge_width)
    for row, out in enumerate((eb1, eb2, eb3, g3)):
        out[...] = bias[row : row + 1, :edge_width]
    m1g[:width, :] = unpack(slab, starts[8], width, width)
    m2g[...] = unpack(slab, starts[9], width, width)
    m1g[width : width + edge_width, :] = unpack(slab, starts[10], edge_width, width)
    m1g[width + edge_width :, :] = unpack(far_slab, 0, width, width)
    bias = unpack(slab, starts[11], 16, width)
    b1[...] = bias[0:1]
    b2[...] = bias[1:2]


def weights_out(codes, base, halves_in, width, edge_width):
    shapes = [(2 * width + edge_width, width), (1, width), (width, width), (1, width)]
    shapes += [(width, width), (edge_width, 2 * width + edge_width)]
    shapes += [(edge_width, edge_width)] * 2 + [(1, width)] * 4 + [(1, edge_width)] * 4
    chunks = len(codes)
    tiles = slab_part(width, edge_width, chunks) * chunks
    far_tiles = far_part_tiles(width, chunks) * chunks
    return small_call(
        functools.partial(weights_out_kernel, codes),
        (base, *halves_in), [(s, F32) for s in shapes], "weight_gradients",
        [slab_scratch(tiles), slab_scratch(far_tiles)], moved=10 * MIB, scalars=1,
    )


def exchange(value, mask, devices):
    return lax.ppermute(value, AXES, [(d, d ^ mask) for d in range(devices)])


def mask_groups(masks):
    return [masks[i : min(i + 2, len(masks) - 1)] for i in range(0, len(masks) - 1, 2)] + [masks[-1:]]


def order_codes(groups):
    masks = [mask for group in groups for mask in group]
    return [
        sum(mask for bit, mask in enumerate(masks) if place >> bit & 1)
        for place in range(1 << len(masks))
    ]


def combined(group, code):
    return sum(mask for bit, mask in enumerate(group) if code >> bit & 1)


def sent_around(value, group, devices):
    return [value] + [
        exchange(value, combined(group, code), devices) for code in range(1, 1 << len(group))
    ]


def shared_out(total, group, devices):
    parts = 1 << len(group)
    rows = total.shape[0] // parts
    return [total[:rows]] + [
        exchange(total[code * rows : (code + 1) * rows].astype(BF16), combined(group, code), devices)
        for code in range(1, parts)
    ]


def add_up(terms):
    total = terms[0].astype(F32)
    for term in terms[1:]:
        total = total + term.astype(F32)
    return total


def tied(*values):
    return lax.optimization_barrier(values)


def split_three(value):
    rows = []
    for _ in range(3):
        high = lax.reduce_precision(value, 8, 7)
        rows.append(high.astype(BF16))
        value = value - high
    return jnp.concatenate(rows + [jnp.zeros((13, value.shape[1]), BF16)], axis=0)


def per_device(
    node_in,
    edge_in,
    neighbours,
    live_counts,
    message_first,
    message_first_bias,
    message_second,
    message_second_bias,
    message_third,
    message_third_bias,
    norm_one,
    feed_first,
    feed_first_bias,
    feed_second,
    feed_second_bias,
    norm_two,
    edge_first,
    edge_first_bias,
    edge_second,
    edge_second_bias,
    edge_third,
    edge_third_bias,
    norm_three,
    node_cotangent,
    edge_cotangent,
):
    rows, slots = neighbours.shape
    width = node_in.shape[1]
    edge_width = edge_in.shape[2]
    edges = rows * slots
    hid_count = lax.axis_size("hid")
    res_count = lax.axis_size("res")
    devices = res_count * hid_count
    bits = devices.bit_length() - 1
    masks = [1 << b for b in range(bits - 1, -1, -1)]
    groups = mask_groups(masks)
    codes = order_codes(groups)
    me = lax.axis_index("res") * hid_count + lax.axis_index("hid")
    base = me.reshape(1)
    row = lambda vector: vector.reshape(1, -1)

    names = neighbours.T.reshape(edges)
    apart = (names // rows) ^ me
    place = jnp.zeros_like(names)
    for bit, mask in enumerate(masks):
        place = place | jnp.where((apart & mask) != 0, 1 << bit, 0)
    idx_row = (place * rows + names % rows).reshape(1, edges)
    live_col = jnp.broadcast_to(live_counts[:, None], (rows, LANES))
    edge = edge_in.transpose(1, 0, 2)
    cot = edge_cotangent.transpose(1, 0, 2)
    e_first = edge_first.T
    e_far = e_first[:, width + edge_width :]
    f1x = jnp.concatenate([feed_first, split_three(row(feed_first_bias))], axis=0)
    f2x = feed_second

    tiled = lambda value, per: value.reshape(-1, per, 16, LANES)
    stack = lambda pieces: jnp.concatenate(pieces, axis=0)
    *outer, near = groups

    held = stack(sent_around(node_in, outer[0], devices))
    held, idx_row, live_col, e_far = tied(held, idx_row, live_col, e_far)
    for group in outer[1:]:
        held = stack(sent_around(held, group, devices))
    held, f1x, f2x = tied(held, f1x, f2x)
    node_lo, node_hi = sent_around(held, near, devices)

    f1, f2 = [f1x], [f2x]
    hid_masks = [m for m in masks if m < hid_count]
    for mask in hid_masks[:-1]:
        f1, f2 = [pieces + [exchange(p, mask, devices) for p in pieces] for pieces in (f1, f2)]

    sb = slot_block(slots)
    blocks = slots // sb
    cut = max(1, 5 * blocks // 6)
    message_args = (
        node_in, edge, idx_row, live_col, message_first, row(message_first_bias), message_second,
        row(message_second_bias),
    )
    a1, s1, s2, total, own_part, far_lo, far_hi = message_forward(
        0, cut, *message_args, (node_lo, node_hi)
    )
    total, f1, f2 = tied(total, f1, f2)
    f1, f2 = [
        pieces + [exchange(p, hid_masks[-1], devices) for p in pieces] for pieces in (f1, f2)
    ]
    a1, s1, s2, total = message_forward(
        cut, blocks - cut, *message_args, (far_lo, far_hi, own_part, total, a1, s1, s2)
    )
    h1b, n1, sc1, n2, sc2, slope, h2b, far_part, own_part = residue_forward(
        node_in, total, message_third, row(message_third_bias), row(norm_one),
        row(feed_second_bias), row(norm_two), e_first, e_far, row(edge_first_bias), f1, f2,
    )

    held = stack(sent_around(far_part, outer[0], devices))
    h_held = stack(sent_around(h1b, outer[0], devices))
    for group in outer[1:]:
        held = stack(sent_around(held, group, devices))
    held, h_held = tied(held, h_held)
    q_lo, q_hi = sent_around(held, near, devices)
    for group in outer[1:]:
        h_held = stack(sent_around(h_held, group, devices))

    edge_out, act_one, act_two, low_three, low_two, low_one, hi, lo, own_sum, edge_gain = edge_branch(
        q_lo, q_hi, own_part, edge, cot, idx_row, live_col, e_first,
        edge_second, row(edge_second_bias), edge_third, row(edge_third_bias), row(norm_three),
    )
    lo, h_held = tied(lo, h_held)
    h_all = sent_around(h_held, near, devices)

    work = [
        lambda: edge_weights((act_two, act_one), (low_three, low_two), rows),
        lambda: edge_weights((low_one,), (edge,), rows),
    ]
    made = []
    terms = [lo, exchange(hi, near[0], devices)]
    for group in reversed(outer):
        terms = shared_out(add_up(terms), group, devices)
        if work:
            terms, got = tied(terms, work.pop(0)())
            made.append(got)
    while work:
        made.append(work.pop(0)())
    (e3g, e2g, eb3, eb2), (e1g, eb1) = made
    g_u1, v, gy2, early = residue_backward(
        (
            node_cotangent, own_sum, e_first, e_far, h2b, n1, sc1, n2, sc2, slope, row(norm_one),
            row(norm_two), message_third, total, e1g, e2g, e3g, eb1, eb2, eb3, edge_gain,
        ),
        terms, f1, f2,
    )

    g_held = stack(sent_around(gy2, outer[0], devices))
    low_a, *sums = message_backward(
        0, blocks // 2, v, a1, s1, s2, edge, live_col, message_second
    )
    v, g_held = tied(v, g_held)
    for group in outer[1:]:
        g_held = stack(sent_around(g_held, group, devices))
    low_b, own, keep, send = message_backward(
        blocks // 2, blocks - blocks // 2, v, a1, s1, s2, edge, live_col, message_second,
        (codes, base, node_in, early, *sums),
    )

    terms = [keep, exchange(send, near[0], devices)]
    hi, m1fg = far_sums(node_lo.shape[0], idx_row, low_a, low_b, node_hi, rows)
    total, m1fg = tied(add_up(terms), m1fg)
    first, *others = reversed(outer)
    terms = shared_out(total, first, devices)
    got = exchange(hi, near[0], devices)
    lo, keep, send = far_sums(0, idx_row, low_a, low_b, node_lo, rows, (codes, base, m1fg))
    for group in others:
        terms = shared_out(add_up(terms), group, devices)
    slab_chunk = add_up(terms).astype(BF16)

    g_all = sent_around(g_held, near, devices)
    sums_part, far_part = rows * width // (16 * LANES), far_part_tiles(width, devices)
    total = jnp.concatenate(
        [
            tiled(add_up([lo, got]), sums_part),
            tiled(add_up([keep, exchange(send, near[0], devices)]), far_part),
        ],
        axis=1,
    )
    terms = [total]
    work = [
        lambda: edge_gradient(slots, low_three, low_one, low_a, low_b, e_first, message_first),
        lambda: feed_gradients(h_all, g_all, feed_first, row(feed_first_bias), feed_second),
    ]
    made = []
    for group in reversed(outer):
        terms = shared_out(add_up(terms), group, devices)
        if work:
            terms, out = tied(terms, work.pop(0)())
            made.append(out)
    while work:
        made.append(work.pop(0)())
    edge_grad, (f1g, f2g, fb1g) = made
    node_gradient = node_last(
        g_u1, own, message_first, [t[0, :sums_part] for t in terms]
    )
    far_chunk = add_up([t[:, sums_part:] for t in terms]).astype(BF16)

    held = jnp.concatenate(
        [
            stack(sent_around(tiled(slab_chunk, slab_chunk.shape[0]), outer[0], devices)),
            stack(sent_around(far_chunk, outer[0], devices)),
        ],
        axis=1,
    )
    for group in outer[1:]:
        held = stack(sent_around(held, group, devices))
    weights = [w.reshape(-1, 16, LANES) for w in sent_around(held, near, devices)]
    m1g, b1, m2g, b2, m3g, e1g, e2g, e3g, b3, g1, g2, fb2, eb1, eb2, eb3, g3 = weights_out(
        codes, base, weights, width, edge_width
    )
    flat = lambda vector: vector.reshape(-1)
    return (
        h2b,
        edge_out.transpose(1, 0, 2),
        node_gradient,
        edge_grad.transpose(1, 0, 2),
        m1g,
        flat(b1),
        m2g,
        flat(b2),
        m3g,
        flat(b3),
        flat(g1),
        f1g,
        flat(fb1g),
        f2g,
        flat(fb2),
        flat(g2),
        e1g.T,
        flat(eb1),
        e2g,
        flat(eb2),
        e3g,
        flat(eb3),
        flat(g3),
    )


def solution(mesh):
    nodes, edges, shared = P(AXES, None), P(AXES, None, None), P()
    return jax.shard_map(
        per_device,
        mesh=mesh,
        in_specs=(nodes, edges, nodes, P(AXES))
        + (shared,) * 7
        + (P(None, "hid"), P("hid"), P("hid", None))
        + (shared,) * 9
        + (nodes, edges),
        out_specs=(nodes, edges, nodes, edges)
        + (shared,) * 7
        + (P(None, "hid"), P("hid"), P("hid", None))
        + (shared,) * 9,
        check_vma=False,
    )
```

```python
import functools

import jax
import jax.numpy as jnp
from jax import lax
from jax.experimental import pallas as pl
from jax.experimental.pallas import tpu as pltpu
from jax.sharding import PartitionSpec as P

EPS = 1e-05
AXES = ("res", "hid")
F32 = jnp.float32
BF16 = jnp.bfloat16
TANH_SCALE = 0.7978845608028654
TANH_CUBE = 0.044715
LANES = 128
CHUNK = 2048
MIB = 1024 * 1024
VMEM = 58 * MIB


def dot(left, right):
    return lax.dot_general(left, right, (((1,), (0,)), ((), ())), preferred_element_type=F32)


def dot_rows(left, right):
    return lax.dot_general(left, right, (((0,), (0,)), ((), ())), preferred_element_type=F32)


def dot_back(left, right):
    return lax.dot_general(left, right, (((1,), (1,)), ((), ())), preferred_element_type=F32)


def halves(value):
    high = value.astype(BF16)
    return high, (value - high.astype(F32)).astype(BF16)


def fine(product, value, weights):
    high, low = halves(value)
    return product(high, weights) + product(low, weights)


def gelu_parts(x):
    square = x * x
    t = jnp.tanh(x * (TANH_SCALE + (TANH_SCALE * TANH_CUBE) * square))
    gate = 0.5 + 0.5 * t
    act = x * gate
    slope = gate + act * (1.0 - gate) * (2 * TANH_SCALE + (6 * TANH_SCALE * TANH_CUBE) * square)
    return act, slope


def index_columns(idx_row):
    parts = [
        jnp.broadcast_to(idx_row[:, first : first + LANES], (LANES, LANES)).T
        for first in range(0, idx_row.shape[1], LANES)
    ]
    return jnp.concatenate(parts, axis=0)


def one_hot_columns(idx, start, count):
    lane = lax.broadcasted_iota(jnp.int32, idx.shape, 1)
    parts = [
        jnp.where(idx == lane + (start + first), 1.0, 0.0).astype(BF16)
        for first in range(0, count, LANES)
    ]
    return jnp.concatenate(parts, axis=1)


def pick_rows(idx, table_refs):
    total, start = None, 0
    for ref in table_refs:
        rows = ref.shape[0]
        step = min(rows, CHUNK)
        for first in range(0, rows, step):
            part = dot(one_hot_columns(idx, start + first, step), ref[first : first + step, :])
            total = part if total is None else total + part
        start += rows
    return total


def one_hot_rows(idx_row, start, count):
    row = lax.broadcasted_iota(jnp.int32, (count, idx_row.shape[1]), 0) + start
    return jnp.where(jnp.broadcast_to(idx_row, row.shape) == row, 1.0, 0.0).astype(BF16)


def spread(column, width):
    return jnp.concatenate([column] * (width // LANES), axis=1)


def norm(value):
    centre = value - jnp.mean(value, -1, keepdims=True)
    scale = lax.rsqrt(jnp.mean(centre * centre, -1, keepdims=True) + EPS)
    return centre * scale, scale


def norm_back(inner, normed, scale):
    mean_first = jnp.mean(inner, -1, keepdims=True)
    mean_second = jnp.mean(inner * normed, -1, keepdims=True)
    return scale * (inner - mean_first - normed * mean_second)


def column_sum(value):
    return jnp.sum(value, axis=0, keepdims=True)


def whole(*_):
    return (0, 0)


def const_spec(shape):
    return pl.BlockSpec(shape, lambda *_: (0,) * len(shape), pipeline_mode=pl.Buffered(1))


def small_call(kernel, args, shapes, name, scratch=(), flops=0, moved=0, exps=0, scalars=0):
    return pl.pallas_call(
        kernel,
        grid=(1,),
        in_specs=[pl.BlockSpec(memory_space=pltpu.SMEM)] * scalars
        + [const_spec(a.shape) for a in args[scalars:]],
        out_specs=[pl.BlockSpec(s, lambda *_, n=len(s): (0,) * n) for s, _ in shapes],
        out_shape=[jax.ShapeDtypeStruct(*s) for s in shapes],
        scratch_shapes=list(scratch),
        compiler_params=pltpu.CompilerParams(vmem_limit_bytes=VMEM),
        name=name,
        cost_estimate=pl.CostEstimate(flops=flops, bytes_accessed=moved, transcendentals=exps),
    )(*args)


def tile_count(shape):
    return pl.cdiv(shape[0], 16) * pl.cdiv(shape[1], LANES)


def all_tiles(shapes):
    return sum(tile_count(s) for s in shapes)


def pack(slab, values, at=0):
    for value in values:
        rows, columns = value.shape
        count = rows // 16
        for first in range(0, columns, LANES):
            take = min(LANES, columns - first)
            tile = value[:, first : first + take].astype(BF16).reshape(count, 16, take)
            slab[at : at + count, :, :take] = tile
            at += count


def unpack(slab, at, rows, columns):
    count = rows // 16
    parts = [
        slab[at + i * count : at + (i + 1) * count].reshape(rows, LANES).astype(F32)
        for i in range(pl.cdiv(columns, LANES))
    ]
    return jnp.concatenate(parts, axis=1)


def order_out(slab, base, codes, keep, send):
    size = slab.shape[0] // len(codes)
    half = len(codes) // 2
    for place, code in enumerate(codes):
        out = keep if place < half else send
        at = (place % half) * size
        out[at : at + size] = slab[pl.ds((base ^ code) * size, size)]


def half_shapes(tiles):
    return [((tiles // 2, 16, LANES), BF16)] * 2


def slab_scratch(tiles):
    return pltpu.VMEM((tiles, 16, LANES), BF16)


def slab_part(width, edge_width, chunks):
    return pl.cdiv(all_tiles(early_shapes(width, edge_width) + late_shapes(width, edge_width)), chunks)


def far_part_tiles(width, chunks):
    return pl.cdiv(all_tiles([(width, width)]), chunks)


def order_in(slabs, base, codes, first, second):
    sizes = [slab.shape[0] // len(codes) for slab in slabs]
    half = len(codes) // 2
    for place, code in enumerate(codes):
        source = first if place < half else second
        at = (place % half) * sum(sizes)
        for slab, size in zip(slabs, sizes):
            slab[pl.ds((base ^ code) * size, size)] = source[at : at + size]
            at += size


def padded_rows(parts, width):
    return jnp.concatenate(parts + [jnp.zeros((16 - len(parts), width), F32)], axis=0)


def slot_block(slots):
    for size in (10, 12, 8, 6, 5, 4, 3, 2):
        if slots % size == 0:
            return size
    return 1


def message_forward_kernel(sb, first_block, blocks, fresh, node_own, edge, idx_row, live_col, m1, b1, m2, b2, *refs):
    if fresh:
        node_lo, node_hi = refs[:2]
        a1_out, s1_out, s2_out, sum_out, own_part, lo_out, hi_out, far_lo, far_hi, sems = refs[2:]
    else:
        far_lo, far_hi, own_part, sum_in = refs[:4]
        a1_out, s1_out, s2_out, sum_out = refs[7:]
    step = pl.program_id(0)
    width = node_own.shape[1]
    edge_width = edge.shape[2]
    rows = edge.shape[1]

    @pl.when(step == 0)
    def _():
        if not fresh:
            sum_out[...] = sum_in[...]
            return
        sum_out[...] = jnp.zeros_like(sum_out)
        own_part[...] = dot(node_own[...], m1[:width, :]) + b1[...]
        tile = min(512, node_lo.shape[0])
        for source, target in ((node_lo, far_lo), (node_hi, far_hi)):
            def body(i, carry, source=source, target=target):
                at = pl.ds(pl.multiple_of(i * tile, tile), tile)
                target[at, :] = dot(source[at, :], m1[width + edge_width :, :]).astype(BF16)
                return carry
            lax.fori_loop(0, source.shape[0] // tile, body, 0)
        pltpu.make_async_copy(far_lo, lo_out, sems.at[0]).start()
        pltpu.make_async_copy(far_hi, hi_out, sems.at[1]).start()

    flat = edge[...].reshape(sb * rows, edge_width)
    mixed = pick_rows(index_columns(idx_row[...]), (far_lo, far_hi)) + dot(flat, m1[width : width + edge_width, :])
    z_one = (mixed.reshape(sb, rows, width) + own_part[...][None]).reshape(sb * rows, width)
    act, slope = gelu_parts(z_one)
    act = act.astype(BF16)
    a1_out[...] = act
    s1_out[...] = slope.astype(BF16)
    act, slope = gelu_parts(dot(act, m2[...]) + b2[...])
    s2_out[...] = slope.astype(BF16)
    act = act.astype(BF16).astype(F32).reshape(sb, rows, width)
    count = live_col[...]
    inverse = 1.0 / count.astype(F32)
    total = sum_out[...]
    for s in range(sb):
        share = jnp.where(count > (step + first_block) * sb + s, inverse, 0.0)
        total = total + act[s] * spread(share, width)
    sum_out[...] = total

    if fresh:
        @pl.when(step == blocks - 1)
        def _():
            pltpu.make_async_copy(far_lo, lo_out, sems.at[0]).wait()
            pltpu.make_async_copy(far_hi, hi_out, sems.at[1]).wait()


def message_forward(first_block, blocks, node_own, edge, idx_row, live_col, m1, b1, m2, b2, more):
    slots, rows, edge_width = edge.shape
    width = node_own.shape[1]
    sb = slot_block(slots)
    block = sb * rows
    edges = blocks * block
    fresh = len(more) == 2
    half = more[0].shape
    out_specs = [pl.BlockSpec((block, width), lambda i: (i + first_block, 0))] * 3
    out_specs += [pl.BlockSpec((rows, width), whole)]
    out_shape = [jax.ShapeDtypeStruct((slots * rows, width), BF16)] * 3 + [
        jax.ShapeDtypeStruct((rows, width), F32)
    ]
    scratch = []
    if fresh:
        out_specs += [pl.BlockSpec((rows, width), whole)] + [pl.BlockSpec(memory_space=pl.ANY)] * 2
        out_shape += [jax.ShapeDtypeStruct((rows, width), F32)] + [jax.ShapeDtypeStruct(half, BF16)] * 2
        scratch = [pltpu.VMEM(half, BF16), pltpu.VMEM(half, BF16), pltpu.SemaphoreType.DMA((2,))]
    return pl.pallas_call(
        functools.partial(message_forward_kernel, sb, first_block, blocks, fresh),
        grid=(blocks,),
        in_specs=[
            const_spec(node_own.shape),
            pl.BlockSpec((sb, rows, edge_width), lambda i: (i + first_block, 0, 0)),
            pl.BlockSpec((1, block), lambda i: (0, i + first_block)),
            const_spec(live_col.shape),
            const_spec(m1.shape),
            const_spec(b1.shape),
            const_spec(m2.shape),
            const_spec(b2.shape),
        ]
        + [const_spec(a.shape) for a in more[:4]]
        + [pl.BlockSpec(memory_space=pl.ANY)] * len(more[4:]),
        out_specs=out_specs,
        out_shape=out_shape,
        scratch_shapes=scratch,
        input_output_aliases={} if fresh else {12: 0, 13: 1, 14: 2},
        compiler_params=pltpu.CompilerParams(vmem_limit_bytes=VMEM),
        name="message_forward",
        cost_estimate=pl.CostEstimate(
            flops=2 * edges * width * (2 * half[0] + edge_width + width),
            bytes_accessed=edges * width * 6 + edges * edge_width * 2 + edges * LANES * 4,
            transcendentals=2 * edges * width,
        ),
    )(node_own, edge, idx_row, live_col, m1, b1, m2, b2, *more)


def residue_forward_kernel(parts, node, total, m3, b3, g1, fb2, g2, e_first, e_far, eb, *refs):
    f1, f2 = refs[:parts], refs[parts : 2 * parts]
    h1b_out, n1_out, sc1_out, n2_out, sc2_out, slope_out, h2b_out, far_out, own_out = refs[2 * parts :]
    width, hidden = node.shape[1], f1[0].shape[1]
    u1 = node[...].astype(F32) + fine(dot, total[...], m3[...]) + b3[...]
    n1, sc1 = norm(u1)
    h1 = n1 * g1[...]
    h1b = h1.astype(BF16)
    h1b_out[...] = h1b
    n1_out[...] = n1
    sc1_out[...] = jnp.broadcast_to(sc1, sc1_out.shape)
    y2 = None
    for p in range(parts):
        bias = f1[p][width : width + 16, :].astype(F32)
        bias = bias[0:1] + bias[1:2] + bias[2:3]
        act, slope = gelu_parts(dot(h1b, f1[p][:width, :]) + bias)
        slope_out[:, p * hidden : (p + 1) * hidden] = slope
        part = dot(act.astype(BF16), f2[p][...])
        y2 = part if y2 is None else y2 + part
    n2, sc2 = norm(h1 + (y2 + fb2[...]))
    h2b = (n2 * g2[...]).astype(BF16)
    n2_out[...] = n2
    sc2_out[...] = jnp.broadcast_to(sc2, sc2_out.shape)
    h2b_out[...] = h2b
    far_out[...] = dot_back(h2b, e_far[...]).astype(BF16)
    own_out[...] = dot_back(h2b, e_first[:, :width]) + eb[...]


def residue_forward(node, total, m3, b3, g1, fb2, g2, e_first, e_far, eb, f1, f2):
    rows, width = node.shape
    edge_width = e_first.shape[0]
    hidden = len(f1) * f1[0].shape[1]
    shapes = [
        ((rows, width), BF16),
        ((rows, width), F32),
        ((rows, LANES), F32),
        ((rows, width), F32),
        ((rows, LANES), F32),
        ((rows, hidden), F32),
        ((rows, width), BF16),
        ((rows, edge_width), BF16),
        ((rows, edge_width), F32),
    ]
    return small_call(
        functools.partial(residue_forward_kernel, len(f1)),
        (node, total, m3, b3, g1, fb2, g2, e_first, e_far, eb, *f1, *f2),
        shapes, "residue_forward", flops=4 * rows * width * hidden, moved=5 * MIB,
        exps=rows * hidden,
    )


def edge_kernel(
    sb, blocks, hi_chunks, far_lo, far_hi, own, edge, cot, idx, idx_row, live_col,
    e_first, e2, eb2, e3, eb3, g3,
    edge_out, act_one_out, act_two_out, low_three_out, low_two_out, low_one_out, hi_out, lo_out, own_out, gain_out,
    low_first, gs,
):
    step = pl.program_id(0)
    rows, width = own.shape
    node_width = (e_first.shape[1] - width) // 2
    e_mid = e_first.at[:, node_width : node_width + width]

    @pl.when(step == 0)
    def _():
        own_out[...] = jnp.zeros_like(own_out)
        gs[...] = jnp.zeros_like(gs)

    @pl.when(step < blocks)
    def _():
        block = sb * rows
        flat = edge[...].reshape(block, width)
        mixed = pick_rows(index_columns(idx[...]), (far_lo, far_hi)) + dot_back(flat, e_mid[...])
        w_one = (mixed.reshape(sb, rows, width) + own[...][None]).reshape(block, width)
        act_one, slope_one = gelu_parts(w_one)
        act_one = act_one.astype(BF16)
        act_one_out[...] = act_one
        act_two, slope_two = gelu_parts(dot(act_one, e2[...]) + eb2[...])
        act_two = act_two.astype(BF16)
        act_two_out[...] = act_two
        w_three = dot(act_two, e3[...]) + eb3[...]
        normed, scale = norm(flat.astype(F32) + w_three)
        count = spread(live_col[...], pl.cdiv(width, LANES) * LANES)[:, :width]
        live = jnp.concatenate(
            [jnp.where(count > step * sb + s, 1.0, 0.0) for s in range(sb)], axis=0
        )
        edge_out[...] = (normed * g3[...] * live).astype(BF16).reshape(sb, rows, width)
        grad = cot[...].reshape(block, width).astype(F32) * live
        gs[...] += jnp.sum((grad * normed).reshape(sb, rows, width), axis=0)
        low_three = norm_back(grad * g3[...], normed, scale).astype(BF16)
        low_three_out[...] = low_three
        low_two = (dot_back(low_three, e3[...]) * slope_two).astype(BF16)
        low_two_out[...] = low_two
        low_one = (dot_back(low_two, e2[...]) * slope_one).astype(BF16)
        low_one_out[...] = low_one
        own_out[...] += jnp.sum(low_one.astype(F32).reshape(sb, rows, width), axis=0)
        low_first[pl.ds(pl.multiple_of(step * block, block), block), :] = low_one

    chunk = hi_out.shape[0]

    @pl.when((step >= blocks) & (step < blocks + hi_chunks))
    def _():
        start = (step - blocks + hi_chunks) * chunk
        hi_out[...] = dot(one_hot_rows(idx_row[...], start, chunk), low_first[...]).astype(BF16)

    @pl.when(step >= blocks + hi_chunks)
    def _():
        start = (step - blocks - hi_chunks) * chunk
        lo_out[...] = dot(one_hot_rows(idx_row[...], start, chunk), low_first[...])

    @pl.when(step == blocks + 2 * hi_chunks - 1)
    def _():
        gain_out[...] = column_sum(gs[...])


def edge_branch(far_lo, far_hi, own, edge, cot, idx_row, live_col, e_first, e2, eb2, e3, eb3, g3):
    slots, rows, width = edge.shape
    sb = slot_block(slots)
    edges = slots * rows
    block = sb * rows
    blocks = slots // sb
    half = far_lo.shape[0]
    chunk = min(512, half)
    hi_chunks = half // chunk
    blk = lambda i: jnp.minimum(i, blocks - 1)
    hi_at = lambda i: (jnp.clip(i - blocks, 0, hi_chunks - 1), 0)
    lo_at = lambda i: (jnp.clip(i - blocks - hi_chunks, 0, hi_chunks - 1), 0)
    slot_spec = pl.BlockSpec((sb, rows, width), lambda i: (blk(i), 0, 0))
    row_spec = pl.BlockSpec((block, width), lambda i: (blk(i), 0))
    return pl.pallas_call(
        functools.partial(edge_kernel, sb, blocks, hi_chunks),
        grid=(blocks + 2 * hi_chunks,),
        in_specs=[
            const_spec(far_lo.shape),
            const_spec(far_hi.shape),
            const_spec(own.shape),
            slot_spec,
            slot_spec,
            pl.BlockSpec((1, block), lambda i: (0, blk(i))),
            const_spec(idx_row.shape),
            const_spec(live_col.shape),
            const_spec(e_first.shape),
            const_spec(e2.shape),
            const_spec(eb2.shape),
            const_spec(e3.shape),
            const_spec(eb3.shape),
            const_spec(g3.shape),
        ],
        out_specs=[slot_spec]
        + [row_spec] * 5
        + [
            pl.BlockSpec((chunk, width), hi_at),
            pl.BlockSpec((chunk, width), lo_at),
            pl.BlockSpec((rows, width), whole),
            pl.BlockSpec((1, width), whole),
        ],
        out_shape=[jax.ShapeDtypeStruct((slots, rows, width), BF16)]
        + [jax.ShapeDtypeStruct((edges, width), BF16)] * 5
        + [
            jax.ShapeDtypeStruct((half, width), BF16),
            jax.ShapeDtypeStruct((half, width), F32),
            jax.ShapeDtypeStruct((rows, width), F32),
            jax.ShapeDtypeStruct((1, width), F32),
        ],
        scratch_shapes=[pltpu.VMEM((edges, width), BF16), pltpu.VMEM((rows, width), F32)],
        compiler_params=pltpu.CompilerParams(vmem_limit_bytes=VMEM),
        name="edge_branch",
        cost_estimate=pl.CostEstimate(
            flops=2 * edges * width * (4 * half + 5 * width),
            bytes_accessed=edges * width * 16,
            transcendentals=2 * edges * width,
        ),
    )(far_lo, far_hi, own, edge, cot, idx_row, idx_row, live_col, e_first, e2, eb2, e3, eb3, g3)


def edge_weights_kernel(blocks, pairs, *refs):
    step = pl.program_id(0)
    lefts, rights = refs[:pairs], refs[pairs : 2 * pairs]
    grads, biases, sums = refs[2 * pairs : 3 * pairs], refs[3 * pairs : 4 * pairs], refs[-1]
    rows = sums.shape[1]

    @pl.when(step == 0)
    def _():
        for ref in (*grads, sums):
            ref[...] = jnp.zeros_like(ref)

    for at in range(pairs):
        left, right = [r[...].reshape(-1, r.shape[-1]) for r in (lefts[at], rights[at])]
        grads[at][...] += dot_rows(left, right)
        low = left if lefts[at].ndim < rights[at].ndim else right
        sums[at] += jnp.sum(low.astype(F32).reshape(-1, rows, low.shape[1]), axis=0)

    @pl.when(step == blocks - 1)
    def _():
        for at in range(pairs):
            biases[at][...] = column_sum(sums[at])


def edge_weights(lefts, rights, rows):
    pairs = len(lefts)
    edges, width = lefts[0].shape
    slots = edges // rows
    sb = slot_block(slots)

    def spec(array):
        if array.ndim == 3:
            return pl.BlockSpec((sb, rows, width), lambda i: (i, 0, 0))
        return pl.BlockSpec((sb * rows, width), lambda i: (i, 0))

    shapes = [(width, width)] * pairs + [(1, width)] * pairs
    return pl.pallas_call(
        functools.partial(edge_weights_kernel, slots // sb, pairs),
        grid=(slots // sb,),
        in_specs=[spec(array) for array in (*lefts, *rights)],
        out_specs=[pl.BlockSpec(s, whole) for s in shapes],
        out_shape=[jax.ShapeDtypeStruct(s, F32) for s in shapes],
        scratch_shapes=[pltpu.VMEM((pairs, rows, width), F32)],
        compiler_params=pltpu.CompilerParams(vmem_limit_bytes=VMEM),
        name="edge_weights",
        cost_estimate=pl.CostEstimate(
            flops=2 * pairs * edges * width * width,
            bytes_accessed=pairs * edges * width * 4,
            transcendentals=0,
        ),
    )(*lefts, *rights)


def early_shapes(width, edge_width):
    return [
        (width, width),
        (edge_width, width),
        (edge_width, edge_width),
        (edge_width, width),
        (edge_width, edge_width),
        (edge_width, edge_width),
        (16, width),
        (16, edge_width),
    ]


def residue_backward_kernel(
    parts, pieces, node_cot, own_sum, e_first, e_far, h2b, n1, sc1, n2, sc2, slope, g1, g2, m3,
    total, e1g, e2g, e3g, eb1, eb2, eb3, edge_gain, *refs,
):
    far = refs[:pieces]
    f1 = refs[pieces : pieces + parts]
    f2 = refs[pieces + parts : pieces + 2 * parts]
    gu1_out, v_out, gy2_out, slab = refs[pieces + 2 * parts :]
    width, hidden = h2b.shape[1], f1[0].shape[1]
    far_sum = far[0][...]
    for ref in far[1:]:
        far_sum = far_sum + ref[...].astype(F32)
    own = own_sum[...]
    g_h2 = (
        node_cot[...].astype(F32)
        + fine(dot, own, e_first[:, :width])
        + fine(dot, far_sum, e_far[...])
    )
    gain_two = column_sum(g_h2 * n2[...])
    g_u2 = norm_back(g_h2 * g2[...], n2[...], sc2[:, :1])
    gy2 = g_u2.astype(BF16)
    gy2_out[...] = gy2
    g_h1 = g_u2
    for p in range(parts):
        gy1 = dot_back(gy2, f2[p][...]) * slope[:, p * hidden : (p + 1) * hidden]
        g_h1 = g_h1 + dot_back(gy1.astype(BF16), f1[p][:width, :])
    gain_one = column_sum(g_h1 * n1[...])
    g_u1 = norm_back(g_h1 * g1[...], n1[...], sc1[:, :1])
    gu1_out[...] = g_u1
    v_out[...] = fine(dot_back, g_u1, m3[...])
    bias = [gain_one, gain_two, column_sum(gy2.astype(F32)), column_sum(g_u1)]
    slab[...] = jnp.zeros_like(slab)
    pack(
        slab,
        [
            dot_rows(total[...].astype(BF16), g_u1.astype(BF16)),
            dot_rows(own.astype(BF16), h2b[...]),
            e1g[...],
            dot_rows(far_sum.astype(BF16), h2b[...]),
            e2g[...],
            e3g[...],
            padded_rows(bias, width),
            padded_rows([eb1[...], eb2[...], eb3[...], edge_gain[...]], own.shape[1]),
        ],
    )


def residue_backward(args, far, f1, f2):
    node_cot, e_first, slope = args[0], args[2], args[9]
    rows, width = node_cot.shape
    tiles = all_tiles(early_shapes(width, e_first.shape[0]))
    shapes = [
        ((rows, width), F32),
        ((rows, width), F32),
        ((rows, width), BF16),
        ((tiles, 16, LANES), BF16),
    ]
    return small_call(
        functools.partial(residue_backward_kernel, len(f1), len(far)),
        (*args, *far, *f1, *f2),
        shapes, "residue_backward",
        flops=4 * rows * width * slope.shape[1], moved=8 * MIB,
    )


def feed_kernel(h_lo, h_hi, g_lo, g_hi, f1, fb1, f2, f1g, f2g, fb1g):

    @pl.when(pl.program_id(0) == 0)
    def _():
        for ref in (f1g, f2g, fb1g):
            ref[...] = jnp.zeros_like(ref)

    for h1b, gy2 in ((h_lo[...], g_lo[...]), (h_hi[...], g_hi[...])):
        act, slope = gelu_parts(dot(h1b, f1[...]) + fb1[...])
        gy1 = (dot_back(gy2, f2[...]) * slope).astype(BF16)
        f1g[...] += dot_rows(h1b, gy1)
        f2g[...] += dot_rows(act.astype(BF16), gy2)
        fb1g[...] += column_sum(gy1.astype(F32))


def feed_gradients(h1b, gy2, f1, fb1, f2):
    width, hidden = f1.shape
    half = h1b[0].shape[0]
    chunk = min(512, half)
    shapes = [(width, hidden), (hidden, width), (1, hidden)]
    return pl.pallas_call(
        feed_kernel,
        grid=(half // chunk,),
        in_specs=[pl.BlockSpec((chunk, width), lambda i: (i, 0))] * 4
        + [const_spec(a.shape) for a in (f1, fb1, f2)],
        out_specs=[pl.BlockSpec(s, whole) for s in shapes],
        out_shape=[jax.ShapeDtypeStruct(s, F32) for s in shapes],
        compiler_params=pltpu.CompilerParams(vmem_limit_bytes=VMEM),
        name="feed_gradients",
        cost_estimate=pl.CostEstimate(
            flops=16 * half * width * hidden,
            bytes_accessed=8 * half * width,
            transcendentals=2 * half * hidden,
        ),
    )(*h1b, *gy2, f1, fb1, f2)


def late_shapes(width, edge_width):
    return [(width, width), (width, width), (edge_width, width), (16, width)]


def message_backward_kernel(sb, first_block, blocks, codes, *refs):
    last = codes is not None
    if last:
        base, refs = refs[0], refs[1:]
    v, a1, s1, s2, edge, live_col, m2 = refs[:7]
    refs = refs[7:]
    if last:
        node, early, own_in, m2g_in, m1eg_in, b2_in, low_out, own, keep, send, m2g, m1eg, b2s, slab = refs
    else:
        low_out, own, m2g, m1eg, b2s = refs
    step = pl.program_id(0)
    rows, width = v.shape
    edge_width = edge.shape[2]
    block = sb * rows

    @pl.when(step == 0)
    def _():
        if last:
            own[...] = own_in[...]
            m2g[...] = m2g_in[...]
            m1eg[...] = m1eg_in[...]
            b2s[...] = b2_in[...]
        else:
            for ref in (own, m2g, m1eg, b2s):
                ref[...] = jnp.zeros_like(ref)

    count = live_col[...]
    inverse = 1.0 / count.astype(F32)
    grads = [
        v[...] * spread(jnp.where(count > (step + first_block) * sb + s, inverse, 0.0), width)
        for s in range(sb)
    ]
    low_two = (jnp.concatenate(grads, axis=0) * s2[...].astype(F32)).astype(BF16)
    m2g[...] += dot_rows(a1[...], low_two)
    b2s[...] += jnp.sum(low_two.astype(F32).reshape(sb, rows, width), axis=0)
    low_one = (dot_back(low_two, m2[...]) * s1[...].astype(F32)).astype(BF16)
    low_out[...] = low_one
    m1eg[...] += dot_rows(edge[...].reshape(block, edge_width), low_one)
    own[...] += jnp.sum(low_one.astype(F32).reshape(sb, rows, width), axis=0)

    if last:
        @pl.when(step == blocks - 1)
        def _():
            count = early.shape[0]
            slab[:count] = early[...]
            slab[count:] = jnp.zeros_like(slab[count:])
            bias = [column_sum(own[...]), column_sum(b2s[...])]
            pack(
                slab,
                [
                    dot_rows(node[...], own[...].astype(BF16)),
                    m2g[...],
                    m1eg[...],
                    padded_rows(bias, width),
                ],
                count,
            )
            order_out(slab, base[0], codes, keep, send)


def message_backward(first_block, blocks, v, a1, s1, s2, edge, live_col, m2, more=()):
    slots, rows, edge_width = edge.shape
    width = v.shape[1]
    sb = slot_block(slots)
    block = sb * rows
    edges = blocks * block
    row_spec = pl.BlockSpec((block, width), lambda i: (i + first_block, 0))
    sums = [(rows, width), (width, width), (edge_width, width), (rows, width)]
    in_specs = [
        const_spec(v.shape),
        row_spec,
        row_spec,
        row_spec,
        pl.BlockSpec((sb, rows, edge_width), lambda i: (i + first_block, 0, 0)),
        const_spec(live_col.shape),
        const_spec(m2.shape),
    ]
    args = (v, a1, s1, s2, edge, live_col, m2)
    codes, scratch = None, []
    outs = [(s, F32) for s in sums]
    if more:
        codes, base, *rest = more
        args = (base, *args, *rest)
        in_specs = [pl.BlockSpec(memory_space=pltpu.SMEM)] + in_specs
        in_specs += [const_spec(a.shape) for a in rest]
        tiles = slab_part(width, edge_width, len(codes)) * len(codes)
        outs = [(sums[0], F32)] + half_shapes(tiles)
        scratch = [pltpu.VMEM(s, F32) for s in sums[1:]] + [slab_scratch(tiles)]
    return pl.pallas_call(
        functools.partial(message_backward_kernel, sb, first_block, blocks, codes),
        grid=(blocks,),
        in_specs=in_specs,
        out_specs=[pl.BlockSpec((block, width), lambda i: (i, 0))]
        + [pl.BlockSpec(s, lambda i, n=len(s): (0,) * n) for s, _ in outs],
        out_shape=[jax.ShapeDtypeStruct((edges, width), BF16)]
        + [jax.ShapeDtypeStruct(*s) for s in outs],
        scratch_shapes=scratch,
        compiler_params=pltpu.CompilerParams(vmem_limit_bytes=VMEM),
        name="message_backward",
        cost_estimate=pl.CostEstimate(
            flops=2 * edges * width * (2 * width + 2 * edge_width),
            bytes_accessed=edges * width * 8 + edges * edge_width * 2,
            transcendentals=0,
        ),
    )(*args)


def far_sums_kernel(start, steps, rows, codes, *refs):
    last = codes is not None
    if last:
        base, idx_row, low_a, low_b, node, m1fg_in, out, keep, send, m1fg, slab = refs
    else:
        idx_row, low_a, low_b, node, out, m1fg = refs
    step = pl.program_id(0)
    cut = low_a.shape[0]
    chunk, width = node.shape
    height = rows // 16

    @pl.when(step == 0)
    def _():
        m1fg[...] = m1fg_in[...] if last else jnp.zeros_like(m1fg)

    first = start + step * chunk
    sums = dot(one_hot_rows(idx_row[:, :cut], first, chunk), low_a[...]) + dot(
        one_hot_rows(idx_row[:, cut:], first, chunk), low_b[...]
    )
    sums = sums.astype(BF16)
    m1fg[...] += dot_rows(node[...], sums)
    at = 0
    for place in range(chunk // rows):
        for lane in range(0, width, LANES):
            tile = sums[place * rows : (place + 1) * rows, lane : lane + LANES]
            out[at : at + height] = tile.reshape(height, 16, LANES)
            at += height

    if last:
        @pl.when(step == steps - 1)
        def _():
            if tile_count(m1fg.shape) < slab.shape[0]:
                slab[...] = jnp.zeros_like(slab)
            pack(slab, [m1fg[...]])
            order_out(slab, base[0], codes, keep, send)


def far_sums(start, idx_row, low_a, low_b, node, rows, more=()):
    half, width = node.shape
    chunk = min(512, half)
    steps = half // chunk
    tiles = chunk * width // (16 * LANES)
    args = [idx_row, low_a, low_b, node]
    in_specs = [const_spec(a.shape) for a in args[:3]] + [pl.BlockSpec((chunk, width), lambda i: (i, 0))]
    outs, codes, scratch = [((width, width), F32)], None, []
    if more:
        codes, base, m1fg = more
        args = [base] + args + [m1fg]
        in_specs = [pl.BlockSpec(memory_space=pltpu.SMEM)] + in_specs + [const_spec(m1fg.shape)]
        far = far_part_tiles(width, len(codes)) * len(codes)
        outs = half_shapes(far)
        scratch = [pltpu.VMEM((width, width), F32), slab_scratch(far)]
    edges = idx_row.shape[1]
    return pl.pallas_call(
        functools.partial(far_sums_kernel, start, steps, rows, codes),
        grid=(steps,),
        in_specs=in_specs,
        out_specs=[pl.BlockSpec((tiles, 16, LANES), lambda i: (i, 0, 0))]
        + [pl.BlockSpec(s, lambda i, n=len(s): (0,) * n) for s, _ in outs],
        out_shape=[jax.ShapeDtypeStruct((tiles * steps, 16, LANES), BF16)]
        + [jax.ShapeDtypeStruct(*s) for s in outs],
        scratch_shapes=scratch,
        compiler_params=pltpu.CompilerParams(vmem_limit_bytes=VMEM),
        name="far_sums",
        cost_estimate=pl.CostEstimate(
            flops=2 * width * half * (edges + width),
            bytes_accessed=edges * width * 2 + half * width * 4,
            transcendentals=0,
        ),
    )(*args)


def edge_gradient_kernel(sb, cut, low_three, low_edge, low_a, low_b, e_first, m1, out):
    step = pl.program_id(0)
    shape = out.shape
    edge_width, width = shape[2], low_a.shape[1]
    for low, use in ((low_a, step < cut), (low_b, step >= cut)):
        @pl.when(use)
        def _(low=low):
            total = (
                low_three[...].astype(F32)
                + dot(low_edge[...], e_first[:, width : width + edge_width])
                + dot_back(low[...], m1[width : width + edge_width, :])
            )
            out[...] = total.reshape(shape)


def edge_gradient(slots, low_three, low_edge, low_a, low_b, e_first, m1):
    edges, edge_width = low_three.shape
    rows = edges // slots
    width = low_a.shape[1]
    sb = slot_block(slots)
    block = sb * rows
    cut = low_a.shape[0] // block
    edge_spec = pl.BlockSpec((block, edge_width), lambda i: (i, 0))
    return pl.pallas_call(
        functools.partial(edge_gradient_kernel, sb, cut),
        grid=(slots // sb,),
        in_specs=[
            edge_spec,
            edge_spec,
            pl.BlockSpec((block, width), lambda i: (jnp.minimum(i, cut - 1), 0)),
            pl.BlockSpec((block, width), lambda i: (jnp.maximum(i - cut, 0), 0)),
            const_spec(e_first.shape),
            const_spec(m1.shape),
        ],
        out_specs=pl.BlockSpec((sb, rows, edge_width), lambda i: (i, 0, 0)),
        out_shape=jax.ShapeDtypeStruct((slots, rows, edge_width), F32),
        compiler_params=pltpu.CompilerParams(vmem_limit_bytes=VMEM),
        name="edge_gradient",
        cost_estimate=pl.CostEstimate(
            flops=2 * edges * edge_width * (width + edge_width),
            bytes_accessed=edges * (width * 2 + 2048),
            transcendentals=0,
        ),
    )(low_three, low_edge, low_a, low_b, e_first, m1)


def node_kernel(pieces, g_u1, own, m1, *refs):
    far, grad_out = refs[:pieces], refs[pieces]
    rows, width = own.shape
    height = rows // 16
    sums = far[0][...].astype(F32)
    for ref in far[1:]:
        sums = sums + ref[...].astype(F32)
    far_sum = jnp.concatenate(
        [sums[j * height : (j + 1) * height].reshape(rows, LANES) for j in range(width // LANES)],
        axis=1,
    )
    far_first = m1.shape[0] - width
    grad_out[...] = (
        g_u1[...]
        + fine(dot_back, own[...], m1[:width, :])
        + fine(dot_back, far_sum, m1[far_first:, :])
    )


def node_last(g_u1, own, m1, far):
    return small_call(
        functools.partial(node_kernel, len(far)),
        (g_u1, own, m1, *far), [(own.shape, F32)], "node_gradient",
        flops=8 * own.size * own.shape[1], moved=2 * MIB,
    )[0]


def weights_out_kernel(
    codes, base, first, second,
    m1g, b1, m2g, b2, m3g, e1g, e2g, e3g, b3, g1, g2, fb2, eb1, eb2, eb3, g3, slab, far_slab,
):
    order_in((slab, far_slab), base[0], codes, first, second)
    width, edge_width = m3g.shape[0], e2g.shape[0]
    starts, at = [], 0
    for shape in early_shapes(width, edge_width) + late_shapes(width, edge_width):
        starts.append(at)
        at += tile_count(shape)
    m3g[...] = unpack(slab, starts[0], width, width)
    e1g[:, :width] = unpack(slab, starts[1], edge_width, width)
    middle = unpack(slab, starts[2], edge_width, edge_width)
    far = unpack(slab, starts[3], edge_width, width)
    over = edge_width % LANES
    base_col = width + edge_width - over
    e1g[:, width:base_col] = middle[:, : edge_width - over]
    far = pltpu.roll(jnp.concatenate([far, jnp.zeros((edge_width, LANES), F32)], axis=1), over, 1)
    lane = lax.broadcasted_iota(jnp.int32, (edge_width, LANES), 1)
    e1g[:, base_col : base_col + LANES] = jnp.where(
        lane < over, middle[:, edge_width - over : edge_width - over + LANES], far[:, :LANES]
    )
    rest = e1g.shape[1] - base_col - LANES
    e1g[:, base_col + LANES :] = far[:, LANES : LANES + rest]
    e2g[...] = unpack(slab, starts[4], edge_width, edge_width)[:, :edge_width]
    e3g[...] = unpack(slab, starts[5], edge_width, edge_width)[:, :edge_width]
    bias = unpack(slab, starts[6], 16, width)
    for row, out in enumerate((g1, g2, fb2, b3)):
        out[...] = bias[row : row + 1]
    bias = unpack(slab, starts[7], 16, edge_width)
    for row, out in enumerate((eb1, eb2, eb3, g3)):
        out[...] = bias[row : row + 1, :edge_width]
    m1g[:width, :] = unpack(slab, starts[8], width, width)
    m2g[...] = unpack(slab, starts[9], width, width)
    m1g[width : width + edge_width, :] = unpack(slab, starts[10], edge_width, width)
    m1g[width + edge_width :, :] = unpack(far_slab, 0, width, width)
    bias = unpack(slab, starts[11], 16, width)
    b1[...] = bias[0:1]
    b2[...] = bias[1:2]


def weights_out(codes, base, halves_in, width, edge_width):
    shapes = [(2 * width + edge_width, width), (1, width), (width, width), (1, width)]
    shapes += [(width, width), (edge_width, 2 * width + edge_width)]
    shapes += [(edge_width, edge_width)] * 2 + [(1, width)] * 4 + [(1, edge_width)] * 4
    chunks = len(codes)
    tiles = slab_part(width, edge_width, chunks) * chunks
    far_tiles = far_part_tiles(width, chunks) * chunks
    return small_call(
        functools.partial(weights_out_kernel, codes),
        (base, *halves_in), [(s, F32) for s in shapes], "weight_gradients",
        [slab_scratch(tiles), slab_scratch(far_tiles)], moved=10 * MIB, scalars=1,
    )


def exchange(value, mask, devices):
    return lax.ppermute(value, AXES, [(d, d ^ mask) for d in range(devices)])


def mask_groups(masks):
    return [masks[i : min(i + 2, len(masks) - 1)] for i in range(0, len(masks) - 1, 2)] + [masks[-1:]]


def order_codes(groups):
    masks = [mask for group in groups for mask in group]
    return [
        sum(mask for bit, mask in enumerate(masks) if place >> bit & 1)
        for place in range(1 << len(masks))
    ]


def combined(group, code):
    return sum(mask for bit, mask in enumerate(group) if code >> bit & 1)


def members(group, devices):
    inside = sum(group)
    return [
        [d | combined(group, code) for code in range(1 << len(group))]
        for d in range(devices)
        if not d & inside
    ]


def traded(parts, group, devices):
    return lax.all_to_all(
        parts, AXES, 0, 0, axis_index_groups=members(group, devices), tiled=True
    )


def gathered(value, group, devices):
    return lax.all_gather(
        value, AXES, axis=0, axis_index_groups=members(group, devices), tiled=True
    )


def traded_around(value, group, devices):
    copies = jnp.broadcast_to(value[None], (1 << len(group), *value.shape))
    return traded(copies.reshape(-1, *value.shape[1:]), group, devices)


def sent_around(value, group, devices):
    return [value] + [
        exchange(value, combined(group, code), devices) for code in range(1, 1 << len(group))
    ]


def shared_out(total, group, devices):
    count = 1 << len(group)
    got = traded(total.astype(BF16), group, devices)
    rows = got.shape[0] // count
    return [got[i * rows : (i + 1) * rows] for i in range(count)]


def add_up(terms):
    total = terms[0].astype(F32)
    for term in terms[1:]:
        total = total + term.astype(F32)
    return total


def tied(*values):
    return lax.optimization_barrier(values)


def split_three(value):
    rows = []
    for _ in range(3):
        high = lax.reduce_precision(value, 8, 7)
        rows.append(high.astype(BF16))
        value = value - high
    return jnp.concatenate(rows + [jnp.zeros((13, value.shape[1]), BF16)], axis=0)


def per_device(
    node_in,
    edge_in,
    neighbours,
    live_counts,
    message_first,
    message_first_bias,
    message_second,
    message_second_bias,
    message_third,
    message_third_bias,
    norm_one,
    feed_first,
    feed_first_bias,
    feed_second,
    feed_second_bias,
    norm_two,
    edge_first,
    edge_first_bias,
    edge_second,
    edge_second_bias,
    edge_third,
    edge_third_bias,
    norm_three,
    node_cotangent,
    edge_cotangent,
):
    rows, slots = neighbours.shape
    width = node_in.shape[1]
    edge_width = edge_in.shape[2]
    edges = rows * slots
    hid_count = lax.axis_size("hid")
    res_count = lax.axis_size("res")
    devices = res_count * hid_count
    bits = devices.bit_length() - 1
    masks = [1 << b for b in range(bits - 1, -1, -1)]
    groups = mask_groups(masks)
    codes = order_codes(groups)
    me = lax.axis_index("res") * hid_count + lax.axis_index("hid")
    base = me.reshape(1)
    core = me & 1
    near_base = core.reshape(1)
    row = lambda vector: vector.reshape(1, -1)

    names = neighbours.T.reshape(edges)
    apart = (names // rows) ^ core
    place = jnp.zeros_like(names)
    for bit, mask in enumerate(masks):
        place = place | jnp.where((apart & mask) != 0, 1 << bit, 0)
    idx_row = (place * rows + names % rows).reshape(1, edges)
    live_col = jnp.broadcast_to(live_counts[:, None], (rows, LANES))
    edge = edge_in.transpose(1, 0, 2)
    cot = edge_cotangent.transpose(1, 0, 2)
    e_first = edge_first.T
    e_far = e_first[:, width + edge_width :]
    f1x = jnp.concatenate([feed_first, split_three(row(feed_first_bias))], axis=0)
    f2x = feed_second

    tiled = lambda value, per: value.reshape(-1, per, 16, LANES)
    stack = lambda pieces: jnp.concatenate(pieces, axis=0)
    *outer, near = groups

    held = traded_around(node_in, outer[0], devices)
    held, idx_row, live_col, e_far = tied(held, idx_row, live_col, e_far)
    for group in outer[1:]:
        held = traded_around(held, group, devices)
    held, f1x, f2x = tied(held, f1x, f2x)
    node_lo, node_hi = sent_around(held, near, devices)

    f1, f2 = [f1x], [f2x]
    hid_masks = [m for m in masks if m < hid_count]
    for mask in hid_masks[:-1]:
        f1, f2 = [pieces + [exchange(p, mask, devices) for p in pieces] for pieces in (f1, f2)]

    sb = slot_block(slots)
    blocks = slots // sb
    cut = max(1, 5 * blocks // 6)
    message_args = (
        node_in, edge, idx_row, live_col, message_first, row(message_first_bias), message_second,
        row(message_second_bias),
    )
    a1, s1, s2, total, own_part, far_lo, far_hi = message_forward(
        0, cut, *message_args, (node_lo, node_hi)
    )
    total, f1, f2 = tied(total, f1, f2)
    f1, f2 = [
        pieces + [exchange(p, hid_masks[-1], devices) for p in pieces] for pieces in (f1, f2)
    ]
    a1, s1, s2, total = message_forward(
        cut, blocks - cut, *message_args, (far_lo, far_hi, own_part, total, a1, s1, s2)
    )
    h1b, n1, sc1, n2, sc2, slope, h2b, far_part, own_part = residue_forward(
        node_in, total, message_third, row(message_third_bias), row(norm_one),
        row(feed_second_bias), row(norm_two), e_first, e_far, row(edge_first_bias), f1, f2,
    )

    held = gathered(far_part, outer[0], devices)
    h_held = stack(sent_around(h1b, outer[0], devices))
    for group in outer[1:]:
        held = gathered(held, group, devices)
    held, h_held = tied(held, h_held)
    q_lo, q_hi = sent_around(held, near, devices)
    for group in outer[1:]:
        h_held = stack(sent_around(h_held, group, devices))

    edge_out, act_one, act_two, low_three, low_two, low_one, hi, lo, own_sum, edge_gain = edge_branch(
        q_lo, q_hi, own_part, edge, cot, idx_row, live_col, e_first,
        edge_second, row(edge_second_bias), edge_third, row(edge_third_bias), row(norm_three),
    )
    lo, h_held = tied(lo, h_held)
    h_all = sent_around(h_held, near, devices)

    work = [
        lambda: edge_weights((act_two, act_one), (low_three, low_two), rows),
        lambda: edge_weights((low_one,), (edge,), rows),
    ]
    made = []
    terms = [lo, exchange(hi, near[0], devices)]
    for group in reversed(outer):
        terms = shared_out(add_up(terms), group, devices)
        if work:
            terms, got = tied(terms, work.pop(0)())
            made.append(got)
    while work:
        made.append(work.pop(0)())
    (e3g, e2g, eb3, eb2), (e1g, eb1) = made
    g_u1, v, gy2, early = residue_backward(
        (
            node_cotangent, own_sum, e_first, e_far, h2b, n1, sc1, n2, sc2, slope, row(norm_one),
            row(norm_two), message_third, total, e1g, e2g, e3g, eb1, eb2, eb3, edge_gain,
        ),
        terms, f1, f2,
    )

    g_held = stack(sent_around(gy2, outer[0], devices))
    low_a, *sums = message_backward(
        0, blocks // 2, v, a1, s1, s2, edge, live_col, message_second
    )
    v, g_held = tied(v, g_held)
    for group in outer[1:]:
        g_held = stack(sent_around(g_held, group, devices))
    low_b, own, keep, send = message_backward(
        blocks // 2, blocks - blocks // 2, v, a1, s1, s2, edge, live_col, message_second,
        (codes, near_base, node_in, early, *sums),
    )

    terms = [keep, exchange(send, near[0], devices)]
    hi, m1fg = far_sums(node_lo.shape[0], idx_row, low_a, low_b, node_hi, rows)
    total, m1fg = tied(add_up(terms), m1fg)
    first, *others = reversed(outer)
    terms = shared_out(total, first, devices)
    got = exchange(hi, near[0], devices)
    lo, keep, send = far_sums(0, idx_row, low_a, low_b, node_lo, rows, (codes, near_base, m1fg))
    for group in others:
        terms = shared_out(add_up(terms), group, devices)
    slab_chunk = add_up(terms).astype(BF16)

    g_all = sent_around(g_held, near, devices)
    sums_part, far_part = rows * width // (16 * LANES), far_part_tiles(width, devices)
    total = jnp.concatenate(
        [
            tiled(add_up([lo, got]), sums_part),
            tiled(add_up([keep, exchange(send, near[0], devices)]), far_part),
        ],
        axis=1,
    )
    terms = [total]
    work = [
        lambda low: edge_gradient(slots, low_three, low_one, low, low_b, e_first, message_first),
        lambda low: feed_gradients((h_all[0], low), g_all, feed_first, row(feed_first_bias), feed_second),
    ]
    after = [low_a, h_all[1]]
    made = []
    for group in reversed(outer):
        total = add_up(terms)
        if work:
            total, low = tied(total, after.pop(0))
        terms = shared_out(total, group, devices)
        if work:
            terms, out = tied(terms, work.pop(0)(low))
            made.append(out)
    edge_grad, (f1g, f2g, fb1g) = made
    node_gradient = node_last(
        g_u1, own, message_first, [t[0, :sums_part] for t in terms]
    )
    far_chunk = add_up([t[:, sums_part:] for t in terms]).astype(BF16)

    held = jnp.concatenate(
        [
            stack(sent_around(tiled(slab_chunk, slab_chunk.shape[0]), outer[0], devices)),
            stack(sent_around(far_chunk, outer[0], devices)),
        ],
        axis=1,
    )
    for group in outer[1:]:
        held = stack(sent_around(held, group, devices))
    weights = [w.reshape(-1, 16, LANES) for w in sent_around(held, near, devices)]
    m1g, b1, m2g, b2, m3g, e1g, e2g, e3g, b3, g1, g2, fb2, eb1, eb2, eb3, g3 = weights_out(
        codes, base, weights, width, edge_width
    )
    flat = lambda vector: vector.reshape(-1)
    return (
        h2b,
        edge_out.transpose(1, 0, 2),
        node_gradient,
        edge_grad.transpose(1, 0, 2),
        m1g,
        flat(b1),
        m2g,
        flat(b2),
        m3g,
        flat(b3),
        flat(g1),
        f1g,
        flat(fb1g),
        f2g,
        flat(fb2),
        flat(g2),
        e1g.T,
        flat(eb1),
        e2g,
        flat(eb2),
        e3g,
        flat(eb3),
        flat(g3),
    )


def solution(mesh):
    nodes, edges, shared = P(AXES, None), P(AXES, None, None), P()
    return jax.shard_map(
        per_device,
        mesh=mesh,
        in_specs=(nodes, edges, nodes, P(AXES))
        + (shared,) * 7
        + (P(None, "hid"), P("hid"), P("hid", None))
        + (shared,) * 9
        + (nodes, edges),
        out_specs=(nodes, edges, nodes, edges)
        + (shared,) * 7
        + (P(None, "hid"), P("hid"), P("hid", None))
        + (shared,) * 9,
        check_vma=False,
    )
```

```python
import functools

import jax
import jax.numpy as jnp
from jax import lax
from jax.experimental import pallas as pl
from jax.experimental.pallas import tpu as pltpu
from jax.sharding import PartitionSpec as P

EPS = 1e-05
AXES = ("res", "hid")
F32 = jnp.float32
BF16 = jnp.bfloat16
TANH_SCALE = 0.7978845608028654
TANH_CUBE = 0.044715
LANES = 128
CHUNK = 2048
MIB = 1024 * 1024
VMEM = 58 * MIB


def dot(left, right):
    return lax.dot_general(left, right, (((1,), (0,)), ((), ())), preferred_element_type=F32)


def dot_rows(left, right):
    return lax.dot_general(left, right, (((0,), (0,)), ((), ())), preferred_element_type=F32)


def dot_back(left, right):
    return lax.dot_general(left, right, (((1,), (1,)), ((), ())), preferred_element_type=F32)


def halves(value):
    high = value.astype(BF16)
    return high, (value - high.astype(F32)).astype(BF16)


def fine(product, value, weights):
    high, low = halves(value)
    return product(high, weights) + product(low, weights)


def gelu_parts(x):
    square = x * x
    t = jnp.tanh(x * (TANH_SCALE + (TANH_SCALE * TANH_CUBE) * square))
    gate = 0.5 + 0.5 * t
    act = x * gate
    slope = gate + act * (1.0 - gate) * (2 * TANH_SCALE + (6 * TANH_SCALE * TANH_CUBE) * square)
    return act, slope


def index_columns(idx_row):
    parts = [
        jnp.broadcast_to(idx_row[:, first : first + LANES], (LANES, LANES)).T
        for first in range(0, idx_row.shape[1], LANES)
    ]
    return jnp.concatenate(parts, axis=0)


def one_hot_columns(idx, start, count):
    lane = lax.broadcasted_iota(jnp.int32, idx.shape, 1)
    parts = [
        jnp.where(idx == lane + (start + first), 1.0, 0.0).astype(BF16)
        for first in range(0, count, LANES)
    ]
    return jnp.concatenate(parts, axis=1)


def pick_rows(idx, table_refs):
    total, start = None, 0
    for ref in table_refs:
        rows = ref.shape[0]
        step = min(rows, CHUNK)
        for first in range(0, rows, step):
            part = dot(one_hot_columns(idx, start + first, step), ref[first : first + step, :])
            total = part if total is None else total + part
        start += rows
    return total


def one_hot_rows(idx_row, start, count):
    row = lax.broadcasted_iota(jnp.int32, (count, idx_row.shape[1]), 0) + start
    return jnp.where(jnp.broadcast_to(idx_row, row.shape) == row, 1.0, 0.0).astype(BF16)


def spread(column, width):
    return jnp.concatenate([column] * (width // LANES), axis=1)


def norm(value):
    centre = value - jnp.mean(value, -1, keepdims=True)
    scale = lax.rsqrt(jnp.mean(centre * centre, -1, keepdims=True) + EPS)
    return centre * scale, scale


def norm_back(inner, normed, scale):
    mean_first = jnp.mean(inner, -1, keepdims=True)
    mean_second = jnp.mean(inner * normed, -1, keepdims=True)
    return scale * (inner - mean_first - normed * mean_second)


def column_sum(value):
    return jnp.sum(value, axis=0, keepdims=True)


def whole(*_):
    return (0, 0)


def const_spec(shape):
    return pl.BlockSpec(shape, lambda *_: (0,) * len(shape), pipeline_mode=pl.Buffered(1))


def small_call(kernel, args, shapes, name, scratch=(), flops=0, moved=0, exps=0, scalars=0):
    return pl.pallas_call(
        kernel,
        grid=(1,),
        in_specs=[pl.BlockSpec(memory_space=pltpu.SMEM)] * scalars
        + [const_spec(a.shape) for a in args[scalars:]],
        out_specs=[pl.BlockSpec(s, lambda *_, n=len(s): (0,) * n) for s, _ in shapes],
        out_shape=[jax.ShapeDtypeStruct(*s) for s in shapes],
        scratch_shapes=list(scratch),
        compiler_params=pltpu.CompilerParams(vmem_limit_bytes=VMEM),
        name=name,
        cost_estimate=pl.CostEstimate(flops=flops, bytes_accessed=moved, transcendentals=exps),
    )(*args)


def tile_count(shape):
    return pl.cdiv(shape[0], 16) * pl.cdiv(shape[1], LANES)


def all_tiles(shapes):
    return sum(tile_count(s) for s in shapes)


def pack(slab, values, at=0):
    for value in values:
        rows, columns = value.shape
        count = rows // 16
        for first in range(0, columns, LANES):
            take = min(LANES, columns - first)
            tile = value[:, first : first + take].astype(BF16).reshape(count, 16, take)
            slab[at : at + count, :, :take] = tile
            at += count


def unpack(slab, at, rows, columns):
    count = rows // 16
    parts = [
        slab[at + i * count : at + (i + 1) * count].reshape(rows, LANES).astype(F32)
        for i in range(pl.cdiv(columns, LANES))
    ]
    return jnp.concatenate(parts, axis=1)


def order_in(slab, base, codes, first, second):
    size = slab.shape[0] // len(codes)
    half = len(codes) // 2
    for place, code in enumerate(codes):
        source = first if place < half else second
        at = (place % half) * size
        slab[pl.ds((base ^ code) * size, size)] = source[at : at + size]


def padded_rows(parts, width):
    return jnp.concatenate(parts + [jnp.zeros((16 - len(parts), width), F32)], axis=0)


def slot_block(slots):
    for size in (10, 12, 8, 6, 5, 4, 3, 2):
        if slots % size == 0:
            return size
    return 1


def message_forward_kernel(
    sb, part, first_block, blocks, fresh, residues, node_own, edge, idx_row, live_col, m1, b1, m2, b2, *refs
):
    if fresh:
        node_lo, node_hi, a1_out, s1_out, s2_out, sum_out, table_out, lhs, z_one, z_two, table, sem = refs
    else:
        table, sum_in, _, _, _, a1_out, s1_out, s2_out, sum_out, lhs, z_one, z_two = refs
    step = pl.program_id(0)
    width = node_own.shape[1]
    edge_width = edge.shape[2]
    rows = edge.shape[1]
    depth = table.shape[0]

    @pl.when(step == 0)
    def _():
        shape = (rows, depth - residues - edge_width)
        eye = lax.broadcasted_iota(jnp.int32, shape, 0) == lax.broadcasted_iota(jnp.int32, shape, 1)
        eye = jnp.where(eye, 1.0, 0.0).astype(BF16)
        for at in range(0, lhs.shape[0], rows):
            lhs[at : at + rows, residues + edge_width :] = eye
        if not fresh:
            sum_out[...] = sum_in[...]
            return
        sum_out[...] = jnp.zeros_like(sum_out)
        tile = min(512, node_lo.shape[0])
        for source, start in ((node_lo, 0), (node_hi, node_lo.shape[0])):
            def body(i, carry, source=source, start=start):
                at = pl.multiple_of(i * tile, tile)
                table[pl.ds(start + at, tile), :] = dot(
                    source[pl.ds(at, tile), :], m1[width + edge_width :, :]
                ).astype(BF16)
                return carry
            lax.fori_loop(0, source.shape[0] // tile, body, 0)
        table[residues : residues + edge_width, :] = m1[width : width + edge_width, :]
        table[residues + edge_width : residues + edge_width + rows, :] = (
            dot(node_own[...], m1[:width, :]) + b1[...]
        ).astype(BF16)
        if depth > residues + edge_width + rows:
            table[residues + edge_width + rows :, :] = jnp.zeros_like(
                table[residues + edge_width + rows :, :]
            )
        pltpu.make_async_copy(table, table_out, sem).start()

    parts = sb * rows // part
    slots = part // rows

    def first_product(p):
        at = p * part
        lane = lax.broadcasted_iota(jnp.int32, (part, LANES), 1)
        names = index_columns(idx_row[:, at : at + part])
        for first in range(0, residues, LANES):
            lhs[at : at + part, first : first + LANES] = jnp.where(
                names == lane + first, 1.0, 0.0
            ).astype(BF16)
        lhs[at : at + part, residues : residues + edge_width] = edge[
            p * slots : (p + 1) * slots
        ].reshape(part, edge_width)
        z_one[at : at + part, :] = dot(lhs[at : at + part, :], table[...])

    def first_gelu(p):
        for at in range(p * part, (p + 1) * part, 16):
            act, slope = gelu_parts(z_one[at : at + 16, :])
            s1_out[at : at + 16, :] = slope.astype(BF16)
            z_one[at : at + 16, :] = act

    def second_product(p):
        at = p * part
        act = z_one[at : at + part, :].astype(BF16)
        a1_out[:, at : at + part] = act.T
        z_two[at : at + part, :] = dot(act, m2[...])

    def second_gelu(p):
        bias = b2[...]
        for row in range(0, rows, 16):
            count = live_col[row : row + 16, :]
            inverse = 1.0 / count.astype(F32)
            total = sum_out[row : row + 16, :]
            for s in range(slots):
                at = p * part + s * rows + row
                act, slope = gelu_parts(z_two[at : at + 16, :] + bias)
                s2_out[at : at + 16, :] = slope.astype(BF16)
                slot = (step + first_block) * sb + p * slots + s
                share = jnp.where(count > slot, inverse, 0.0)
                total = total + act.astype(BF16).astype(F32) * spread(share, width)
            sum_out[row : row + 16, :] = total

    for t in range(parts + 2):
        if t < parts:
            first_product(t)
        if 1 <= t <= parts:
            first_gelu(t - 1)
            second_product(t - 1)
        if t >= 2:
            second_gelu(t - 2)

    if fresh:
        @pl.when(step == blocks - 1)
        def _():
            pltpu.make_async_copy(table, table_out, sem).wait()


def message_forward(sb, first_block, blocks, residues, node_own, edge, idx_row, live_col, m1, b1, m2, b2, more):
    slots, rows, edge_width = edge.shape
    width = node_own.shape[1]
    block = sb * rows
    part = 4 * rows
    edges = blocks * block
    fresh = len(more) == 2
    depth = residues + pl.cdiv(edge_width + rows, LANES) * LANES
    whole_edges = slots * rows
    out_specs = [
        pl.BlockSpec((width, block), lambda i: (0, i + first_block)),
        pl.BlockSpec((block, width), lambda i: (i + first_block, 0)),
        pl.BlockSpec((block, width), lambda i: (i + first_block, 0)),
        pl.BlockSpec((rows, width), whole),
    ]
    out_shape = [
        jax.ShapeDtypeStruct((width, whole_edges), BF16),
        jax.ShapeDtypeStruct((whole_edges, width), BF16),
        jax.ShapeDtypeStruct((whole_edges, width), BF16),
        jax.ShapeDtypeStruct((rows, width), F32),
    ]
    scratch = [
        pltpu.VMEM((block, depth), BF16),
        pltpu.VMEM((block, width), F32),
        pltpu.VMEM((block, width), F32),
    ]
    if fresh:
        out_specs += [pl.BlockSpec(memory_space=pl.ANY)]
        out_shape += [jax.ShapeDtypeStruct((depth, width), BF16)]
        scratch += [pltpu.VMEM((depth, width), BF16), pltpu.SemaphoreType.DMA]
    return pl.pallas_call(
        functools.partial(message_forward_kernel, sb, part, first_block, blocks, fresh, residues),
        grid=(blocks,),
        in_specs=[
            const_spec(node_own.shape),
            pl.BlockSpec((sb, rows, edge_width), lambda i: (i + first_block, 0, 0)),
            pl.BlockSpec((1, block), lambda i: (0, i + first_block)),
            const_spec(live_col.shape),
            const_spec(m1.shape),
            const_spec(b1.shape),
            const_spec(m2.shape),
            const_spec(b2.shape),
        ]
        + [const_spec(a.shape) for a in more[:2]]
        + [pl.BlockSpec(memory_space=pl.ANY)] * len(more[2:]),
        out_specs=out_specs,
        out_shape=out_shape,
        scratch_shapes=scratch,
        input_output_aliases={} if fresh else {10: 0, 11: 1, 12: 2},
        compiler_params=pltpu.CompilerParams(vmem_limit_bytes=VMEM),
        name="message_forward",
        cost_estimate=pl.CostEstimate(
            flops=2 * edges * width * (depth + width),
            bytes_accessed=edges * width * 6 + edges * edge_width * 2 + edges * LANES * 4,
            transcendentals=2 * edges * width,
        ),
    )(node_own, edge, idx_row, live_col, m1, b1, m2, b2, *more)


def residue_forward_kernel(parts, node, total, m3, b3, g1, fb2, g2, e_first, e_far, eb, *refs):
    f1, f2 = refs[:parts], refs[parts : 2 * parts]
    h1b_out, n1_out, sc1_out, n2_out, sc2_out, slope_out, h2b_out, far_out, own_out = refs[2 * parts :]
    width, hidden = node.shape[1], f1[0].shape[1]
    u1 = node[...].astype(F32) + fine(dot, total[...], m3[...]) + b3[...]
    n1, sc1 = norm(u1)
    h1 = n1 * g1[...]
    h1b = h1.astype(BF16)
    h1b_out[...] = h1b
    n1_out[...] = n1
    sc1_out[...] = jnp.broadcast_to(sc1, sc1_out.shape)
    y2 = None
    for p in range(parts):
        bias = f1[p][width : width + 16, :].astype(F32)
        bias = bias[0:1] + bias[1:2] + bias[2:3]
        act, slope = gelu_parts(dot(h1b, f1[p][:width, :]) + bias)
        slope_out[:, p * hidden : (p + 1) * hidden] = slope
        part = dot(act.astype(BF16), f2[p][...])
        y2 = part if y2 is None else y2 + part
    n2, sc2 = norm(h1 + (y2 + fb2[...]))
    h2b = (n2 * g2[...]).astype(BF16)
    n2_out[...] = n2
    sc2_out[...] = jnp.broadcast_to(sc2, sc2_out.shape)
    h2b_out[...] = h2b
    far_out[...] = dot_back(h2b, e_far[...]).astype(BF16)
    own_out[...] = dot_back(h2b, e_first[:, :width]) + eb[...]


def residue_forward(node, total, m3, b3, g1, fb2, g2, e_first, e_far, eb, f1, f2):
    rows, width = node.shape
    edge_width = e_first.shape[0]
    hidden = len(f1) * f1[0].shape[1]
    shapes = [
        ((rows, width), BF16),
        ((rows, width), F32),
        ((rows, LANES), F32),
        ((rows, width), F32),
        ((rows, LANES), F32),
        ((rows, hidden), F32),
        ((rows, width), BF16),
        ((rows, edge_width), BF16),
        ((rows, edge_width), F32),
    ]
    return small_call(
        functools.partial(residue_forward_kernel, len(f1)),
        (node, total, m3, b3, g1, fb2, g2, e_first, e_far, eb, *f1, *f2),
        shapes, "residue_forward", flops=4 * rows * width * hidden, moved=5 * MIB,
        exps=rows * hidden,
    )


def edge_kernel(
    sb, blocks, hi_chunks, far_lo, far_hi, own, edge, cot, idx, idx_row, live_col,
    e_first, e2, eb2, e3, eb3, g3,
    edge_out, act_one_out, act_two_out, low_three_out, low_two_out, low_one_out, hi_out, lo_out, own_out, gain_out,
    low_first, gs,
):
    step = pl.program_id(0)
    rows, width = own.shape
    node_width = (e_first.shape[1] - width) // 2
    e_mid = e_first.at[:, node_width : node_width + width]

    @pl.when(step == 0)
    def _():
        own_out[...] = jnp.zeros_like(own_out)
        gs[...] = jnp.zeros_like(gs)

    @pl.when(step < blocks)
    def _():
        block = sb * rows
        flat = edge[...].reshape(block, width)
        mixed = pick_rows(index_columns(idx[...]), (far_lo, far_hi)) + dot_back(flat, e_mid[...])
        w_one = (mixed.reshape(sb, rows, width) + own[...][None]).reshape(block, width)
        act_one, slope_one = gelu_parts(w_one)
        act_one = act_one.astype(BF16)
        act_one_out[...] = act_one
        act_two, slope_two = gelu_parts(dot(act_one, e2[...]) + eb2[...])
        act_two = act_two.astype(BF16)
        act_two_out[...] = act_two
        w_three = dot(act_two, e3[...]) + eb3[...]
        normed, scale = norm(flat.astype(F32) + w_three)
        count = spread(live_col[...], pl.cdiv(width, LANES) * LANES)[:, :width]
        live = jnp.concatenate(
            [jnp.where(count > step * sb + s, 1.0, 0.0) for s in range(sb)], axis=0
        )
        edge_out[...] = (normed * g3[...] * live).astype(BF16).reshape(sb, rows, width)
        grad = cot[...].reshape(block, width).astype(F32) * live
        gs[...] += jnp.sum((grad * normed).reshape(sb, rows, width), axis=0)
        low_three = norm_back(grad * g3[...], normed, scale).astype(BF16)
        low_three_out[...] = low_three
        low_two = (dot_back(low_three, e3[...]) * slope_two).astype(BF16)
        low_two_out[...] = low_two
        low_one = (dot_back(low_two, e2[...]) * slope_one).astype(BF16)
        low_one_out[...] = low_one
        own_out[...] += jnp.sum(low_one.astype(F32).reshape(sb, rows, width), axis=0)
        low_first[pl.ds(pl.multiple_of(step * block, block), block), :] = low_one

    chunk = hi_out.shape[0]

    @pl.when((step >= blocks) & (step < blocks + hi_chunks))
    def _():
        start = (step - blocks + hi_chunks) * chunk
        hi_out[...] = dot(one_hot_rows(idx_row[...], start, chunk), low_first[...]).astype(BF16)

    @pl.when(step >= blocks + hi_chunks)
    def _():
        start = (step - blocks - hi_chunks) * chunk
        lo_out[...] = dot(one_hot_rows(idx_row[...], start, chunk), low_first[...])

    @pl.when(step == blocks + 2 * hi_chunks - 1)
    def _():
        gain_out[...] = column_sum(gs[...])


def edge_branch(far_lo, far_hi, own, edge, cot, idx_row, live_col, e_first, e2, eb2, e3, eb3, g3):
    slots, rows, width = edge.shape
    sb = slot_block(slots)
    edges = slots * rows
    block = sb * rows
    blocks = slots // sb
    half = far_lo.shape[0]
    chunk = min(512, half)
    hi_chunks = half // chunk
    blk = lambda i: jnp.minimum(i, blocks - 1)
    hi_at = lambda i: (jnp.clip(i - blocks, 0, hi_chunks - 1), 0)
    lo_at = lambda i: (jnp.clip(i - blocks - hi_chunks, 0, hi_chunks - 1), 0)
    slot_spec = pl.BlockSpec((sb, rows, width), lambda i: (blk(i), 0, 0))
    row_spec = pl.BlockSpec((block, width), lambda i: (blk(i), 0))
    return pl.pallas_call(
        functools.partial(edge_kernel, sb, blocks, hi_chunks),
        grid=(blocks + 2 * hi_chunks,),
        in_specs=[
            const_spec(far_lo.shape),
            const_spec(far_hi.shape),
            const_spec(own.shape),
            slot_spec,
            slot_spec,
            pl.BlockSpec((1, block), lambda i: (0, blk(i))),
            const_spec(idx_row.shape),
            const_spec(live_col.shape),
            const_spec(e_first.shape),
            const_spec(e2.shape),
            const_spec(eb2.shape),
            const_spec(e3.shape),
            const_spec(eb3.shape),
            const_spec(g3.shape),
        ],
        out_specs=[slot_spec]
        + [row_spec] * 5
        + [
            pl.BlockSpec((chunk, width), hi_at),
            pl.BlockSpec((chunk, width), lo_at),
            pl.BlockSpec((rows, width), whole),
            pl.BlockSpec((1, width), whole),
        ],
        out_shape=[jax.ShapeDtypeStruct((slots, rows, width), BF16)]
        + [jax.ShapeDtypeStruct((edges, width), BF16)] * 5
        + [
            jax.ShapeDtypeStruct((half, width), BF16),
            jax.ShapeDtypeStruct((half, width), F32),
            jax.ShapeDtypeStruct((rows, width), F32),
            jax.ShapeDtypeStruct((1, width), F32),
        ],
        scratch_shapes=[pltpu.VMEM((edges, width), BF16), pltpu.VMEM((rows, width), F32)],
        compiler_params=pltpu.CompilerParams(vmem_limit_bytes=VMEM),
        name="edge_branch",
        cost_estimate=pl.CostEstimate(
            flops=2 * edges * width * (4 * half + 5 * width),
            bytes_accessed=edges * width * 16,
            transcendentals=2 * edges * width,
        ),
    )(far_lo, far_hi, own, edge, cot, idx_row, idx_row, live_col, e_first, e2, eb2, e3, eb3, g3)


def edge_weights_kernel(blocks, pairs, *refs):
    step = pl.program_id(0)
    lefts, rights = refs[:pairs], refs[pairs : 2 * pairs]
    grads, biases, sums = refs[2 * pairs : 3 * pairs], refs[3 * pairs : 4 * pairs], refs[-1]
    rows = sums.shape[1]

    @pl.when(step == 0)
    def _():
        for ref in (*grads, sums):
            ref[...] = jnp.zeros_like(ref)

    for at in range(pairs):
        left, right = [r[...].reshape(-1, r.shape[-1]) for r in (lefts[at], rights[at])]
        grads[at][...] += dot_rows(left, right)
        low = left if lefts[at].ndim < rights[at].ndim else right
        sums[at] += jnp.sum(low.astype(F32).reshape(-1, rows, low.shape[1]), axis=0)

    @pl.when(step == blocks - 1)
    def _():
        for at in range(pairs):
            biases[at][...] = column_sum(sums[at])


def edge_weights(lefts, rights, rows):
    pairs = len(lefts)
    edges, width = lefts[0].shape
    slots = edges // rows
    sb = slot_block(slots)

    def spec(array):
        if array.ndim == 3:
            return pl.BlockSpec((sb, rows, width), lambda i: (i, 0, 0))
        return pl.BlockSpec((sb * rows, width), lambda i: (i, 0))

    shapes = [(width, width)] * pairs + [(1, width)] * pairs
    return pl.pallas_call(
        functools.partial(edge_weights_kernel, slots // sb, pairs),
        grid=(slots // sb,),
        in_specs=[spec(array) for array in (*lefts, *rights)],
        out_specs=[pl.BlockSpec(s, whole) for s in shapes],
        out_shape=[jax.ShapeDtypeStruct(s, F32) for s in shapes],
        scratch_shapes=[pltpu.VMEM((pairs, rows, width), F32)],
        compiler_params=pltpu.CompilerParams(vmem_limit_bytes=VMEM),
        name="edge_weights",
        cost_estimate=pl.CostEstimate(
            flops=2 * pairs * edges * width * width,
            bytes_accessed=pairs * edges * width * 4,
            transcendentals=0,
        ),
    )(*lefts, *rights)


def early_shapes(width, edge_width):
    return [
        (width, width),
        (edge_width, width),
        (edge_width, edge_width),
        (edge_width, width),
        (edge_width, edge_width),
        (edge_width, edge_width),
        (16, width),
        (16, edge_width),
    ]


def residue_backward_kernel(
    parts, pieces, node_cot, own_sum, e_first, e_far, h2b, n1, sc1, n2, sc2, slope, g1, g2, m3,
    total, e1g, e2g, e3g, eb1, eb2, eb3, edge_gain, *refs,
):
    far = refs[:pieces]
    f1 = refs[pieces : pieces + parts]
    f2 = refs[pieces + parts : pieces + 2 * parts]
    gu1_out, v_out, gy2_out, slab = refs[pieces + 2 * parts :]
    width, hidden = h2b.shape[1], f1[0].shape[1]
    far_sum = far[0][...]
    for ref in far[1:]:
        far_sum = far_sum + ref[...].astype(F32)
    own = own_sum[...]
    g_h2 = (
        node_cot[...].astype(F32)
        + fine(dot, own, e_first[:, :width])
        + fine(dot, far_sum, e_far[...])
    )
    gain_two = column_sum(g_h2 * n2[...])
    g_u2 = norm_back(g_h2 * g2[...], n2[...], sc2[:, :1])
    gy2 = g_u2.astype(BF16)
    gy2_out[...] = gy2
    g_h1 = g_u2
    for p in range(parts):
        gy1 = dot_back(gy2, f2[p][...]) * slope[:, p * hidden : (p + 1) * hidden]
        g_h1 = g_h1 + dot_back(gy1.astype(BF16), f1[p][:width, :])
    gain_one = column_sum(g_h1 * n1[...])
    g_u1 = norm_back(g_h1 * g1[...], n1[...], sc1[:, :1])
    gu1_out[...] = g_u1
    v_out[...] = fine(dot_back, g_u1, m3[...])
    bias = [gain_one, gain_two, column_sum(gy2.astype(F32)), column_sum(g_u1)]
    slab[...] = jnp.zeros_like(slab)
    pack(
        slab,
        [
            dot_rows(total[...].astype(BF16), g_u1.astype(BF16)),
            dot_rows(own.astype(BF16), h2b[...]),
            e1g[...],
            dot_rows(far_sum.astype(BF16), h2b[...]),
            e2g[...],
            e3g[...],
            padded_rows(bias, width),
            padded_rows([eb1[...], eb2[...], eb3[...], edge_gain[...]], own.shape[1]),
        ],
    )


def residue_backward(args, far, f1, f2):
    node_cot, e_first, slope = args[0], args[2], args[9]
    rows, width = node_cot.shape
    tiles = all_tiles(early_shapes(width, e_first.shape[0]))
    shapes = [
        ((rows, width), F32),
        ((rows, width), F32),
        ((rows, width), BF16),
        ((tiles, 16, LANES), BF16),
    ]
    return small_call(
        functools.partial(residue_backward_kernel, len(f1), len(far)),
        (*args, *far, *f1, *f2),
        shapes, "residue_backward",
        flops=4 * rows * width * slope.shape[1], moved=8 * MIB,
    )


def feed_kernel(h_lo, h_hi, g_lo, g_hi, f1, fb1, f2, f1g, f2g, fb1g):

    @pl.when(pl.program_id(0) == 0)
    def _():
        for ref in (f1g, f2g, fb1g):
            ref[...] = jnp.zeros_like(ref)

    for h1b, gy2 in ((h_lo[...], g_lo[...]), (h_hi[...], g_hi[...])):
        act, slope = gelu_parts(dot(h1b, f1[...]) + fb1[...])
        gy1 = (dot_back(gy2, f2[...]) * slope).astype(BF16)
        f1g[...] += dot_rows(h1b, gy1)
        f2g[...] += dot_rows(act.astype(BF16), gy2)
        fb1g[...] += column_sum(gy1.astype(F32))


def feed_gradients(h1b, gy2, f1, fb1, f2):
    width, hidden = f1.shape
    half = h1b[0].shape[0]
    chunk = min(512, half)
    shapes = [(width, hidden), (hidden, width), (1, hidden)]
    return pl.pallas_call(
        feed_kernel,
        grid=(half // chunk,),
        in_specs=[pl.BlockSpec((chunk, width), lambda i: (i, 0))] * 4
        + [const_spec(a.shape) for a in (f1, fb1, f2)],
        out_specs=[pl.BlockSpec(s, whole) for s in shapes],
        out_shape=[jax.ShapeDtypeStruct(s, F32) for s in shapes],
        compiler_params=pltpu.CompilerParams(vmem_limit_bytes=VMEM),
        name="feed_gradients",
        cost_estimate=pl.CostEstimate(
            flops=16 * half * width * hidden,
            bytes_accessed=8 * half * width,
            transcendentals=2 * half * hidden,
        ),
    )(*h1b, *gy2, f1, fb1, f2)


def late_shapes(width, edge_width):
    return [(width, width), (width, width), (edge_width, width), (16, width)]


def message_backward_kernel(sb, first_block, blocks, last, v, a1, s1, s2, edge_t, live_col, m2, *refs):
    if last:
        node, own_in, m2g_in, m1eg_in, b2_in, low_out, own, slab, m2g, m1eg, b2s, low_two, grad = refs
    else:
        low_out, own, m2g, m1eg, b2s, low_two, grad = refs
    step = pl.program_id(0)
    rows, width = v.shape
    block = sb * rows

    @pl.when(step == 0)
    def _():
        if last:
            own[...] = own_in[...]
            m2g[...] = m2g_in[...]
            m1eg[...] = m1eg_in[...]
            b2s[...] = b2_in[...]
        else:
            for ref in (own, m2g, m1eg, b2s):
                ref[...] = jnp.zeros_like(ref)

    for row in range(0, rows, 16):
        count = live_col[row : row + 16, :]
        inverse = 1.0 / count.astype(F32)
        value = v[row : row + 16, :]
        total = b2s[row : row + 16, :]
        for s in range(sb):
            at = s * rows + row
            share = jnp.where(count > (step + first_block) * sb + s, inverse, 0.0)
            low = (value * spread(share, width) * s2[at : at + 16, :].astype(F32)).astype(BF16)
            low_two[at : at + 16, :] = low
            total = total + low.astype(F32)
        b2s[row : row + 16, :] = total
    grad[...] = dot_back(low_two[...], m2[...])
    m2g[...] += dot(a1[...], low_two[...])
    for row in range(0, rows, 16):
        total = own[row : row + 16, :]
        for s in range(sb):
            at = s * rows + row
            low = (grad[at : at + 16, :] * s1[at : at + 16, :].astype(F32)).astype(BF16)
            low_out[at : at + 16, :] = low
            total = total + low.astype(F32)
        own[row : row + 16, :] = total
    m1eg[...] += dot(edge_t[...], low_out[...])

    if last:
        @pl.when(step == blocks - 1)
        def _():
            pack(
                slab,
                [
                    dot_rows(node[...], own[...].astype(BF16)),
                    m2g[...],
                    m1eg[...],
                    padded_rows([column_sum(own[...]), column_sum(b2s[...])], width),
                ],
            )


def message_backward(first_block, blocks, v, a1, s1, s2, edge_t, live_col, m2, more=()):
    rows, width = v.shape
    edge_width, all_edges = edge_t.shape
    sb = slot_block(all_edges // rows)
    block = sb * rows
    edges = blocks * block
    row_spec = pl.BlockSpec((block, width), lambda i: (i + first_block, 0))
    sums = [(rows, width), (width, width), (edge_width, width), (rows, width)]
    outs = [(s, F32) for s in sums]
    scratch = []
    if more:
        tiles = all_tiles(late_shapes(width, edge_width))
        outs = [(sums[0], F32), ((tiles, 16, LANES), BF16)]
        scratch = [pltpu.VMEM(s, F32) for s in sums[1:]]
    scratch += [pltpu.VMEM((block, width), BF16), pltpu.VMEM((block, width), F32)]
    return pl.pallas_call(
        functools.partial(message_backward_kernel, sb, first_block, blocks, bool(more)),
        grid=(blocks,),
        in_specs=[
            const_spec(v.shape),
            pl.BlockSpec((width, block), lambda i: (0, i + first_block)),
            row_spec,
            row_spec,
            pl.BlockSpec((edge_width, block), lambda i: (0, i + first_block)),
            const_spec(live_col.shape),
            const_spec(m2.shape),
        ]
        + [const_spec(a.shape) for a in more],
        out_specs=[pl.BlockSpec((block, width), lambda i: (i, 0))]
        + [pl.BlockSpec(s, lambda i, n=len(s): (0,) * n) for s, _ in outs],
        out_shape=[jax.ShapeDtypeStruct((edges, width), BF16)]
        + [jax.ShapeDtypeStruct(*s) for s in outs],
        scratch_shapes=scratch,
        compiler_params=pltpu.CompilerParams(vmem_limit_bytes=VMEM),
        name="message_backward",
        cost_estimate=pl.CostEstimate(
            flops=2 * edges * width * (2 * width + 2 * edge_width),
            bytes_accessed=edges * width * 8 + edges * edge_width * 2,
            transcendentals=0,
        ),
    )(v, a1, s1, s2, edge_t, live_col, m2, *more)


def far_sums_kernel(steps, rows, codes, base, idx_row, low_a, low_b, node_lo, node_hi, late, keep, send, m1fg, slab):
    step = pl.program_id(0)
    cut = low_a.shape[0]
    width, chunk = node_lo.shape
    size = keep.shape[0] // (len(codes) // 2)
    part = slab.shape[0] // len(codes)
    height = rows // 16

    @pl.when(step == 0)
    def _():
        m1fg[...] = jnp.zeros_like(m1fg)

    for node, out, start in ((node_lo, keep, 0), (node_hi, send, steps * chunk)):
        first = start + step * chunk
        sums = dot(one_hot_rows(idx_row[:, :cut], first, chunk), low_a[...]) + dot(
            one_hot_rows(idx_row[:, cut:], first, chunk), low_b[...]
        )
        sums = sums.astype(BF16)
        m1fg[...] += dot(node[...], sums)
        for place in range(chunk // rows):
            at = (step * (chunk // rows) + place) * size
            for lane in range(0, width, LANES):
                tile = sums[place * rows : (place + 1) * rows, lane : lane + LANES]
                out[pl.ds(at + lane // LANES * height, height)] = tile.reshape(height, 16, LANES)

    @pl.when(step == steps - 1)
    def _():
        count = late.shape[0]
        slab[:count] = late[...]
        pack(slab, [m1fg[...]], count)
        count += tile_count((width, width))
        if count < slab.shape[0]:
            slab[count:] = jnp.zeros_like(slab[count:])
        half = len(codes) // 2
        for place, code in enumerate(codes):
            out = keep if place < half else send
            out[(place % half + 1) * size - part : (place % half + 1) * size] = slab[
                pl.ds((base[0] ^ code) * part, part)
            ]


def chunk_tiles(width, edge_width, chunks):
    return pl.cdiv(all_tiles(late_shapes(width, edge_width) + [(width, width)]), chunks)


def far_sums(codes, base, idx_row, low_a, low_b, node_lo, node_hi, late, rows, edge_width):
    width, half = node_lo.shape
    chunk = min(512, half)
    steps = half // chunk
    part = chunk_tiles(width, edge_width, len(codes))
    tiles = len(codes) // 2 * (rows * width // (16 * LANES) + part)
    node_spec = pl.BlockSpec((width, chunk), lambda i: (0, i))
    edges = idx_row.shape[1]
    return pl.pallas_call(
        functools.partial(far_sums_kernel, steps, rows, codes),
        grid=(steps,),
        in_specs=[pl.BlockSpec(memory_space=pltpu.SMEM)]
        + [const_spec(a.shape) for a in (idx_row, low_a, low_b)]
        + [node_spec, node_spec, const_spec(late.shape)],
        out_specs=[
            pl.BlockSpec((tiles, 16, LANES), lambda i: (0, 0, 0), pipeline_mode=pl.Buffered(1))
        ]
        * 2,
        out_shape=[jax.ShapeDtypeStruct((tiles, 16, LANES), BF16)] * 2,
        scratch_shapes=[
            pltpu.VMEM((width, width), F32),
            pltpu.VMEM((part * len(codes), 16, LANES), BF16),
        ],
        compiler_params=pltpu.CompilerParams(vmem_limit_bytes=VMEM),
        name="far_sums",
        cost_estimate=pl.CostEstimate(
            flops=4 * width * half * (edges + width),
            bytes_accessed=edges * width * 2 + half * width * 10,
            transcendentals=0,
        ),
    )(base, idx_row, low_a, low_b, node_lo, node_hi, late)


def edge_gradient_kernel(sb, cut, low_three, low_edge, low_a, low_b, e_first, m1, out):
    step = pl.program_id(0)
    shape = out.shape
    edge_width, width = shape[2], low_a.shape[1]
    for low, use in ((low_a, step < cut), (low_b, step >= cut)):
        @pl.when(use)
        def _(low=low):
            total = (
                low_three[...].astype(F32)
                + dot(low_edge[...], e_first[:, width : width + edge_width])
                + dot_back(low[...], m1[width : width + edge_width, :])
            )
            out[...] = total.reshape(shape)


def edge_gradient(slots, low_three, low_edge, low_a, low_b, e_first, m1):
    edges, edge_width = low_three.shape
    rows = edges // slots
    width = low_a.shape[1]
    sb = slot_block(slots)
    block = sb * rows
    cut = low_a.shape[0] // block
    edge_spec = pl.BlockSpec((block, edge_width), lambda i: (i, 0))
    return pl.pallas_call(
        functools.partial(edge_gradient_kernel, sb, cut),
        grid=(slots // sb,),
        in_specs=[
            edge_spec,
            edge_spec,
            pl.BlockSpec((block, width), lambda i: (jnp.minimum(i, cut - 1), 0)),
            pl.BlockSpec((block, width), lambda i: (jnp.maximum(i - cut, 0), 0)),
            const_spec(e_first.shape),
            const_spec(m1.shape),
        ],
        out_specs=pl.BlockSpec((sb, rows, edge_width), lambda i: (i, 0, 0)),
        out_shape=jax.ShapeDtypeStruct((slots, rows, edge_width), F32),
        compiler_params=pltpu.CompilerParams(vmem_limit_bytes=VMEM),
        name="edge_gradient",
        cost_estimate=pl.CostEstimate(
            flops=2 * edges * edge_width * (width + edge_width),
            bytes_accessed=edges * (width * 2 + 2048),
            transcendentals=0,
        ),
    )(low_three, low_edge, low_a, low_b, e_first, m1)


def node_kernel(pieces, g_u1, own, m1, *refs):
    far, grad_out = refs[:pieces], refs[pieces]
    rows, width = own.shape
    height = rows // 16
    sums = far[0][...].astype(F32)
    for ref in far[1:]:
        sums = sums + ref[...].astype(F32)
    far_sum = jnp.concatenate(
        [sums[j * height : (j + 1) * height].reshape(rows, LANES) for j in range(width // LANES)],
        axis=1,
    )
    far_first = m1.shape[0] - width
    grad_out[...] = (
        g_u1[...]
        + fine(dot_back, own[...], m1[:width, :])
        + fine(dot_back, far_sum, m1[far_first:, :])
    )


def node_last(g_u1, own, m1, far):
    return small_call(
        functools.partial(node_kernel, len(far)),
        (g_u1, own, m1, *far), [(own.shape, F32)], "node_gradient",
        flops=8 * own.size * own.shape[1], moved=2 * MIB,
    )[0]


def starts_of(shapes):
    starts, at = [], 0
    for shape in shapes:
        starts.append(at)
        at += tile_count(shape)
    return starts


def edge_weights_out_kernel(slab, m3g, e1g, e2g, e3g, b3, g1, g2, fb2, eb1, eb2, eb3, g3):
    width, edge_width = m3g.shape[0], e2g.shape[0]
    starts = starts_of(early_shapes(width, edge_width))
    m3g[...] = unpack(slab, starts[0], width, width)
    e1g[:, :width] = unpack(slab, starts[1], edge_width, width)
    middle = unpack(slab, starts[2], edge_width, edge_width)
    far = unpack(slab, starts[3], edge_width, width)
    over = edge_width % LANES
    base_col = width + edge_width - over
    e1g[:, width:base_col] = middle[:, : edge_width - over]
    far = pltpu.roll(jnp.concatenate([far, jnp.zeros((edge_width, LANES), F32)], axis=1), over, 1)
    lane = lax.broadcasted_iota(jnp.int32, (edge_width, LANES), 1)
    e1g[:, base_col : base_col + LANES] = jnp.where(
        lane < over, middle[:, edge_width - over : edge_width - over + LANES], far[:, :LANES]
    )
    rest = e1g.shape[1] - base_col - LANES
    e1g[:, base_col + LANES :] = far[:, LANES : LANES + rest]
    e2g[...] = unpack(slab, starts[4], edge_width, edge_width)[:, :edge_width]
    e3g[...] = unpack(slab, starts[5], edge_width, edge_width)[:, :edge_width]
    bias = unpack(slab, starts[6], 16, width)
    for row, out in enumerate((g1, g2, fb2, b3)):
        out[...] = bias[row : row + 1]
    bias = unpack(slab, starts[7], 16, edge_width)
    for row, out in enumerate((eb1, eb2, eb3, g3)):
        out[...] = bias[row : row + 1, :edge_width]


def edge_weights_out(slab, width, edge_width):
    shapes = [(width, width), (edge_width, 2 * width + edge_width)]
    shapes += [(edge_width, edge_width)] * 2 + [(1, width)] * 4 + [(1, edge_width)] * 4
    return small_call(
        edge_weights_out_kernel, (slab,), [(s, F32) for s in shapes], "edge_weight_gradients",
        moved=4 * MIB,
    )


def weights_out_kernel(codes, base, first, second, m1g, b1, m2g, b2, slab):
    order_in(slab, base[0], codes, first, second)
    width = m2g.shape[0]
    edge_width = m1g.shape[0] - 2 * width
    shapes = late_shapes(width, edge_width)
    starts = starts_of(shapes)
    m1g[:width, :] = unpack(slab, starts[0], width, width)
    m2g[...] = unpack(slab, starts[1], width, width)
    m1g[width : width + edge_width, :] = unpack(slab, starts[2], edge_width, width)
    m1g[width + edge_width :, :] = unpack(slab, all_tiles(shapes), width, width)
    bias = unpack(slab, starts[3], 16, width)
    b1[...] = bias[0:1]
    b2[...] = bias[1:2]


def weights_out(codes, base, halves_in, width, edge_width):
    shapes = [(2 * width + edge_width, width), (1, width), (width, width), (1, width)]
    tiles = chunk_tiles(width, edge_width, len(codes)) * len(codes)
    return small_call(
        functools.partial(weights_out_kernel, codes),
        (base, *halves_in), [(s, F32) for s in shapes], "weight_gradients",
        [pltpu.VMEM((tiles, 16, LANES), BF16)], moved=8 * MIB, scalars=1,
    )


def exchange(value, mask, devices):
    return lax.ppermute(value, AXES, [(d, d ^ mask) for d in range(devices)])


def mask_groups(masks):
    return [masks[i : min(i + 2, len(masks) - 1)] for i in range(0, len(masks) - 1, 2)] + [masks[-1:]]


def order_codes(groups):
    masks = [mask for group in groups for mask in group]
    return [
        sum(mask for bit, mask in enumerate(masks) if place >> bit & 1)
        for place in range(1 << len(masks))
    ]


def combined(group, code):
    return sum(mask for bit, mask in enumerate(group) if code >> bit & 1)


def sent_around(value, group, devices):
    return [value] + [
        exchange(value, combined(group, code), devices) for code in range(1, 1 << len(group))
    ]


def shared_out(total, group, devices):
    parts = 1 << len(group)
    rows = total.shape[0] // parts
    return [total[:rows]] + [
        exchange(total[code * rows : (code + 1) * rows].astype(BF16), combined(group, code), devices)
        for code in range(1, parts)
    ]


def add_up(terms):
    total = terms[0].astype(F32)
    for term in terms[1:]:
        total = total + term.astype(F32)
    return total


def tied(*values):
    return lax.optimization_barrier(values)


def split_three(value):
    rows = []
    for _ in range(3):
        high = lax.reduce_precision(value, 8, 7)
        rows.append(high.astype(BF16))
        value = value - high
    return jnp.concatenate(rows + [jnp.zeros((13, value.shape[1]), BF16)], axis=0)


def per_device(
    node_in,
    edge_in,
    neighbours,
    live_counts,
    message_first,
    message_first_bias,
    message_second,
    message_second_bias,
    message_third,
    message_third_bias,
    norm_one,
    feed_first,
    feed_first_bias,
    feed_second,
    feed_second_bias,
    norm_two,
    edge_first,
    edge_first_bias,
    edge_second,
    edge_second_bias,
    edge_third,
    edge_third_bias,
    norm_three,
    node_cotangent,
    edge_cotangent,
):
    rows, slots = neighbours.shape
    width = node_in.shape[1]
    edge_width = edge_in.shape[2]
    edges = rows * slots
    hid_count = lax.axis_size("hid")
    res_count = lax.axis_size("res")
    devices = res_count * hid_count
    bits = devices.bit_length() - 1
    masks = [1 << b for b in range(bits - 1, -1, -1)]
    groups = mask_groups(masks)
    codes = order_codes(groups)
    me = lax.axis_index("res") * hid_count + lax.axis_index("hid")
    base = me.reshape(1)
    row = lambda vector: vector.reshape(1, -1)

    names = neighbours.T.reshape(edges)
    apart = (names // rows) ^ me
    place = jnp.zeros_like(names)
    for bit, mask in enumerate(masks):
        place = place | jnp.where((apart & mask) != 0, 1 << bit, 0)
    idx_row = (place * rows + names % rows).reshape(1, edges)
    live_col = jnp.broadcast_to(live_counts[:, None], (rows, LANES))
    edge = edge_in.transpose(1, 0, 2)
    cot = edge_cotangent.transpose(1, 0, 2)
    e_first = edge_first.T
    e_far = e_first[:, width + edge_width :]
    edge_t = edge.reshape(edges, edge_width).T
    f1x = jnp.concatenate([feed_first, split_three(row(feed_first_bias))], axis=0)
    f2x = feed_second

    tiled = lambda value, per: value.reshape(-1, per, 16, LANES)
    stack = lambda pieces: jnp.concatenate(pieces, axis=0)
    *outer, near = groups

    held = stack(sent_around(node_in, outer[0], devices))
    held, idx_row, live_col, e_far, edge_t = tied(held, idx_row, live_col, e_far, edge_t)
    for group in outer[1:]:
        held = stack(sent_around(held, group, devices))
    held, f1x, f2x = tied(held, f1x, f2x)
    node_lo, node_hi = sent_around(held, near, devices)

    f1, f2 = [f1x], [f2x]
    hid_masks = [m for m in masks if m < hid_count]
    for mask in hid_masks[:-1]:
        f1, f2 = [pieces + [exchange(p, mask, devices) for p in pieces] for pieces in (f1, f2)]

    residues = devices * rows
    sb = 20 if residues <= 4096 else 4
    blocks = slots // sb
    cut = 2 * blocks // 3
    message_args = (
        residues, node_in, edge, idx_row, live_col, message_first, row(message_first_bias),
        message_second, row(message_second_bias),
    )
    a1, s1, s2, total, table = message_forward(sb, 0, cut, *message_args, (node_lo, node_hi))
    total, f1, f2 = tied(total, f1, f2)
    f1, f2 = [
        pieces + [exchange(p, hid_masks[-1], devices) for p in pieces] for pieces in (f1, f2)
    ]
    a1, s1, s2, total = message_forward(
        sb, cut, blocks - cut, *message_args, (table, total, a1, s1, s2)
    )
    h1b, n1, sc1, n2, sc2, slope, h2b, far_part, own_part = residue_forward(
        node_in, total, message_third, row(message_third_bias), row(norm_one),
        row(feed_second_bias), row(norm_two), e_first, e_far, row(edge_first_bias), f1, f2,
    )

    held = stack(sent_around(far_part, outer[0], devices))
    h_held = stack(sent_around(h1b, outer[0], devices))
    held, node_lo, node_hi = tied(held, node_lo.T, node_hi.T)
    for group in outer[1:]:
        held = stack(sent_around(held, group, devices))
    held, h_held = tied(held, h_held)
    q_lo, q_hi = sent_around(held, near, devices)
    for group in outer[1:]:
        h_held = stack(sent_around(h_held, group, devices))

    edge_out, act_one, act_two, low_three, low_two, low_one, hi, lo, own_sum, edge_gain = edge_branch(
        q_lo, q_hi, own_part, edge, cot, idx_row, live_col, e_first,
        edge_second, row(edge_second_bias), edge_third, row(edge_third_bias), row(norm_three),
    )
    lo, h_held = tied(lo, h_held)
    h_all = sent_around(h_held, near, devices)

    work = [
        lambda: edge_weights((act_two, act_one), (low_three, low_two), rows),
        lambda: edge_weights((low_one,), (edge,), rows),
    ]
    made = []
    terms = [lo, exchange(hi, near[0], devices)]
    for group in reversed(outer):
        terms = shared_out(add_up(terms), group, devices)
        if work:
            terms, got = tied(terms, work.pop(0)())
            made.append(got)
    while work:
        made.append(work.pop(0)())
    (e3g, e2g, eb3, eb2), (e1g, eb1) = made
    g_u1, v, gy2, early = residue_backward(
        (
            node_cotangent, own_sum, e_first, e_far, h2b, n1, sc1, n2, sc2, slope, row(norm_one),
            row(norm_two), message_third, total, e1g, e2g, e3g, eb1, eb2, eb3, edge_gain,
        ),
        terms, f1, f2,
    )

    early = lax.psum(early, AXES)

    g_held = stack(sent_around(gy2, outer[0], devices))
    blocks = slots // slot_block(slots)
    low_a, *sums = message_backward(
        0, blocks // 2, v, a1, s1, s2, edge_t, live_col, message_second
    )
    v, g_held = tied(v, g_held)
    for group in outer[1:]:
        g_held = stack(sent_around(g_held, group, devices))
    low_b, own, late = message_backward(
        blocks // 2, blocks - blocks // 2, v, a1, s1, s2, edge_t, live_col, message_second,
        (node_in, *sums),
    )
    keep, send = far_sums(
        codes, base, idx_row, low_a, low_b, node_lo, node_hi, late, rows, edge_width
    )

    terms = [keep, exchange(send, near[0], devices)]
    g_all = sent_around(g_held, near, devices)
    work = [
        lambda low: edge_gradient(slots, low_three, low_one, low, low_b, e_first, message_first),
        lambda low: feed_gradients((h_all[0], low), g_all, feed_first, row(feed_first_bias), feed_second),
    ]
    after = [low_a, h_all[1]]
    made = []
    for group in reversed(outer):
        total = add_up(terms)
        if work:
            total, low = tied(total, after.pop(0))
        terms = shared_out(total, group, devices)
        if work:
            terms, out = tied(terms, work.pop(0)(low))
            made.append(out)
    edge_grad, (f1g, f2g, fb1g) = made
    sums_part = rows * width // (16 * LANES)
    held = add_up([t[sums_part:] for t in terms]).astype(BF16)

    node_terms = [t[:sums_part] for t in terms]
    for at, group in enumerate(outer):
        around = sent_around(held, group, devices)
        if at == 0:
            around, node_gradient = tied(around, node_last(g_u1, own, message_first, node_terms))
        held = stack(around)
    m1g, b1, m2g, b2 = weights_out(
        codes, base, sent_around(held, near, devices), width, edge_width
    )
    m3g, e1g, e2g, e3g, b3, g1, g2, fb2, eb1, eb2, eb3, g3 = edge_weights_out(
        early, width, edge_width
    )
    flat = lambda vector: vector.reshape(-1)
    return (
        h2b,
        edge_out.transpose(1, 0, 2),
        node_gradient,
        edge_grad.transpose(1, 0, 2),
        m1g,
        flat(b1),
        m2g,
        flat(b2),
        m3g,
        flat(b3),
        flat(g1),
        f1g,
        flat(fb1g),
        f2g,
        flat(fb2),
        flat(g2),
        e1g.T,
        flat(eb1),
        e2g,
        flat(eb2),
        e3g,
        flat(eb3),
        flat(g3),
    )


def solution(mesh):
    nodes, edges, shared = P(AXES, None), P(AXES, None, None), P()
    return jax.shard_map(
        per_device,
        mesh=mesh,
        in_specs=(nodes, edges, nodes, P(AXES))
        + (shared,) * 7
        + (P(None, "hid"), P("hid"), P("hid", None))
        + (shared,) * 9
        + (nodes, edges),
        out_specs=(nodes, edges, nodes, edges)
        + (shared,) * 7
        + (P(None, "hid"), P("hid"), P("hid", None))
        + (shared,) * 9,
        check_vma=False,
    )
```

```python
import functools

import jax
import jax.numpy as jnp
from jax import lax
from jax.experimental import pallas as pl
from jax.experimental.pallas import tpu as pltpu
from jax.sharding import PartitionSpec as P

EPS = 1e-05
AXES = ("res", "hid")
F32 = jnp.float32
BF16 = jnp.bfloat16
TANH_SCALE = 0.7978845608028654
TANH_CUBE = 0.044715
LANES = 128
CHUNK = 2048
MIB = 1024 * 1024
VMEM = 58 * MIB


def dot(left, right):
    return lax.dot_general(left, right, (((1,), (0,)), ((), ())), preferred_element_type=F32)


def dot_rows(left, right):
    return lax.dot_general(left, right, (((0,), (0,)), ((), ())), preferred_element_type=F32)


def dot_back(left, right):
    return lax.dot_general(left, right, (((1,), (1,)), ((), ())), preferred_element_type=F32)


def halves(value):
    high = value.astype(BF16)
    return high, (value - high.astype(F32)).astype(BF16)


def fine(product, value, weights):
    high, low = halves(value)
    return product(high, weights) + product(low, weights)


def gelu_parts(x):
    square = x * x
    t = jnp.tanh(x * (TANH_SCALE + (TANH_SCALE * TANH_CUBE) * square))
    gate = 0.5 + 0.5 * t
    act = x * gate
    slope = gate + act * (1.0 - gate) * (2 * TANH_SCALE + (6 * TANH_SCALE * TANH_CUBE) * square)
    return act, slope


def index_columns(idx_row):
    parts = [
        jnp.broadcast_to(idx_row[:, first : first + LANES], (LANES, LANES)).T
        for first in range(0, idx_row.shape[1], LANES)
    ]
    return jnp.concatenate(parts, axis=0)


def one_hot_columns(idx, start, count):
    one, zero = jnp.ones((), BF16), jnp.zeros((), BF16)
    idx = idx.astype(jnp.int16)
    lane = lax.broadcasted_iota(jnp.int32, idx.shape, 1).astype(jnp.int16)
    parts = [
        jnp.where(idx == lane + jnp.int16(start + first), one, zero)
        for first in range(0, count, LANES)
    ]
    return jnp.concatenate(parts, axis=1)


def pick_rows(idx, table_refs):
    total, start = None, 0
    for ref in table_refs:
        rows = ref.shape[0]
        step = min(rows, CHUNK)
        for first in range(0, rows, step):
            part = dot(one_hot_columns(idx, start + first, step), ref[first : first + step, :])
            total = part if total is None else total + part
        start += rows
    return total


def one_hot_rows(idx_row, start, count):
    shape = (count, idx_row.shape[1])
    row = (lax.broadcasted_iota(jnp.int32, shape, 0) + start).astype(jnp.int16)
    names = jnp.broadcast_to(idx_row, shape).astype(jnp.int16)
    return jnp.where(names == row, jnp.ones((), BF16), jnp.zeros((), BF16))


def spread(column, width):
    return jnp.concatenate([column] * (width // LANES), axis=1)


def norm(value):
    centre = value - jnp.mean(value, -1, keepdims=True)
    scale = lax.rsqrt(jnp.mean(centre * centre, -1, keepdims=True) + EPS)
    return centre * scale, scale


def norm_back(inner, normed, scale):
    mean_first = jnp.mean(inner, -1, keepdims=True)
    mean_second = jnp.mean(inner * normed, -1, keepdims=True)
    return scale * (inner - mean_first - normed * mean_second)


def column_sum(value):
    return jnp.sum(value, axis=0, keepdims=True)


def whole(*_):
    return (0, 0)


def const_spec(shape):
    return pl.BlockSpec(shape, lambda *_: (0,) * len(shape), pipeline_mode=pl.Buffered(1))


def small_call(kernel, args, shapes, name, scratch=(), flops=0, moved=0, exps=0, scalars=0):
    return pl.pallas_call(
        kernel,
        grid=(1,),
        in_specs=[pl.BlockSpec(memory_space=pltpu.SMEM)] * scalars
        + [const_spec(a.shape) for a in args[scalars:]],
        out_specs=[pl.BlockSpec(s, lambda *_, n=len(s): (0,) * n) for s, _ in shapes],
        out_shape=[jax.ShapeDtypeStruct(*s) for s in shapes],
        scratch_shapes=list(scratch),
        compiler_params=pltpu.CompilerParams(vmem_limit_bytes=VMEM),
        name=name,
        cost_estimate=pl.CostEstimate(flops=flops, bytes_accessed=moved, transcendentals=exps),
    )(*args)


def tile_count(shape):
    return pl.cdiv(shape[0], 16) * pl.cdiv(shape[1], LANES)


def all_tiles(shapes):
    return sum(tile_count(s) for s in shapes)


def pack(slab, values, at=0):
    for value in values:
        rows, columns = value.shape
        count = rows // 16
        for first in range(0, columns, LANES):
            take = min(LANES, columns - first)
            tile = value[:, first : first + take].astype(BF16).reshape(count, 16, take)
            slab[at : at + count, :, :take] = tile
            at += count


def unpack(slab, at, rows, columns):
    count = rows // 16
    parts = [
        slab[at + i * count : at + (i + 1) * count].reshape(rows, LANES).astype(F32)
        for i in range(pl.cdiv(columns, LANES))
    ]
    return jnp.concatenate(parts, axis=1)


def order_out(slab, base, codes, keep, send):
    size = slab.shape[0] // len(codes)
    half = len(codes) // 2
    for place, code in enumerate(codes):
        out = keep if place < half else send
        at = (place % half) * size
        out[at : at + size] = slab[pl.ds((base ^ code) * size, size)]


def half_shapes(tiles):
    return [((tiles // 2, 16, LANES), BF16)] * 2


def slab_scratch(tiles):
    return pltpu.VMEM((tiles, 16, LANES), BF16)


def slab_part(width, edge_width, chunks):
    return pl.cdiv(all_tiles(early_shapes(width, edge_width) + late_shapes(width, edge_width)), chunks)


def far_part_tiles(width, chunks):
    return pl.cdiv(all_tiles([(width, width)]), chunks)


def order_in(slabs, base, codes, first, second):
    sizes = [slab.shape[0] // len(codes) for slab in slabs]
    half = len(codes) // 2
    for place, code in enumerate(codes):
        source = first if place < half else second
        at = (place % half) * sum(sizes)
        for slab, size in zip(slabs, sizes):
            slab[pl.ds((base ^ code) * size, size)] = source[at : at + size]
            at += size


def padded_rows(parts, width):
    return jnp.concatenate(parts + [jnp.zeros((16 - len(parts), width), F32)], axis=0)


def slot_block(slots):
    for size in (10, 12, 8, 6, 5, 4, 3, 2):
        if slots % size == 0:
            return size
    return 1


def far_table(node_lo, node_hi, weights, put):
    tile = min(512, node_lo.shape[0])
    for source, start in ((node_lo, 0), (node_hi, node_lo.shape[0])):
        def body(i, carry, source=source, start=start):
            at = pl.multiple_of(i * tile, tile)
            put(start + at, dot(source[pl.ds(at, tile), :], weights))
            return carry
        lax.fori_loop(0, source.shape[0] // tile, body, 0)


def message_forward_kernel(
    sb, by_rows, node_lo, node_hi, node_own, edge, idx_row, names, live_col, m1, b1, m2, b2,
    a1_out, s1_out, s2_out, sum_out, table, far, near, lhs, z,
):
    step = pl.program_id(0)
    width = node_own.shape[1]
    edge_width = edge.shape[2]
    rows = edge.shape[1]
    block = sb * rows
    lanes = width // LANES

    @pl.when(step == 0)
    def _():
        weights = m1[width + edge_width :, :]
        if by_rows:
            def put(first, value):
                for at in range(8):
                    column = at % lanes * LANES
                    table[pl.ds(first * 8 + at, value.shape[0], stride=8), :] = value[
                        :, column : column + LANES
                    ]
        else:
            def put(first, value):
                table[pl.ds(first, value.shape[0]), :] = value.astype(BF16)
        far_table(node_lo, node_hi, weights, put)
        near[:edge_width, :] = m1[width : width + edge_width, :]
        near[edge_width:, :] = jnp.zeros_like(near[edge_width:, :])
        near[edge_width : edge_width + rows, :] = (
            dot(node_own[...], m1[:width, :]) + b1[...]
        ).astype(BF16)
        shape = (rows, near.shape[0] - edge_width)
        eye = lax.broadcasted_iota(jnp.int32, shape, 0) == lax.broadcasted_iota(jnp.int32, shape, 1)
        for at in range(0, block, rows):
            lhs[at : at + rows, edge_width:] = jnp.where(eye, 1.0, 0.0).astype(BF16)
        sum_out[...] = jnp.zeros_like(sum_out)

    lhs[:, :edge_width] = edge[...].reshape(block, edge_width)
    z[...] = dot(lhs[...], near[...])
    if not by_rows:
        z[...] += pick_rows(index_columns(idx_row[...]), (table,))
    upper = lax.broadcasted_iota(jnp.int32, (8, LANES), 0) < lanes

    def fetch(at):
        for e in range(at, at + 16, 2):
            pair = [
                table[pl.ds(pl.multiple_of(names[0, step * block + e + i] * 8, 8), 8), :]
                for i in range(2)
            ]
            far[e * lanes : e * lanes + 8, :] = jnp.where(upper, *pair)

    def fetched(at):
        return jnp.concatenate(
            [far[pl.ds(at * lanes + j, 16, stride=lanes), :] for j in range(lanes)], axis=1
        )

    if by_rows:
        fetch(0)
    for at in range(0, block, 16):
        value = z[at : at + 16, :]
        if by_rows:
            if at + 16 < block:
                fetch(at + 16)
            value = value + fetched(at)
        act, slope = gelu_parts(value)
        a1_out[at : at + 16, :] = act.astype(BF16)
        s1_out[at : at + 16, :] = slope.astype(BF16)
    z[...] = dot(a1_out[...], m2[...])
    bias = b2[...]
    for row in range(0, rows, 16):
        count = live_col[row : row + 16, :]
        inverse = 1.0 / count.astype(F32)
        total = sum_out[row : row + 16, :]
        for s in range(sb):
            at = s * rows + row
            act, slope = gelu_parts(z[at : at + 16, :] + bias)
            s2_out[at : at + 16, :] = slope.astype(BF16)
            share = jnp.where(count > step * sb + s, inverse, 0.0)
            total = total + act.astype(BF16).astype(F32) * spread(share, width)
        sum_out[row : row + 16, :] = total


def message_forward(node_lo, node_hi, node_own, edge, idx_row, live_col, m1, b1, m2, b2):
    slots, rows, edge_width = edge.shape
    width = node_own.shape[1]
    residues = 2 * node_lo.shape[0]
    by_rows = residues <= 4096 and width == 4 * LANES
    sb = slot_block(slots) if by_rows else 4
    block = sb * rows
    edges = slots * rows
    near = pl.cdiv(edge_width + rows, LANES) * LANES
    row_spec = pl.BlockSpec((block, width), lambda i: (i, 0))
    return pl.pallas_call(
        functools.partial(message_forward_kernel, sb, by_rows),
        grid=(slots // sb,),
        in_specs=[
            const_spec(node_lo.shape),
            const_spec(node_hi.shape),
            const_spec(node_own.shape),
            pl.BlockSpec((sb, rows, edge_width), lambda i: (i, 0, 0)),
            pl.BlockSpec((1, block), lambda i: (0, i)),
            pl.BlockSpec(memory_space=pltpu.SMEM),
            const_spec(live_col.shape),
            const_spec(m1.shape),
            const_spec(b1.shape),
            const_spec(m2.shape),
            const_spec(b2.shape),
        ],
        out_specs=[row_spec, row_spec, row_spec, pl.BlockSpec((rows, width), whole)],
        out_shape=[jax.ShapeDtypeStruct((edges, width), BF16)] * 3
        + [jax.ShapeDtypeStruct((rows, width), F32)],
        scratch_shapes=[
            pltpu.VMEM((residues * 8, LANES), F32) if by_rows else pltpu.VMEM((residues, width), BF16),
            pltpu.VMEM((block * 4 if by_rows else 8, LANES), F32),
            pltpu.VMEM((near, width), BF16),
            pltpu.VMEM((block, near), BF16),
            pltpu.VMEM((block, width), F32),
        ],
        compiler_params=pltpu.CompilerParams(vmem_limit_bytes=VMEM),
        name="message_forward",
        cost_estimate=pl.CostEstimate(
            flops=2 * edges * width * (residues + edge_width + width),
            bytes_accessed=edges * width * 6 + edges * edge_width * 2 + edges * LANES * 4,
            transcendentals=2 * edges * width,
        ),
    )(node_lo, node_hi, node_own, edge, idx_row, idx_row, live_col, m1, b1, m2, b2)


def residue_forward_kernel(parts, node, total, m3, b3, g1, fb2, g2, e_first, e_far, eb, *refs):
    f1, f2 = refs[:parts], refs[parts : 2 * parts]
    h1b_out, n1_out, sc1_out, n2_out, sc2_out, slope_out, h2b_out, far_out, own_out = refs[2 * parts :]
    width, hidden = node.shape[1], f1[0].shape[1]
    u1 = node[...].astype(F32) + fine(dot, total[...], m3[...]) + b3[...]
    n1, sc1 = norm(u1)
    h1 = n1 * g1[...]
    h1b = h1.astype(BF16)
    h1b_out[...] = h1b
    n1_out[...] = n1
    sc1_out[...] = jnp.broadcast_to(sc1, sc1_out.shape)
    y2 = None
    for p in range(parts):
        bias = f1[p][width : width + 16, :].astype(F32)
        bias = bias[0:1] + bias[1:2] + bias[2:3]
        act, slope = gelu_parts(dot(h1b, f1[p][:width, :]) + bias)
        slope_out[:, p * hidden : (p + 1) * hidden] = slope
        part = dot(act.astype(BF16), f2[p][...])
        y2 = part if y2 is None else y2 + part
    n2, sc2 = norm(h1 + (y2 + fb2[...]))
    h2b = (n2 * g2[...]).astype(BF16)
    n2_out[...] = n2
    sc2_out[...] = jnp.broadcast_to(sc2, sc2_out.shape)
    h2b_out[...] = h2b
    far_out[...] = dot_back(h2b, e_far[...]).astype(BF16)
    own_out[...] = dot_back(h2b, e_first[:, :width]) + eb[...]


def residue_forward(node, total, m3, b3, g1, fb2, g2, e_first, e_far, eb, f1, f2):
    rows, width = node.shape
    edge_width = e_first.shape[0]
    hidden = len(f1) * f1[0].shape[1]
    shapes = [
        ((rows, width), BF16),
        ((rows, width), F32),
        ((rows, LANES), F32),
        ((rows, width), F32),
        ((rows, LANES), F32),
        ((rows, hidden), F32),
        ((rows, width), BF16),
        ((rows, edge_width), BF16),
        ((rows, edge_width), F32),
    ]
    return small_call(
        functools.partial(residue_forward_kernel, len(f1)),
        (node, total, m3, b3, g1, fb2, g2, e_first, e_far, eb, *f1, *f2),
        shapes, "residue_forward", flops=4 * rows * width * hidden, moved=5 * MIB,
        exps=rows * hidden,
    )


def edge_kernel(
    sb, blocks, hi_chunks, far_lo, far_hi, own, edge, cot, idx, idx_row, live_col,
    e_first, e2, eb2, e3, eb3, g3,
    edge_out, act_one_out, act_two_out, low_three_out, low_two_out, low_one_out, hi_out, lo_out, own_out, gain_out,
    low_first, gs,
):
    step = pl.program_id(0)
    rows, width = own.shape
    node_width = (e_first.shape[1] - width) // 2
    e_mid = e_first.at[:, node_width : node_width + width]

    @pl.when(step == 0)
    def _():
        own_out[...] = jnp.zeros_like(own_out)
        gs[...] = jnp.zeros_like(gs)

    @pl.when(step < blocks)
    def _():
        block = sb * rows
        flat = edge[...].reshape(block, width)
        mixed = pick_rows(index_columns(idx[...]), (far_lo, far_hi)) + dot_back(flat, e_mid[...])
        w_one = (mixed.reshape(sb, rows, width) + own[...][None]).reshape(block, width)
        act_one, slope_one = gelu_parts(w_one)
        act_one = act_one.astype(BF16)
        act_one_out[...] = act_one
        act_two, slope_two = gelu_parts(dot(act_one, e2[...]) + eb2[...])
        act_two = act_two.astype(BF16)
        act_two_out[...] = act_two
        w_three = dot(act_two, e3[...]) + eb3[...]
        normed, scale = norm(flat.astype(F32) + w_three)
        count = spread(live_col[...], pl.cdiv(width, LANES) * LANES)[:, :width]
        live = jnp.concatenate(
            [jnp.where(count > step * sb + s, 1.0, 0.0) for s in range(sb)], axis=0
        )
        edge_out[...] = (normed * g3[...] * live).astype(BF16).reshape(sb, rows, width)
        grad = cot[...].reshape(block, width).astype(F32) * live
        gs[...] += jnp.sum((grad * normed).reshape(sb, rows, width), axis=0)
        low_three = norm_back(grad * g3[...], normed, scale).astype(BF16)
        low_three_out[...] = low_three
        low_two = (dot_back(low_three, e3[...]) * slope_two).astype(BF16)
        low_two_out[...] = low_two
        low_one = (dot_back(low_two, e2[...]) * slope_one).astype(BF16)
        low_one_out[...] = low_one
        own_out[...] += jnp.sum(low_one.astype(F32).reshape(sb, rows, width), axis=0)
        low_first[pl.ds(pl.multiple_of(step * block, block), block), :] = low_one

    chunk = hi_out.shape[0]

    @pl.when((step >= blocks) & (step < blocks + hi_chunks))
    def _():
        start = (step - blocks + hi_chunks) * chunk
        hi_out[...] = dot(one_hot_rows(idx_row[...], start, chunk), low_first[...]).astype(BF16)

    @pl.when(step >= blocks + hi_chunks)
    def _():
        start = (step - blocks - hi_chunks) * chunk
        lo_out[...] = dot(one_hot_rows(idx_row[...], start, chunk), low_first[...])

    @pl.when(step == blocks + 2 * hi_chunks - 1)
    def _():
        gain_out[...] = column_sum(gs[...])


def edge_branch(far_lo, far_hi, own, edge, cot, idx_row, live_col, e_first, e2, eb2, e3, eb3, g3):
    slots, rows, width = edge.shape
    sb = slot_block(slots)
    edges = slots * rows
    block = sb * rows
    blocks = slots // sb
    half = far_lo.shape[0]
    chunk = min(512, half)
    hi_chunks = half // chunk
    blk = lambda i: jnp.minimum(i, blocks - 1)
    hi_at = lambda i: (jnp.clip(i - blocks, 0, hi_chunks - 1), 0)
    lo_at = lambda i: (jnp.clip(i - blocks - hi_chunks, 0, hi_chunks - 1), 0)
    slot_spec = pl.BlockSpec((sb, rows, width), lambda i: (blk(i), 0, 0))
    row_spec = pl.BlockSpec((block, width), lambda i: (blk(i), 0))
    return pl.pallas_call(
        functools.partial(edge_kernel, sb, blocks, hi_chunks),
        grid=(blocks + 2 * hi_chunks,),
        in_specs=[
            const_spec(far_lo.shape),
            const_spec(far_hi.shape),
            const_spec(own.shape),
            slot_spec,
            slot_spec,
            pl.BlockSpec((1, block), lambda i: (0, blk(i))),
            const_spec(idx_row.shape),
            const_spec(live_col.shape),
            const_spec(e_first.shape),
            const_spec(e2.shape),
            const_spec(eb2.shape),
            const_spec(e3.shape),
            const_spec(eb3.shape),
            const_spec(g3.shape),
        ],
        out_specs=[slot_spec]
        + [row_spec] * 5
        + [
            pl.BlockSpec((chunk, width), hi_at),
            pl.BlockSpec((chunk, width), lo_at),
            pl.BlockSpec((rows, width), whole),
            pl.BlockSpec((1, width), whole),
        ],
        out_shape=[jax.ShapeDtypeStruct((slots, rows, width), BF16)]
        + [jax.ShapeDtypeStruct((edges, width), BF16)] * 5
        + [
            jax.ShapeDtypeStruct((half, width), BF16),
            jax.ShapeDtypeStruct((half, width), F32),
            jax.ShapeDtypeStruct((rows, width), F32),
            jax.ShapeDtypeStruct((1, width), F32),
        ],
        scratch_shapes=[pltpu.VMEM((edges, width), BF16), pltpu.VMEM((rows, width), F32)],
        compiler_params=pltpu.CompilerParams(vmem_limit_bytes=VMEM),
        name="edge_branch",
        cost_estimate=pl.CostEstimate(
            flops=2 * edges * width * (4 * half + 5 * width),
            bytes_accessed=edges * width * 16,
            transcendentals=2 * edges * width,
        ),
    )(far_lo, far_hi, own, edge, cot, idx_row, idx_row, live_col, e_first, e2, eb2, e3, eb3, g3)


def edge_weights_kernel(blocks, pairs, *refs):
    step = pl.program_id(0)
    lefts, rights = refs[:pairs], refs[pairs : 2 * pairs]
    grads, biases, sums = refs[2 * pairs : 3 * pairs], refs[3 * pairs : 4 * pairs], refs[-1]
    rows = sums.shape[1]

    @pl.when(step == 0)
    def _():
        for ref in (*grads, sums):
            ref[...] = jnp.zeros_like(ref)

    for at in range(pairs):
        left, right = [r[...].reshape(-1, r.shape[-1]) for r in (lefts[at], rights[at])]
        grads[at][...] += dot_rows(left, right)
        low = left if lefts[at].ndim < rights[at].ndim else right
        sums[at] += jnp.sum(low.astype(F32).reshape(-1, rows, low.shape[1]), axis=0)

    @pl.when(step == blocks - 1)
    def _():
        for at in range(pairs):
            biases[at][...] = column_sum(sums[at])


def edge_weights(lefts, rights, rows):
    pairs = len(lefts)
    edges, width = lefts[0].shape
    slots = edges // rows
    sb = slot_block(slots)

    def spec(array):
        if array.ndim == 3:
            return pl.BlockSpec((sb, rows, width), lambda i: (i, 0, 0))
        return pl.BlockSpec((sb * rows, width), lambda i: (i, 0))

    shapes = [(width, width)] * pairs + [(1, width)] * pairs
    return pl.pallas_call(
        functools.partial(edge_weights_kernel, slots // sb, pairs),
        grid=(slots // sb,),
        in_specs=[spec(array) for array in (*lefts, *rights)],
        out_specs=[pl.BlockSpec(s, whole) for s in shapes],
        out_shape=[jax.ShapeDtypeStruct(s, F32) for s in shapes],
        scratch_shapes=[pltpu.VMEM((pairs, rows, width), F32)],
        compiler_params=pltpu.CompilerParams(vmem_limit_bytes=VMEM),
        name="edge_weights",
        cost_estimate=pl.CostEstimate(
            flops=2 * pairs * edges * width * width,
            bytes_accessed=pairs * edges * width * 4,
            transcendentals=0,
        ),
    )(*lefts, *rights)


def early_shapes(width, edge_width):
    return [
        (width, width),
        (edge_width, width),
        (edge_width, edge_width),
        (edge_width, width),
        (edge_width, edge_width),
        (edge_width, edge_width),
        (16, width),
        (16, edge_width),
    ]


def residue_backward_kernel(
    parts, pieces, node_cot, own_sum, e_first, e_far, h2b, n1, sc1, n2, sc2, slope, g1, g2, m3,
    total, e1g, e2g, e3g, eb1, eb2, eb3, edge_gain, *refs,
):
    far = refs[:pieces]
    f1 = refs[pieces : pieces + parts]
    f2 = refs[pieces + parts : pieces + 2 * parts]
    gu1_out, v_out, gy2_out, slab = refs[pieces + 2 * parts :]
    width, hidden = h2b.shape[1], f1[0].shape[1]
    far_sum = far[0][...]
    for ref in far[1:]:
        far_sum = far_sum + ref[...].astype(F32)
    own = own_sum[...]
    g_h2 = (
        node_cot[...].astype(F32)
        + fine(dot, own, e_first[:, :width])
        + fine(dot, far_sum, e_far[...])
    )
    gain_two = column_sum(g_h2 * n2[...])
    g_u2 = norm_back(g_h2 * g2[...], n2[...], sc2[:, :1])
    gy2 = g_u2.astype(BF16)
    gy2_out[...] = gy2
    g_h1 = g_u2
    for p in range(parts):
        gy1 = dot_back(gy2, f2[p][...]) * slope[:, p * hidden : (p + 1) * hidden]
        g_h1 = g_h1 + dot_back(gy1.astype(BF16), f1[p][:width, :])
    gain_one = column_sum(g_h1 * n1[...])
    g_u1 = norm_back(g_h1 * g1[...], n1[...], sc1[:, :1])
    gu1_out[...] = g_u1
    v_out[...] = fine(dot_back, g_u1, m3[...])
    bias = [gain_one, gain_two, column_sum(gy2.astype(F32)), column_sum(g_u1)]
    slab[...] = jnp.zeros_like(slab)
    pack(
        slab,
        [
            dot_rows(total[...].astype(BF16), g_u1.astype(BF16)),
            dot_rows(own.astype(BF16), h2b[...]),
            e1g[...],
            dot_rows(far_sum.astype(BF16), h2b[...]),
            e2g[...],
            e3g[...],
            padded_rows(bias, width),
            padded_rows([eb1[...], eb2[...], eb3[...], edge_gain[...]], own.shape[1]),
        ],
    )


def residue_backward(args, far, f1, f2):
    node_cot, e_first, slope = args[0], args[2], args[9]
    rows, width = node_cot.shape
    tiles = all_tiles(early_shapes(width, e_first.shape[0]))
    shapes = [
        ((rows, width), F32),
        ((rows, width), F32),
        ((rows, width), BF16),
        ((tiles, 16, LANES), BF16),
    ]
    return small_call(
        functools.partial(residue_backward_kernel, len(f1), len(far)),
        (*args, *far, *f1, *f2),
        shapes, "residue_backward",
        flops=4 * rows * width * slope.shape[1], moved=8 * MIB,
    )


def feed_kernel(h_lo, h_hi, g_lo, g_hi, f1, fb1, f2, f1g, f2g, fb1g):

    @pl.when(pl.program_id(0) == 0)
    def _():
        for ref in (f1g, f2g, fb1g):
            ref[...] = jnp.zeros_like(ref)

    for h1b, gy2 in ((h_lo[...], g_lo[...]), (h_hi[...], g_hi[...])):
        act, slope = gelu_parts(dot(h1b, f1[...]) + fb1[...])
        gy1 = (dot_back(gy2, f2[...]) * slope).astype(BF16)
        f1g[...] += dot_rows(h1b, gy1)
        f2g[...] += dot_rows(act.astype(BF16), gy2)
        fb1g[...] += column_sum(gy1.astype(F32))


def feed_gradients(h1b, gy2, f1, fb1, f2):
    width, hidden = f1.shape
    half = h1b[0].shape[0]
    chunk = min(512, half)
    shapes = [(width, hidden), (hidden, width), (1, hidden)]
    return pl.pallas_call(
        feed_kernel,
        grid=(half // chunk,),
        in_specs=[pl.BlockSpec((chunk, width), lambda i: (i, 0))] * 4
        + [const_spec(a.shape) for a in (f1, fb1, f2)],
        out_specs=[pl.BlockSpec(s, whole) for s in shapes],
        out_shape=[jax.ShapeDtypeStruct(s, F32) for s in shapes],
        compiler_params=pltpu.CompilerParams(vmem_limit_bytes=VMEM),
        name="feed_gradients",
        cost_estimate=pl.CostEstimate(
            flops=16 * half * width * hidden,
            bytes_accessed=8 * half * width,
            transcendentals=2 * half * hidden,
        ),
    )(*h1b, *gy2, f1, fb1, f2)


def late_shapes(width, edge_width):
    return [(width, width), (width, width), (edge_width, width), (16, width)]


def message_backward_kernel(sb, first_block, blocks, codes, *refs):
    last = codes is not None
    if last:
        base, refs = refs[0], refs[1:]
    v, a1, s1, s2, edge, live_col, m2 = refs[:7]
    refs = refs[7:]
    if last:
        node, early, own_in, m2g_in, m1eg_in, b2_in, low_out, own, keep, send, m2g, m1eg, b2s, slab, low_two, grad = refs
    else:
        low_out, own, m2g, m1eg, b2s, low_two, grad = refs
    step = pl.program_id(0)
    rows, width = v.shape
    edge_width = edge.shape[2]
    block = sb * rows

    @pl.when(step == 0)
    def _():
        if last:
            own[...] = own_in[...]
            m2g[...] = m2g_in[...]
            m1eg[...] = m1eg_in[...]
            b2s[...] = b2_in[...]
        else:
            for ref in (own, m2g, m1eg, b2s):
                ref[...] = jnp.zeros_like(ref)

    for row in range(0, rows, 16):
        count = live_col[row : row + 16, :]
        inverse = 1.0 / count.astype(F32)
        value = v[row : row + 16, :]
        total = b2s[row : row + 16, :]
        for s in range(sb):
            at = s * rows + row
            share = jnp.where(count > (step + first_block) * sb + s, inverse, 0.0)
            low = (value * spread(share, width) * s2[at : at + 16, :].astype(F32)).astype(BF16)
            low_two[at : at + 16, :] = low
            total = total + low.astype(F32)
        b2s[row : row + 16, :] = total
    grad[...] = dot_back(low_two[...], m2[...])
    m2g[...] += dot_rows(a1[...], low_two[...])
    for row in range(0, rows, 16):
        total = own[row : row + 16, :]
        for s in range(sb):
            at = s * rows + row
            low = (grad[at : at + 16, :] * s1[at : at + 16, :].astype(F32)).astype(BF16)
            low_out[at : at + 16, :] = low
            total = total + low.astype(F32)
        own[row : row + 16, :] = total
    m1eg[...] += dot_rows(edge[...].reshape(block, edge_width), low_out[...])

    if last:
        @pl.when(step == blocks - 1)
        def _():
            count = early.shape[0]
            slab[:count] = early[...]
            slab[count:] = jnp.zeros_like(slab[count:])
            bias = [column_sum(own[...]), column_sum(b2s[...])]
            pack(
                slab,
                [
                    dot_rows(node[...], own[...].astype(BF16)),
                    m2g[...],
                    m1eg[...],
                    padded_rows(bias, width),
                ],
                count,
            )
            order_out(slab, base[0], codes, keep, send)


def message_backward(first_block, blocks, v, a1, s1, s2, edge, live_col, m2, more=()):
    slots, rows, edge_width = edge.shape
    width = v.shape[1]
    sb = slot_block(slots)
    block = sb * rows
    edges = blocks * block
    row_spec = pl.BlockSpec((block, width), lambda i: (i + first_block, 0))
    sums = [(rows, width), (width, width), (edge_width, width), (rows, width)]
    in_specs = [
        const_spec(v.shape),
        row_spec,
        row_spec,
        row_spec,
        pl.BlockSpec((sb, rows, edge_width), lambda i: (i + first_block, 0, 0)),
        const_spec(live_col.shape),
        const_spec(m2.shape),
    ]
    args = (v, a1, s1, s2, edge, live_col, m2)
    codes, scratch = None, []
    outs = [(s, F32) for s in sums]
    if more:
        codes, base, *rest = more
        args = (base, *args, *rest)
        in_specs = [pl.BlockSpec(memory_space=pltpu.SMEM)] + in_specs
        in_specs += [const_spec(a.shape) for a in rest]
        tiles = slab_part(width, edge_width, len(codes)) * len(codes)
        outs = [(sums[0], F32)] + half_shapes(tiles)
        scratch = [pltpu.VMEM(s, F32) for s in sums[1:]] + [slab_scratch(tiles)]
    scratch += [pltpu.VMEM((block, width), BF16), pltpu.VMEM((block, width), F32)]
    return pl.pallas_call(
        functools.partial(message_backward_kernel, sb, first_block, blocks, codes),
        grid=(blocks,),
        in_specs=in_specs,
        out_specs=[pl.BlockSpec((block, width), lambda i: (i, 0))]
        + [pl.BlockSpec(s, lambda i, n=len(s): (0,) * n) for s, _ in outs],
        out_shape=[jax.ShapeDtypeStruct((edges, width), BF16)]
        + [jax.ShapeDtypeStruct(*s) for s in outs],
        scratch_shapes=scratch,
        compiler_params=pltpu.CompilerParams(vmem_limit_bytes=VMEM),
        name="message_backward",
        cost_estimate=pl.CostEstimate(
            flops=2 * edges * width * (2 * width + 2 * edge_width),
            bytes_accessed=edges * width * 8 + edges * edge_width * 2,
            transcendentals=0,
        ),
    )(*args)


def far_sums_kernel(start, steps, rows, codes, *refs):
    last = codes is not None
    if last:
        base, idx_row, low_a, low_b, node, m1fg_in, out, keep, send, m1fg, slab = refs
    else:
        idx_row, low_a, low_b, node, out, m1fg = refs
    step = pl.program_id(0)
    cut = low_a.shape[0]
    chunk, width = node.shape
    height = rows // 16

    @pl.when(step == 0)
    def _():
        m1fg[...] = m1fg_in[...] if last else jnp.zeros_like(m1fg)

    first = start + step * chunk
    sums = dot(one_hot_rows(idx_row[:, :cut], first, chunk), low_a[...]) + dot(
        one_hot_rows(idx_row[:, cut:], first, chunk), low_b[...]
    )
    sums = sums.astype(BF16)
    m1fg[...] += dot_rows(node[...], sums)
    at = 0
    for place in range(chunk // rows):
        for lane in range(0, width, LANES):
            tile = sums[place * rows : (place + 1) * rows, lane : lane + LANES]
            out[at : at + height] = tile.reshape(height, 16, LANES)
            at += height

    if last:
        @pl.when(step == steps - 1)
        def _():
            if tile_count(m1fg.shape) < slab.shape[0]:
                slab[...] = jnp.zeros_like(slab)
            pack(slab, [m1fg[...]])
            order_out(slab, base[0], codes, keep, send)


def far_sums(start, idx_row, low_a, low_b, node, rows, more=()):
    half, width = node.shape
    chunk = min(512, half)
    steps = half // chunk
    tiles = chunk * width // (16 * LANES)
    args = [idx_row, low_a, low_b, node]
    in_specs = [const_spec(a.shape) for a in args[:3]] + [pl.BlockSpec((chunk, width), lambda i: (i, 0))]
    outs, codes, scratch = [((width, width), F32)], None, []
    if more:
        codes, base, m1fg = more
        args = [base] + args + [m1fg]
        in_specs = [pl.BlockSpec(memory_space=pltpu.SMEM)] + in_specs + [const_spec(m1fg.shape)]
        far = far_part_tiles(width, len(codes)) * len(codes)
        outs = half_shapes(far)
        scratch = [pltpu.VMEM((width, width), F32), slab_scratch(far)]
    edges = idx_row.shape[1]
    return pl.pallas_call(
        functools.partial(far_sums_kernel, start, steps, rows, codes),
        grid=(steps,),
        in_specs=in_specs,
        out_specs=[pl.BlockSpec((tiles, 16, LANES), lambda i: (i, 0, 0))]
        + [pl.BlockSpec(s, lambda i, n=len(s): (0,) * n) for s, _ in outs],
        out_shape=[jax.ShapeDtypeStruct((tiles * steps, 16, LANES), BF16)]
        + [jax.ShapeDtypeStruct(*s) for s in outs],
        scratch_shapes=scratch,
        compiler_params=pltpu.CompilerParams(vmem_limit_bytes=VMEM),
        name="far_sums",
        cost_estimate=pl.CostEstimate(
            flops=2 * width * half * (edges + width),
            bytes_accessed=edges * width * 2 + half * width * 4,
            transcendentals=0,
        ),
    )(*args)


def edge_gradient_kernel(sb, cut, low_three, low_edge, low_a, low_b, e_first, m1, out):
    step = pl.program_id(0)
    shape = out.shape
    edge_width, width = shape[2], low_a.shape[1]
    for low, use in ((low_a, step < cut), (low_b, step >= cut)):
        @pl.when(use)
        def _(low=low):
            total = (
                low_three[...].astype(F32)
                + dot(low_edge[...], e_first[:, width : width + edge_width])
                + dot_back(low[...], m1[width : width + edge_width, :])
            )
            out[...] = total.reshape(shape)


def edge_gradient(slots, low_three, low_edge, low_a, low_b, e_first, m1):
    edges, edge_width = low_three.shape
    rows = edges // slots
    width = low_a.shape[1]
    sb = slot_block(slots)
    block = sb * rows
    cut = low_a.shape[0] // block
    edge_spec = pl.BlockSpec((block, edge_width), lambda i: (i, 0))
    return pl.pallas_call(
        functools.partial(edge_gradient_kernel, sb, cut),
        grid=(slots // sb,),
        in_specs=[
            edge_spec,
            edge_spec,
            pl.BlockSpec((block, width), lambda i: (jnp.minimum(i, cut - 1), 0)),
            pl.BlockSpec((block, width), lambda i: (jnp.maximum(i - cut, 0), 0)),
            const_spec(e_first.shape),
            const_spec(m1.shape),
        ],
        out_specs=pl.BlockSpec((sb, rows, edge_width), lambda i: (i, 0, 0)),
        out_shape=jax.ShapeDtypeStruct((slots, rows, edge_width), F32),
        compiler_params=pltpu.CompilerParams(vmem_limit_bytes=VMEM),
        name="edge_gradient",
        cost_estimate=pl.CostEstimate(
            flops=2 * edges * edge_width * (width + edge_width),
            bytes_accessed=edges * (width * 2 + 2048),
            transcendentals=0,
        ),
    )(low_three, low_edge, low_a, low_b, e_first, m1)


def node_kernel(pieces, g_u1, own, m1, *refs):
    far, grad_out = refs[:pieces], refs[pieces]
    rows, width = own.shape
    height = rows // 16
    tiles = height * (width // LANES)
    sums = far[0][0, :tiles].astype(F32)
    for ref in far[1:]:
        sums = sums + ref[0, :tiles].astype(F32)
    far_sum = jnp.concatenate(
        [sums[j * height : (j + 1) * height].reshape(rows, LANES) for j in range(width // LANES)],
        axis=1,
    )
    far_first = m1.shape[0] - width
    grad_out[...] = (
        g_u1[...]
        + fine(dot_back, own[...], m1[:width, :])
        + fine(dot_back, far_sum, m1[far_first:, :])
    )


def node_last(g_u1, own, m1, far):
    return small_call(
        functools.partial(node_kernel, len(far)),
        (g_u1, own, m1, *far), [(own.shape, F32)], "node_gradient",
        flops=8 * own.size * own.shape[1], moved=2 * MIB,
    )[0]


def weights_out_kernel(
    codes, base, first, second,
    m1g, b1, m2g, b2, m3g, e1g, e2g, e3g, b3, g1, g2, fb2, eb1, eb2, eb3, g3, slab, far_slab,
):
    order_in((slab, far_slab), base[0], codes, first, second)
    width, edge_width = m3g.shape[0], e2g.shape[0]
    starts, at = [], 0
    for shape in early_shapes(width, edge_width) + late_shapes(width, edge_width):
        starts.append(at)
        at += tile_count(shape)
    m3g[...] = unpack(slab, starts[0], width, width)
    e1g[:, :width] = unpack(slab, starts[1], edge_width, width)
    middle = unpack(slab, starts[2], edge_width, edge_width)
    far = unpack(slab, starts[3], edge_width, width)
    over = edge_width % LANES
    base_col = width + edge_width - over
    e1g[:, width:base_col] = middle[:, : edge_width - over]
    far = pltpu.roll(jnp.concatenate([far, jnp.zeros((edge_width, LANES), F32)], axis=1), over, 1)
    lane = lax.broadcasted_iota(jnp.int32, (edge_width, LANES), 1)
    e1g[:, base_col : base_col + LANES] = jnp.where(
        lane < over, middle[:, edge_width - over : edge_width - over + LANES], far[:, :LANES]
    )
    rest = e1g.shape[1] - base_col - LANES
    e1g[:, base_col + LANES :] = far[:, LANES : LANES + rest]
    e2g[...] = unpack(slab, starts[4], edge_width, edge_width)[:, :edge_width]
    e3g[...] = unpack(slab, starts[5], edge_width, edge_width)[:, :edge_width]
    bias = unpack(slab, starts[6], 16, width)
    for row, out in enumerate((g1, g2, fb2, b3)):
        out[...] = bias[row : row + 1]
    bias = unpack(slab, starts[7], 16, edge_width)
    for row, out in enumerate((eb1, eb2, eb3, g3)):
        out[...] = bias[row : row + 1, :edge_width]
    m1g[:width, :] = unpack(slab, starts[8], width, width)
    m2g[...] = unpack(slab, starts[9], width, width)
    m1g[width : width + edge_width, :] = unpack(slab, starts[10], edge_width, width)
    m1g[width + edge_width :, :] = unpack(far_slab, 0, width, width)
    bias = unpack(slab, starts[11], 16, width)
    b1[...] = bias[0:1]
    b2[...] = bias[1:2]


def weights_out(codes, base, halves_in, width, edge_width):
    shapes = [(2 * width + edge_width, width), (1, width), (width, width), (1, width)]
    shapes += [(width, width), (edge_width, 2 * width + edge_width)]
    shapes += [(edge_width, edge_width)] * 2 + [(1, width)] * 4 + [(1, edge_width)] * 4
    chunks = len(codes)
    tiles = slab_part(width, edge_width, chunks) * chunks
    far_tiles = far_part_tiles(width, chunks) * chunks
    return small_call(
        functools.partial(weights_out_kernel, codes),
        (base, *halves_in), [(s, F32) for s in shapes], "weight_gradients",
        [slab_scratch(tiles), slab_scratch(far_tiles)], moved=10 * MIB, scalars=1,
    )


def exchange(value, mask, devices):
    return lax.ppermute(value, AXES, [(d, d ^ mask) for d in range(devices)])


def mask_groups(masks):
    return [masks[i : min(i + 2, len(masks) - 1)] for i in range(0, len(masks) - 1, 2)] + [masks[-1:]]


def order_codes(groups):
    masks = [mask for group in groups for mask in group]
    return [
        sum(mask for bit, mask in enumerate(masks) if place >> bit & 1)
        for place in range(1 << len(masks))
    ]


def combined(group, code):
    return sum(mask for bit, mask in enumerate(group) if code >> bit & 1)


def sent_around(value, group, devices):
    return [value] + [
        exchange(value, combined(group, code), devices) for code in range(1, 1 << len(group))
    ]


def shared_out(total, group, devices):
    parts = 1 << len(group)
    rows = total.shape[0] // parts
    return [total[:rows]] + [
        exchange(total[code * rows : (code + 1) * rows].astype(BF16), combined(group, code), devices)
        for code in range(1, parts)
    ]


def add_up(terms):
    total = terms[0].astype(F32)
    for term in terms[1:]:
        total = total + term.astype(F32)
    return total


def tied(*values):
    return lax.optimization_barrier(values)


def split_three(value):
    rows = []
    for _ in range(3):
        high = lax.reduce_precision(value, 8, 7)
        rows.append(high.astype(BF16))
        value = value - high
    return jnp.concatenate(rows + [jnp.zeros((13, value.shape[1]), BF16)], axis=0)


def per_device(
    node_in,
    edge_in,
    neighbours,
    live_counts,
    message_first,
    message_first_bias,
    message_second,
    message_second_bias,
    message_third,
    message_third_bias,
    norm_one,
    feed_first,
    feed_first_bias,
    feed_second,
    feed_second_bias,
    norm_two,
    edge_first,
    edge_first_bias,
    edge_second,
    edge_second_bias,
    edge_third,
    edge_third_bias,
    norm_three,
    node_cotangent,
    edge_cotangent,
):
    rows, slots = neighbours.shape
    width = node_in.shape[1]
    edge_width = edge_in.shape[2]
    edges = rows * slots
    hid_count = lax.axis_size("hid")
    res_count = lax.axis_size("res")
    devices = res_count * hid_count
    bits = devices.bit_length() - 1
    masks = [1 << b for b in range(bits - 1, -1, -1)]
    groups = mask_groups(masks)
    codes = order_codes(groups)
    me = lax.axis_index("res") * hid_count + lax.axis_index("hid")
    base = me.reshape(1)
    row = lambda vector: vector.reshape(1, -1)

    names = neighbours.T.reshape(edges)
    apart = (names // rows) ^ me
    place = jnp.zeros_like(names)
    for bit, mask in enumerate(masks):
        place = place | jnp.where((apart & mask) != 0, 1 << bit, 0)
    idx_row = (place * rows + names % rows).reshape(1, edges)
    live_col = jnp.broadcast_to(live_counts[:, None], (rows, LANES))
    edge = edge_in.transpose(1, 0, 2)
    cot = edge_cotangent.transpose(1, 0, 2)
    e_first = edge_first.T
    e_far = e_first[:, width + edge_width :]
    f1x = jnp.concatenate([feed_first, split_three(row(feed_first_bias))], axis=0)
    f2x = feed_second

    tiled = lambda value, per: value.reshape(-1, per, 16, LANES)
    stack = lambda pieces: jnp.concatenate(pieces, axis=0)
    *outer, near = groups

    held = stack(sent_around(node_in, outer[0], devices))
    held, idx_row, live_col, e_far = tied(held, idx_row, live_col, e_far)
    for group in outer[1:]:
        held = stack(sent_around(held, group, devices))
    held, f1x, f2x = tied(held, f1x, f2x)
    node_lo, node_hi = sent_around(held, near, devices)

    f1, f2 = [f1x], [f2x]
    hid_masks = [m for m in masks if m < hid_count]
    for mask in hid_masks[:-1]:
        f1, f2 = [pieces + [exchange(p, mask, devices) for p in pieces] for pieces in (f1, f2)]

    blocks = slots // slot_block(slots)
    a1, s1, s2, total = message_forward(
        node_lo, node_hi, node_in, edge, idx_row, live_col, message_first,
        row(message_first_bias), message_second, row(message_second_bias),
    )
    total, f1, f2 = tied(total, f1, f2)
    f1, f2 = [
        pieces + [exchange(p, hid_masks[-1], devices) for p in pieces] for pieces in (f1, f2)
    ]
    h1b, n1, sc1, n2, sc2, slope, h2b, far_part, own_part = residue_forward(
        node_in, total, message_third, row(message_third_bias), row(norm_one),
        row(feed_second_bias), row(norm_two), e_first, e_far, row(edge_first_bias), f1, f2,
    )

    held = stack(sent_around(far_part, outer[0], devices))
    h_held = stack(sent_around(h1b, outer[0], devices))
    for group in outer[1:]:
        held = stack(sent_around(held, group, devices))
    held, h_held = tied(held, h_held)
    q_lo, q_hi = sent_around(held, near, devices)
    for group in outer[1:]:
        h_held = stack(sent_around(h_held, group, devices))

    edge_out, act_one, act_two, low_three, low_two, low_one, hi, lo, own_sum, edge_gain = edge_branch(
        q_lo, q_hi, own_part, edge, cot, idx_row, live_col, e_first,
        edge_second, row(edge_second_bias), edge_third, row(edge_third_bias), row(norm_three),
    )
    lo, h_held = tied(lo, h_held)
    h_all = sent_around(h_held, near, devices)

    work = [
        lambda: edge_weights((act_two, act_one), (low_three, low_two), rows),
        lambda: edge_weights((low_one,), (edge,), rows),
    ]
    made = []
    terms = [lo, exchange(hi, near[0], devices)]
    for group in reversed(outer):
        terms = shared_out(add_up(terms), group, devices)
        if work:
            terms, got = tied(terms, work.pop(0)())
            made.append(got)
    while work:
        made.append(work.pop(0)())
    (e3g, e2g, eb3, eb2), (e1g, eb1) = made
    g_u1, v, gy2, early = residue_backward(
        (
            node_cotangent, own_sum, e_first, e_far, h2b, n1, sc1, n2, sc2, slope, row(norm_one),
            row(norm_two), message_third, total, e1g, e2g, e3g, eb1, eb2, eb3, edge_gain,
        ),
        terms, f1, f2,
    )

    g_held = stack(sent_around(gy2, outer[0], devices))
    low_a, *sums = message_backward(
        0, blocks // 2, v, a1, s1, s2, edge, live_col, message_second
    )
    v, g_held = tied(v, g_held)
    for group in outer[1:]:
        g_held = stack(sent_around(g_held, group, devices))
    low_b, own, keep, send = message_backward(
        blocks // 2, blocks - blocks // 2, v, a1, s1, s2, edge, live_col, message_second,
        (codes, base, node_in, early, *sums),
    )

    terms = [keep, exchange(send, near[0], devices)]
    hi, m1fg = far_sums(node_lo.shape[0], idx_row, low_a, low_b, node_hi, rows)
    total, m1fg = tied(add_up(terms), m1fg)
    first, *others = reversed(outer)
    terms = shared_out(total, first, devices)
    got = exchange(hi, near[0], devices)
    lo, keep, send = far_sums(0, idx_row, low_a, low_b, node_lo, rows, (codes, base, m1fg))
    for group in others:
        terms = shared_out(add_up(terms), group, devices)
    slab_chunk = add_up(terms).astype(BF16)

    g_all = sent_around(g_held, near, devices)
    sums_part, far_part = rows * width // (16 * LANES), far_part_tiles(width, devices)
    total = jnp.concatenate(
        [
            tiled(add_up([lo, got]), sums_part),
            tiled(add_up([keep, exchange(send, near[0], devices)]), far_part),
        ],
        axis=1,
    )
    terms = [total]
    work = [
        lambda low: edge_gradient(slots, low_three, low_one, low, low_b, e_first, message_first),
        lambda low: feed_gradients((h_all[0], low), g_all, feed_first, row(feed_first_bias), feed_second),
    ]
    after = [low_a, h_all[1]]
    made = []
    for group in reversed(outer):
        total = add_up(terms)
        if work:
            total, low = tied(total, after.pop(0))
        terms = shared_out(total, group, devices)
        if work:
            terms, out = tied(terms, work.pop(0)(low))
            made.append(out)
    edge_grad, (f1g, f2g, fb1g) = made
    node_gradient = node_last(g_u1, own, message_first, terms)
    far_chunk = add_up([t[:, sums_part:] for t in terms]).astype(BF16)

    held = jnp.concatenate(
        [
            stack(sent_around(tiled(slab_chunk, slab_chunk.shape[0]), outer[0], devices)),
            stack(sent_around(far_chunk, outer[0], devices)),
        ],
        axis=1,
    )
    for group in outer[1:]:
        held = stack(sent_around(held, group, devices))
    weights = [w.reshape(-1, 16, LANES) for w in sent_around(held, near, devices)]
    m1g, b1, m2g, b2, m3g, e1g, e2g, e3g, b3, g1, g2, fb2, eb1, eb2, eb3, g3 = weights_out(
        codes, base, weights, width, edge_width
    )
    flat = lambda vector: vector.reshape(-1)
    return (
        h2b,
        edge_out.transpose(1, 0, 2),
        node_gradient,
        edge_grad.transpose(1, 0, 2),
        m1g,
        flat(b1),
        m2g,
        flat(b2),
        m3g,
        flat(b3),
        flat(g1),
        f1g,
        flat(fb1g),
        f2g,
        flat(fb2),
        flat(g2),
        e1g.T,
        flat(eb1),
        e2g,
        flat(eb2),
        e3g,
        flat(eb3),
        flat(g3),
    )


def solution(mesh):
    nodes, edges, shared = P(AXES, None), P(AXES, None, None), P()
    return jax.shard_map(
        per_device,
        mesh=mesh,
        in_specs=(nodes, edges, nodes, P(AXES))
        + (shared,) * 7
        + (P(None, "hid"), P("hid"), P("hid", None))
        + (shared,) * 9
        + (nodes, edges),
        out_specs=(nodes, edges, nodes, edges)
        + (shared,) * 7
        + (P(None, "hid"), P("hid"), P("hid", None))
        + (shared,) * 9,
        check_vma=False,
    )
```

```python
import functools

import jax
import jax.numpy as jnp
from jax import lax
from jax.experimental import pallas as pl
from jax.experimental.pallas import tpu as pltpu
from jax.sharding import PartitionSpec as P

EPS = 1e-05
AXES = ("res", "hid")
F32 = jnp.float32
BF16 = jnp.bfloat16
TANH_SCALE = 0.7978845608028654
TANH_CUBE = 0.044715
LANES = 128
CHUNK = 2048
MIB = 1024 * 1024
VMEM = 58 * MIB


def dot(left, right):
    return lax.dot_general(left, right, (((1,), (0,)), ((), ())), preferred_element_type=F32)


def dot_rows(left, right):
    return lax.dot_general(left, right, (((0,), (0,)), ((), ())), preferred_element_type=F32)


def dot_back(left, right):
    return lax.dot_general(left, right, (((1,), (1,)), ((), ())), preferred_element_type=F32)


def halves(value):
    high = value.astype(BF16)
    return high, (value - high.astype(F32)).astype(BF16)


def fine(product, value, weights):
    high, low = halves(value)
    return product(high, weights) + product(low, weights)


def gelu_parts(x):
    square = x * x
    t = jnp.tanh(x * (TANH_SCALE + (TANH_SCALE * TANH_CUBE) * square))
    gate = 0.5 + 0.5 * t
    act = x * gate
    slope = gate + act * (1.0 - gate) * (2 * TANH_SCALE + (6 * TANH_SCALE * TANH_CUBE) * square)
    return act, slope


def index_columns(idx_row):
    parts = [
        jnp.broadcast_to(idx_row[:, first : first + LANES], (LANES, LANES)).T
        for first in range(0, idx_row.shape[1], LANES)
    ]
    return jnp.concatenate(parts, axis=0)


def one_hot_columns(idx, start, count):
    one, zero = jnp.ones((), BF16), jnp.zeros((), BF16)
    idx = idx.astype(jnp.int16)
    lane = lax.broadcasted_iota(jnp.int32, idx.shape, 1).astype(jnp.int16)
    parts = [
        jnp.where(idx == lane + jnp.int16(start + first), one, zero)
        for first in range(0, count, LANES)
    ]
    return jnp.concatenate(parts, axis=1)


def pick_rows(idx, table_refs):
    total, start = None, 0
    for ref in table_refs:
        rows = ref.shape[0]
        step = min(rows, CHUNK)
        for first in range(0, rows, step):
            part = dot(one_hot_columns(idx, start + first, step), ref[first : first + step, :])
            total = part if total is None else total + part
        start += rows
    return total


def row_mover(places, first, rows_ref, sorted_ref):
    def move(start, count):
        for e in range(start, start + count):
            at = pl.multiple_of(places[0, first + e] * 8, 8)
            sorted_ref[pl.ds(at, 8), :] = rows_ref[e * 8 : e * 8 + 8, :]
    return move


def group_rows(sorted_ref, first, count, width):
    def column(at):
        return sorted_ref[pl.ds(first * 8 + at, count, stride=8), :]
    tiles = pl.cdiv(width, LANES)
    parts = [column(at)[:, : min(LANES, width - at * LANES)] for at in range(tiles)]
    return jnp.concatenate(parts, axis=1).astype(BF16), column(tiles)


def group_sums(sorted_ref, group, count, width, residues):
    rows, local = group_rows(sorted_ref, group * count, count, width)
    lane = lax.broadcasted_iota(jnp.int32, local.shape, 1).astype(F32)
    picks = [
        jnp.where(local == lane + float(first), 1.0, 0.0).astype(BF16)
        for first in range(0, residues, LANES)
    ]
    return dot_rows(jnp.concatenate(picks, axis=1), rows)


def place_kernel(groups, count, names, out):
    rows = names.shape[0]
    row = lax.broadcasted_iota(jnp.int32, (LANES, LANES), 0)
    column = lax.broadcasted_iota(jnp.int32, (LANES, LANES), 1)
    upto = jnp.where(row <= column, 1.0, 0.0).astype(BF16)
    ones = jnp.ones((LANES, LANES), BF16)
    row = lax.broadcasted_iota(jnp.int32, (rows, rows), 0)
    column = lax.broadcasted_iota(jnp.int32, (rows, rows), 1)
    before = jnp.where(column < row, 1.0, 0.0).astype(BF16)
    place = jnp.zeros(names.shape, F32)
    for group in range(groups):
        here = jnp.where(names[...] == group, 1.0, 0.0)
        low = here.astype(BF16)
        rank = dot(low, upto) + dot(before, dot(low, ones).astype(BF16))
        place = place + here * (rank + float(group * count - 1))
    out[...] = place.astype(jnp.int32)


def group_places(names, groups):
    edges = names.shape[0]
    rows = pl.cdiv(pl.cdiv(edges, LANES), 8) * 8
    padded = jnp.pad(names, (0, rows * LANES - edges), constant_values=groups)
    out = small_call(
        functools.partial(place_kernel, groups, edges // groups),
        (padded.reshape(rows, LANES),), [((rows, LANES), jnp.int32)], "group_places",
    )[0]
    return out.reshape(1, -1)


def spread(column, width):
    return jnp.concatenate([column] * (width // LANES), axis=1)


def norm(value):
    centre = value - jnp.mean(value, -1, keepdims=True)
    scale = lax.rsqrt(jnp.mean(centre * centre, -1, keepdims=True) + EPS)
    return centre * scale, scale


def norm_back(inner, normed, scale):
    mean_first = jnp.mean(inner, -1, keepdims=True)
    mean_second = jnp.mean(inner * normed, -1, keepdims=True)
    return scale * (inner - mean_first - normed * mean_second)


def column_sum(value):
    return jnp.sum(value, axis=0, keepdims=True)


def whole(*_):
    return (0, 0)


def const_spec(shape):
    return pl.BlockSpec(shape, lambda *_: (0,) * len(shape), pipeline_mode=pl.Buffered(1))


def small_call(kernel, args, shapes, name, scratch=(), flops=0, moved=0, exps=0, scalars=0):
    return pl.pallas_call(
        kernel,
        grid=(1,),
        in_specs=[pl.BlockSpec(memory_space=pltpu.SMEM)] * scalars
        + [const_spec(a.shape) for a in args[scalars:]],
        out_specs=[pl.BlockSpec(s, lambda *_, n=len(s): (0,) * n) for s, _ in shapes],
        out_shape=[jax.ShapeDtypeStruct(*s) for s in shapes],
        scratch_shapes=list(scratch),
        compiler_params=pltpu.CompilerParams(vmem_limit_bytes=VMEM),
        name=name,
        cost_estimate=pl.CostEstimate(flops=flops, bytes_accessed=moved, transcendentals=exps),
    )(*args)


def tile_count(shape):
    return pl.cdiv(shape[0], 16) * pl.cdiv(shape[1], LANES)


def all_tiles(shapes):
    return sum(tile_count(s) for s in shapes)


def pack(slab, values, at=0):
    for value in values:
        rows, columns = value.shape
        count = rows // 16
        for first in range(0, columns, LANES):
            take = min(LANES, columns - first)
            tile = value[:, first : first + take].astype(BF16).reshape(count, 16, take)
            slab[at : at + count, :, :take] = tile
            at += count


def unpack(slab, at, rows, columns):
    count = rows // 16
    parts = [
        slab[at + i * count : at + (i + 1) * count].reshape(rows, LANES).astype(F32)
        for i in range(pl.cdiv(columns, LANES))
    ]
    return jnp.concatenate(parts, axis=1)


def order_out(slab, base, codes, keep, send):
    size = slab.shape[0] // len(codes)
    half = len(codes) // 2
    for place, code in enumerate(codes):
        out = keep if place < half else send
        at = (place % half) * size
        out[at : at + size] = slab[pl.ds((base ^ code) * size, size)]


def half_shapes(tiles):
    return [((tiles // 2, 16, LANES), BF16)] * 2


def slab_scratch(tiles):
    return pltpu.VMEM((tiles, 16, LANES), BF16)


def slab_tiles(width, edge_width, chunks):
    shapes = early_shapes(width, edge_width) + late_shapes(width, edge_width) + [(width, width)]
    return pl.cdiv(all_tiles(shapes), chunks)


def order_in(slab, base, codes, first, second):
    size = slab.shape[0] // len(codes)
    half = len(codes) // 2
    for place, code in enumerate(codes):
        source = first if place < half else second
        at = (place % half) * size
        slab[pl.ds((base ^ code) * size, size)] = source[at : at + size]


def padded_rows(parts, width):
    return jnp.concatenate(parts + [jnp.zeros((16 - len(parts), width), F32)], axis=0)


def slot_block(slots):
    for size in (10, 12, 8, 6, 5, 4, 3, 2):
        if slots % size == 0:
            return size
    return 1


def far_table(node_lo, node_hi, weights, put):
    tile = min(512, node_lo.shape[0])
    for source, start in ((node_lo, 0), (node_hi, node_lo.shape[0])):
        def body(i, carry, source=source, start=start):
            at = pl.multiple_of(i * tile, tile)
            put(start + at, dot(source[pl.ds(at, tile), :], weights))
            return carry
        lax.fori_loop(0, source.shape[0] // tile, body, 0)


def message_forward_kernel(
    sb, by_rows, node_lo, node_hi, node_own, edge, idx_row, names, live_col, m1, b1, m2, b2,
    a1_out, s1_out, s2_out, sum_out, table, far, near, lhs, z,
):
    step = pl.program_id(0)
    width = node_own.shape[1]
    edge_width = edge.shape[2]
    rows = edge.shape[1]
    block = sb * rows
    lanes = width // LANES

    @pl.when(step == 0)
    def _():
        weights = m1[width + edge_width :, :]
        if by_rows:
            def put(first, value):
                for at in range(8):
                    column = at % lanes * LANES
                    table[pl.ds(first * 8 + at, value.shape[0], stride=8), :] = value[
                        :, column : column + LANES
                    ]
        else:
            def put(first, value):
                table[pl.ds(first, value.shape[0]), :] = value.astype(BF16)
        far_table(node_lo, node_hi, weights, put)
        near[:edge_width, :] = m1[width : width + edge_width, :]
        near[edge_width:, :] = jnp.zeros_like(near[edge_width:, :])
        near[edge_width : edge_width + rows, :] = (
            dot(node_own[...], m1[:width, :]) + b1[...]
        ).astype(BF16)
        shape = (rows, near.shape[0] - edge_width)
        eye = lax.broadcasted_iota(jnp.int32, shape, 0) == lax.broadcasted_iota(jnp.int32, shape, 1)
        for at in range(0, block, rows):
            lhs[at : at + rows, edge_width:] = jnp.where(eye, 1.0, 0.0).astype(BF16)
        sum_out[...] = jnp.zeros_like(sum_out)

    lhs[:, :edge_width] = edge[...].reshape(block, edge_width)
    z[...] = dot(lhs[...], near[...])
    if not by_rows:
        z[...] += pick_rows(index_columns(idx_row[...]), (table,))
    upper = lax.broadcasted_iota(jnp.int32, (8, LANES), 0) < lanes

    def fetch(at):
        for e in range(at, at + 16, 2):
            pair = [
                table[pl.ds(pl.multiple_of(names[0, step * block + e + i] * 8, 8), 8), :]
                for i in range(2)
            ]
            far[e * lanes : e * lanes + 8, :] = jnp.where(upper, *pair)

    def fetched(at):
        return jnp.concatenate(
            [far[pl.ds(at * lanes + j, 16, stride=lanes), :] for j in range(lanes)], axis=1
        )

    if by_rows:
        fetch(0)
    for at in range(0, block, 16):
        value = z[at : at + 16, :]
        if by_rows:
            if at + 16 < block:
                fetch(at + 16)
            value = value + fetched(at)
        act, slope = gelu_parts(value)
        a1_out[at : at + 16, :] = act.astype(BF16)
        s1_out[at : at + 16, :] = slope.astype(BF16)
    z[...] = dot(a1_out[...], m2[...])
    bias = b2[...]
    for row in range(0, rows, 16):
        count = live_col[row : row + 16, :]
        inverse = 1.0 / count.astype(F32)
        total = sum_out[row : row + 16, :]
        for s in range(sb):
            at = s * rows + row
            act, slope = gelu_parts(z[at : at + 16, :] + bias)
            s2_out[at : at + 16, :] = slope.astype(BF16)
            share = jnp.where(count > step * sb + s, inverse, 0.0)
            total = total + act.astype(BF16).astype(F32) * spread(share, width)
        sum_out[row : row + 16, :] = total


def message_forward(node_lo, node_hi, node_own, edge, idx_row, live_col, m1, b1, m2, b2):
    slots, rows, edge_width = edge.shape
    width = node_own.shape[1]
    residues = 2 * node_lo.shape[0]
    by_rows = residues <= 4096 and width == 4 * LANES
    sb = slot_block(slots) if by_rows else 4
    block = sb * rows
    edges = slots * rows
    near = pl.cdiv(edge_width + rows, LANES) * LANES
    row_spec = pl.BlockSpec((block, width), lambda i: (i, 0))
    return pl.pallas_call(
        functools.partial(message_forward_kernel, sb, by_rows),
        grid=(slots // sb,),
        in_specs=[
            const_spec(node_lo.shape),
            const_spec(node_hi.shape),
            const_spec(node_own.shape),
            pl.BlockSpec((sb, rows, edge_width), lambda i: (i, 0, 0)),
            pl.BlockSpec((1, block), lambda i: (0, i)),
            pl.BlockSpec(memory_space=pltpu.SMEM),
            const_spec(live_col.shape),
            const_spec(m1.shape),
            const_spec(b1.shape),
            const_spec(m2.shape),
            const_spec(b2.shape),
        ],
        out_specs=[row_spec, row_spec, row_spec, pl.BlockSpec((rows, width), whole)],
        out_shape=[jax.ShapeDtypeStruct((edges, width), BF16)] * 3
        + [jax.ShapeDtypeStruct((rows, width), F32)],
        scratch_shapes=[
            pltpu.VMEM((residues * 8, LANES), F32) if by_rows else pltpu.VMEM((residues, width), BF16),
            pltpu.VMEM((block * 4 if by_rows else 8, LANES), F32),
            pltpu.VMEM((near, width), BF16),
            pltpu.VMEM((block, near), BF16),
            pltpu.VMEM((block, width), F32),
        ],
        compiler_params=pltpu.CompilerParams(vmem_limit_bytes=VMEM),
        name="message_forward",
        cost_estimate=pl.CostEstimate(
            flops=2 * edges * width * (residues + edge_width + width),
            bytes_accessed=edges * width * 6 + edges * edge_width * 2 + edges * LANES * 4,
            transcendentals=2 * edges * width,
        ),
    )(node_lo, node_hi, node_own, edge, idx_row, idx_row, live_col, m1, b1, m2, b2)


def residue_forward_kernel(parts, node, total, m3, b3, g1, fb2, g2, e_first, e_far, eb, *refs):
    f1, f2 = refs[:parts], refs[parts : 2 * parts]
    h1b_out, n1_out, sc1_out, n2_out, sc2_out, slope_out, h2b_out, far_out, own_out = refs[2 * parts :]
    width, hidden = node.shape[1], f1[0].shape[1]
    u1 = node[...].astype(F32) + fine(dot, total[...], m3[...]) + b3[...]
    n1, sc1 = norm(u1)
    h1 = n1 * g1[...]
    h1b = h1.astype(BF16)
    h1b_out[...] = h1b
    n1_out[...] = n1
    sc1_out[...] = jnp.broadcast_to(sc1, sc1_out.shape)
    y2 = None
    for p in range(parts):
        bias = f1[p][width : width + 16, :].astype(F32)
        bias = bias[0:1] + bias[1:2] + bias[2:3]
        act, slope = gelu_parts(dot(h1b, f1[p][:width, :]) + bias)
        slope_out[:, p * hidden : (p + 1) * hidden] = slope
        part = dot(act.astype(BF16), f2[p][...])
        y2 = part if y2 is None else y2 + part
    n2, sc2 = norm(h1 + (y2 + fb2[...]))
    h2b = (n2 * g2[...]).astype(BF16)
    n2_out[...] = n2
    sc2_out[...] = jnp.broadcast_to(sc2, sc2_out.shape)
    h2b_out[...] = h2b
    far_out[...] = dot_back(h2b, e_far[...]).astype(BF16)
    own_out[...] = dot_back(h2b, e_first[:, :width]) + eb[...]


def residue_forward(node, total, m3, b3, g1, fb2, g2, e_first, e_far, eb, f1, f2):
    rows, width = node.shape
    edge_width = e_first.shape[0]
    hidden = len(f1) * f1[0].shape[1]
    shapes = [
        ((rows, width), BF16),
        ((rows, width), F32),
        ((rows, LANES), F32),
        ((rows, width), F32),
        ((rows, LANES), F32),
        ((rows, hidden), F32),
        ((rows, width), BF16),
        ((rows, edge_width), BF16),
        ((rows, edge_width), F32),
    ]
    return small_call(
        functools.partial(residue_forward_kernel, len(f1)),
        (node, total, m3, b3, g1, fb2, g2, e_first, e_far, eb, *f1, *f2),
        shapes, "residue_forward", flops=4 * rows * width * hidden, moved=5 * MIB,
        exps=rows * hidden,
    )


def edge_kernel(
    sb, blocks, groups, by_rows, far_lo, far_hi, own, edge, cot, idx_row, local_row, names, places, live_col,
    e_first, e2, eb2, e3, eb3, g3,
    edge_out, act_one_out, act_two_out, low_three_out, low_two_out, low_one_out, hi_out, lo_out, own_out, gain_out,
    table, far, z, slope_one, slope_two, rows_ref, sorted_ref, gs,
):
    step = pl.program_id(0)
    rows, width = own.shape
    node_width = (e_first.shape[1] - width) // 2
    e_mid = e_first.at[:, node_width : node_width + width]
    tiles = pl.cdiv(width, LANES)
    per = 8 // tiles
    size = 32

    @pl.when(step == 0)
    def _():
        own_out[...] = jnp.zeros_like(own_out)
        gs[...] = jnp.zeros_like(gs)
        half = far_lo.shape[0]
        if by_rows:
            for source, start in ((far_lo, 0), (far_hi, half)):
                for first in range(0, half, 512):
                    value = source[first : first + 512, :].astype(F32)
                    for at in range(8):
                        column = at % tiles * LANES
                        take = min(LANES, width - column)
                        table[pl.ds((start + first) * 8 + at, value.shape[0], stride=8), :take] = value[
                            :, column : column + take
                        ]
        else:
            table[:half, :] = far_lo[...]
            table[half:, :] = far_hi[...]

    @pl.when(step < blocks)
    def _():
        block = sb * rows
        first = step * block
        flat = edge[...].reshape(block, width)
        z[...] = dot_back(flat, e_mid[...])
        if not by_rows:
            z[...] += pick_rows(index_columns(idx_row[...]), (table,))
        sub = lax.broadcasted_iota(jnp.int32, (8, LANES), 0)

        def fetch(at):
            for e in range(at, at + size, per):
                got = [
                    table[pl.ds(pl.multiple_of(names[0, first + e + i] * 8, 8), 8), :]
                    for i in range(per)
                ]
                value = got[-1]
                for i in range(per - 2, -1, -1):
                    value = jnp.where(sub < (i + 1) * tiles, got[i], value)
                far[e * tiles : e * tiles + 8, :] = value

        def fetched(at):
            parts = [
                far[pl.ds(at * tiles + j, size, stride=tiles), :][:, : min(LANES, width - j * LANES)]
                for j in range(tiles)
            ]
            return jnp.concatenate(parts, axis=1)

        if by_rows:
            fetch(0)
        for at in range(0, block, size):
            value = z[at : at + size, :] + own[at % rows : at % rows + size, :]
            if by_rows:
                if at + size < block:
                    fetch(at + size)
                value = value + fetched(at)
            act, slope = gelu_parts(value)
            act_one_out[at : at + size, :] = act.astype(BF16)
            slope_one[at : at + size, :] = slope
        z[...] = dot(act_one_out[...], e2[...])
        for at in range(0, block, size):
            act, slope = gelu_parts(z[at : at + size, :] + eb2[...])
            act_two_out[at : at + size, :] = act.astype(BF16)
            slope_two[at : at + size, :] = slope
        z[...] = dot(act_two_out[...], e3[...])
        for row in range(0, rows, size):
            count = spread(live_col[row : row + size, :], tiles * LANES)[:, :width]
            gains = gs[row : row + size, :]
            for s in range(sb):
                at = s * rows + row
                value = edge[s, row : row + size, :].astype(F32) + (z[at : at + size, :] + eb3[...])
                normed, scale = norm(value)
                live = jnp.where(count > step * sb + s, 1.0, 0.0)
                edge_out[s, row : row + size, :] = (normed * g3[...] * live).astype(BF16)
                grad = cot[s, row : row + size, :].astype(F32) * live
                gains = gains + grad * normed
                low_three_out[at : at + size, :] = norm_back(grad * g3[...], normed, scale).astype(BF16)
            gs[row : row + size, :] = gains
        z[...] = dot_back(low_three_out[...], e3[...])
        for at in range(0, block, size):
            low_two_out[at : at + size, :] = (
                z[at : at + size, :] * slope_two[at : at + size, :]
            ).astype(BF16)
        z[...] = dot_back(low_two_out[...], e2[...])
        rows_ref[pl.ds(tiles, block, stride=8), :] = index_columns(local_row[...]).astype(F32)
        move = row_mover(places, first, rows_ref, sorted_ref)
        waiting = None
        for row in range(0, rows, size):
            total = own_out[row : row + size, :]
            for s in range(sb):
                at = s * rows + row
                low = (z[at : at + size, :] * slope_one[at : at + size, :]).astype(BF16)
                low_one_out[at : at + size, :] = low
                low = low.astype(F32)
                total = total + low
                for j in range(tiles):
                    take = min(LANES, width - j * LANES)
                    rows_ref[pl.ds(at * 8 + j, size, stride=8), :take] = low[
                        :, j * LANES : j * LANES + take
                    ]
                if waiting is not None:
                    move(waiting, size)
                waiting = at
            own_out[row : row + size, :] = total
        move(waiting, size)

    @pl.when(step >= blocks)
    def _():
        deep = lo_out.shape[0]
        sums = group_sums(
            sorted_ref, step - blocks, sb * rows * blocks // groups, width, 2 * deep * rows
        )
        for at in range(deep):
            lo_out[at, 0] = sums[at * rows : (at + 1) * rows]
            hi_out[at, 0] = sums[(deep + at) * rows : (deep + at + 1) * rows].astype(BF16)

    @pl.when(step == blocks + groups - 1)
    def _():
        gain_out[...] = column_sum(gs[...])


def edge_branch(groups, far_lo, far_hi, own, edge, cot, idx_row, local_row, places, live_col, e_first, e2, eb2, e3, eb3, g3):
    slots, rows, width = edge.shape
    sb = slot_block(slots)
    edges = slots * rows
    block = sb * rows
    blocks = slots // sb
    half = far_lo.shape[0]
    by_rows = half <= 2048 and 8 % pl.cdiv(width, LANES) == 0
    deep = half // rows // groups
    blk = lambda i: jnp.minimum(i, blocks - 1)
    slot_spec = pl.BlockSpec((sb, rows, width), lambda i: (blk(i), 0, 0))
    row_spec = pl.BlockSpec((block, width), lambda i: (blk(i), 0))
    name_spec = pl.BlockSpec((1, block), lambda i: (0, blk(i)))
    sum_spec = pl.BlockSpec((deep, 1, rows, width), lambda i: (0, jnp.maximum(i - blocks, 0), 0, 0))
    smem = pl.BlockSpec(memory_space=pltpu.SMEM)
    return pl.pallas_call(
        functools.partial(edge_kernel, sb, blocks, groups, by_rows),
        grid=(blocks + groups,),
        in_specs=[
            const_spec(far_lo.shape),
            const_spec(far_hi.shape),
            const_spec(own.shape),
            slot_spec,
            slot_spec,
            name_spec,
            name_spec,
            smem,
            smem,
            const_spec(live_col.shape),
            const_spec(e_first.shape),
            const_spec(e2.shape),
            const_spec(eb2.shape),
            const_spec(e3.shape),
            const_spec(eb3.shape),
            const_spec(g3.shape),
        ],
        out_specs=[slot_spec]
        + [row_spec] * 5
        + [
            sum_spec,
            sum_spec,
            pl.BlockSpec((rows, width), whole),
            pl.BlockSpec((1, width), whole),
        ],
        out_shape=[jax.ShapeDtypeStruct((slots, rows, width), BF16)]
        + [jax.ShapeDtypeStruct((edges, width), BF16)] * 5
        + [
            jax.ShapeDtypeStruct((deep, groups, rows, width), BF16),
            jax.ShapeDtypeStruct((deep, groups, rows, width), F32),
            jax.ShapeDtypeStruct((rows, width), F32),
            jax.ShapeDtypeStruct((1, width), F32),
        ],
        scratch_shapes=[
            pltpu.VMEM((half * 16, LANES), F32) if by_rows else pltpu.VMEM((2 * half, width), BF16),
            pltpu.VMEM((block * 8 if by_rows else 8, LANES), F32),
            pltpu.VMEM((block, width), F32),
            pltpu.VMEM((block, width), F32),
            pltpu.VMEM((block, width), F32),
            pltpu.VMEM((block * 8, LANES), F32),
            pltpu.VMEM((edges * 8, LANES), F32),
            pltpu.VMEM((rows, width), F32),
        ],
        compiler_params=pltpu.CompilerParams(vmem_limit_bytes=VMEM),
        name="edge_branch",
        cost_estimate=pl.CostEstimate(
            flops=2 * edges * width * (half + 5 * width),
            bytes_accessed=edges * width * 16,
            transcendentals=2 * edges * width,
        ),
    )(far_lo, far_hi, own, edge, cot, idx_row, local_row, idx_row, places, live_col, e_first, e2, eb2, e3, eb3, g3)


def edge_weights_kernel(blocks, pairs, *refs):
    step = pl.program_id(0)
    lefts, rights = refs[:pairs], refs[pairs : 2 * pairs]
    grads, biases, sums = refs[2 * pairs : 3 * pairs], refs[3 * pairs : 4 * pairs], refs[-1]
    rows = sums.shape[1]

    @pl.when(step == 0)
    def _():
        for ref in (*grads, sums):
            ref[...] = jnp.zeros_like(ref)

    for at in range(pairs):
        left, right = [r[...].reshape(-1, r.shape[-1]) for r in (lefts[at], rights[at])]
        grads[at][...] += dot_rows(left, right)
        low = left if lefts[at].ndim < rights[at].ndim else right
        sums[at] += jnp.sum(low.astype(F32).reshape(-1, rows, low.shape[1]), axis=0)

    @pl.when(step == blocks - 1)
    def _():
        for at in range(pairs):
            biases[at][...] = column_sum(sums[at])


def edge_weights(lefts, rights, rows):
    pairs = len(lefts)
    edges, width = lefts[0].shape
    slots = edges // rows
    sb = slot_block(slots)

    def spec(array):
        if array.ndim == 3:
            return pl.BlockSpec((sb, rows, width), lambda i: (i, 0, 0))
        return pl.BlockSpec((sb * rows, width), lambda i: (i, 0))

    shapes = [(width, width)] * pairs + [(1, width)] * pairs
    return pl.pallas_call(
        functools.partial(edge_weights_kernel, slots // sb, pairs),
        grid=(slots // sb,),
        in_specs=[spec(array) for array in (*lefts, *rights)],
        out_specs=[pl.BlockSpec(s, whole) for s in shapes],
        out_shape=[jax.ShapeDtypeStruct(s, F32) for s in shapes],
        scratch_shapes=[pltpu.VMEM((pairs, rows, width), F32)],
        compiler_params=pltpu.CompilerParams(vmem_limit_bytes=VMEM),
        name="edge_weights",
        cost_estimate=pl.CostEstimate(
            flops=2 * pairs * edges * width * width,
            bytes_accessed=pairs * edges * width * 4,
            transcendentals=0,
        ),
    )(*lefts, *rights)


def early_shapes(width, edge_width):
    return [
        (width, width),
        (edge_width, width),
        (edge_width, edge_width),
        (edge_width, width),
        (edge_width, edge_width),
        (edge_width, edge_width),
        (16, width),
        (16, edge_width),
    ]


def residue_backward_kernel(
    parts, pieces, node_cot, own_sum, e_first, e_far, h2b, n1, sc1, n2, sc2, slope, g1, g2, m3,
    total, e1g, e2g, e3g, eb1, eb2, eb3, edge_gain, *refs,
):
    far = refs[:pieces]
    f1 = refs[pieces : pieces + parts]
    f2 = refs[pieces + parts : pieces + 2 * parts]
    gu1_out, v_out, gy2_out, slab = refs[pieces + 2 * parts :]
    width, hidden = h2b.shape[1], f1[0].shape[1]
    far_sum = far[0][...]
    for ref in far[1:]:
        far_sum = far_sum + ref[...].astype(F32)
    own = own_sum[...]
    g_h2 = (
        node_cot[...].astype(F32)
        + fine(dot, own, e_first[:, :width])
        + fine(dot, far_sum, e_far[...])
    )
    gain_two = column_sum(g_h2 * n2[...])
    g_u2 = norm_back(g_h2 * g2[...], n2[...], sc2[:, :1])
    gy2 = g_u2.astype(BF16)
    gy2_out[...] = gy2
    g_h1 = g_u2
    for p in range(parts):
        gy1 = dot_back(gy2, f2[p][...]) * slope[:, p * hidden : (p + 1) * hidden]
        g_h1 = g_h1 + dot_back(gy1.astype(BF16), f1[p][:width, :])
    gain_one = column_sum(g_h1 * n1[...])
    g_u1 = norm_back(g_h1 * g1[...], n1[...], sc1[:, :1])
    gu1_out[...] = g_u1
    v_out[...] = fine(dot_back, g_u1, m3[...])
    bias = [gain_one, gain_two, column_sum(gy2.astype(F32)), column_sum(g_u1)]
    slab[...] = jnp.zeros_like(slab)
    pack(
        slab,
        [
            dot_rows(total[...].astype(BF16), g_u1.astype(BF16)),
            dot_rows(own.astype(BF16), h2b[...]),
            e1g[...],
            dot_rows(far_sum.astype(BF16), h2b[...]),
            e2g[...],
            e3g[...],
            padded_rows(bias, width),
            padded_rows([eb1[...], eb2[...], eb3[...], edge_gain[...]], own.shape[1]),
        ],
    )


def residue_backward(args, far, f1, f2):
    node_cot, e_first, slope = args[0], args[2], args[9]
    rows, width = node_cot.shape
    tiles = all_tiles(early_shapes(width, e_first.shape[0]))
    shapes = [
        ((rows, width), F32),
        ((rows, width), F32),
        ((rows, width), BF16),
        ((tiles, 16, LANES), BF16),
    ]
    return small_call(
        functools.partial(residue_backward_kernel, len(f1), len(far)),
        (*args, *far, *f1, *f2),
        shapes, "residue_backward",
        flops=4 * rows * width * slope.shape[1], moved=8 * MIB,
    )


def feed_kernel(h_lo, h_hi, g_lo, g_hi, f1, fb1, f2, f1g, f2g, fb1g):

    @pl.when(pl.program_id(0) == 0)
    def _():
        for ref in (f1g, f2g, fb1g):
            ref[...] = jnp.zeros_like(ref)

    for h1b, gy2 in ((h_lo[...], g_lo[...]), (h_hi[...], g_hi[...])):
        act, slope = gelu_parts(dot(h1b, f1[...]) + fb1[...])
        gy1 = (dot_back(gy2, f2[...]) * slope).astype(BF16)
        f1g[...] += dot_rows(h1b, gy1)
        f2g[...] += dot_rows(act.astype(BF16), gy2)
        fb1g[...] += column_sum(gy1.astype(F32))


def feed_gradients(h1b, gy2, f1, fb1, f2):
    width, hidden = f1.shape
    half = h1b[0].shape[0]
    chunk = min(512, half)
    shapes = [(width, hidden), (hidden, width), (1, hidden)]
    return pl.pallas_call(
        feed_kernel,
        grid=(half // chunk,),
        in_specs=[pl.BlockSpec((chunk, width), lambda i: (i, 0))] * 4
        + [const_spec(a.shape) for a in (f1, fb1, f2)],
        out_specs=[pl.BlockSpec(s, whole) for s in shapes],
        out_shape=[jax.ShapeDtypeStruct(s, F32) for s in shapes],
        compiler_params=pltpu.CompilerParams(vmem_limit_bytes=VMEM),
        name="feed_gradients",
        cost_estimate=pl.CostEstimate(
            flops=16 * half * width * hidden,
            bytes_accessed=8 * half * width,
            transcendentals=2 * half * hidden,
        ),
    )(*h1b, *gy2, f1, fb1, f2)


def late_shapes(width, edge_width):
    return [(width, width), (width, width), (edge_width, width), (16, width)]


def message_backward_kernel(
    sb, blocks, groups, codes, base, places, v, a1, s1, s2, edge, low_three, low_edge, local_row, live_col,
    m1, m2, e_first, node_lo, node_hi, node, early,
    edge_grad, far_keep, far_send, own, keep, send,
    low_two, low_one, grad, rows_ref, sorted_ref, m2g, m1eg, m1fg, b2s, slab,
):
    step = pl.program_id(0)
    rows, width = v.shape
    edge_width = edge.shape[2]
    block = sb * rows
    tiles = width // LANES
    size = 16

    @pl.when(step == 0)
    def _():
        for ref in (own, m2g, m1eg, m1fg, b2s):
            ref[...] = jnp.zeros_like(ref)

    @pl.when(step < blocks)
    def _():
        for row in range(0, rows, size):
            count = live_col[row : row + size, :]
            inverse = 1.0 / count.astype(F32)
            value = v[row : row + size, :]
            total = b2s[row : row + size, :]
            for s in range(sb):
                at = s * rows + row
                share = jnp.where(count > step * sb + s, inverse, 0.0)
                low = (value * spread(share, width) * s2[at : at + size, :].astype(F32)).astype(BF16)
                low_two[at : at + size, :] = low
                total = total + low.astype(F32)
            b2s[row : row + size, :] = total
        grad[...] = dot_back(low_two[...], m2[...])
        m2g[...] += dot_rows(a1[...], low_two[...])
        rows_ref[pl.ds(tiles, block, stride=8), :] = index_columns(local_row[...]).astype(F32)
        move = row_mover(places, step * block, rows_ref, sorted_ref)
        waiting = None
        for row in range(0, rows, size):
            total = own[row : row + size, :]
            for s in range(sb):
                at = s * rows + row
                low = (grad[at : at + size, :] * s1[at : at + size, :].astype(F32)).astype(BF16)
                low_one[at : at + size, :] = low
                low = low.astype(F32)
                total = total + low
                for j in range(tiles):
                    rows_ref[pl.ds(at * 8 + j, size, stride=8), :] = low[:, j * LANES : (j + 1) * LANES]
                if waiting is not None:
                    move(waiting, size)
                waiting = at
            own[row : row + size, :] = total
        move(waiting, size)
        m1eg[...] += dot_rows(edge[...].reshape(block, edge_width), low_one[...])
        total = (
            low_three[...].astype(F32)
            + dot(low_edge[...], e_first[:, width : width + edge_width])
            + dot_back(low_one[...], m1[width : width + edge_width, :])
        )
        edge_grad[...] = total.reshape(sb, rows, edge_width)

    @pl.when(step >= blocks)
    def _():
        deep = far_keep.shape[0]
        sums = group_sums(sorted_ref, step - blocks, block * blocks // groups, width, 2 * deep * rows)
        sums = sums.astype(BF16)
        near = jnp.concatenate(
            [ref[at, 0] for ref in (node_lo, node_hi) for at in range(deep)], axis=0
        )
        m1fg[...] += dot_rows(near, sums)
        height = rows // 16
        for at in range(2 * deep):
            out = (far_keep if at < deep else far_send).at[at % deep, 0]
            for j in range(tiles):
                tile = sums[at * rows : (at + 1) * rows, j * LANES : (j + 1) * LANES]
                out[j * height : (j + 1) * height] = tile.reshape(height, 16, LANES)

    @pl.when(step == blocks + groups - 1)
    def _():
        count = early.shape[0]
        slab[:count] = early[...]
        pack(
            slab,
            [
                dot_rows(node[...], own[...].astype(BF16)),
                m2g[...],
                m1eg[...],
                padded_rows([column_sum(own[...]), column_sum(b2s[...])], width),
                m1fg[...],
            ],
            count,
        )
        count += all_tiles(late_shapes(width, edge_width) + [(width, width)])
        if count < slab.shape[0]:
            slab[count:] = jnp.zeros_like(slab[count:])
        order_out(slab, base[0], codes, keep, send)


def message_backward(
    groups, codes, base, places, v, a1, s1, s2, edge, low_three, low_edge, local_row, live_col, m1, m2,
    e_first, node_lo, node_hi, node, early,
):
    slots, rows, edge_width = edge.shape
    width = v.shape[1]
    sb = slot_block(slots)
    block = sb * rows
    blocks = slots // sb
    edges = slots * rows
    half = node_lo.shape[0]
    deep = half // rows // groups
    tiles = rows * width // (16 * LANES)
    slab = slab_tiles(width, edge_width, len(codes)) * len(codes)
    node_lo, node_hi = [n.reshape(deep, groups, rows, width) for n in (node_lo, node_hi)]
    blk = lambda i: jnp.minimum(i, blocks - 1)
    group_at = lambda i: (0, jnp.maximum(i - blocks, 0))
    row_spec = pl.BlockSpec((block, width), lambda i: (blk(i), 0))
    slot_spec = pl.BlockSpec((sb, rows, edge_width), lambda i: (blk(i), 0, 0))
    edge_spec = pl.BlockSpec((block, edge_width), lambda i: (blk(i), 0))
    node_spec = pl.BlockSpec((deep, 1, rows, width), lambda i: (*group_at(i), 0, 0))
    far_spec = pl.BlockSpec((deep, 1, tiles, 16, LANES), lambda i: (*group_at(i), 0, 0, 0))
    slab_spec = pl.BlockSpec((slab // 2, 16, LANES), lambda i: (0, 0, 0))
    smem = pl.BlockSpec(memory_space=pltpu.SMEM)
    return pl.pallas_call(
        functools.partial(message_backward_kernel, sb, blocks, groups, codes),
        grid=(blocks + groups,),
        in_specs=[
            smem,
            smem,
            const_spec(v.shape),
            row_spec,
            row_spec,
            row_spec,
            slot_spec,
            edge_spec,
            edge_spec,
            pl.BlockSpec((1, block), lambda i: (0, blk(i))),
            const_spec(live_col.shape),
            const_spec(m1.shape),
            const_spec(m2.shape),
            const_spec(e_first.shape),
            node_spec,
            node_spec,
            const_spec(node.shape),
            const_spec(early.shape),
        ],
        out_specs=[slot_spec, far_spec, far_spec, pl.BlockSpec((rows, width), whole), slab_spec, slab_spec],
        out_shape=[
            jax.ShapeDtypeStruct((slots, rows, edge_width), F32),
            jax.ShapeDtypeStruct((deep, groups, tiles, 16, LANES), BF16),
            jax.ShapeDtypeStruct((deep, groups, tiles, 16, LANES), BF16),
            jax.ShapeDtypeStruct((rows, width), F32),
            jax.ShapeDtypeStruct((slab // 2, 16, LANES), BF16),
            jax.ShapeDtypeStruct((slab // 2, 16, LANES), BF16),
        ],
        scratch_shapes=[
            pltpu.VMEM((block, width), BF16),
            pltpu.VMEM((block, width), BF16),
            pltpu.VMEM((block, width), F32),
            pltpu.VMEM((block * 8, LANES), F32),
            pltpu.VMEM((edges * 8, LANES), F32),
            pltpu.VMEM((width, width), F32),
            pltpu.VMEM((edge_width, width), F32),
            pltpu.VMEM((width, width), F32),
            pltpu.VMEM((rows, width), F32),
            slab_scratch(slab),
        ],
        compiler_params=pltpu.CompilerParams(vmem_limit_bytes=VMEM),
        name="message_backward",
        cost_estimate=pl.CostEstimate(
            flops=2 * edges * width * (2 * width + 3 * edge_width + half // groups),
            bytes_accessed=edges * width * 6 + edges * edge_width * 10,
            transcendentals=0,
        ),
    )(
        base, places, v, a1, s1, s2, edge, low_three, low_edge, local_row, live_col, m1, m2, e_first,
        node_lo, node_hi, node, early,
    )


def node_kernel(pieces, g_u1, own, m1, *refs):
    far, grad_out = refs[:pieces], refs[pieces]
    rows, width = own.shape
    height = rows // 16
    tiles = height * (width // LANES)
    sums = far[0][:tiles].astype(F32)
    for ref in far[1:]:
        sums = sums + ref[:tiles].astype(F32)
    far_sum = jnp.concatenate(
        [sums[j * height : (j + 1) * height].reshape(rows, LANES) for j in range(width // LANES)],
        axis=1,
    )
    far_first = m1.shape[0] - width
    grad_out[...] = (
        g_u1[...]
        + fine(dot_back, own[...], m1[:width, :])
        + fine(dot_back, far_sum, m1[far_first:, :])
    )


def node_last(g_u1, own, m1, far):
    return small_call(
        functools.partial(node_kernel, len(far)),
        (g_u1, own, m1, *far), [(own.shape, F32)], "node_gradient",
        flops=8 * own.size * own.shape[1], moved=2 * MIB,
    )[0]


def weights_out_kernel(
    codes, base, first, second,
    m1g, b1, m2g, b2, m3g, e1g, e2g, e3g, b3, g1, g2, fb2, eb1, eb2, eb3, g3, slab,
):
    order_in(slab, base[0], codes, first, second)
    width, edge_width = m3g.shape[0], e2g.shape[0]
    starts, at = [], 0
    for shape in early_shapes(width, edge_width) + late_shapes(width, edge_width):
        starts.append(at)
        at += tile_count(shape)
    m3g[...] = unpack(slab, starts[0], width, width)
    e1g[:, :width] = unpack(slab, starts[1], edge_width, width)
    middle = unpack(slab, starts[2], edge_width, edge_width)
    far = unpack(slab, starts[3], edge_width, width)
    over = edge_width % LANES
    base_col = width + edge_width - over
    e1g[:, width:base_col] = middle[:, : edge_width - over]
    far = pltpu.roll(jnp.concatenate([far, jnp.zeros((edge_width, LANES), F32)], axis=1), over, 1)
    lane = lax.broadcasted_iota(jnp.int32, (edge_width, LANES), 1)
    e1g[:, base_col : base_col + LANES] = jnp.where(
        lane < over, middle[:, edge_width - over : edge_width - over + LANES], far[:, :LANES]
    )
    rest = e1g.shape[1] - base_col - LANES
    e1g[:, base_col + LANES :] = far[:, LANES : LANES + rest]
    e2g[...] = unpack(slab, starts[4], edge_width, edge_width)[:, :edge_width]
    e3g[...] = unpack(slab, starts[5], edge_width, edge_width)[:, :edge_width]
    bias = unpack(slab, starts[6], 16, width)
    for row, out in enumerate((g1, g2, fb2, b3)):
        out[...] = bias[row : row + 1]
    bias = unpack(slab, starts[7], 16, edge_width)
    for row, out in enumerate((eb1, eb2, eb3, g3)):
        out[...] = bias[row : row + 1, :edge_width]
    m1g[:width, :] = unpack(slab, starts[8], width, width)
    m2g[...] = unpack(slab, starts[9], width, width)
    m1g[width : width + edge_width, :] = unpack(slab, starts[10], edge_width, width)
    m1g[width + edge_width :, :] = unpack(slab, at, width, width)
    bias = unpack(slab, starts[11], 16, width)
    b1[...] = bias[0:1]
    b2[...] = bias[1:2]


def weights_out(codes, base, halves_in, width, edge_width):
    shapes = [(2 * width + edge_width, width), (1, width), (width, width), (1, width)]
    shapes += [(width, width), (edge_width, 2 * width + edge_width)]
    shapes += [(edge_width, edge_width)] * 2 + [(1, width)] * 4 + [(1, edge_width)] * 4
    tiles = slab_tiles(width, edge_width, len(codes)) * len(codes)
    return small_call(
        functools.partial(weights_out_kernel, codes),
        (base, *halves_in), [(s, F32) for s in shapes], "weight_gradients",
        [slab_scratch(tiles)], moved=10 * MIB, scalars=1,
    )


def exchange(value, mask, devices):
    return lax.ppermute(value, AXES, [(d, d ^ mask) for d in range(devices)])


def mask_groups(masks):
    return [masks[i : min(i + 2, len(masks) - 1)] for i in range(0, len(masks) - 1, 2)] + [masks[-1:]]


def order_codes(groups):
    masks = [mask for group in groups for mask in group]
    return [
        sum(mask for bit, mask in enumerate(masks) if place >> bit & 1)
        for place in range(1 << len(masks))
    ]


def combined(group, code):
    return sum(mask for bit, mask in enumerate(group) if code >> bit & 1)


def sent_around(value, group, devices):
    return [value] + [
        exchange(value, combined(group, code), devices) for code in range(1, 1 << len(group))
    ]


def shared_out(total, group, devices):
    parts = 1 << len(group)
    rows = total.shape[0] // parts
    return [total[:rows]] + [
        exchange(total[code * rows : (code + 1) * rows].astype(BF16), combined(group, code), devices)
        for code in range(1, parts)
    ]


def add_up(terms):
    total = terms[0].astype(F32)
    for term in terms[1:]:
        total = total + term.astype(F32)
    return total


def tied(*values):
    return lax.optimization_barrier(values)


def split_three(value):
    rows = []
    for _ in range(3):
        high = lax.reduce_precision(value, 8, 7)
        rows.append(high.astype(BF16))
        value = value - high
    return jnp.concatenate(rows + [jnp.zeros((13, value.shape[1]), BF16)], axis=0)


def per_device(
    node_in,
    edge_in,
    neighbours,
    live_counts,
    message_first,
    message_first_bias,
    message_second,
    message_second_bias,
    message_third,
    message_third_bias,
    norm_one,
    feed_first,
    feed_first_bias,
    feed_second,
    feed_second_bias,
    norm_two,
    edge_first,
    edge_first_bias,
    edge_second,
    edge_second_bias,
    edge_third,
    edge_third_bias,
    norm_three,
    node_cotangent,
    edge_cotangent,
):
    rows, slots = neighbours.shape
    width = node_in.shape[1]
    edge_width = edge_in.shape[2]
    edges = rows * slots
    hid_count = lax.axis_size("hid")
    res_count = lax.axis_size("res")
    devices = res_count * hid_count
    bits = devices.bit_length() - 1
    masks = [1 << b for b in range(bits - 1, -1, -1)]
    groups = mask_groups(masks)
    codes = order_codes(groups)
    me = lax.axis_index("res") * hid_count + lax.axis_index("hid")
    base = me.reshape(1)
    row = lambda vector: vector.reshape(1, -1)

    names = neighbours.T.reshape(edges)
    apart = (names // rows) ^ me
    place = jnp.zeros_like(names)
    for bit, mask in enumerate(masks):
        place = place | jnp.where((apart & mask) != 0, 1 << bit, 0)
    idx_row = (place * rows + names % rows).reshape(1, edges)
    res_count = devices // hid_count
    local_row = (place // res_count * rows + names % rows).reshape(1, edges)
    places = group_places(place % res_count, res_count)
    live_col = jnp.broadcast_to(live_counts[:, None], (rows, LANES))
    edge = edge_in.transpose(1, 0, 2)
    cot = edge_cotangent.transpose(1, 0, 2)
    e_first = edge_first.T
    e_far = e_first[:, width + edge_width :]
    f1x = jnp.concatenate([feed_first, split_three(row(feed_first_bias))], axis=0)
    f2x = feed_second

    stack = lambda pieces: jnp.concatenate(pieces, axis=0)
    *outer, near = groups

    held = stack(sent_around(node_in, outer[0], devices))
    held, idx_row, local_row, places, live_col, e_far = tied(
        held, idx_row, local_row, places, live_col, e_far
    )
    for group in outer[1:]:
        held = stack(sent_around(held, group, devices))
    held, f1x, f2x = tied(held, f1x, f2x)
    node_lo, node_hi = sent_around(held, near, devices)

    f1, f2 = [f1x], [f2x]
    hid_masks = [m for m in masks if m < hid_count]
    for mask in hid_masks[:-1]:
        f1, f2 = [pieces + [exchange(p, mask, devices) for p in pieces] for pieces in (f1, f2)]

    a1, s1, s2, total = message_forward(
        node_lo, node_hi, node_in, edge, idx_row, live_col, message_first,
        row(message_first_bias), message_second, row(message_second_bias),
    )
    total, f1, f2 = tied(total, f1, f2)
    f1, f2 = [
        pieces + [exchange(p, hid_masks[-1], devices) for p in pieces] for pieces in (f1, f2)
    ]
    h1b, n1, sc1, n2, sc2, slope, h2b, far_part, own_part = residue_forward(
        node_in, total, message_third, row(message_third_bias), row(norm_one),
        row(feed_second_bias), row(norm_two), e_first, e_far, row(edge_first_bias), f1, f2,
    )

    held = stack(sent_around(far_part, outer[0], devices))
    h_held = stack(sent_around(h1b, outer[0], devices))
    for group in outer[1:]:
        held = stack(sent_around(held, group, devices))
    held, h_held = tied(held, h_held)
    q_lo, q_hi = sent_around(held, near, devices)
    for group in outer[1:]:
        h_held = stack(sent_around(h_held, group, devices))

    edge_out, act_one, act_two, low_three, low_two, low_one, hi, lo, own_sum, edge_gain = edge_branch(
        res_count, q_lo, q_hi, own_part, edge, cot, idx_row, local_row, places, live_col, e_first,
        edge_second, row(edge_second_bias), edge_third, row(edge_third_bias), row(norm_three),
    )
    lo, h_held = tied(lo, h_held)
    h_all = sent_around(h_held, near, devices)

    work = [
        lambda: edge_weights((act_two, act_one), (low_three, low_two), rows),
        lambda: edge_weights((low_one,), (edge,), rows),
    ]
    made = []
    hi, lo = [part.reshape(-1, edge_width) for part in (hi, lo)]
    terms = [lo, exchange(hi, near[0], devices)]
    for group in reversed(outer):
        terms = shared_out(add_up(terms), group, devices)
        if work:
            terms, got = tied(terms, work.pop(0)())
            made.append(got)
    while work:
        made.append(work.pop(0)())
    (e3g, e2g, eb3, eb2), (e1g, eb1) = made
    g_u1, v, gy2, early = residue_backward(
        (
            node_cotangent, own_sum, e_first, e_far, h2b, n1, sc1, n2, sc2, slope, row(norm_one),
            row(norm_two), message_third, total, e1g, e2g, e3g, eb1, eb2, eb3, edge_gain,
        ),
        terms, f1, f2,
    )

    g_held = stack(sent_around(gy2, outer[0], devices))
    v, g_held = tied(v, g_held)
    for group in outer[1:]:
        g_held = stack(sent_around(g_held, group, devices))
    edge_grad, far_keep, far_send, own, keep, send = message_backward(
        res_count, codes, base, places, v, a1, s1, s2, edge, low_three, low_one, local_row, live_col,
        message_first, message_second, e_first, node_lo, node_hi, node_in, early,
    )

    keep, g_held = tied(keep, g_held)
    terms = [keep, exchange(send, near[0], devices)]
    far_keep, far_send = [far.reshape(-1, 16, LANES) for far in (far_keep, far_send)]
    far_terms = [far_keep, exchange(far_send, near[0], devices)]
    g_all = sent_around(g_held, near, devices)
    feed = None
    for group in reversed(outer):
        terms = shared_out(add_up(terms), group, devices)
        total = add_up(far_terms)
        if feed is None:
            total, h_last = tied(total, h_all[1])
        far_terms = shared_out(total, group, devices)
        if feed is None:
            feed = feed_gradients(
                (h_all[0], h_last), g_all, feed_first, row(feed_first_bias), feed_second
            )
            terms, feed = tied(terms, feed)
    f1g, f2g, fb1g = feed
    held = add_up(terms).astype(BF16)

    for at, group in enumerate(outer):
        around = sent_around(held, group, devices)
        if at + 1 == len(outer):
            around, node_gradient = tied(around, node_last(g_u1, own, message_first, far_terms))
        held = stack(around)
    m1g, b1, m2g, b2, m3g, e1g, e2g, e3g, b3, g1, g2, fb2, eb1, eb2, eb3, g3 = weights_out(
        codes, base, sent_around(held, near, devices), width, edge_width
    )
    flat = lambda vector: vector.reshape(-1)
    return (
        h2b,
        edge_out.transpose(1, 0, 2),
        node_gradient,
        edge_grad.transpose(1, 0, 2),
        m1g,
        flat(b1),
        m2g,
        flat(b2),
        m3g,
        flat(b3),
        flat(g1),
        f1g,
        flat(fb1g),
        f2g,
        flat(fb2),
        flat(g2),
        e1g.T,
        flat(eb1),
        e2g,
        flat(eb2),
        e3g,
        flat(eb3),
        flat(g3),
    )


def solution(mesh):
    nodes, edges, shared = P(AXES, None), P(AXES, None, None), P()
    return jax.shard_map(
        per_device,
        mesh=mesh,
        in_specs=(nodes, edges, nodes, P(AXES))
        + (shared,) * 7
        + (P(None, "hid"), P("hid"), P("hid", None))
        + (shared,) * 9
        + (nodes, edges),
        out_specs=(nodes, edges, nodes, edges)
        + (shared,) * 7
        + (P(None, "hid"), P("hid"), P("hid", None))
        + (shared,) * 9,
        check_vma=False,
    )
```

```python
import functools

import jax
import jax.numpy as jnp
from jax import lax
from jax.experimental import pallas as pl
from jax.experimental.pallas import tpu as pltpu
from jax.sharding import PartitionSpec as P

EPS = 1e-05
AXES = ("res", "hid")
F32 = jnp.float32
BF16 = jnp.bfloat16
TANH_SCALE = 0.7978845608028654
TANH_CUBE = 0.044715
LANES = 128
CHUNK = 2048
MIB = 1024 * 1024
VMEM = 58 * MIB


def dot(left, right):
    return lax.dot_general(left, right, (((1,), (0,)), ((), ())), preferred_element_type=F32)


def dot_rows(left, right):
    return lax.dot_general(left, right, (((0,), (0,)), ((), ())), preferred_element_type=F32)


def dot_back(left, right):
    return lax.dot_general(left, right, (((1,), (1,)), ((), ())), preferred_element_type=F32)


def halves(value):
    high = value.astype(BF16)
    return high, (value - high.astype(F32)).astype(BF16)


def fine(product, value, weights):
    high, low = halves(value)
    return product(high, weights) + product(low, weights)


def gelu_parts(x):
    square = x * x
    t = jnp.tanh(x * (TANH_SCALE + (TANH_SCALE * TANH_CUBE) * square))
    gate = 0.5 + 0.5 * t
    act = x * gate
    slope = gate + act * (1.0 - gate) * (2 * TANH_SCALE + (6 * TANH_SCALE * TANH_CUBE) * square)
    return act, slope


def index_columns(idx_row):
    parts = [
        jnp.broadcast_to(idx_row[:, first : first + LANES], (LANES, LANES)).T
        for first in range(0, idx_row.shape[1], LANES)
    ]
    return jnp.concatenate(parts, axis=0)


def one_hot_columns(idx, start, count):
    one, zero = jnp.ones((), BF16), jnp.zeros((), BF16)
    idx = idx.astype(jnp.int16)
    lane = lax.broadcasted_iota(jnp.int32, idx.shape, 1).astype(jnp.int16)
    parts = [
        jnp.where(idx == lane + jnp.int16(start + first), one, zero)
        for first in range(0, count, LANES)
    ]
    return jnp.concatenate(parts, axis=1)


def pick_rows(idx, table_refs):
    total, start = None, 0
    for ref in table_refs:
        rows = ref.shape[0]
        step = min(rows, CHUNK)
        for first in range(0, rows, step):
            part = dot(one_hot_columns(idx, start + first, step), ref[first : first + step, :])
            total = part if total is None else total + part
        start += rows
    return total


def one_hot_rows(idx_row, start, count):
    shape = (count, idx_row.shape[1])
    row = (lax.broadcasted_iota(jnp.int32, shape, 0) + start).astype(jnp.int16)
    names = jnp.broadcast_to(idx_row, shape).astype(jnp.int16)
    return jnp.where(names == row, jnp.ones((), BF16), jnp.zeros((), BF16))


def group_rows(order, first, count, rows_ref, moved, width):
    for e in range(count):
        at = pl.multiple_of(order[0, first + e] * 8, 8)
        moved[e * 8 : e * 8 + 8, :] = rows_ref[pl.ds(at, 8), :]

    def column(at):
        return moved[pl.ds(at, count, stride=8), :]

    tiles = pl.cdiv(width, LANES)
    parts = [column(at)[:, : min(LANES, width - at * LANES)] for at in range(tiles)]
    return jnp.concatenate(parts, axis=1).astype(BF16), column(tiles)


def group_sums(rows, local, residues):
    lane = lax.broadcasted_iota(jnp.int32, local.shape, 1).astype(F32)
    picks = [
        jnp.where(local == lane + float(first), 1.0, 0.0).astype(BF16)
        for first in range(0, residues, LANES)
    ]
    return dot_rows(jnp.concatenate(picks, axis=1), rows)


def order_kernel(groups, count, names, out):
    rows = names.shape[0]
    row = lax.broadcasted_iota(jnp.int32, (LANES, LANES), 0)
    column = lax.broadcasted_iota(jnp.int32, (LANES, LANES), 1)
    upto = jnp.where(row <= column, 1.0, 0.0).astype(BF16)
    ones = jnp.ones((LANES, LANES), BF16)
    above = lax.broadcasted_iota(jnp.int32, (rows, rows), 0)
    before = jnp.where(lax.broadcasted_iota(jnp.int32, (rows, rows), 1) < above, 1.0, 0.0).astype(BF16)
    place = jnp.full(names.shape, float(LANES * LANES), F32)
    for group in range(groups):
        here = names[...] == group
        low = jnp.where(here, 1.0, 0.0).astype(BF16)
        rank = dot(low, upto) + dot(before, dot(low, ones).astype(BF16))
        place = jnp.where(here, rank + float(group * count - 1), place)
    high = total = None
    for at in range(rows):
        where = jnp.broadcast_to(place[at : at + 1, :], (LANES, LANES)).T.astype(jnp.int32)
        left = jnp.where(where // 64 == column, 1.0, 0.0)
        right = jnp.where((where % 64 == column), 1.0, 0.0)
        part = dot_rows(left.astype(BF16), (right * float(at)).astype(BF16))
        high = part if high is None else high + part
        part = dot_rows(left.astype(BF16), (right * row.astype(F32)).astype(BF16))
        total = part if total is None else total + part
    number = high * float(LANES) + total
    out[...] = number[: out.shape[0], : out.shape[1]].astype(jnp.int32)


def group_order(names, groups):
    edges = names.shape[0]
    rows = pl.cdiv(pl.cdiv(edges, LANES), 8) * 8
    padded = jnp.pad(names, (0, rows * LANES - edges), constant_values=groups)
    out = small_call(
        functools.partial(order_kernel, groups, edges // groups),
        (padded.reshape(rows, LANES),), [((edges // 64, 64), jnp.int32)], "group_order",
    )[0]
    return out.reshape(1, edges)


def spread(column, width):
    return jnp.concatenate([column] * (width // LANES), axis=1)


def norm(value):
    centre = value - jnp.mean(value, -1, keepdims=True)
    scale = lax.rsqrt(jnp.mean(centre * centre, -1, keepdims=True) + EPS)
    return centre * scale, scale


def norm_back(inner, normed, scale):
    mean_first = jnp.mean(inner, -1, keepdims=True)
    mean_second = jnp.mean(inner * normed, -1, keepdims=True)
    return scale * (inner - mean_first - normed * mean_second)


def column_sum(value):
    return jnp.sum(value, axis=0, keepdims=True)


def whole(*_):
    return (0, 0)


def const_spec(shape):
    return pl.BlockSpec(shape, lambda *_: (0,) * len(shape), pipeline_mode=pl.Buffered(1))


def small_call(kernel, args, shapes, name, scratch=(), flops=0, moved=0, exps=0, scalars=0):
    return pl.pallas_call(
        kernel,
        grid=(1,),
        in_specs=[pl.BlockSpec(memory_space=pltpu.SMEM)] * scalars
        + [const_spec(a.shape) for a in args[scalars:]],
        out_specs=[pl.BlockSpec(s, lambda *_, n=len(s): (0,) * n) for s, _ in shapes],
        out_shape=[jax.ShapeDtypeStruct(*s) for s in shapes],
        scratch_shapes=list(scratch),
        compiler_params=pltpu.CompilerParams(vmem_limit_bytes=VMEM),
        name=name,
        cost_estimate=pl.CostEstimate(flops=flops, bytes_accessed=moved, transcendentals=exps),
    )(*args)


def tile_count(shape):
    return pl.cdiv(shape[0], 16) * pl.cdiv(shape[1], LANES)


def all_tiles(shapes):
    return sum(tile_count(s) for s in shapes)


def pack(slab, values, at=0):
    for value in values:
        rows, columns = value.shape
        count = rows // 16
        for first in range(0, columns, LANES):
            take = min(LANES, columns - first)
            tile = value[:, first : first + take].astype(BF16).reshape(count, 16, take)
            slab[at : at + count, :, :take] = tile
            at += count


def unpack(slab, at, rows, columns):
    count = rows // 16
    parts = [
        slab[at + i * count : at + (i + 1) * count].reshape(rows, LANES).astype(F32)
        for i in range(pl.cdiv(columns, LANES))
    ]
    return jnp.concatenate(parts, axis=1)


def order_out(slab, base, codes, keep, send):
    size = slab.shape[0] // len(codes)
    half = len(codes) // 2
    for place, code in enumerate(codes):
        out = keep if place < half else send
        at = (place % half) * size
        out[at : at + size] = slab[pl.ds((base ^ code) * size, size)]


def half_shapes(tiles):
    return [((tiles // 2, 16, LANES), BF16)] * 2


def slab_scratch(tiles):
    return pltpu.VMEM((tiles, 16, LANES), BF16)


def slab_tiles(shapes, chunks):
    return pl.cdiv(all_tiles(shapes), chunks)


def order_in(slabs, base, codes, first, second):
    sizes = [slab.shape[0] // len(codes) for slab in slabs]
    half = len(codes) // 2
    for place, code in enumerate(codes):
        source = first if place < half else second
        at = (place % half) * sum(sizes)
        for slab, size in zip(slabs, sizes):
            slab[pl.ds((base ^ code) * size, size)] = source[at : at + size]
            at += size


def padded_rows(parts, width):
    return jnp.concatenate(parts + [jnp.zeros((16 - len(parts), width), F32)], axis=0)


def slot_block(slots):
    for size in (10, 12, 8, 6, 5, 4, 3, 2):
        if slots % size == 0:
            return size
    return 1


def far_table(node_lo, node_hi, weights, put):
    tile = min(512, node_lo.shape[0])
    for source, start in ((node_lo, 0), (node_hi, node_lo.shape[0])):
        def body(i, carry, source=source, start=start):
            at = pl.multiple_of(i * tile, tile)
            put(start + at, dot(source[pl.ds(at, tile), :], weights))
            return carry
        lax.fori_loop(0, source.shape[0] // tile, body, 0)


def message_forward_kernel(
    sb, by_rows, node_lo, node_hi, node_own, edge, idx_row, names, live_col, m1, b1, m2, b2,
    a1_out, s1_out, s2_out, sum_out, table, far, near, lhs, z,
):
    step = pl.program_id(0)
    width = node_own.shape[1]
    edge_width = edge.shape[2]
    rows = edge.shape[1]
    block = sb * rows
    lanes = width // LANES

    @pl.when(step == 0)
    def _():
        weights = m1[width + edge_width :, :]
        if by_rows:
            def put(first, value):
                for at in range(8):
                    column = at % lanes * LANES
                    table[pl.ds(first * 8 + at, value.shape[0], stride=8), :] = value[
                        :, column : column + LANES
                    ]
        else:
            def put(first, value):
                table[pl.ds(first, value.shape[0]), :] = value.astype(BF16)
        far_table(node_lo, node_hi, weights, put)
        near[:edge_width, :] = m1[width : width + edge_width, :]
        near[edge_width:, :] = jnp.zeros_like(near[edge_width:, :])
        near[edge_width : edge_width + rows, :] = (
            dot(node_own[...], m1[:width, :]) + b1[...]
        ).astype(BF16)
        shape = (rows, near.shape[0] - edge_width)
        eye = lax.broadcasted_iota(jnp.int32, shape, 0) == lax.broadcasted_iota(jnp.int32, shape, 1)
        for at in range(0, block, rows):
            lhs[at : at + rows, edge_width:] = jnp.where(eye, 1.0, 0.0).astype(BF16)
        sum_out[...] = jnp.zeros_like(sum_out)

    lhs[:, :edge_width] = edge[...].reshape(block, edge_width)
    z[...] = dot(lhs[...], near[...])
    if not by_rows:
        z[...] += pick_rows(index_columns(idx_row[...]), (table,))
    upper = lax.broadcasted_iota(jnp.int32, (8, LANES), 0) < lanes

    def fetch(at):
        for e in range(at, at + 16, 2):
            pair = [
                table[pl.ds(pl.multiple_of(names[0, step * block + e + i] * 8, 8), 8), :]
                for i in range(2)
            ]
            far[e * lanes : e * lanes + 8, :] = jnp.where(upper, *pair)

    def fetched(at):
        return jnp.concatenate(
            [far[pl.ds(at * lanes + j, 16, stride=lanes), :] for j in range(lanes)], axis=1
        )

    if by_rows:
        fetch(0)
    for at in range(0, block, 16):
        value = z[at : at + 16, :]
        if by_rows:
            if at + 16 < block:
                fetch(at + 16)
            value = value + fetched(at)
        act, slope = gelu_parts(value)
        a1_out[at : at + 16, :] = act.astype(BF16)
        s1_out[at : at + 16, :] = slope.astype(BF16)
    z[...] = dot(a1_out[...], m2[...])
    bias = b2[...]
    for row in range(0, rows, 16):
        count = live_col[row : row + 16, :]
        inverse = 1.0 / count.astype(F32)
        total = sum_out[row : row + 16, :]
        for s in range(sb):
            at = s * rows + row
            act, slope = gelu_parts(z[at : at + 16, :] + bias)
            s2_out[at : at + 16, :] = slope.astype(BF16)
            share = jnp.where(count > step * sb + s, inverse, 0.0)
            total = total + act.astype(BF16).astype(F32) * spread(share, width)
        sum_out[row : row + 16, :] = total


def message_forward(node_lo, node_hi, node_own, edge, idx_row, live_col, m1, b1, m2, b2):
    slots, rows, edge_width = edge.shape
    width = node_own.shape[1]
    residues = 2 * node_lo.shape[0]
    by_rows = residues <= 4096 and width == 4 * LANES
    sb = slot_block(slots) if by_rows else 4
    block = sb * rows
    edges = slots * rows
    near = pl.cdiv(edge_width + rows, LANES) * LANES
    row_spec = pl.BlockSpec((block, width), lambda i: (i, 0))
    return pl.pallas_call(
        functools.partial(message_forward_kernel, sb, by_rows),
        grid=(slots // sb,),
        in_specs=[
            const_spec(node_lo.shape),
            const_spec(node_hi.shape),
            const_spec(node_own.shape),
            pl.BlockSpec((sb, rows, edge_width), lambda i: (i, 0, 0)),
            pl.BlockSpec((1, block), lambda i: (0, i)),
            pl.BlockSpec(memory_space=pltpu.SMEM),
            const_spec(live_col.shape),
            const_spec(m1.shape),
            const_spec(b1.shape),
            const_spec(m2.shape),
            const_spec(b2.shape),
        ],
        out_specs=[row_spec, row_spec, row_spec, pl.BlockSpec((rows, width), whole)],
        out_shape=[jax.ShapeDtypeStruct((edges, width), BF16)] * 3
        + [jax.ShapeDtypeStruct((rows, width), F32)],
        scratch_shapes=[
            pltpu.VMEM((residues * 8, LANES), F32) if by_rows else pltpu.VMEM((residues, width), BF16),
            pltpu.VMEM((block * 4 if by_rows else 8, LANES), F32),
            pltpu.VMEM((near, width), BF16),
            pltpu.VMEM((block, near), BF16),
            pltpu.VMEM((block, width), F32),
        ],
        compiler_params=pltpu.CompilerParams(vmem_limit_bytes=VMEM),
        name="message_forward",
        cost_estimate=pl.CostEstimate(
            flops=2 * edges * width * (residues + edge_width + width),
            bytes_accessed=edges * width * 6 + edges * edge_width * 2 + edges * LANES * 4,
            transcendentals=2 * edges * width,
        ),
    )(node_lo, node_hi, node_own, edge, idx_row, idx_row, live_col, m1, b1, m2, b2)


def residue_forward_kernel(parts, node, total, m3, b3, g1, fb2, g2, e_first, e_far, eb, *refs):
    f1, f2 = refs[:parts], refs[parts : 2 * parts]
    h1b_out, n1_out, sc1_out, n2_out, sc2_out, slope_out, h2b_out, far_out, own_out = refs[2 * parts :]
    width, hidden = node.shape[1], f1[0].shape[1]
    u1 = node[...].astype(F32) + fine(dot, total[...], m3[...]) + b3[...]
    n1, sc1 = norm(u1)
    h1 = n1 * g1[...]
    h1b = h1.astype(BF16)
    h1b_out[...] = h1b
    n1_out[...] = n1
    sc1_out[...] = jnp.broadcast_to(sc1, sc1_out.shape)
    y2 = None
    for p in range(parts):
        bias = f1[p][width : width + 16, :].astype(F32)
        bias = bias[0:1] + bias[1:2] + bias[2:3]
        act, slope = gelu_parts(dot(h1b, f1[p][:width, :]) + bias)
        slope_out[:, p * hidden : (p + 1) * hidden] = slope
        part = dot(act.astype(BF16), f2[p][...])
        y2 = part if y2 is None else y2 + part
    n2, sc2 = norm(h1 + (y2 + fb2[...]))
    h2b = (n2 * g2[...]).astype(BF16)
    n2_out[...] = n2
    sc2_out[...] = jnp.broadcast_to(sc2, sc2_out.shape)
    h2b_out[...] = h2b
    far_out[...] = dot_back(h2b, e_far[...]).astype(BF16)
    own_out[...] = dot_back(h2b, e_first[:, :width]) + eb[...]


def residue_forward(node, total, m3, b3, g1, fb2, g2, e_first, e_far, eb, f1, f2):
    rows, width = node.shape
    edge_width = e_first.shape[0]
    hidden = len(f1) * f1[0].shape[1]
    shapes = [
        ((rows, width), BF16),
        ((rows, width), F32),
        ((rows, LANES), F32),
        ((rows, width), F32),
        ((rows, LANES), F32),
        ((rows, hidden), F32),
        ((rows, width), BF16),
        ((rows, edge_width), BF16),
        ((rows, edge_width), F32),
    ]
    return small_call(
        functools.partial(residue_forward_kernel, len(f1)),
        (node, total, m3, b3, g1, fb2, g2, e_first, e_far, eb, *f1, *f2),
        shapes, "residue_forward", flops=4 * rows * width * hidden, moved=5 * MIB,
        exps=rows * hidden,
    )


def edge_kernel(
    sb, blocks, hi_chunks, by_rows, far_lo, far_hi, own, edge, cot, idx, idx_row, names, live_col,
    e_first, e2, eb2, e3, eb3, g3,
    edge_out, act_one_out, act_two_out, low_three_out, low_two_out, low_one_out, hi_out, lo_out, own_out, gain_out,
    low_first, gs, table, far, z, slope_ref,
):
    step = pl.program_id(0)
    rows, width = own.shape
    node_width = (e_first.shape[1] - width) // 2
    e_mid = e_first.at[:, node_width : node_width + width]
    tiles = pl.cdiv(width, LANES)
    per = 8 // tiles
    size = 32

    @pl.when(step == 0)
    def _():
        own_out[...] = jnp.zeros_like(own_out)
        gs[...] = jnp.zeros_like(gs)
        half = far_lo.shape[0]
        if by_rows:
            for source, start in ((far_lo, 0), (far_hi, half)):
                for first in range(0, half, 512):
                    value = source[first : first + 512, :].astype(F32)
                    for at in range(8):
                        column = at % tiles * LANES
                        take = min(LANES, width - column)
                        table[pl.ds((start + first) * 8 + at, value.shape[0], stride=8), :take] = value[
                            :, column : column + take
                        ]

    @pl.when(step < blocks)
    def _():
        block = sb * rows
        flat = edge[...].reshape(block, width)
        z[...] = dot_back(flat, e_mid[...])
        if not by_rows:
            z[...] += pick_rows(index_columns(idx[...]), (far_lo, far_hi))
        sub = lax.broadcasted_iota(jnp.int32, (8, LANES), 0)

        def fetch(at):
            for e in range(at, at + size, per):
                got = [
                    table[pl.ds(pl.multiple_of(names[0, step * block + e + i] * 8, 8), 8), :]
                    for i in range(per)
                ]
                value = got[-1]
                for i in range(per - 2, -1, -1):
                    value = jnp.where(sub < (i + 1) * tiles, got[i], value)
                far[e * tiles : e * tiles + 8, :] = value

        def fetched(at):
            parts = [
                far[pl.ds(at * tiles + j, size, stride=tiles), :][:, : min(LANES, width - j * LANES)]
                for j in range(tiles)
            ]
            return jnp.concatenate(parts, axis=1)

        if by_rows:
            fetch(0)
        for at in range(0, block, size):
            value = z[at : at + size, :] + own[at % rows : at % rows + size, :]
            if by_rows:
                if at + size < block:
                    fetch(at + size)
                value = value + fetched(at)
            act, slope = gelu_parts(value)
            act_one_out[at : at + size, :] = act.astype(BF16)
            slope_ref[at : at + size, :] = slope
        act_one = act_one_out[...]
        act_two, slope_two = gelu_parts(dot(act_one, e2[...]) + eb2[...])
        act_two = act_two.astype(BF16)
        act_two_out[...] = act_two
        w_three = dot(act_two, e3[...]) + eb3[...]
        normed, scale = norm(flat.astype(F32) + w_three)
        count = spread(live_col[...], pl.cdiv(width, LANES) * LANES)[:, :width]
        live = jnp.concatenate(
            [jnp.where(count > step * sb + s, 1.0, 0.0) for s in range(sb)], axis=0
        )
        edge_out[...] = (normed * g3[...] * live).astype(BF16).reshape(sb, rows, width)
        grad = cot[...].reshape(block, width).astype(F32) * live
        gs[...] += jnp.sum((grad * normed).reshape(sb, rows, width), axis=0)
        low_three = norm_back(grad * g3[...], normed, scale).astype(BF16)
        low_three_out[...] = low_three
        low_two = (dot_back(low_three, e3[...]) * slope_two).astype(BF16)
        low_two_out[...] = low_two
        low_one = (dot_back(low_two, e2[...]) * slope_ref[...]).astype(BF16)
        low_one_out[...] = low_one
        own_out[...] += jnp.sum(low_one.astype(F32).reshape(sb, rows, width), axis=0)
        low_first[pl.ds(pl.multiple_of(step * block, block), block), :] = low_one

    chunk = hi_out.shape[0]

    @pl.when((step >= blocks) & (step < blocks + hi_chunks))
    def _():
        start = (step - blocks + hi_chunks) * chunk
        hi_out[...] = dot(one_hot_rows(idx_row[...], start, chunk), low_first[...]).astype(BF16)

    @pl.when(step >= blocks + hi_chunks)
    def _():
        start = (step - blocks - hi_chunks) * chunk
        lo_out[...] = dot(one_hot_rows(idx_row[...], start, chunk), low_first[...])

    @pl.when(step == blocks + 2 * hi_chunks - 1)
    def _():
        gain_out[...] = column_sum(gs[...])


def edge_branch(far_lo, far_hi, own, edge, cot, idx_row, live_col, e_first, e2, eb2, e3, eb3, g3):
    slots, rows, width = edge.shape
    sb = slot_block(slots)
    edges = slots * rows
    block = sb * rows
    blocks = slots // sb
    half = far_lo.shape[0]
    chunk = min(512, half)
    hi_chunks = half // chunk
    by_rows = half <= 2048 and 8 % pl.cdiv(width, LANES) == 0
    blk = lambda i: jnp.minimum(i, blocks - 1)
    hi_at = lambda i: (jnp.clip(i - blocks, 0, hi_chunks - 1), 0)
    lo_at = lambda i: (jnp.clip(i - blocks - hi_chunks, 0, hi_chunks - 1), 0)
    slot_spec = pl.BlockSpec((sb, rows, width), lambda i: (blk(i), 0, 0))
    row_spec = pl.BlockSpec((block, width), lambda i: (blk(i), 0))
    return pl.pallas_call(
        functools.partial(edge_kernel, sb, blocks, hi_chunks, by_rows),
        grid=(blocks + 2 * hi_chunks,),
        in_specs=[
            const_spec(far_lo.shape),
            const_spec(far_hi.shape),
            const_spec(own.shape),
            slot_spec,
            slot_spec,
            pl.BlockSpec((1, block), lambda i: (0, blk(i))),
            const_spec(idx_row.shape),
            pl.BlockSpec(memory_space=pltpu.SMEM),
            const_spec(live_col.shape),
            const_spec(e_first.shape),
            const_spec(e2.shape),
            const_spec(eb2.shape),
            const_spec(e3.shape),
            const_spec(eb3.shape),
            const_spec(g3.shape),
        ],
        out_specs=[slot_spec]
        + [row_spec] * 5
        + [
            pl.BlockSpec((chunk, width), hi_at),
            pl.BlockSpec((chunk, width), lo_at),
            pl.BlockSpec((rows, width), whole),
            pl.BlockSpec((1, width), whole),
        ],
        out_shape=[jax.ShapeDtypeStruct((slots, rows, width), BF16)]
        + [jax.ShapeDtypeStruct((edges, width), BF16)] * 5
        + [
            jax.ShapeDtypeStruct((half, width), BF16),
            jax.ShapeDtypeStruct((half, width), F32),
            jax.ShapeDtypeStruct((rows, width), F32),
            jax.ShapeDtypeStruct((1, width), F32),
        ],
        scratch_shapes=[
            pltpu.VMEM((edges, width), BF16),
            pltpu.VMEM((rows, width), F32),
            pltpu.VMEM((half * 16 if by_rows else 8, LANES), F32),
            pltpu.VMEM((block * 8, LANES), F32),
            pltpu.VMEM((block, width), F32),
            pltpu.VMEM((block, width), F32),
        ],
        compiler_params=pltpu.CompilerParams(vmem_limit_bytes=VMEM),
        name="edge_branch",
        cost_estimate=pl.CostEstimate(
            flops=2 * edges * width * (4 * half + 5 * width),
            bytes_accessed=edges * width * 16,
            transcendentals=2 * edges * width,
        ),
    )(far_lo, far_hi, own, edge, cot, idx_row, idx_row, idx_row, live_col, e_first, e2, eb2, e3, eb3, g3)


def edge_weights_kernel(blocks, pairs, *refs):
    step = pl.program_id(0)
    lefts, rights = refs[:pairs], refs[pairs : 2 * pairs]
    grads, biases, sums = refs[2 * pairs : 3 * pairs], refs[3 * pairs : 4 * pairs], refs[-1]
    rows = sums.shape[1]

    @pl.when(step == 0)
    def _():
        for ref in (*grads, sums):
            ref[...] = jnp.zeros_like(ref)

    for at in range(pairs):
        left, right = [r[...].reshape(-1, r.shape[-1]) for r in (lefts[at], rights[at])]
        grads[at][...] += dot_rows(left, right)
        low = left if lefts[at].ndim < rights[at].ndim else right
        sums[at] += jnp.sum(low.astype(F32).reshape(-1, rows, low.shape[1]), axis=0)

    @pl.when(step == blocks - 1)
    def _():
        for at in range(pairs):
            biases[at][...] = column_sum(sums[at])


def edge_weights(lefts, rights, rows):
    pairs = len(lefts)
    edges, width = lefts[0].shape
    slots = edges // rows
    sb = slot_block(slots)

    def spec(array):
        if array.ndim == 3:
            return pl.BlockSpec((sb, rows, width), lambda i: (i, 0, 0))
        return pl.BlockSpec((sb * rows, width), lambda i: (i, 0))

    shapes = [(width, width)] * pairs + [(1, width)] * pairs
    return pl.pallas_call(
        functools.partial(edge_weights_kernel, slots // sb, pairs),
        grid=(slots // sb,),
        in_specs=[spec(array) for array in (*lefts, *rights)],
        out_specs=[pl.BlockSpec(s, whole) for s in shapes],
        out_shape=[jax.ShapeDtypeStruct(s, F32) for s in shapes],
        scratch_shapes=[pltpu.VMEM((pairs, rows, width), F32)],
        compiler_params=pltpu.CompilerParams(vmem_limit_bytes=VMEM),
        name="edge_weights",
        cost_estimate=pl.CostEstimate(
            flops=2 * pairs * edges * width * width,
            bytes_accessed=pairs * edges * width * 4,
            transcendentals=0,
        ),
    )(*lefts, *rights)


def early_shapes(width, edge_width):
    return [
        (width, width),
        (edge_width, width),
        (edge_width, edge_width),
        (edge_width, width),
        (edge_width, edge_width),
        (edge_width, edge_width),
        (16, width),
        (16, edge_width),
    ]


def residue_backward_kernel(
    parts, pieces, codes, base, node_cot, own_sum, e_first, e_far, h1b, h2b, n1, sc1, n2, sc2, slope, g1, g2, m3,
    total, e1g, e2g, e3g, eb1, eb2, eb3, edge_gain, *refs,
):
    far = refs[:pieces]
    f1 = refs[pieces : pieces + parts]
    f2 = refs[pieces + parts : pieces + 2 * parts]
    gu1_out, v_out, both_out, keep, send, slab = refs[pieces + 2 * parts :]
    width, hidden = h2b.shape[1], f1[0].shape[1]
    far_sum = far[0][...]
    for ref in far[1:]:
        far_sum = far_sum + ref[...].astype(F32)
    own = own_sum[...]
    g_h2 = (
        node_cot[...].astype(F32)
        + fine(dot, own, e_first[:, :width])
        + fine(dot, far_sum, e_far[...])
    )
    gain_two = column_sum(g_h2 * n2[...])
    g_u2 = norm_back(g_h2 * g2[...], n2[...], sc2[:, :1])
    gy2 = g_u2.astype(BF16)
    both_out[:, :width] = h1b[...]
    both_out[:, width:] = gy2
    g_h1 = g_u2
    for p in range(parts):
        gy1 = dot_back(gy2, f2[p][...]) * slope[:, p * hidden : (p + 1) * hidden]
        g_h1 = g_h1 + dot_back(gy1.astype(BF16), f1[p][:width, :])
    gain_one = column_sum(g_h1 * n1[...])
    g_u1 = norm_back(g_h1 * g1[...], n1[...], sc1[:, :1])
    gu1_out[...] = g_u1
    v_out[...] = fine(dot_back, g_u1, m3[...])
    bias = [gain_one, gain_two, column_sum(gy2.astype(F32)), column_sum(g_u1)]
    slab[...] = jnp.zeros_like(slab)
    pack(
        slab,
        [
            dot_rows(total[...].astype(BF16), g_u1.astype(BF16)),
            dot_rows(own.astype(BF16), h2b[...]),
            e1g[...],
            dot_rows(far_sum.astype(BF16), h2b[...]),
            e2g[...],
            e3g[...],
            padded_rows(bias, width),
            padded_rows([eb1[...], eb2[...], eb3[...], edge_gain[...]], own.shape[1]),
        ],
    )
    order_out(slab, base[0], codes, keep, send)


def residue_backward(codes, base, args, far, f1, f2):
    node_cot, e_first, slope = args[0], args[2], args[10]
    rows, width = node_cot.shape
    tiles = slab_tiles(early_shapes(width, e_first.shape[0]), len(codes)) * len(codes)
    shapes = [
        ((rows, width), F32),
        ((rows, width), F32),
        ((rows, 2 * width), BF16),
    ] + half_shapes(tiles)
    return small_call(
        functools.partial(residue_backward_kernel, len(f1), len(far), codes),
        (base, *args, *far, *f1, *f2),
        shapes, "residue_backward", [slab_scratch(tiles)],
        flops=4 * rows * width * slope.shape[1], moved=8 * MIB, scalars=1,
    )


def feed_kernel(first, second, f1, fb1, f2, f1g, f2g, fb1g):
    width = f1.shape[0]

    @pl.when(pl.program_id(0) == 0)
    def _():
        for ref in (f1g, f2g, fb1g):
            ref[...] = jnp.zeros_like(ref)

    for both in (first, second):
        h1b, gy2 = both[:, :width], both[:, width:]
        act, slope = gelu_parts(dot(h1b, f1[...]) + fb1[...])
        gy1 = (dot_back(gy2, f2[...]) * slope).astype(BF16)
        f1g[...] += dot_rows(h1b, gy1)
        f2g[...] += dot_rows(act.astype(BF16), gy2)
        fb1g[...] += column_sum(gy1.astype(F32))


def feed_gradients(both, f1, fb1, f2):
    width, hidden = f1.shape
    half = both[0].shape[0]
    chunk = min(512, half)
    shapes = [(width, hidden), (hidden, width), (1, hidden)]
    return pl.pallas_call(
        feed_kernel,
        grid=(half // chunk,),
        in_specs=[pl.BlockSpec((chunk, 2 * width), lambda i: (i, 0))] * 2
        + [const_spec(a.shape) for a in (f1, fb1, f2)],
        out_specs=[pl.BlockSpec(s, whole) for s in shapes],
        out_shape=[jax.ShapeDtypeStruct(s, F32) for s in shapes],
        compiler_params=pltpu.CompilerParams(vmem_limit_bytes=VMEM),
        name="feed_gradients",
        cost_estimate=pl.CostEstimate(
            flops=16 * half * width * hidden,
            bytes_accessed=8 * half * width,
            transcendentals=2 * half * hidden,
        ),
    )(*both, f1, fb1, f2)


def late_shapes(width, edge_width):
    return [(width, width), (width, width), (edge_width, width), (16, width), (width, width)]


def message_backward_kernel(
    sb, blocks, groups, codes, base, order, v, a1, s1, s2, edge, low_three, low_edge, local_row, live_col,
    m1, m2, e_first, node_lo, node_hi, node,
    edge_grad, far_keep, far_send, own, keep, send,
    low_two, low_one, grad, rows_ref, moved, m2g, m1eg, m1fg, b2s, slab,
):
    step = pl.program_id(0)
    rows, width = v.shape
    edge_width = edge.shape[2]
    block = sb * rows
    tiles = width // LANES
    size = 16

    @pl.when(step == 0)
    def _():
        for ref in (own, m2g, m1eg, m1fg, b2s):
            ref[...] = jnp.zeros_like(ref)

    @pl.when(step < blocks)
    def _():
        for row in range(0, rows, size):
            count = live_col[row : row + size, :]
            inverse = 1.0 / count.astype(F32)
            value = v[row : row + size, :]
            total = b2s[row : row + size, :]
            for s in range(sb):
                at = s * rows + row
                share = jnp.where(count > step * sb + s, inverse, 0.0)
                low = (value * spread(share, width) * s2[at : at + size, :].astype(F32)).astype(BF16)
                low_two[at : at + size, :] = low
                total = total + low.astype(F32)
            b2s[row : row + size, :] = total
        grad[...] = dot_back(low_two[...], m2[...])
        m2g[...] += dot_rows(a1[...], low_two[...])
        first = pl.multiple_of(step * (block * 8), 8)
        rows_ref[pl.ds(first + tiles, block, stride=8), :] = index_columns(local_row[...]).astype(F32)
        for row in range(0, rows, size):
            total = own[row : row + size, :]
            for s in range(sb):
                at = s * rows + row
                low = (grad[at : at + size, :] * s1[at : at + size, :].astype(F32)).astype(BF16)
                low_one[at : at + size, :] = low
                low = low.astype(F32)
                total = total + low
                for j in range(tiles):
                    rows_ref[pl.ds(first + at * 8 + j, size, stride=8), :] = low[
                        :, j * LANES : (j + 1) * LANES
                    ]
            own[row : row + size, :] = total
        m1eg[...] += dot_rows(edge[...].reshape(block, edge_width), low_one[...])
        total = (
            low_three[...].astype(F32)
            + dot(low_edge[...], e_first[:, width : width + edge_width])
            + dot_back(low_one[...], m1[width : width + edge_width, :])
        )
        edge_grad[...] = total.reshape(sb, rows, edge_width)

    @pl.when(step >= blocks)
    def _():
        deep = far_keep.shape[0]
        count = block * blocks // groups
        values, local = group_rows(order, (step - blocks) * count, count, rows_ref, moved, width)
        sums = group_sums(values, local, 2 * deep * rows).astype(BF16)
        near = jnp.concatenate(
            [ref[at, 0] for ref in (node_lo, node_hi) for at in range(deep)], axis=0
        )
        m1fg[...] += dot_rows(near, sums)
        height = rows // 16
        for at in range(2 * deep):
            out = (far_keep if at < deep else far_send).at[at % deep, 0]
            for j in range(tiles):
                tile = sums[at * rows : (at + 1) * rows, j * LANES : (j + 1) * LANES]
                out[j * height : (j + 1) * height] = tile.reshape(height, 16, LANES)

    @pl.when(step == blocks + groups - 1)
    def _():
        pack(
            slab,
            [
                dot_rows(node[...], own[...].astype(BF16)),
                m2g[...],
                m1eg[...],
                padded_rows([column_sum(own[...]), column_sum(b2s[...])], width),
                m1fg[...],
            ],
        )
        count = all_tiles(late_shapes(width, edge_width))
        if count < slab.shape[0]:
            slab[count:] = jnp.zeros_like(slab[count:])
        order_out(slab, base[0], codes, keep, send)


def message_backward(
    groups, codes, base, order, v, a1, s1, s2, edge, low_three, low_edge, local_row, live_col, m1, m2,
    e_first, node_lo, node_hi, node,
):
    slots, rows, edge_width = edge.shape
    width = v.shape[1]
    sb = slot_block(slots)
    block = sb * rows
    blocks = slots // sb
    edges = slots * rows
    half = node_lo.shape[0]
    deep = half // rows // groups
    tiles = rows * width // (16 * LANES)
    slab = slab_tiles(late_shapes(width, edge_width), len(codes)) * len(codes)
    node_lo, node_hi = [n.reshape(deep, groups, rows, width) for n in (node_lo, node_hi)]
    blk = lambda i: jnp.minimum(i, blocks - 1)
    group_at = lambda i: (0, jnp.maximum(i - blocks, 0))
    row_spec = pl.BlockSpec((block, width), lambda i: (blk(i), 0))
    slot_spec = pl.BlockSpec((sb, rows, edge_width), lambda i: (blk(i), 0, 0))
    edge_spec = pl.BlockSpec((block, edge_width), lambda i: (blk(i), 0))
    node_spec = pl.BlockSpec((deep, 1, rows, width), lambda i: (*group_at(i), 0, 0))
    far_spec = pl.BlockSpec((deep, 1, tiles, 16, LANES), lambda i: (*group_at(i), 0, 0, 0))
    slab_spec = pl.BlockSpec((slab // 2, 16, LANES), lambda i: (0, 0, 0))
    smem = pl.BlockSpec(memory_space=pltpu.SMEM)
    return pl.pallas_call(
        functools.partial(message_backward_kernel, sb, blocks, groups, codes),
        grid=(blocks + groups,),
        in_specs=[
            smem,
            smem,
            const_spec(v.shape),
            row_spec,
            row_spec,
            row_spec,
            slot_spec,
            edge_spec,
            edge_spec,
            pl.BlockSpec((1, block), lambda i: (0, blk(i))),
            const_spec(live_col.shape),
            const_spec(m1.shape),
            const_spec(m2.shape),
            const_spec(e_first.shape),
            node_spec,
            node_spec,
            const_spec(node.shape),
        ],
        out_specs=[slot_spec, far_spec, far_spec, pl.BlockSpec((rows, width), whole), slab_spec, slab_spec],
        out_shape=[
            jax.ShapeDtypeStruct((slots, rows, edge_width), F32),
            jax.ShapeDtypeStruct((deep, groups, tiles, 16, LANES), BF16),
            jax.ShapeDtypeStruct((deep, groups, tiles, 16, LANES), BF16),
            jax.ShapeDtypeStruct((rows, width), F32),
            jax.ShapeDtypeStruct((slab // 2, 16, LANES), BF16),
            jax.ShapeDtypeStruct((slab // 2, 16, LANES), BF16),
        ],
        scratch_shapes=[
            pltpu.VMEM((block, width), BF16),
            pltpu.VMEM((block, width), BF16),
            pltpu.VMEM((block, width), F32),
            pltpu.VMEM((edges * 8, LANES), F32),
            pltpu.VMEM((edges // groups * 8, LANES), F32),
            pltpu.VMEM((width, width), F32),
            pltpu.VMEM((edge_width, width), F32),
            pltpu.VMEM((width, width), F32),
            pltpu.VMEM((rows, width), F32),
            slab_scratch(slab),
        ],
        compiler_params=pltpu.CompilerParams(vmem_limit_bytes=VMEM),
        name="message_backward",
        cost_estimate=pl.CostEstimate(
            flops=2 * edges * width * (2 * width + 3 * edge_width + half // groups),
            bytes_accessed=edges * width * 6 + edges * edge_width * 10,
            transcendentals=0,
        ),
    )(
        base, order, v, a1, s1, s2, edge, low_three, low_edge, local_row, live_col, m1, m2, e_first,
        node_lo, node_hi, node,
    )


def node_kernel(pieces, g_u1, own, m1, *refs):
    far, grad_out = refs[:pieces], refs[pieces]
    rows, width = own.shape
    height = rows // 16
    tiles = height * (width // LANES)
    sums = far[0][:tiles].astype(F32)
    for ref in far[1:]:
        sums = sums + ref[:tiles].astype(F32)
    far_sum = jnp.concatenate(
        [sums[j * height : (j + 1) * height].reshape(rows, LANES) for j in range(width // LANES)],
        axis=1,
    )
    far_first = m1.shape[0] - width
    grad_out[...] = (
        g_u1[...]
        + fine(dot_back, own[...], m1[:width, :])
        + fine(dot_back, far_sum, m1[far_first:, :])
    )


def node_last(g_u1, own, m1, far):
    return small_call(
        functools.partial(node_kernel, len(far)),
        (g_u1, own, m1, *far), [(own.shape, F32)], "node_gradient",
        flops=8 * own.size * own.shape[1], moved=2 * MIB,
    )[0]


def weights_out_kernel(
    codes, base, first, second,
    m1g, b1, m2g, b2, m3g, e1g, e2g, e3g, b3, g1, g2, fb2, eb1, eb2, eb3, g3, slab, late,
):
    order_in((slab, late), base[0], codes, first, second)
    width, edge_width = m3g.shape[0], e2g.shape[0]
    starts, late_starts = [
        [all_tiles(shapes[:at]) for at in range(len(shapes))]
        for shapes in (early_shapes(width, edge_width), late_shapes(width, edge_width))
    ]
    m3g[...] = unpack(slab, starts[0], width, width)
    e1g[:, :width] = unpack(slab, starts[1], edge_width, width)
    middle = unpack(slab, starts[2], edge_width, edge_width)
    far = unpack(slab, starts[3], edge_width, width)
    over = edge_width % LANES
    base_col = width + edge_width - over
    e1g[:, width:base_col] = middle[:, : edge_width - over]
    far = pltpu.roll(jnp.concatenate([far, jnp.zeros((edge_width, LANES), F32)], axis=1), over, 1)
    lane = lax.broadcasted_iota(jnp.int32, (edge_width, LANES), 1)
    e1g[:, base_col : base_col + LANES] = jnp.where(
        lane < over, middle[:, edge_width - over : edge_width - over + LANES], far[:, :LANES]
    )
    rest = e1g.shape[1] - base_col - LANES
    e1g[:, base_col + LANES :] = far[:, LANES : LANES + rest]
    e2g[...] = unpack(slab, starts[4], edge_width, edge_width)[:, :edge_width]
    e3g[...] = unpack(slab, starts[5], edge_width, edge_width)[:, :edge_width]
    bias = unpack(slab, starts[6], 16, width)
    for row, out in enumerate((g1, g2, fb2, b3)):
        out[...] = bias[row : row + 1]
    bias = unpack(slab, starts[7], 16, edge_width)
    for row, out in enumerate((eb1, eb2, eb3, g3)):
        out[...] = bias[row : row + 1, :edge_width]
    m1g[:width, :] = unpack(late, late_starts[0], width, width)
    m2g[...] = unpack(late, late_starts[1], width, width)
    m1g[width : width + edge_width, :] = unpack(late, late_starts[2], edge_width, width)
    m1g[width + edge_width :, :] = unpack(late, late_starts[4], width, width)
    bias = unpack(late, late_starts[3], 16, width)
    b1[...] = bias[0:1]
    b2[...] = bias[1:2]


def weights_out(codes, base, halves_in, width, edge_width):
    shapes = [(2 * width + edge_width, width), (1, width), (width, width), (1, width)]
    shapes += [(width, width), (edge_width, 2 * width + edge_width)]
    shapes += [(edge_width, edge_width)] * 2 + [(1, width)] * 4 + [(1, edge_width)] * 4
    tiles, late = [
        slab_tiles(shapes, len(codes)) * len(codes)
        for shapes in (early_shapes(width, edge_width), late_shapes(width, edge_width))
    ]
    return small_call(
        functools.partial(weights_out_kernel, codes),
        (base, *halves_in), [(s, F32) for s in shapes], "weight_gradients",
        [slab_scratch(tiles), slab_scratch(late)], moved=10 * MIB, scalars=1,
    )


def exchange(value, mask, devices):
    return lax.ppermute(value, AXES, [(d, d ^ mask) for d in range(devices)])


def mask_groups(masks):
    return [masks[i : min(i + 2, len(masks) - 1)] for i in range(0, len(masks) - 1, 2)] + [masks[-1:]]


def order_codes(groups):
    masks = [mask for group in groups for mask in group]
    return [
        sum(mask for bit, mask in enumerate(masks) if place >> bit & 1)
        for place in range(1 << len(masks))
    ]


def combined(group, code):
    return sum(mask for bit, mask in enumerate(group) if code >> bit & 1)


def sent_around(value, group, devices):
    return [value] + [
        exchange(value, combined(group, code), devices) for code in range(1, 1 << len(group))
    ]


def shared_out(total, group, devices):
    parts = 1 << len(group)
    rows = total.shape[0] // parts
    return [total[:rows]] + [
        exchange(total[code * rows : (code + 1) * rows].astype(BF16), combined(group, code), devices)
        for code in range(1, parts)
    ]


def add_up(terms):
    total = terms[0].astype(F32)
    for term in terms[1:]:
        total = total + term.astype(F32)
    return total


def tied(*values):
    return lax.optimization_barrier(values)


def split_three(value):
    rows = []
    for _ in range(3):
        high = lax.reduce_precision(value, 8, 7)
        rows.append(high.astype(BF16))
        value = value - high
    return jnp.concatenate(rows + [jnp.zeros((13, value.shape[1]), BF16)], axis=0)


def per_device(
    node_in,
    edge_in,
    neighbours,
    live_counts,
    message_first,
    message_first_bias,
    message_second,
    message_second_bias,
    message_third,
    message_third_bias,
    norm_one,
    feed_first,
    feed_first_bias,
    feed_second,
    feed_second_bias,
    norm_two,
    edge_first,
    edge_first_bias,
    edge_second,
    edge_second_bias,
    edge_third,
    edge_third_bias,
    norm_three,
    node_cotangent,
    edge_cotangent,
):
    rows, slots = neighbours.shape
    width = node_in.shape[1]
    edge_width = edge_in.shape[2]
    edges = rows * slots
    hid_count = lax.axis_size("hid")
    res_count = lax.axis_size("res")
    devices = res_count * hid_count
    bits = devices.bit_length() - 1
    masks = [1 << b for b in range(bits - 1, -1, -1)]
    groups = mask_groups(masks)
    codes = order_codes(groups)
    me = lax.axis_index("res") * hid_count + lax.axis_index("hid")
    base = me.reshape(1)
    row = lambda vector: vector.reshape(1, -1)

    names = neighbours.T.reshape(edges)
    apart = (names // rows) ^ me
    place = jnp.zeros_like(names)
    for bit, mask in enumerate(masks):
        place = place | jnp.where((apart & mask) != 0, 1 << bit, 0)
    idx_row = (place * rows + names % rows).reshape(1, edges)
    res_count = devices // hid_count
    local_row = (place // res_count * rows + names % rows).reshape(1, edges)
    edge_order = group_order(place % res_count, res_count)
    live_col = jnp.broadcast_to(live_counts[:, None], (rows, LANES))
    edge = edge_in.transpose(1, 0, 2)
    cot = edge_cotangent.transpose(1, 0, 2)
    e_first = edge_first.T
    e_far = e_first[:, width + edge_width :]
    f1x = jnp.concatenate([feed_first, split_three(row(feed_first_bias))], axis=0)
    f2x = feed_second

    stack = lambda pieces: jnp.concatenate(pieces, axis=0)
    *outer, near = groups

    held = stack(sent_around(node_in, outer[0], devices))
    held, idx_row, local_row, live_col, e_far = tied(held, idx_row, local_row, live_col, e_far)
    for group in outer[1:]:
        held = stack(sent_around(held, group, devices))
    held, f1x, f2x = tied(held, f1x, f2x)
    node_lo, node_hi = sent_around(held, near, devices)

    f1, f2 = [f1x], [f2x]
    hid_masks = [m for m in masks if m < hid_count]
    for mask in hid_masks[:-1]:
        f1, f2 = [pieces + [exchange(p, mask, devices) for p in pieces] for pieces in (f1, f2)]

    a1, s1, s2, total = message_forward(
        node_lo, node_hi, node_in, edge, idx_row, live_col, message_first,
        row(message_first_bias), message_second, row(message_second_bias),
    )
    total, f1, f2 = tied(total, f1, f2)
    f1, f2 = [
        pieces + [exchange(p, hid_masks[-1], devices) for p in pieces] for pieces in (f1, f2)
    ]
    h1b, n1, sc1, n2, sc2, slope, h2b, far_part, own_part = residue_forward(
        node_in, total, message_third, row(message_third_bias), row(norm_one),
        row(feed_second_bias), row(norm_two), e_first, e_far, row(edge_first_bias), f1, f2,
    )

    held = stack(sent_around(far_part, outer[0], devices))
    held, edge_order = tied(held, edge_order)
    for group in outer[1:]:
        held = stack(sent_around(held, group, devices))
    q_lo, q_hi = sent_around(held, near, devices)

    edge_out, act_one, act_two, low_three, low_two, low_one, hi, lo, own_sum, edge_gain = edge_branch(
        q_lo, q_hi, own_part, edge, cot, idx_row, live_col, e_first,
        edge_second, row(edge_second_bias), edge_third, row(edge_third_bias), row(norm_three),
    )

    work = [
        lambda: edge_weights((act_two, act_one), (low_three, low_two), rows),
        lambda: edge_weights((low_one,), (edge,), rows),
    ]
    made = []
    terms = [lo, exchange(hi, near[0], devices)]
    for group in reversed(outer):
        terms = shared_out(add_up(terms), group, devices)
        if work:
            terms, got = tied(terms, work.pop(0)())
            made.append(got)
    while work:
        made.append(work.pop(0)())
    (e3g, e2g, eb3, eb2), (e1g, eb1) = made
    g_u1, v, both, early_keep, early_send = residue_backward(
        codes, base,
        (
            node_cotangent, own_sum, e_first, e_far, h1b, h2b, n1, sc1, n2, sc2, slope, row(norm_one),
            row(norm_two), message_third, total, e1g, e2g, e3g, eb1, eb2, eb3, edge_gain,
        ),
        terms, f1, f2,
    )

    early = [early_keep, exchange(early_send, near[0], devices)]
    b_held = stack(sent_around(both, outer[0], devices))
    first, *others = reversed(outer)
    early_total = add_up(early)
    v, b_held, early_total = tied(v, b_held, early_total)
    early = shared_out(early_total, first, devices)
    for group in outer[1:]:
        b_held = stack(sent_around(b_held, group, devices))
    edge_grad, far_keep, far_send, own, keep, send = message_backward(
        res_count, codes, base, edge_order, v, a1, s1, s2, edge, low_three, low_one, local_row, live_col,
        message_first, message_second, e_first, node_lo, node_hi, node_in,
    )

    terms = [keep, exchange(send, near[0], devices)]
    early, b_held, far_keep = tied(early, b_held, far_keep)
    for group in others:
        early = shared_out(add_up(early), group, devices)
    total, b_held, far_send = tied(add_up(terms), b_held, far_send)
    terms = shared_out(total, first, devices)
    far_keep, far_send = [far.reshape(-1, 16, LANES) for far in (far_keep, far_send)]
    far_terms = [far_keep, exchange(far_send, near[0], devices)]
    b_near = sent_around(b_held, near, devices)
    total, b_first = tied(add_up(far_terms), b_near[0])
    far_terms = shared_out(total, first, devices)
    feed = feed_gradients((b_first, b_near[1]), feed_first, row(feed_first_bias), feed_second)
    terms, (f1g, f2g, fb1g) = tied(terms, feed)
    for group in others:
        terms = shared_out(add_up(terms), group, devices)
        far_terms = shared_out(add_up(far_terms), group, devices)
    held = jnp.concatenate([add_up(early), add_up(terms)], axis=0).astype(BF16)

    for at, group in enumerate(outer):
        around = sent_around(held, group, devices)
        if at + 1 == len(outer):
            around, node_gradient = tied(around, node_last(g_u1, own, message_first, far_terms))
        held = stack(around)
    m1g, b1, m2g, b2, m3g, e1g, e2g, e3g, b3, g1, g2, fb2, eb1, eb2, eb3, g3 = weights_out(
        codes, base, sent_around(held, near, devices), width, edge_width
    )
    flat = lambda vector: vector.reshape(-1)
    return (
        h2b,
        edge_out.transpose(1, 0, 2),
        node_gradient,
        edge_grad.transpose(1, 0, 2),
        m1g,
        flat(b1),
        m2g,
        flat(b2),
        m3g,
        flat(b3),
        flat(g1),
        f1g,
        flat(fb1g),
        f2g,
        flat(fb2),
        flat(g2),
        e1g.T,
        flat(eb1),
        e2g,
        flat(eb2),
        e3g,
        flat(eb3),
        flat(g3),
    )


def solution(mesh):
    nodes, edges, shared = P(AXES, None), P(AXES, None, None), P()
    return jax.shard_map(
        per_device,
        mesh=mesh,
        in_specs=(nodes, edges, nodes, P(AXES))
        + (shared,) * 7
        + (P(None, "hid"), P("hid"), P("hid", None))
        + (shared,) * 9
        + (nodes, edges),
        out_specs=(nodes, edges, nodes, edges)
        + (shared,) * 7
        + (P(None, "hid"), P("hid"), P("hid", None))
        + (shared,) * 9,
        check_vma=False,
    )
```

```python
import functools

import jax
import jax.numpy as jnp
from jax import lax
from jax.experimental import pallas as pl
from jax.experimental.pallas import tpu as pltpu
from jax.sharding import PartitionSpec as P

EPS = 1e-05
AXES = ("res", "hid")
F32 = jnp.float32
BF16 = jnp.bfloat16
TANH_SCALE = 0.7978845608028654
TANH_CUBE = 0.044715
LANES = 128
CHUNK = 2048
MIB = 1024 * 1024
VMEM = 58 * MIB


def dot(left, right):
    return lax.dot_general(left, right, (((1,), (0,)), ((), ())), preferred_element_type=F32)


def dot_rows(left, right):
    return lax.dot_general(left, right, (((0,), (0,)), ((), ())), preferred_element_type=F32)


def dot_back(left, right):
    return lax.dot_general(left, right, (((1,), (1,)), ((), ())), preferred_element_type=F32)


def halves(value):
    high = value.astype(BF16)
    return high, (value - high.astype(F32)).astype(BF16)


def fine(product, value, weights):
    high, low = halves(value)
    return product(high, weights) + product(low, weights)


def gelu_parts(x):
    square = x * x
    t = jnp.tanh(x * (TANH_SCALE + (TANH_SCALE * TANH_CUBE) * square))
    gate = 0.5 + 0.5 * t
    act = x * gate
    slope = gate + act * (1.0 - gate) * (2 * TANH_SCALE + (6 * TANH_SCALE * TANH_CUBE) * square)
    return act, slope


def index_columns(idx_row):
    parts = [
        jnp.broadcast_to(idx_row[:, first : first + LANES], (LANES, LANES)).T
        for first in range(0, idx_row.shape[1], LANES)
    ]
    return jnp.concatenate(parts, axis=0)


def one_hot_columns(idx, start, count):
    one, zero = jnp.ones((), BF16), jnp.zeros((), BF16)
    idx = idx.astype(jnp.int16)
    lane = lax.broadcasted_iota(jnp.int32, idx.shape, 1).astype(jnp.int16)
    parts = [
        jnp.where(idx == lane + jnp.int16(start + first), one, zero)
        for first in range(0, count, LANES)
    ]
    return jnp.concatenate(parts, axis=1)


def pick_rows(idx, table_refs):
    total, start = None, 0
    for ref in table_refs:
        rows = ref.shape[0]
        step = min(rows, CHUNK)
        for first in range(0, rows, step):
            part = dot(one_hot_columns(idx, start + first, step), ref[first : first + step, :])
            total = part if total is None else total + part
        start += rows
    return total


def one_hot_rows(idx_row, start, count):
    shape = (count, idx_row.shape[1])
    row = (lax.broadcasted_iota(jnp.int32, shape, 0) + start).astype(jnp.int16)
    names = jnp.broadcast_to(idx_row, shape).astype(jnp.int16)
    return jnp.where(names == row, jnp.ones((), BF16), jnp.zeros((), BF16))


def group_rows(order, first, count, rows_ref, moved, width):
    for e in range(count):
        at = pl.multiple_of(order[0, first + e] * 8, 8)
        moved[e * 8 : e * 8 + 8, :] = rows_ref[pl.ds(at, 8), :]

    def column(at):
        return moved[pl.ds(at, count, stride=8), :]

    tiles = pl.cdiv(width, LANES)
    parts = [column(at)[:, : min(LANES, width - at * LANES)] for at in range(tiles)]
    return jnp.concatenate(parts, axis=1).astype(BF16), column(tiles)


def group_sums(rows, local, residues):
    lane = lax.broadcasted_iota(jnp.int32, local.shape, 1).astype(F32)
    picks = [
        jnp.where(local == lane + float(first), 1.0, 0.0).astype(BF16)
        for first in range(0, residues, LANES)
    ]
    return dot_rows(jnp.concatenate(picks, axis=1), rows)


def order_kernel(groups, count, names, out):
    rows = names.shape[0]
    row = lax.broadcasted_iota(jnp.int32, (LANES, LANES), 0)
    column = lax.broadcasted_iota(jnp.int32, (LANES, LANES), 1)
    upto = jnp.where(row <= column, 1.0, 0.0).astype(BF16)
    ones = jnp.ones((LANES, LANES), BF16)
    above = lax.broadcasted_iota(jnp.int32, (rows, rows), 0)
    before = jnp.where(lax.broadcasted_iota(jnp.int32, (rows, rows), 1) < above, 1.0, 0.0).astype(BF16)
    place = jnp.full(names.shape, float(2 * LANES * LANES), F32)
    for group in range(groups):
        here = names[...] == group
        low = jnp.where(here, 1.0, 0.0).astype(BF16)
        rank = dot(low, upto) + dot(before, dot(low, ones).astype(BF16))
        place = jnp.where(here, rank + float(group * count - 1), place)
    high = total = None
    for at in range(rows):
        where = jnp.broadcast_to(place[at : at + 1, :], (LANES, LANES)).T.astype(jnp.int32)
        left = jnp.where(where // LANES == column, 1.0, 0.0)
        right = jnp.where(where % LANES == column, 1.0, 0.0)
        part = dot_rows(left.astype(BF16), (right * float(at)).astype(BF16))
        high = part if high is None else high + part
        part = dot_rows(left.astype(BF16), (right * row.astype(F32)).astype(BF16))
        total = part if total is None else total + part
    number = high * float(LANES) + total
    out[...] = number[: out.shape[0], : out.shape[1]].astype(jnp.int32)


def group_order(names, groups):
    edges = names.shape[0]
    rows = pl.cdiv(pl.cdiv(edges, LANES), 8) * 8
    padded = jnp.pad(names, (0, rows * LANES - edges), constant_values=groups)
    out = small_call(
        functools.partial(order_kernel, groups, edges // groups),
        (padded.reshape(rows, LANES),), [((edges // LANES, LANES), jnp.int32)], "group_order",
    )[0]
    return out.reshape(1, edges)


def spread(column, width):
    return jnp.concatenate([column] * (width // LANES), axis=1)


def norm(value):
    centre = value - jnp.mean(value, -1, keepdims=True)
    scale = lax.rsqrt(jnp.mean(centre * centre, -1, keepdims=True) + EPS)
    return centre * scale, scale


def norm_back(inner, normed, scale):
    mean_first = jnp.mean(inner, -1, keepdims=True)
    mean_second = jnp.mean(inner * normed, -1, keepdims=True)
    return scale * (inner - mean_first - normed * mean_second)


def column_sum(value):
    return jnp.sum(value, axis=0, keepdims=True)


def whole(*_):
    return (0, 0)


def const_spec(shape):
    return pl.BlockSpec(shape, lambda *_: (0,) * len(shape), pipeline_mode=pl.Buffered(1))


def small_call(kernel, args, shapes, name, scratch=(), flops=0, moved=0, exps=0, scalars=0):
    return pl.pallas_call(
        kernel,
        grid=(1,),
        in_specs=[pl.BlockSpec(memory_space=pltpu.SMEM)] * scalars
        + [const_spec(a.shape) for a in args[scalars:]],
        out_specs=[pl.BlockSpec(s, lambda *_, n=len(s): (0,) * n) for s, _ in shapes],
        out_shape=[jax.ShapeDtypeStruct(*s) for s in shapes],
        scratch_shapes=list(scratch),
        compiler_params=pltpu.CompilerParams(vmem_limit_bytes=VMEM),
        name=name,
        cost_estimate=pl.CostEstimate(flops=flops, bytes_accessed=moved, transcendentals=exps),
    )(*args)


def tile_count(shape):
    return pl.cdiv(shape[0], 16) * pl.cdiv(shape[1], LANES)


def all_tiles(shapes):
    return sum(tile_count(s) for s in shapes)


def pack(slab, values, at=0):
    for value in values:
        rows, columns = value.shape
        count = rows // 16
        for first in range(0, columns, LANES):
            take = min(LANES, columns - first)
            tile = value[:, first : first + take].astype(BF16).reshape(count, 16, take)
            slab[at : at + count, :, :take] = tile
            at += count


def unpack(slab, at, rows, columns):
    count = rows // 16
    parts = [
        slab[at + i * count : at + (i + 1) * count].reshape(rows, LANES).astype(F32)
        for i in range(pl.cdiv(columns, LANES))
    ]
    return jnp.concatenate(parts, axis=1)


def order_out(slab, base, codes, keep, send):
    size = slab.shape[0] // len(codes)
    half = len(codes) // 2
    for place, code in enumerate(codes):
        out = keep if place < half else send
        at = (place % half) * size
        out[at : at + size] = slab[pl.ds((base ^ code) * size, size)]


def half_shapes(tiles):
    return [((tiles // 2, 16, LANES), BF16)] * 2


def slab_scratch(tiles):
    return pltpu.VMEM((tiles, 16, LANES), BF16)


def slab_tiles(shapes, chunks):
    return pl.cdiv(all_tiles(shapes), chunks)


def order_in(slab, base, codes, first, second):
    size = slab.shape[0] // len(codes)
    half = len(codes) // 2
    for place, code in enumerate(codes):
        source = first if place < half else second
        at = (place % half) * size
        slab[pl.ds((base ^ code) * size, size)] = source[at : at + size]


def padded_rows(parts, width):
    return jnp.concatenate(parts + [jnp.zeros((16 - len(parts), width), F32)], axis=0)


def slot_block(slots):
    for size in (10, 12, 8, 6, 5, 4, 3, 2):
        if slots % size == 0:
            return size
    return 1


def far_table(node_lo, node_hi, weights, put):
    tile = min(512, node_lo.shape[0])
    for source, start in ((node_lo, 0), (node_hi, node_lo.shape[0])):
        def body(i, carry, source=source, start=start):
            at = pl.multiple_of(i * tile, tile)
            put(start + at, dot(source[pl.ds(at, tile), :], weights))
            return carry
        lax.fori_loop(0, source.shape[0] // tile, body, 0)


def message_forward_kernel(
    sb, by_rows, node_lo, node_hi, node_own, edge, idx_row, names, live_col, m1, b1, m2, b2,
    a1_out, s1_out, s2_out, sum_out, table, far, near, lhs, z,
):
    step = pl.program_id(0)
    width = node_own.shape[1]
    edge_width = edge.shape[2]
    rows = edge.shape[1]
    block = sb * rows
    lanes = width // LANES

    @pl.when(step == 0)
    def _():
        weights = m1[width + edge_width :, :]
        if by_rows:
            def put(first, value):
                for at in range(8):
                    column = at % lanes * LANES
                    table[pl.ds(first * 8 + at, value.shape[0], stride=8), :] = value[
                        :, column : column + LANES
                    ]
        else:
            def put(first, value):
                table[pl.ds(first, value.shape[0]), :] = value.astype(BF16)
        far_table(node_lo, node_hi, weights, put)
        near[:edge_width, :] = m1[width : width + edge_width, :]
        near[edge_width:, :] = jnp.zeros_like(near[edge_width:, :])
        near[edge_width : edge_width + rows, :] = (
            dot(node_own[...], m1[:width, :]) + b1[...]
        ).astype(BF16)
        shape = (rows, near.shape[0] - edge_width)
        eye = lax.broadcasted_iota(jnp.int32, shape, 0) == lax.broadcasted_iota(jnp.int32, shape, 1)
        for at in range(0, block, rows):
            lhs[at : at + rows, edge_width:] = jnp.where(eye, 1.0, 0.0).astype(BF16)
        sum_out[...] = jnp.zeros_like(sum_out)

    lhs[:, :edge_width] = edge[...].reshape(block, edge_width)
    z[...] = dot(lhs[...], near[...])
    if not by_rows:
        z[...] += pick_rows(index_columns(idx_row[...]), (table,))
    upper = lax.broadcasted_iota(jnp.int32, (8, LANES), 0) < lanes

    def fetch(at):
        for e in range(at, at + 16, 2):
            pair = [
                table[pl.ds(pl.multiple_of(names[0, step * block + e + i] * 8, 8), 8), :]
                for i in range(2)
            ]
            far[e * lanes : e * lanes + 8, :] = jnp.where(upper, *pair)

    def fetched(at):
        return jnp.concatenate(
            [far[pl.ds(at * lanes + j, 16, stride=lanes), :] for j in range(lanes)], axis=1
        )

    if by_rows:
        fetch(0)
    for at in range(0, block, 16):
        value = z[at : at + 16, :]
        if by_rows:
            if at + 16 < block:
                fetch(at + 16)
            value = value + fetched(at)
        act, slope = gelu_parts(value)
        a1_out[at : at + 16, :] = act.astype(BF16)
        s1_out[at : at + 16, :] = slope.astype(BF16)
    z[...] = dot(a1_out[...], m2[...])
    bias = b2[...]
    for row in range(0, rows, 16):
        count = live_col[row : row + 16, :]
        inverse = 1.0 / count.astype(F32)
        total = sum_out[row : row + 16, :]
        for s in range(sb):
            at = s * rows + row
            act, slope = gelu_parts(z[at : at + 16, :] + bias)
            s2_out[at : at + 16, :] = slope.astype(BF16)
            share = jnp.where(count > step * sb + s, inverse, 0.0)
            total = total + act.astype(BF16).astype(F32) * spread(share, width)
        sum_out[row : row + 16, :] = total


def message_forward(node_lo, node_hi, node_own, edge, idx_row, live_col, m1, b1, m2, b2):
    slots, rows, edge_width = edge.shape
    width = node_own.shape[1]
    residues = 2 * node_lo.shape[0]
    by_rows = residues <= 4096 and width == 4 * LANES
    sb = slot_block(slots) if by_rows else 4
    block = sb * rows
    edges = slots * rows
    near = pl.cdiv(edge_width + rows, LANES) * LANES
    row_spec = pl.BlockSpec((block, width), lambda i: (i, 0))
    return pl.pallas_call(
        functools.partial(message_forward_kernel, sb, by_rows),
        grid=(slots // sb,),
        in_specs=[
            const_spec(node_lo.shape),
            const_spec(node_hi.shape),
            const_spec(node_own.shape),
            pl.BlockSpec((sb, rows, edge_width), lambda i: (i, 0, 0)),
            pl.BlockSpec((1, block), lambda i: (0, i)),
            pl.BlockSpec(memory_space=pltpu.SMEM),
            const_spec(live_col.shape),
            const_spec(m1.shape),
            const_spec(b1.shape),
            const_spec(m2.shape),
            const_spec(b2.shape),
        ],
        out_specs=[row_spec, row_spec, row_spec, pl.BlockSpec((rows, width), whole)],
        out_shape=[jax.ShapeDtypeStruct((edges, width), BF16)] * 3
        + [jax.ShapeDtypeStruct((rows, width), F32)],
        scratch_shapes=[
            pltpu.VMEM((residues * 8, LANES), F32) if by_rows else pltpu.VMEM((residues, width), BF16),
            pltpu.VMEM((block * 4 if by_rows else 8, LANES), F32),
            pltpu.VMEM((near, width), BF16),
            pltpu.VMEM((block, near), BF16),
            pltpu.VMEM((block, width), F32),
        ],
        compiler_params=pltpu.CompilerParams(vmem_limit_bytes=VMEM),
        name="message_forward",
        cost_estimate=pl.CostEstimate(
            flops=2 * edges * width * (residues + edge_width + width),
            bytes_accessed=edges * width * 6 + edges * edge_width * 2 + edges * LANES * 4,
            transcendentals=2 * edges * width,
        ),
    )(node_lo, node_hi, node_own, edge, idx_row, idx_row, live_col, m1, b1, m2, b2)


def residue_forward_kernel(parts, node, total, m3, b3, g1, fb2, g2, e_first, e_far, eb, *refs):
    f1, f2 = refs[:parts], refs[parts : 2 * parts]
    h1b_out, n1_out, sc1_out, n2_out, sc2_out, slope_out, h2b_out, far_out, own_out = refs[2 * parts :]
    width, hidden = node.shape[1], f1[0].shape[1]
    u1 = node[...].astype(F32) + fine(dot, total[...], m3[...]) + b3[...]
    n1, sc1 = norm(u1)
    h1 = n1 * g1[...]
    h1b = h1.astype(BF16)
    h1b_out[...] = h1b
    n1_out[...] = n1
    sc1_out[...] = jnp.broadcast_to(sc1, sc1_out.shape)
    y2 = None
    for p in range(parts):
        bias = f1[p][width : width + 16, :].astype(F32)
        bias = bias[0:1] + bias[1:2] + bias[2:3]
        act, slope = gelu_parts(dot(h1b, f1[p][:width, :]) + bias)
        slope_out[:, p * hidden : (p + 1) * hidden] = slope
        part = dot(act.astype(BF16), f2[p][...])
        y2 = part if y2 is None else y2 + part
    n2, sc2 = norm(h1 + (y2 + fb2[...]))
    h2b = (n2 * g2[...]).astype(BF16)
    n2_out[...] = n2
    sc2_out[...] = jnp.broadcast_to(sc2, sc2_out.shape)
    h2b_out[...] = h2b
    far_out[...] = dot_back(h2b, e_far[...]).astype(BF16)
    own_out[...] = dot_back(h2b, e_first[:, :width]) + eb[...]


def residue_forward(node, total, m3, b3, g1, fb2, g2, e_first, e_far, eb, f1, f2):
    rows, width = node.shape
    edge_width = e_first.shape[0]
    hidden = len(f1) * f1[0].shape[1]
    shapes = [
        ((rows, width), BF16),
        ((rows, width), F32),
        ((rows, LANES), F32),
        ((rows, width), F32),
        ((rows, LANES), F32),
        ((rows, hidden), F32),
        ((rows, width), BF16),
        ((rows, edge_width), BF16),
        ((rows, edge_width), F32),
    ]
    return small_call(
        functools.partial(residue_forward_kernel, len(f1)),
        (node, total, m3, b3, g1, fb2, g2, e_first, e_far, eb, *f1, *f2),
        shapes, "residue_forward", flops=4 * rows * width * hidden, moved=5 * MIB,
        exps=rows * hidden,
    )


def edge_kernel(
    sb, blocks, hi_chunks, by_rows, far_lo, far_hi, own, edge, cot, idx, idx_row, names, live_col,
    e_first, e2, eb2, e3, eb3, g3,
    edge_out, act_one_out, act_two_out, low_three_out, low_two_out, low_one_out, hi_out, lo_out, own_out, gain_out,
    low_first, gs, table, far, z, slope_ref,
):
    step = pl.program_id(0)
    rows, width = own.shape
    node_width = (e_first.shape[1] - width) // 2
    e_mid = e_first.at[:, node_width : node_width + width]
    tiles = pl.cdiv(width, LANES)
    per = 8 // tiles
    size = 32

    @pl.when(step == 0)
    def _():
        own_out[...] = jnp.zeros_like(own_out)
        gs[...] = jnp.zeros_like(gs)
        half = far_lo.shape[0]
        if by_rows:
            for source, start in ((far_lo, 0), (far_hi, half)):
                for first in range(0, half, 512):
                    value = source[first : first + 512, :].astype(F32)
                    for at in range(8):
                        column = at % tiles * LANES
                        take = min(LANES, width - column)
                        table[pl.ds((start + first) * 8 + at, value.shape[0], stride=8), :take] = value[
                            :, column : column + take
                        ]

    @pl.when(step < blocks)
    def _():
        block = sb * rows
        flat = edge[...].reshape(block, width)
        z[...] = dot_back(flat, e_mid[...])
        if not by_rows:
            z[...] += pick_rows(index_columns(idx[...]), (far_lo, far_hi))
        sub = lax.broadcasted_iota(jnp.int32, (8, LANES), 0)

        def fetch(at):
            for e in range(at, at + size, per):
                got = [
                    table[pl.ds(pl.multiple_of(names[0, step * block + e + i] * 8, 8), 8), :]
                    for i in range(per)
                ]
                value = got[-1]
                for i in range(per - 2, -1, -1):
                    value = jnp.where(sub < (i + 1) * tiles, got[i], value)
                far[e * tiles : e * tiles + 8, :] = value

        def fetched(at):
            parts = [
                far[pl.ds(at * tiles + j, size, stride=tiles), :][:, : min(LANES, width - j * LANES)]
                for j in range(tiles)
            ]
            return jnp.concatenate(parts, axis=1)

        if by_rows:
            fetch(0)
        for at in range(0, block, size):
            value = z[at : at + size, :] + own[at % rows : at % rows + size, :]
            if by_rows:
                if at + size < block:
                    fetch(at + size)
                value = value + fetched(at)
            act, slope = gelu_parts(value)
            act_one_out[at : at + size, :] = act.astype(BF16)
            slope_ref[at : at + size, :] = slope
        act_one = act_one_out[...]
        act_two, slope_two = gelu_parts(dot(act_one, e2[...]) + eb2[...])
        act_two = act_two.astype(BF16)
        act_two_out[...] = act_two
        w_three = dot(act_two, e3[...]) + eb3[...]
        normed, scale = norm(flat.astype(F32) + w_three)
        count = spread(live_col[...], pl.cdiv(width, LANES) * LANES)[:, :width]
        live = jnp.concatenate(
            [jnp.where(count > step * sb + s, 1.0, 0.0) for s in range(sb)], axis=0
        )
        edge_out[...] = (normed * g3[...] * live).astype(BF16).reshape(sb, rows, width)
        grad = cot[...].reshape(block, width).astype(F32) * live
        gs[...] += jnp.sum((grad * normed).reshape(sb, rows, width), axis=0)
        low_three = norm_back(grad * g3[...], normed, scale).astype(BF16)
        low_three_out[...] = low_three
        low_two = (dot_back(low_three, e3[...]) * slope_two).astype(BF16)
        low_two_out[...] = low_two
        low_one = (dot_back(low_two, e2[...]) * slope_ref[...]).astype(BF16)
        low_one_out[...] = low_one
        own_out[...] += jnp.sum(low_one.astype(F32).reshape(sb, rows, width), axis=0)
        low_first[pl.ds(pl.multiple_of(step * block, block), block), :] = low_one

    chunk = hi_out.shape[0]

    @pl.when((step >= blocks) & (step < blocks + hi_chunks))
    def _():
        start = (step - blocks + hi_chunks) * chunk
        hi_out[...] = dot(one_hot_rows(idx_row[...], start, chunk), low_first[...]).astype(BF16)

    @pl.when(step >= blocks + hi_chunks)
    def _():
        start = (step - blocks - hi_chunks) * chunk
        lo_out[...] = dot(one_hot_rows(idx_row[...], start, chunk), low_first[...])

    @pl.when(step == blocks + 2 * hi_chunks - 1)
    def _():
        gain_out[...] = column_sum(gs[...])


def edge_branch(far_lo, far_hi, own, edge, cot, idx_row, live_col, e_first, e2, eb2, e3, eb3, g3):
    slots, rows, width = edge.shape
    sb = slot_block(slots)
    edges = slots * rows
    block = sb * rows
    blocks = slots // sb
    half = far_lo.shape[0]
    chunk = min(512, half)
    hi_chunks = half // chunk
    by_rows = half <= 2048 and 8 % pl.cdiv(width, LANES) == 0
    blk = lambda i: jnp.minimum(i, blocks - 1)
    hi_at = lambda i: (jnp.clip(i - blocks, 0, hi_chunks - 1), 0)
    lo_at = lambda i: (jnp.clip(i - blocks - hi_chunks, 0, hi_chunks - 1), 0)
    slot_spec = pl.BlockSpec((sb, rows, width), lambda i: (blk(i), 0, 0))
    row_spec = pl.BlockSpec((block, width), lambda i: (blk(i), 0))
    return pl.pallas_call(
        functools.partial(edge_kernel, sb, blocks, hi_chunks, by_rows),
        grid=(blocks + 2 * hi_chunks,),
        in_specs=[
            const_spec(far_lo.shape),
            const_spec(far_hi.shape),
            const_spec(own.shape),
            slot_spec,
            slot_spec,
            pl.BlockSpec((1, block), lambda i: (0, blk(i))),
            const_spec(idx_row.shape),
            pl.BlockSpec(memory_space=pltpu.SMEM),
            const_spec(live_col.shape),
            const_spec(e_first.shape),
            const_spec(e2.shape),
            const_spec(eb2.shape),
            const_spec(e3.shape),
            const_spec(eb3.shape),
            const_spec(g3.shape),
        ],
        out_specs=[slot_spec]
        + [row_spec] * 5
        + [
            pl.BlockSpec((chunk, width), hi_at),
            pl.BlockSpec((chunk, width), lo_at),
            pl.BlockSpec((rows, width), whole),
            pl.BlockSpec((1, width), whole),
        ],
        out_shape=[jax.ShapeDtypeStruct((slots, rows, width), BF16)]
        + [jax.ShapeDtypeStruct((edges, width), BF16)] * 5
        + [
            jax.ShapeDtypeStruct((half, width), BF16),
            jax.ShapeDtypeStruct((half, width), F32),
            jax.ShapeDtypeStruct((rows, width), F32),
            jax.ShapeDtypeStruct((1, width), F32),
        ],
        scratch_shapes=[
            pltpu.VMEM((edges, width), BF16),
            pltpu.VMEM((rows, width), F32),
            pltpu.VMEM((half * 16 if by_rows else 8, LANES), F32),
            pltpu.VMEM((block * 8, LANES), F32),
            pltpu.VMEM((block, width), F32),
            pltpu.VMEM((block, width), F32),
        ],
        compiler_params=pltpu.CompilerParams(vmem_limit_bytes=VMEM),
        name="edge_branch",
        cost_estimate=pl.CostEstimate(
            flops=2 * edges * width * (4 * half + 5 * width),
            bytes_accessed=edges * width * 16,
            transcendentals=2 * edges * width,
        ),
    )(far_lo, far_hi, own, edge, cot, idx_row, idx_row, idx_row, live_col, e_first, e2, eb2, e3, eb3, g3)


def edge_weights_kernel(blocks, pairs, *refs):
    step = pl.program_id(0)
    lefts, rights = refs[:pairs], refs[pairs : 2 * pairs]
    grads, biases, sums = refs[2 * pairs : 3 * pairs], refs[3 * pairs : 4 * pairs], refs[-1]
    rows = sums.shape[1]

    @pl.when(step == 0)
    def _():
        for ref in (*grads, sums):
            ref[...] = jnp.zeros_like(ref)

    for at in range(pairs):
        left, right = [r[...].reshape(-1, r.shape[-1]) for r in (lefts[at], rights[at])]
        grads[at][...] += dot_rows(left, right)
        low = left if lefts[at].ndim < rights[at].ndim else right
        sums[at] += jnp.sum(low.astype(F32).reshape(-1, rows, low.shape[1]), axis=0)

    @pl.when(step == blocks - 1)
    def _():
        for at in range(pairs):
            biases[at][...] = column_sum(sums[at])


def edge_weights(lefts, rights, rows):
    pairs = len(lefts)
    edges, width = lefts[0].shape
    slots = edges // rows
    sb = slot_block(slots)

    def spec(array):
        if array.ndim == 3:
            return pl.BlockSpec((sb, rows, width), lambda i: (i, 0, 0))
        return pl.BlockSpec((sb * rows, width), lambda i: (i, 0))

    shapes = [(width, width)] * pairs + [(1, width)] * pairs
    return pl.pallas_call(
        functools.partial(edge_weights_kernel, slots // sb, pairs),
        grid=(slots // sb,),
        in_specs=[spec(array) for array in (*lefts, *rights)],
        out_specs=[pl.BlockSpec(s, whole) for s in shapes],
        out_shape=[jax.ShapeDtypeStruct(s, F32) for s in shapes],
        scratch_shapes=[pltpu.VMEM((pairs, rows, width), F32)],
        compiler_params=pltpu.CompilerParams(vmem_limit_bytes=VMEM),
        name="edge_weights",
        cost_estimate=pl.CostEstimate(
            flops=2 * pairs * edges * width * width,
            bytes_accessed=pairs * edges * width * 4,
            transcendentals=0,
        ),
    )(*lefts, *rights)


def early_shapes(width, edge_width):
    return [
        (width, width),
        (edge_width, width),
        (edge_width, width),
        (edge_width, edge_width),
        (edge_width, edge_width),
        (16, width),
        (16, edge_width),
    ]


def residue_backward_kernel(
    parts, pieces, node_cot, own_sum, e_first, e_far, h1b, h2b, n1, sc1, n2, sc2, slope, g1, g2, m3,
    total, e2g, e3g, eb2, eb3, edge_gain, *refs,
):
    far = refs[:pieces]
    f1 = refs[pieces : pieces + parts]
    f2 = refs[pieces + parts : pieces + 2 * parts]
    gu1_out, v_out, both_out, slab = refs[pieces + 2 * parts :]
    width, hidden = h2b.shape[1], f1[0].shape[1]
    far_sum = far[0][...]
    for ref in far[1:]:
        far_sum = far_sum + ref[...].astype(F32)
    own = own_sum[...]
    g_h2 = (
        node_cot[...].astype(F32)
        + fine(dot, own, e_first[:, :width])
        + fine(dot, far_sum, e_far[...])
    )
    gain_two = column_sum(g_h2 * n2[...])
    g_u2 = norm_back(g_h2 * g2[...], n2[...], sc2[:, :1])
    gy2 = g_u2.astype(BF16)
    both_out[:, :width] = h1b[...]
    both_out[:, width:] = gy2
    g_h1 = g_u2
    for p in range(parts):
        gy1 = dot_back(gy2, f2[p][...]) * slope[:, p * hidden : (p + 1) * hidden]
        g_h1 = g_h1 + dot_back(gy1.astype(BF16), f1[p][:width, :])
    gain_one = column_sum(g_h1 * n1[...])
    g_u1 = norm_back(g_h1 * g1[...], n1[...], sc1[:, :1])
    gu1_out[...] = g_u1
    v_out[...] = fine(dot_back, g_u1, m3[...])
    bias = [gain_one, gain_two, column_sum(gy2.astype(F32)), column_sum(g_u1)]
    slab[...] = jnp.zeros_like(slab)
    pack(
        slab,
        [
            dot_rows(total[...].astype(BF16), g_u1.astype(BF16)),
            dot_rows(own.astype(BF16), h2b[...]),
            dot_rows(far_sum.astype(BF16), h2b[...]),
            e2g[...],
            e3g[...],
            padded_rows(bias, width),
            padded_rows([eb2[...], eb3[...], edge_gain[...]], own.shape[1]),
        ],
    )


def residue_backward(args, far, f1, f2):
    node_cot, e_first, slope = args[0], args[2], args[10]
    rows, width = node_cot.shape
    shapes = [
        ((rows, width), F32),
        ((rows, width), F32),
        ((rows, 2 * width), BF16),
        ((all_tiles(early_shapes(width, e_first.shape[0])), 16, LANES), BF16),
    ]
    return small_call(
        functools.partial(residue_backward_kernel, len(f1), len(far)),
        (*args, *far, *f1, *f2),
        shapes, "residue_backward",
        flops=4 * rows * width * slope.shape[1], moved=8 * MIB,
    )


def feed_kernel(first, second, f1, fb1, f2, f1g, f2g, fb1g):
    width = f1.shape[0]

    @pl.when(pl.program_id(0) == 0)
    def _():
        for ref in (f1g, f2g, fb1g):
            ref[...] = jnp.zeros_like(ref)

    for both in (first, second):
        h1b, gy2 = both[:, :width], both[:, width:]
        act, slope = gelu_parts(dot(h1b, f1[...]) + fb1[...])
        gy1 = (dot_back(gy2, f2[...]) * slope).astype(BF16)
        f1g[...] += dot_rows(h1b, gy1)
        f2g[...] += dot_rows(act.astype(BF16), gy2)
        fb1g[...] += column_sum(gy1.astype(F32))


def feed_gradients(both, f1, fb1, f2):
    width, hidden = f1.shape
    half = both[0].shape[0]
    chunk = min(512, half)
    shapes = [(width, hidden), (hidden, width), (1, hidden)]
    return pl.pallas_call(
        feed_kernel,
        grid=(half // chunk,),
        in_specs=[pl.BlockSpec((chunk, 2 * width), lambda i: (i, 0))] * 2
        + [const_spec(a.shape) for a in (f1, fb1, f2)],
        out_specs=[pl.BlockSpec(s, whole) for s in shapes],
        out_shape=[jax.ShapeDtypeStruct(s, F32) for s in shapes],
        compiler_params=pltpu.CompilerParams(vmem_limit_bytes=VMEM),
        name="feed_gradients",
        cost_estimate=pl.CostEstimate(
            flops=16 * half * width * hidden,
            bytes_accessed=8 * half * width,
            transcendentals=2 * half * hidden,
        ),
    )(*both, f1, fb1, f2)


def late_shapes(width, edge_width):
    return [
        (width, width),
        (width, width),
        (edge_width, width),
        (16, width),
        (width, width),
        (edge_width, edge_width),
    ]


def weight_shapes(width, edge_width):
    return early_shapes(width, edge_width) + late_shapes(width, edge_width)


def message_backward_kernel(
    sb, blocks, groups, codes, base, order, v, a1, s1, s2, edge, low_three, low_edge, local_row, live_col,
    m1, m2, e_first, node_lo, node_hi, node, early, e1g, eb1,
    edge_grad, far_keep, far_send, own, keep, send,
    low_two, low_one, grad, rows_ref, moved, m2g, m1eg, m1fg, b2s, slab,
):
    step = pl.program_id(0)
    rows, width = v.shape
    edge_width = edge.shape[2]
    block = sb * rows
    tiles = width // LANES
    size = 16

    @pl.when(step == 0)
    def _():
        for ref in (own, m2g, m1eg, m1fg, b2s):
            ref[...] = jnp.zeros_like(ref)

    @pl.when(step < blocks)
    def _():
        for row in range(0, rows, size):
            count = live_col[row : row + size, :]
            inverse = 1.0 / count.astype(F32)
            value = v[row : row + size, :]
            total = b2s[row : row + size, :]
            for s in range(sb):
                at = s * rows + row
                share = jnp.where(count > step * sb + s, inverse, 0.0)
                low = (value * spread(share, width) * s2[at : at + size, :].astype(F32)).astype(BF16)
                low_two[at : at + size, :] = low
                total = total + low.astype(F32)
            b2s[row : row + size, :] = total
        grad[...] = dot_back(low_two[...], m2[...])
        m2g[...] += dot_rows(a1[...], low_two[...])
        first = pl.multiple_of(step * (block * 8), 8)
        rows_ref[pl.ds(first + tiles, block, stride=8), :] = index_columns(local_row[...]).astype(F32)
        for row in range(0, rows, size):
            total = own[row : row + size, :]
            for s in range(sb):
                at = s * rows + row
                low = (grad[at : at + size, :] * s1[at : at + size, :].astype(F32)).astype(BF16)
                low_one[at : at + size, :] = low
                low = low.astype(F32)
                total = total + low
                for j in range(tiles):
                    rows_ref[pl.ds(first + at * 8 + j, size, stride=8), :] = low[
                        :, j * LANES : (j + 1) * LANES
                    ]
            own[row : row + size, :] = total
        m1eg[...] += dot_rows(edge[...].reshape(block, edge_width), low_one[...])
        total = (
            low_three[...].astype(F32)
            + dot(low_edge[...], e_first[:, width : width + edge_width])
            + dot_back(low_one[...], m1[width : width + edge_width, :])
        )
        edge_grad[...] = total.reshape(sb, rows, edge_width)

    @pl.when(step >= blocks)
    def _():
        deep = far_keep.shape[0]
        count = block * blocks // groups
        values, local = group_rows(order, (step - blocks) * count, count, rows_ref, moved, width)
        sums = group_sums(values, local, 2 * deep * rows).astype(BF16)
        near = jnp.concatenate(
            [ref[at, 0] for ref in (node_lo, node_hi) for at in range(deep)], axis=0
        )
        m1fg[...] += dot_rows(near, sums)
        height = rows // 16
        for at in range(2 * deep):
            out = (far_keep if at < deep else far_send).at[at % deep, 0]
            for j in range(tiles):
                tile = sums[at * rows : (at + 1) * rows, j * LANES : (j + 1) * LANES]
                out[j * height : (j + 1) * height] = tile.reshape(height, 16, LANES)

    @pl.when(step == blocks + groups - 1)
    def _():
        count = early.shape[0]
        slab[:count] = early[...]
        slab[count:] = jnp.zeros_like(slab[count:])
        pack(
            slab,
            [
                dot_rows(node[...], own[...].astype(BF16)),
                m2g[...],
                m1eg[...],
                padded_rows([column_sum(own[...]), column_sum(b2s[...]), eb1[...]], width),
                m1fg[...],
                e1g[...],
            ],
            count,
        )
        order_out(slab, base[0], codes, keep, send)


def message_backward(
    groups, codes, base, order, v, a1, s1, s2, edge, low_three, low_edge, local_row, live_col, m1, m2,
    e_first, node_lo, node_hi, node, early, e1g, eb1,
):
    slots, rows, edge_width = edge.shape
    width = v.shape[1]
    sb = slot_block(slots)
    block = sb * rows
    blocks = slots // sb
    edges = slots * rows
    half = node_lo.shape[0]
    deep = half // rows // groups
    tiles = rows * width // (16 * LANES)
    slab = slab_tiles(weight_shapes(width, edge_width), len(codes)) * len(codes)
    node_lo, node_hi = [n.reshape(deep, groups, rows, width) for n in (node_lo, node_hi)]
    blk = lambda i: jnp.minimum(i, blocks - 1)
    group_at = lambda i: (0, jnp.maximum(i - blocks, 0))
    row_spec = pl.BlockSpec((block, width), lambda i: (blk(i), 0))
    slot_spec = pl.BlockSpec((sb, rows, edge_width), lambda i: (blk(i), 0, 0))
    edge_spec = pl.BlockSpec((block, edge_width), lambda i: (blk(i), 0))
    node_spec = pl.BlockSpec((deep, 1, rows, width), lambda i: (*group_at(i), 0, 0))
    far_spec = pl.BlockSpec((deep, 1, tiles, 16, LANES), lambda i: (*group_at(i), 0, 0, 0))
    slab_spec = pl.BlockSpec((slab // 2, 16, LANES), lambda i: (0, 0, 0))
    smem = pl.BlockSpec(memory_space=pltpu.SMEM)
    return pl.pallas_call(
        functools.partial(message_backward_kernel, sb, blocks, groups, codes),
        grid=(blocks + groups,),
        in_specs=[
            smem,
            smem,
            const_spec(v.shape),
            row_spec,
            row_spec,
            row_spec,
            slot_spec,
            edge_spec,
            edge_spec,
            pl.BlockSpec((1, block), lambda i: (0, blk(i))),
            const_spec(live_col.shape),
            const_spec(m1.shape),
            const_spec(m2.shape),
            const_spec(e_first.shape),
            node_spec,
            node_spec,
            const_spec(node.shape),
            const_spec(early.shape),
            const_spec(e1g.shape),
            const_spec(eb1.shape),
        ],
        out_specs=[slot_spec, far_spec, far_spec, pl.BlockSpec((rows, width), whole), slab_spec, slab_spec],
        out_shape=[
            jax.ShapeDtypeStruct((slots, rows, edge_width), F32),
            jax.ShapeDtypeStruct((deep, groups, tiles, 16, LANES), BF16),
            jax.ShapeDtypeStruct((deep, groups, tiles, 16, LANES), BF16),
            jax.ShapeDtypeStruct((rows, width), F32),
            jax.ShapeDtypeStruct((slab // 2, 16, LANES), BF16),
            jax.ShapeDtypeStruct((slab // 2, 16, LANES), BF16),
        ],
        scratch_shapes=[
            pltpu.VMEM((block, width), BF16),
            pltpu.VMEM((block, width), BF16),
            pltpu.VMEM((block, width), F32),
            pltpu.VMEM((edges * 8, LANES), F32),
            pltpu.VMEM((edges // groups * 8, LANES), F32),
            pltpu.VMEM((width, width), F32),
            pltpu.VMEM((edge_width, width), F32),
            pltpu.VMEM((width, width), F32),
            pltpu.VMEM((rows, width), F32),
            slab_scratch(slab),
        ],
        compiler_params=pltpu.CompilerParams(vmem_limit_bytes=VMEM),
        name="message_backward",
        cost_estimate=pl.CostEstimate(
            flops=2 * edges * width * (2 * width + 3 * edge_width + half // groups),
            bytes_accessed=edges * width * 6 + edges * edge_width * 10,
            transcendentals=0,
        ),
    )(
        base, order, v, a1, s1, s2, edge, low_three, low_edge, local_row, live_col, m1, m2, e_first,
        node_lo, node_hi, node, early, e1g, eb1,
    )


def node_kernel(pieces, g_u1, own, m1, *refs):
    far, grad_out = refs[:pieces], refs[pieces]
    rows, width = own.shape
    height = rows // 16
    tiles = height * (width // LANES)
    sums = far[0][:tiles].astype(F32)
    for ref in far[1:]:
        sums = sums + ref[:tiles].astype(F32)
    far_sum = jnp.concatenate(
        [sums[j * height : (j + 1) * height].reshape(rows, LANES) for j in range(width // LANES)],
        axis=1,
    )
    far_first = m1.shape[0] - width
    grad_out[...] = (
        g_u1[...]
        + fine(dot_back, own[...], m1[:width, :])
        + fine(dot_back, far_sum, m1[far_first:, :])
    )


def node_last(g_u1, own, m1, far):
    return small_call(
        functools.partial(node_kernel, len(far)),
        (g_u1, own, m1, *far), [(own.shape, F32)], "node_gradient",
        flops=8 * own.size * own.shape[1], moved=2 * MIB,
    )[0]


def weights_out_kernel(
    codes, base, first, second,
    m1g, b1, m2g, b2, m3g, e1g, e2g, e3g, b3, g1, g2, fb2, eb1, eb2, eb3, g3, slab,
):
    order_in(slab, base[0], codes, first, second)
    width, edge_width = m3g.shape[0], e2g.shape[0]
    shapes = weight_shapes(width, edge_width)
    starts = [all_tiles(shapes[:at]) for at in range(len(shapes))]
    m3g[...] = unpack(slab, starts[0], width, width)
    e1g[:, :width] = unpack(slab, starts[1], edge_width, width)
    middle = unpack(slab, starts[12], edge_width, edge_width)
    far = unpack(slab, starts[2], edge_width, width)
    over = edge_width % LANES
    base_col = width + edge_width - over
    e1g[:, width:base_col] = middle[:, : edge_width - over]
    far = pltpu.roll(jnp.concatenate([far, jnp.zeros((edge_width, LANES), F32)], axis=1), over, 1)
    lane = lax.broadcasted_iota(jnp.int32, (edge_width, LANES), 1)
    e1g[:, base_col : base_col + LANES] = jnp.where(
        lane < over, middle[:, edge_width - over : edge_width - over + LANES], far[:, :LANES]
    )
    rest = e1g.shape[1] - base_col - LANES
    e1g[:, base_col + LANES :] = far[:, LANES : LANES + rest]
    e2g[...] = unpack(slab, starts[3], edge_width, edge_width)[:, :edge_width]
    e3g[...] = unpack(slab, starts[4], edge_width, edge_width)[:, :edge_width]
    bias = unpack(slab, starts[5], 16, width)
    for row, out in enumerate((g1, g2, fb2, b3)):
        out[...] = bias[row : row + 1]
    bias = unpack(slab, starts[6], 16, edge_width)
    for row, out in enumerate((eb2, eb3, g3)):
        out[...] = bias[row : row + 1, :edge_width]
    m1g[:width, :] = unpack(slab, starts[7], width, width)
    m2g[...] = unpack(slab, starts[8], width, width)
    m1g[width : width + edge_width, :] = unpack(slab, starts[9], edge_width, width)
    bias = unpack(slab, starts[10], 16, width)
    b1[...] = bias[0:1]
    b2[...] = bias[1:2]
    eb1[...] = bias[2:3, :edge_width]
    m1g[width + edge_width :, :] = unpack(slab, starts[11], width, width)


def weights_out(codes, base, halves_in, width, edge_width):
    shapes = [(2 * width + edge_width, width), (1, width), (width, width), (1, width)]
    shapes += [(width, width), (edge_width, 2 * width + edge_width)]
    shapes += [(edge_width, edge_width)] * 2 + [(1, width)] * 4 + [(1, edge_width)] * 4
    tiles = slab_tiles(weight_shapes(width, edge_width), len(codes)) * len(codes)
    return small_call(
        functools.partial(weights_out_kernel, codes),
        (base, *halves_in), [(s, F32) for s in shapes], "weight_gradients",
        [slab_scratch(tiles)], moved=10 * MIB, scalars=1,
    )


def exchange(value, mask, devices):
    return lax.ppermute(value, AXES, [(d, d ^ mask) for d in range(devices)])


def mask_groups(masks):
    return [masks[i : min(i + 2, len(masks) - 1)] for i in range(0, len(masks) - 1, 2)] + [masks[-1:]]


def order_codes(groups):
    masks = [mask for group in groups for mask in group]
    return [
        sum(mask for bit, mask in enumerate(masks) if place >> bit & 1)
        for place in range(1 << len(masks))
    ]


def combined(group, code):
    return sum(mask for bit, mask in enumerate(group) if code >> bit & 1)


def sent_around(value, group, devices):
    return [value] + [
        exchange(value, combined(group, code), devices) for code in range(1, 1 << len(group))
    ]


def shared_out(total, group, devices):
    parts = 1 << len(group)
    rows = total.shape[0] // parts
    return [total[:rows]] + [
        exchange(total[code * rows : (code + 1) * rows].astype(BF16), combined(group, code), devices)
        for code in range(1, parts)
    ]


def add_up(terms):
    total = terms[0].astype(F32)
    for term in terms[1:]:
        total = total + term.astype(F32)
    return total


def tied(*values):
    return lax.optimization_barrier(values)


def split_three(value):
    rows = []
    for _ in range(3):
        high = lax.reduce_precision(value, 8, 7)
        rows.append(high.astype(BF16))
        value = value - high
    return jnp.concatenate(rows + [jnp.zeros((13, value.shape[1]), BF16)], axis=0)


def per_device(
    node_in,
    edge_in,
    neighbours,
    live_counts,
    message_first,
    message_first_bias,
    message_second,
    message_second_bias,
    message_third,
    message_third_bias,
    norm_one,
    feed_first,
    feed_first_bias,
    feed_second,
    feed_second_bias,
    norm_two,
    edge_first,
    edge_first_bias,
    edge_second,
    edge_second_bias,
    edge_third,
    edge_third_bias,
    norm_three,
    node_cotangent,
    edge_cotangent,
):
    rows, slots = neighbours.shape
    width = node_in.shape[1]
    edge_width = edge_in.shape[2]
    edges = rows * slots
    hid_count = lax.axis_size("hid")
    res_count = lax.axis_size("res")
    devices = res_count * hid_count
    bits = devices.bit_length() - 1
    masks = [1 << b for b in range(bits - 1, -1, -1)]
    groups = mask_groups(masks)
    codes = order_codes(groups)
    me = lax.axis_index("res") * hid_count + lax.axis_index("hid")
    base = me.reshape(1)
    row = lambda vector: vector.reshape(1, -1)

    names = neighbours.T.reshape(edges)
    apart = (names // rows) ^ me
    place = jnp.zeros_like(names)
    for bit, mask in enumerate(masks):
        place = place | jnp.where((apart & mask) != 0, 1 << bit, 0)
    idx_row = (place * rows + names % rows).reshape(1, edges)
    res_count = devices // hid_count
    local_row = (place // res_count * rows + names % rows).reshape(1, edges)
    edge_order = group_order(place % res_count, res_count)
    live_col = jnp.broadcast_to(live_counts[:, None], (rows, LANES))
    edge = edge_in.transpose(1, 0, 2)
    cot = edge_cotangent.transpose(1, 0, 2)
    e_first = edge_first.T
    e_far = e_first[:, width + edge_width :]
    f1x = jnp.concatenate([feed_first, split_three(row(feed_first_bias))], axis=0)
    f2x = feed_second

    stack = lambda pieces: jnp.concatenate(pieces, axis=0)
    *outer, near = groups

    held = stack(sent_around(node_in, outer[0], devices))
    held, idx_row, local_row, live_col, e_far = tied(held, idx_row, local_row, live_col, e_far)
    for group in outer[1:]:
        held = stack(sent_around(held, group, devices))
    held, f1x, f2x = tied(held, f1x, f2x)
    node_lo, node_hi = sent_around(held, near, devices)

    f1, f2 = [f1x], [f2x]
    hid_masks = [m for m in masks if m < hid_count]
    for mask in hid_masks[:-1]:
        f1, f2 = [pieces + [exchange(p, mask, devices) for p in pieces] for pieces in (f1, f2)]

    a1, s1, s2, total = message_forward(
        node_lo, node_hi, node_in, edge, idx_row, live_col, message_first,
        row(message_first_bias), message_second, row(message_second_bias),
    )
    total, f1, f2 = tied(total, f1, f2)
    f1, f2 = [
        pieces + [exchange(p, hid_masks[-1], devices) for p in pieces] for pieces in (f1, f2)
    ]
    h1b, n1, sc1, n2, sc2, slope, h2b, far_part, own_part = residue_forward(
        node_in, total, message_third, row(message_third_bias), row(norm_one),
        row(feed_second_bias), row(norm_two), e_first, e_far, row(edge_first_bias), f1, f2,
    )

    held = stack(sent_around(far_part, outer[0], devices))
    held, edge_order = tied(held, edge_order)
    for group in outer[1:]:
        held = stack(sent_around(held, group, devices))
    q_lo, q_hi = sent_around(held, near, devices)

    edge_out, act_one, act_two, low_three, low_two, low_one, hi, lo, own_sum, edge_gain = edge_branch(
        q_lo, q_hi, own_part, edge, cot, idx_row, live_col, e_first,
        edge_second, row(edge_second_bias), edge_third, row(edge_third_bias), row(norm_three),
    )

    terms = [lo, exchange(hi, near[0], devices)]
    made = None
    for group in reversed(outer):
        terms = shared_out(add_up(terms), group, devices)
        if made is None:
            made = edge_weights((act_two, act_one), (low_three, low_two), rows)
            terms, made = tied(terms, made)
    e3g, e2g, eb3, eb2 = made
    g_u1, v, both, early = residue_backward(
        (
            node_cotangent, own_sum, e_first, e_far, h1b, h2b, n1, sc1, n2, sc2, slope, row(norm_one),
            row(norm_two), message_third, total, e2g, e3g, eb2, eb3, edge_gain,
        ),
        terms, f1, f2,
    )

    both, low_here = tied(both, low_one)
    b_held = stack(sent_around(both, outer[0], devices))
    e1g, eb1 = edge_weights((low_here,), (edge,), rows)
    v, b_held, e1g, eb1 = tied(v, b_held, e1g, eb1)
    for group in outer[1:]:
        b_held = stack(sent_around(b_held, group, devices))
    eb1 = jnp.pad(eb1, ((0, 0), (0, width - edge_width)))
    edge_grad, far_keep, far_send, own, keep, send = message_backward(
        res_count, codes, base, edge_order, v, a1, s1, s2, edge, low_three, low_one, local_row, live_col,
        message_first, message_second, e_first, node_lo, node_hi, node_in, early, e1g, eb1,
    )
    keep, send, far_keep, far_send, b_held = tied(keep, send, far_keep, far_send, b_held)

    first, *others = reversed(outer)
    terms = [keep, exchange(send, near[0], devices)]
    total, b_held, far_send = tied(add_up(terms), b_held, far_send)
    terms = shared_out(total, first, devices)
    far_keep, far_send = [far.reshape(-1, 16, LANES) for far in (far_keep, far_send)]
    far_terms = [far_keep, exchange(far_send, near[0], devices)]
    b_near = sent_around(b_held, near, devices)
    total, b_first = tied(add_up(far_terms), b_near[0])
    far_terms = shared_out(total, first, devices)
    feed = feed_gradients((b_first, b_near[1]), feed_first, row(feed_first_bias), feed_second)
    terms, (f1g, f2g, fb1g) = tied(terms, feed)
    for group in others:
        terms = shared_out(add_up(terms), group, devices)
        far_terms = shared_out(add_up(far_terms), group, devices)
    held = add_up(terms).astype(BF16)

    for at, group in enumerate(outer):
        around = sent_around(held, group, devices)
        if at + 1 == len(outer):
            around, node_gradient = tied(around, node_last(g_u1, own, message_first, far_terms))
        held = stack(around)
    m1g, b1, m2g, b2, m3g, e1g, e2g, e3g, b3, g1, g2, fb2, eb1, eb2, eb3, g3 = weights_out(
        codes, base, sent_around(held, near, devices), width, edge_width
    )
    flat = lambda vector: vector.reshape(-1)
    return (
        h2b,
        edge_out.transpose(1, 0, 2),
        node_gradient,
        edge_grad.transpose(1, 0, 2),
        m1g,
        flat(b1),
        m2g,
        flat(b2),
        m3g,
        flat(b3),
        flat(g1),
        f1g,
        flat(fb1g),
        f2g,
        flat(fb2),
        flat(g2),
        e1g.T,
        flat(eb1),
        e2g,
        flat(eb2),
        e3g,
        flat(eb3),
        flat(g3),
    )


def solution(mesh):
    nodes, edges, shared = P(AXES, None), P(AXES, None, None), P()
    return jax.shard_map(
        per_device,
        mesh=mesh,
        in_specs=(nodes, edges, nodes, P(AXES))
        + (shared,) * 7
        + (P(None, "hid"), P("hid"), P("hid", None))
        + (shared,) * 9
        + (nodes, edges),
        out_specs=(nodes, edges, nodes, edges)
        + (shared,) * 7
        + (P(None, "hid"), P("hid"), P("hid", None))
        + (shared,) * 9,
        check_vma=False,
    )
```

```python
import functools

import jax
import jax.numpy as jnp
from jax import lax
from jax.experimental import pallas as pl
from jax.experimental.pallas import tpu as pltpu
from jax.sharding import PartitionSpec as P

EPS = 1e-05
AXES = ("res", "hid")
F32 = jnp.float32
BF16 = jnp.bfloat16
TANH_SCALE = 0.7978845608028654
TANH_CUBE = 0.044715
LANES = 128
CHUNK = 2048
MIB = 1024 * 1024
VMEM = 58 * MIB


def dot(left, right):
    return lax.dot_general(left, right, (((1,), (0,)), ((), ())), preferred_element_type=F32)


def dot_rows(left, right):
    return lax.dot_general(left, right, (((0,), (0,)), ((), ())), preferred_element_type=F32)


def dot_back(left, right):
    return lax.dot_general(left, right, (((1,), (1,)), ((), ())), preferred_element_type=F32)


def halves(value):
    high = value.astype(BF16)
    return high, (value - high.astype(F32)).astype(BF16)


def fine(product, value, weights):
    high, low = halves(value)
    return product(high, weights) + product(low, weights)


def gelu_parts(x):
    square = x * x
    t = jnp.tanh(x * (TANH_SCALE + (TANH_SCALE * TANH_CUBE) * square))
    gate = 0.5 + 0.5 * t
    act = x * gate
    slope = gate + act * (1.0 - gate) * (2 * TANH_SCALE + (6 * TANH_SCALE * TANH_CUBE) * square)
    return act, slope


def index_columns(idx_row):
    parts = [
        jnp.broadcast_to(idx_row[:, first : first + LANES], (LANES, LANES)).T
        for first in range(0, idx_row.shape[1], LANES)
    ]
    return jnp.concatenate(parts, axis=0)


def one_hot_columns(idx, start, count):
    one, zero = jnp.ones((), BF16), jnp.zeros((), BF16)
    idx = idx.astype(jnp.int16)
    lane = lax.broadcasted_iota(jnp.int32, idx.shape, 1).astype(jnp.int16)
    parts = [
        jnp.where(idx == lane + jnp.int16(start + first), one, zero)
        for first in range(0, count, LANES)
    ]
    return jnp.concatenate(parts, axis=1)


def pick_rows(idx, table_refs):
    total, start = None, 0
    for ref in table_refs:
        rows = ref.shape[0]
        step = min(rows, CHUNK)
        for first in range(0, rows, step):
            part = dot(one_hot_columns(idx, start + first, step), ref[first : first + step, :])
            total = part if total is None else total + part
        start += rows
    return total


def one_hot_rows(idx_row, start, count):
    shape = (count, idx_row.shape[1])
    row = (lax.broadcasted_iota(jnp.int32, shape, 0) + start).astype(jnp.int16)
    names = jnp.broadcast_to(idx_row, shape).astype(jnp.int16)
    return jnp.where(names == row, jnp.ones((), BF16), jnp.zeros((), BF16))


def group_rows(order, first, count, rows_ref, moved, width):
    for e in range(count):
        at = pl.multiple_of(order[0, first + e] * 8, 8)
        moved[e * 8 : e * 8 + 8, :] = rows_ref[pl.ds(at, 8), :]

    def column(at):
        return moved[pl.ds(at, count, stride=8), :]

    tiles = pl.cdiv(width, LANES)
    parts = [column(at)[:, : min(LANES, width - at * LANES)] for at in range(tiles)]
    return jnp.concatenate(parts, axis=1).astype(BF16), column(tiles)


def group_sums(rows, local, residues):
    lane = lax.broadcasted_iota(jnp.int32, local.shape, 1).astype(F32)
    picks = [
        jnp.where(local == lane + float(first), 1.0, 0.0).astype(BF16)
        for first in range(0, residues, LANES)
    ]
    return dot_rows(jnp.concatenate(picks, axis=1), rows)


def order_kernel(groups, count, names, out):
    rows = names.shape[0]
    row = lax.broadcasted_iota(jnp.int32, (LANES, LANES), 0)
    column = lax.broadcasted_iota(jnp.int32, (LANES, LANES), 1)
    upto = jnp.where(row <= column, 1.0, 0.0).astype(BF16)
    ones = jnp.ones((LANES, LANES), BF16)
    above = lax.broadcasted_iota(jnp.int32, (rows, rows), 0)
    before = jnp.where(lax.broadcasted_iota(jnp.int32, (rows, rows), 1) < above, 1.0, 0.0).astype(BF16)
    place = jnp.full(names.shape, float(2 * LANES * LANES), F32)
    for group in range(groups):
        here = names[...] == group
        low = jnp.where(here, 1.0, 0.0).astype(BF16)
        rank = dot(low, upto) + dot(before, dot(low, ones).astype(BF16))
        place = jnp.where(here, rank + float(group * count - 1), place)
    high = total = None
    for at in range(rows):
        where = jnp.broadcast_to(place[at : at + 1, :], (LANES, LANES)).T.astype(jnp.int32)
        left = jnp.where(where // LANES == column, 1.0, 0.0)
        right = jnp.where(where % LANES == column, 1.0, 0.0)
        part = dot_rows(left.astype(BF16), (right * float(at)).astype(BF16))
        high = part if high is None else high + part
        part = dot_rows(left.astype(BF16), (right * row.astype(F32)).astype(BF16))
        total = part if total is None else total + part
    number = high * float(LANES) + total
    out[...] = number[: out.shape[0], : out.shape[1]].astype(jnp.int32)


def group_order(names, groups):
    edges = names.shape[0]
    rows = pl.cdiv(pl.cdiv(edges, LANES), 8) * 8
    padded = jnp.pad(names, (0, rows * LANES - edges), constant_values=groups)
    out = small_call(
        functools.partial(order_kernel, groups, edges // groups),
        (padded.reshape(rows, LANES),), [((edges // LANES, LANES), jnp.int32)], "group_order",
    )[0]
    return out.reshape(1, edges)


def spread(column, width):
    return jnp.concatenate([column] * (width // LANES), axis=1)


def norm(value):
    centre = value - jnp.mean(value, -1, keepdims=True)
    scale = lax.rsqrt(jnp.mean(centre * centre, -1, keepdims=True) + EPS)
    return centre * scale, scale


def norm_back(inner, normed, scale):
    mean_first = jnp.mean(inner, -1, keepdims=True)
    mean_second = jnp.mean(inner * normed, -1, keepdims=True)
    return scale * (inner - mean_first - normed * mean_second)


def column_sum(value):
    return jnp.sum(value, axis=0, keepdims=True)


def whole(*_):
    return (0, 0)


def const_spec(shape):
    return pl.BlockSpec(shape, lambda *_: (0,) * len(shape), pipeline_mode=pl.Buffered(1))


def small_call(kernel, args, shapes, name, scratch=(), flops=0, moved=0, exps=0, scalars=0):
    return pl.pallas_call(
        kernel,
        grid=(1,),
        in_specs=[pl.BlockSpec(memory_space=pltpu.SMEM)] * scalars
        + [const_spec(a.shape) for a in args[scalars:]],
        out_specs=[pl.BlockSpec(s, lambda *_, n=len(s): (0,) * n) for s, _ in shapes],
        out_shape=[jax.ShapeDtypeStruct(*s) for s in shapes],
        scratch_shapes=list(scratch),
        compiler_params=pltpu.CompilerParams(vmem_limit_bytes=VMEM),
        name=name,
        cost_estimate=pl.CostEstimate(flops=flops, bytes_accessed=moved, transcendentals=exps),
    )(*args)


def tile_count(shape):
    return pl.cdiv(shape[0], 16) * pl.cdiv(shape[1], LANES)


def all_tiles(shapes):
    return sum(tile_count(s) for s in shapes)


def pack(slab, values, at=0):
    for value in values:
        rows, columns = value.shape
        count = rows // 16
        for first in range(0, columns, LANES):
            take = min(LANES, columns - first)
            tile = value[:, first : first + take].astype(BF16).reshape(count, 16, take)
            slab[at : at + count, :, :take] = tile
            at += count


def unpack(slab, at, rows, columns):
    count = rows // 16
    parts = [
        slab[at + i * count : at + (i + 1) * count].reshape(rows, LANES).astype(F32)
        for i in range(pl.cdiv(columns, LANES))
    ]
    return jnp.concatenate(parts, axis=1)


def order_out(slab, base, codes, keep, send):
    size = slab.shape[0] // len(codes)
    half = len(codes) // 2
    for place, code in enumerate(codes):
        out = keep if place < half else send
        at = (place % half) * size
        out[at : at + size] = slab[pl.ds((base ^ code) * size, size)]


def half_shapes(tiles):
    return [((tiles // 2, 16, LANES), BF16)] * 2


def slab_scratch(tiles):
    return pltpu.VMEM((tiles, 16, LANES), BF16)


def slab_tiles(shapes, chunks):
    return pl.cdiv(all_tiles(shapes), chunks)


def order_in(slab, base, codes, first, second):
    size = slab.shape[0] // len(codes)
    half = len(codes) // 2
    for place, code in enumerate(codes):
        source = first if place < half else second
        at = (place % half) * size
        slab[pl.ds((base ^ code) * size, size)] = source[at : at + size]


def padded_rows(parts, width):
    return jnp.concatenate(parts + [jnp.zeros((16 - len(parts), width), F32)], axis=0)


def slot_block(slots):
    for size in (10, 12, 8, 6, 5, 4, 3, 2):
        if slots % size == 0:
            return size
    return 1


def far_table(node_lo, node_hi, weights, put):
    tile = min(512, node_lo.shape[0])
    for source, start in ((node_lo, 0), (node_hi, node_lo.shape[0])):
        def body(i, carry, source=source, start=start):
            at = pl.multiple_of(i * tile, tile)
            put(start + at, dot(source[pl.ds(at, tile), :], weights))
            return carry
        lax.fori_loop(0, source.shape[0] // tile, body, 0)


def message_forward_kernel(
    sb, by_rows, node_lo, node_hi, node_own, edge, idx_row, names, live_col, m1, b1, m2, b2,
    a1_out, s1_out, s2_out, sum_out, table, far, near, lhs, z,
):
    step = pl.program_id(0)
    width = node_own.shape[1]
    edge_width = edge.shape[2]
    rows = edge.shape[1]
    block = sb * rows
    lanes = width // LANES

    @pl.when(step == 0)
    def _():
        weights = m1[width + edge_width :, :]
        if by_rows:
            def put(first, value):
                for at in range(8):
                    column = at % lanes * LANES
                    table[pl.ds(first * 8 + at, value.shape[0], stride=8), :] = value[
                        :, column : column + LANES
                    ]
        else:
            def put(first, value):
                table[pl.ds(first, value.shape[0]), :] = value.astype(BF16)
        far_table(node_lo, node_hi, weights, put)
        near[:edge_width, :] = m1[width : width + edge_width, :]
        near[edge_width:, :] = jnp.zeros_like(near[edge_width:, :])
        near[edge_width : edge_width + rows, :] = (
            dot(node_own[...], m1[:width, :]) + b1[...]
        ).astype(BF16)
        shape = (rows, near.shape[0] - edge_width)
        eye = lax.broadcasted_iota(jnp.int32, shape, 0) == lax.broadcasted_iota(jnp.int32, shape, 1)
        for at in range(0, block, rows):
            lhs[at : at + rows, edge_width:] = jnp.where(eye, 1.0, 0.0).astype(BF16)
        sum_out[...] = jnp.zeros_like(sum_out)

    lhs[:, :edge_width] = edge[...].reshape(block, edge_width)
    z[...] = dot(lhs[...], near[...])
    if not by_rows:
        z[...] += pick_rows(index_columns(idx_row[...]), (table,))
    upper = lax.broadcasted_iota(jnp.int32, (8, LANES), 0) < lanes

    def fetch(at):
        for e in range(at, at + 16, 2):
            pair = [
                table[pl.ds(pl.multiple_of(names[0, step * block + e + i] * 8, 8), 8), :]
                for i in range(2)
            ]
            far[e * lanes : e * lanes + 8, :] = jnp.where(upper, *pair)

    def fetched(at):
        return jnp.concatenate(
            [far[pl.ds(at * lanes + j, 16, stride=lanes), :] for j in range(lanes)], axis=1
        )

    if by_rows:
        fetch(0)
    for at in range(0, block, 16):
        value = z[at : at + 16, :]
        if by_rows:
            if at + 16 < block:
                fetch(at + 16)
            value = value + fetched(at)
        act, slope = gelu_parts(value)
        a1_out[at : at + 16, :] = act.astype(BF16)
        s1_out[at : at + 16, :] = slope.astype(BF16)
    z[...] = dot(a1_out[...], m2[...])
    bias = b2[...]
    for row in range(0, rows, 16):
        count = live_col[row : row + 16, :]
        inverse = 1.0 / count.astype(F32)
        total = sum_out[row : row + 16, :]
        for s in range(sb):
            at = s * rows + row
            act, slope = gelu_parts(z[at : at + 16, :] + bias)
            s2_out[at : at + 16, :] = slope.astype(BF16)
            share = jnp.where(count > step * sb + s, inverse, 0.0)
            total = total + act.astype(BF16).astype(F32) * spread(share, width)
        sum_out[row : row + 16, :] = total


def message_forward(node_lo, node_hi, node_own, edge, idx_row, live_col, m1, b1, m2, b2):
    slots, rows, edge_width = edge.shape
    width = node_own.shape[1]
    residues = 2 * node_lo.shape[0]
    by_rows = residues <= 4096 and width == 4 * LANES
    sb = slot_block(slots) if by_rows else 4
    block = sb * rows
    edges = slots * rows
    near = pl.cdiv(edge_width + rows, LANES) * LANES
    row_spec = pl.BlockSpec((block, width), lambda i: (i, 0))
    return pl.pallas_call(
        functools.partial(message_forward_kernel, sb, by_rows),
        grid=(slots // sb,),
        in_specs=[
            const_spec(node_lo.shape),
            const_spec(node_hi.shape),
            const_spec(node_own.shape),
            pl.BlockSpec((sb, rows, edge_width), lambda i: (i, 0, 0)),
            pl.BlockSpec((1, block), lambda i: (0, i)),
            pl.BlockSpec(memory_space=pltpu.SMEM),
            const_spec(live_col.shape),
            const_spec(m1.shape),
            const_spec(b1.shape),
            const_spec(m2.shape),
            const_spec(b2.shape),
        ],
        out_specs=[row_spec, row_spec, row_spec, pl.BlockSpec((rows, width), whole)],
        out_shape=[jax.ShapeDtypeStruct((edges, width), BF16)] * 3
        + [jax.ShapeDtypeStruct((rows, width), F32)],
        scratch_shapes=[
            pltpu.VMEM((residues * 8, LANES), F32) if by_rows else pltpu.VMEM((residues, width), BF16),
            pltpu.VMEM((block * 4 if by_rows else 8, LANES), F32),
            pltpu.VMEM((near, width), BF16),
            pltpu.VMEM((block, near), BF16),
            pltpu.VMEM((block, width), F32),
        ],
        compiler_params=pltpu.CompilerParams(vmem_limit_bytes=VMEM),
        name="message_forward",
        cost_estimate=pl.CostEstimate(
            flops=2 * edges * width * (residues + edge_width + width),
            bytes_accessed=edges * width * 6 + edges * edge_width * 2 + edges * LANES * 4,
            transcendentals=2 * edges * width,
        ),
    )(node_lo, node_hi, node_own, edge, idx_row, idx_row, live_col, m1, b1, m2, b2)


def residue_forward_kernel(parts, node, total, m3, b3, g1, fb2, g2, e_first, e_far, eb, *refs):
    f1, f2 = refs[:parts], refs[parts : 2 * parts]
    h1b_out, n1_out, sc1_out, n2_out, sc2_out, slope_out, h2b_out, far_out, own_out = refs[2 * parts :]
    width, hidden = node.shape[1], f1[0].shape[1]
    u1 = node[...].astype(F32) + fine(dot, total[...], m3[...]) + b3[...]
    n1, sc1 = norm(u1)
    h1 = n1 * g1[...]
    h1b = h1.astype(BF16)
    h1b_out[...] = h1b
    n1_out[...] = n1
    sc1_out[...] = jnp.broadcast_to(sc1, sc1_out.shape)
    y2 = None
    for p in range(parts):
        bias = f1[p][width : width + 16, :].astype(F32)
        bias = bias[0:1] + bias[1:2] + bias[2:3]
        act, slope = gelu_parts(dot(h1b, f1[p][:width, :]) + bias)
        slope_out[:, p * hidden : (p + 1) * hidden] = slope
        part = dot(act.astype(BF16), f2[p][...])
        y2 = part if y2 is None else y2 + part
    n2, sc2 = norm(h1 + (y2 + fb2[...]))
    h2b = (n2 * g2[...]).astype(BF16)
    n2_out[...] = n2
    sc2_out[...] = jnp.broadcast_to(sc2, sc2_out.shape)
    h2b_out[...] = h2b
    far_out[...] = dot_back(h2b, e_far[...]).astype(BF16)
    own_out[...] = dot_back(h2b, e_first[:, :width]) + eb[...]


def residue_forward(node, total, m3, b3, g1, fb2, g2, e_first, e_far, eb, f1, f2):
    rows, width = node.shape
    edge_width = e_first.shape[0]
    hidden = len(f1) * f1[0].shape[1]
    shapes = [
        ((rows, width), BF16),
        ((rows, width), F32),
        ((rows, LANES), F32),
        ((rows, width), F32),
        ((rows, LANES), F32),
        ((rows, hidden), F32),
        ((rows, width), BF16),
        ((rows, edge_width), BF16),
        ((rows, edge_width), F32),
    ]
    return small_call(
        functools.partial(residue_forward_kernel, len(f1)),
        (node, total, m3, b3, g1, fb2, g2, e_first, e_far, eb, *f1, *f2),
        shapes, "residue_forward", flops=4 * rows * width * hidden, moved=5 * MIB,
        exps=rows * hidden,
    )


def edge_kernel(
    sb, blocks, hi_chunks, by_rows, far_lo, far_hi, own, edge, cot, idx, idx_row, names, live_col,
    e_first, e2, eb2, e3, eb3, g3,
    edge_out, act_one_out, act_two_out, low_three_out, low_two_out, low_one_out, hi_out, lo_out, own_out, gain_out,
    low_first, gs, table, far, z, slope_ref,
):
    step = pl.program_id(0)
    rows, width = own.shape
    node_width = (e_first.shape[1] - width) // 2
    e_mid = e_first.at[:, node_width : node_width + width]
    tiles = pl.cdiv(width, LANES)
    per = 8 // tiles
    size = 32

    @pl.when(step == 0)
    def _():
        own_out[...] = jnp.zeros_like(own_out)
        gs[...] = jnp.zeros_like(gs)
        half = far_lo.shape[0]
        if by_rows:
            for source, start in ((far_lo, 0), (far_hi, half)):
                for first in range(0, half, 512):
                    value = source[first : first + 512, :].astype(F32)
                    for at in range(8):
                        column = at % tiles * LANES
                        take = min(LANES, width - column)
                        table[pl.ds((start + first) * 8 + at, value.shape[0], stride=8), :take] = value[
                            :, column : column + take
                        ]

    @pl.when(step < blocks)
    def _():
        block = sb * rows
        flat = edge[...].reshape(block, width)
        z[...] = dot_back(flat, e_mid[...])
        if not by_rows:
            z[...] += pick_rows(index_columns(idx[...]), (far_lo, far_hi))
        sub = lax.broadcasted_iota(jnp.int32, (8, LANES), 0)

        def fetch(at):
            for e in range(at, at + size, per):
                got = [
                    table[pl.ds(pl.multiple_of(names[0, step * block + e + i] * 8, 8), 8), :]
                    for i in range(per)
                ]
                value = got[-1]
                for i in range(per - 2, -1, -1):
                    value = jnp.where(sub < (i + 1) * tiles, got[i], value)
                far[e * tiles : e * tiles + 8, :] = value

        def fetched(at):
            parts = [
                far[pl.ds(at * tiles + j, size, stride=tiles), :][:, : min(LANES, width - j * LANES)]
                for j in range(tiles)
            ]
            return jnp.concatenate(parts, axis=1)

        if by_rows:
            fetch(0)
        for at in range(0, block, size):
            value = z[at : at + size, :] + own[at % rows : at % rows + size, :]
            if by_rows:
                if at + size < block:
                    fetch(at + size)
                value = value + fetched(at)
            act, slope = gelu_parts(value)
            act_one_out[at : at + size, :] = act.astype(BF16)
            slope_ref[at : at + size, :] = slope
        act_one = act_one_out[...]
        act_two, slope_two = gelu_parts(dot(act_one, e2[...]) + eb2[...])
        act_two = act_two.astype(BF16)
        act_two_out[...] = act_two
        w_three = dot(act_two, e3[...]) + eb3[...]
        normed, scale = norm(flat.astype(F32) + w_three)
        count = spread(live_col[...], pl.cdiv(width, LANES) * LANES)[:, :width]
        live = jnp.concatenate(
            [jnp.where(count > step * sb + s, 1.0, 0.0) for s in range(sb)], axis=0
        )
        edge_out[...] = (normed * g3[...] * live).astype(BF16).reshape(sb, rows, width)
        grad = cot[...].reshape(block, width).astype(F32) * live
        gs[...] += jnp.sum((grad * normed).reshape(sb, rows, width), axis=0)
        low_three = norm_back(grad * g3[...], normed, scale).astype(BF16)
        low_three_out[...] = low_three
        low_two = (dot_back(low_three, e3[...]) * slope_two).astype(BF16)
        low_two_out[...] = low_two
        low_one = (dot_back(low_two, e2[...]) * slope_ref[...]).astype(BF16)
        low_one_out[...] = low_one
        own_out[...] += jnp.sum(low_one.astype(F32).reshape(sb, rows, width), axis=0)
        low_first[pl.ds(pl.multiple_of(step * block, block), block), :] = low_one

    chunk = hi_out.shape[0]

    @pl.when((step >= blocks) & (step < blocks + hi_chunks))
    def _():
        start = (step - blocks + hi_chunks) * chunk
        hi_out[...] = dot(one_hot_rows(idx_row[...], start, chunk), low_first[...]).astype(BF16)

    @pl.when(step >= blocks + hi_chunks)
    def _():
        start = (step - blocks - hi_chunks) * chunk
        lo_out[...] = dot(one_hot_rows(idx_row[...], start, chunk), low_first[...])

    @pl.when(step == blocks + 2 * hi_chunks - 1)
    def _():
        gain_out[...] = column_sum(gs[...])


def edge_branch(far_lo, far_hi, own, edge, cot, idx_row, live_col, e_first, e2, eb2, e3, eb3, g3):
    slots, rows, width = edge.shape
    sb = slot_block(slots)
    edges = slots * rows
    block = sb * rows
    blocks = slots // sb
    half = far_lo.shape[0]
    chunk = min(512, half)
    hi_chunks = half // chunk
    by_rows = half <= 2048 and 8 % pl.cdiv(width, LANES) == 0
    blk = lambda i: jnp.minimum(i, blocks - 1)
    hi_at = lambda i: (jnp.clip(i - blocks, 0, hi_chunks - 1), 0)
    lo_at = lambda i: (jnp.clip(i - blocks - hi_chunks, 0, hi_chunks - 1), 0)
    slot_spec = pl.BlockSpec((sb, rows, width), lambda i: (blk(i), 0, 0))
    row_spec = pl.BlockSpec((block, width), lambda i: (blk(i), 0))
    return pl.pallas_call(
        functools.partial(edge_kernel, sb, blocks, hi_chunks, by_rows),
        grid=(blocks + 2 * hi_chunks,),
        in_specs=[
            const_spec(far_lo.shape),
            const_spec(far_hi.shape),
            const_spec(own.shape),
            slot_spec,
            slot_spec,
            pl.BlockSpec((1, block), lambda i: (0, blk(i))),
            const_spec(idx_row.shape),
            pl.BlockSpec(memory_space=pltpu.SMEM),
            const_spec(live_col.shape),
            const_spec(e_first.shape),
            const_spec(e2.shape),
            const_spec(eb2.shape),
            const_spec(e3.shape),
            const_spec(eb3.shape),
            const_spec(g3.shape),
        ],
        out_specs=[slot_spec]
        + [row_spec] * 5
        + [
            pl.BlockSpec((chunk, width), hi_at),
            pl.BlockSpec((chunk, width), lo_at),
            pl.BlockSpec((rows, width), whole),
            pl.BlockSpec((1, width), whole),
        ],
        out_shape=[jax.ShapeDtypeStruct((slots, rows, width), BF16)]
        + [jax.ShapeDtypeStruct((edges, width), BF16)] * 5
        + [
            jax.ShapeDtypeStruct((half, width), BF16),
            jax.ShapeDtypeStruct((half, width), F32),
            jax.ShapeDtypeStruct((rows, width), F32),
            jax.ShapeDtypeStruct((1, width), F32),
        ],
        scratch_shapes=[
            pltpu.VMEM((edges, width), BF16),
            pltpu.VMEM((rows, width), F32),
            pltpu.VMEM((half * 16 if by_rows else 8, LANES), F32),
            pltpu.VMEM((block * 8, LANES), F32),
            pltpu.VMEM((block, width), F32),
            pltpu.VMEM((block, width), F32),
        ],
        compiler_params=pltpu.CompilerParams(vmem_limit_bytes=VMEM),
        name="edge_branch",
        cost_estimate=pl.CostEstimate(
            flops=2 * edges * width * (4 * half + 5 * width),
            bytes_accessed=edges * width * 16,
            transcendentals=2 * edges * width,
        ),
    )(far_lo, far_hi, own, edge, cot, idx_row, idx_row, idx_row, live_col, e_first, e2, eb2, e3, eb3, g3)


def edge_weights_kernel(blocks, pairs, *refs):
    step = pl.program_id(0)
    lefts, rights = refs[:pairs], refs[pairs : 2 * pairs]
    grads, biases, sums = refs[2 * pairs : 3 * pairs], refs[3 * pairs : 4 * pairs], refs[-1]
    rows = sums.shape[1]

    @pl.when(step == 0)
    def _():
        for ref in (*grads, sums):
            ref[...] = jnp.zeros_like(ref)

    for at in range(pairs):
        left, right = [r[...].reshape(-1, r.shape[-1]) for r in (lefts[at], rights[at])]
        grads[at][...] += dot_rows(left, right)
        low = left if lefts[at].ndim < rights[at].ndim else right
        sums[at] += jnp.sum(low.astype(F32).reshape(-1, rows, low.shape[1]), axis=0)

    @pl.when(step == blocks - 1)
    def _():
        for at in range(pairs):
            biases[at][...] = column_sum(sums[at])


def edge_weights(lefts, rights, rows):
    pairs = len(lefts)
    edges, width = lefts[0].shape
    slots = edges // rows
    sb = slot_block(slots)

    def spec(array):
        if array.ndim == 3:
            return pl.BlockSpec((sb, rows, width), lambda i: (i, 0, 0))
        return pl.BlockSpec((sb * rows, width), lambda i: (i, 0))

    shapes = [(width, width)] * pairs + [(1, width)] * pairs
    return pl.pallas_call(
        functools.partial(edge_weights_kernel, slots // sb, pairs),
        grid=(slots // sb,),
        in_specs=[spec(array) for array in (*lefts, *rights)],
        out_specs=[pl.BlockSpec(s, whole) for s in shapes],
        out_shape=[jax.ShapeDtypeStruct(s, F32) for s in shapes],
        scratch_shapes=[pltpu.VMEM((pairs, rows, width), F32)],
        compiler_params=pltpu.CompilerParams(vmem_limit_bytes=VMEM),
        name="edge_weights",
        cost_estimate=pl.CostEstimate(
            flops=2 * pairs * edges * width * width,
            bytes_accessed=pairs * edges * width * 4,
            transcendentals=0,
        ),
    )(*lefts, *rights)


def early_shapes(width, edge_width):
    return [
        (width, width),
        (edge_width, width),
        (edge_width, width),
        (edge_width, edge_width),
        (edge_width, edge_width),
        (16, width),
        (16, edge_width),
    ]


def residue_backward_kernel(
    parts, pieces, node_cot, own_sum, e_first, e_far, h1b, h2b, n1, sc1, n2, sc2, slope, g1, g2, m3,
    total, e2g, e3g, eb2, eb3, edge_gain, *refs,
):
    far = refs[:pieces]
    f1 = refs[pieces : pieces + parts]
    f2 = refs[pieces + parts : pieces + 2 * parts]
    gu1_out, v_out, both_out, slab = refs[pieces + 2 * parts :]
    width, hidden = h2b.shape[1], f1[0].shape[1]
    far_sum = far[0][...]
    for ref in far[1:]:
        far_sum = far_sum + ref[...].astype(F32)
    own = own_sum[...]
    g_h2 = (
        node_cot[...].astype(F32)
        + fine(dot, own, e_first[:, :width])
        + fine(dot, far_sum, e_far[...])
    )
    gain_two = column_sum(g_h2 * n2[...])
    g_u2 = norm_back(g_h2 * g2[...], n2[...], sc2[:, :1])
    gy2 = g_u2.astype(BF16)
    both_out[:, :width] = h1b[...]
    both_out[:, width:] = gy2
    g_h1 = g_u2
    for p in range(parts):
        gy1 = dot_back(gy2, f2[p][...]) * slope[:, p * hidden : (p + 1) * hidden]
        g_h1 = g_h1 + dot_back(gy1.astype(BF16), f1[p][:width, :])
    gain_one = column_sum(g_h1 * n1[...])
    g_u1 = norm_back(g_h1 * g1[...], n1[...], sc1[:, :1])
    gu1_out[...] = g_u1
    v_out[...] = fine(dot_back, g_u1, m3[...])
    bias = [gain_one, gain_two, column_sum(gy2.astype(F32)), column_sum(g_u1)]
    slab[...] = jnp.zeros_like(slab)
    pack(
        slab,
        [
            dot_rows(total[...].astype(BF16), g_u1.astype(BF16)),
            dot_rows(own.astype(BF16), h2b[...]),
            dot_rows(far_sum.astype(BF16), h2b[...]),
            e2g[...],
            e3g[...],
            padded_rows(bias, width),
            padded_rows([eb2[...], eb3[...], edge_gain[...]], own.shape[1]),
        ],
    )


def residue_backward(args, far, f1, f2):
    node_cot, e_first, slope = args[0], args[2], args[10]
    rows, width = node_cot.shape
    shapes = [
        ((rows, width), F32),
        ((rows, width), F32),
        ((rows, 2 * width), BF16),
        ((all_tiles(early_shapes(width, e_first.shape[0])), 16, LANES), BF16),
    ]
    return small_call(
        functools.partial(residue_backward_kernel, len(f1), len(far)),
        (*args, *far, *f1, *f2),
        shapes, "residue_backward",
        flops=4 * rows * width * slope.shape[1], moved=8 * MIB,
    )


def feed_kernel(first, second, f1, fb1, f2, f1g, f2g, fb1g):
    width = f1.shape[0]

    @pl.when(pl.program_id(0) == 0)
    def _():
        for ref in (f1g, f2g, fb1g):
            ref[...] = jnp.zeros_like(ref)

    for both in (first, second):
        h1b, gy2 = both[:, :width], both[:, width:]
        act, slope = gelu_parts(dot(h1b, f1[...]) + fb1[...])
        gy1 = (dot_back(gy2, f2[...]) * slope).astype(BF16)
        f1g[...] += dot_rows(h1b, gy1)
        f2g[...] += dot_rows(act.astype(BF16), gy2)
        fb1g[...] += column_sum(gy1.astype(F32))


def feed_gradients(both, f1, fb1, f2):
    width, hidden = f1.shape
    half = both[0].shape[0]
    chunk = min(512, half)
    shapes = [(width, hidden), (hidden, width), (1, hidden)]
    return pl.pallas_call(
        feed_kernel,
        grid=(half // chunk,),
        in_specs=[pl.BlockSpec((chunk, 2 * width), lambda i: (i, 0))] * 2
        + [const_spec(a.shape) for a in (f1, fb1, f2)],
        out_specs=[pl.BlockSpec(s, whole) for s in shapes],
        out_shape=[jax.ShapeDtypeStruct(s, F32) for s in shapes],
        compiler_params=pltpu.CompilerParams(vmem_limit_bytes=VMEM),
        name="feed_gradients",
        cost_estimate=pl.CostEstimate(
            flops=16 * half * width * hidden,
            bytes_accessed=8 * half * width,
            transcendentals=2 * half * hidden,
        ),
    )(*both, f1, fb1, f2)


def late_shapes(width, edge_width):
    return [
        (width, width),
        (width, width),
        (edge_width, width),
        (16, width),
        (width, width),
        (edge_width, edge_width),
        (16, edge_width),
    ]


def weight_shapes(width, edge_width):
    return early_shapes(width, edge_width) + late_shapes(width, edge_width)


def message_backward_kernel(
    sb, blocks, groups, codes, base, order, v, a1, s1, s2, edge, low_three, low_edge, local_row, live_col,
    m1, m2, e_first, node_lo, node_hi, node, early, e1g, eb1,
    edge_grad, far_keep, far_send, own, keep, send,
    low_two, low_one, grad, rows_ref, moved, m2g, m1eg, m1fg, b2s, slab,
):
    step = pl.program_id(0)
    rows, width = v.shape
    edge_width = edge.shape[2]
    block = sb * rows
    tiles = width // LANES
    size = 16

    @pl.when(step == 0)
    def _():
        for ref in (own, m2g, m1eg, m1fg, b2s):
            ref[...] = jnp.zeros_like(ref)

    @pl.when(step < blocks)
    def _():
        for row in range(0, rows, size):
            count = live_col[row : row + size, :]
            inverse = 1.0 / count.astype(F32)
            value = v[row : row + size, :]
            total = b2s[row : row + size, :]
            for s in range(sb):
                at = s * rows + row
                share = jnp.where(count > step * sb + s, inverse, 0.0)
                low = (value * spread(share, width) * s2[at : at + size, :].astype(F32)).astype(BF16)
                low_two[at : at + size, :] = low
                total = total + low.astype(F32)
            b2s[row : row + size, :] = total
        grad[...] = dot_back(low_two[...], m2[...])
        m2g[...] += dot_rows(a1[...], low_two[...])
        first = pl.multiple_of(step * (block * 8), 8)
        rows_ref[pl.ds(first + tiles, block, stride=8), :] = index_columns(local_row[...]).astype(F32)
        for row in range(0, rows, size):
            total = own[row : row + size, :]
            for s in range(sb):
                at = s * rows + row
                low = (grad[at : at + size, :] * s1[at : at + size, :].astype(F32)).astype(BF16)
                low_one[at : at + size, :] = low
                low = low.astype(F32)
                total = total + low
                for j in range(tiles):
                    rows_ref[pl.ds(first + at * 8 + j, size, stride=8), :] = low[
                        :, j * LANES : (j + 1) * LANES
                    ]
            own[row : row + size, :] = total
        m1eg[...] += dot_rows(edge[...].reshape(block, edge_width), low_one[...])
        total = (
            low_three[...].astype(F32)
            + dot(low_edge[...], e_first[:, width : width + edge_width])
            + dot_back(low_one[...], m1[width : width + edge_width, :])
        )
        edge_grad[...] = total.reshape(sb, rows, edge_width)

    @pl.when(step >= blocks)
    def _():
        deep = far_keep.shape[0]
        count = block * blocks // groups
        values, local = group_rows(order, (step - blocks) * count, count, rows_ref, moved, width)
        sums = group_sums(values, local, 2 * deep * rows).astype(BF16)
        near = jnp.concatenate(
            [ref[at, 0] for ref in (node_lo, node_hi) for at in range(deep)], axis=0
        )
        m1fg[...] += dot_rows(near, sums)
        height = rows // 16
        for at in range(2 * deep):
            out = (far_keep if at < deep else far_send).at[at % deep, 0]
            for j in range(tiles):
                tile = sums[at * rows : (at + 1) * rows, j * LANES : (j + 1) * LANES]
                out[j * height : (j + 1) * height] = tile.reshape(height, 16, LANES)

    @pl.when(step == blocks + groups - 1)
    def _():
        count = early.shape[0]
        slab[:count] = early[...]
        slab[count:] = jnp.zeros_like(slab[count:])
        pack(
            slab,
            [
                dot_rows(node[...], own[...].astype(BF16)),
                m2g[...],
                m1eg[...],
                padded_rows([column_sum(own[...]), column_sum(b2s[...])], width),
                m1fg[...],
                e1g[...],
                padded_rows([eb1[...]], edge_width),
            ],
            count,
        )
        order_out(slab, base[0], codes, keep, send)


def message_backward(
    groups, codes, base, order, v, a1, s1, s2, edge, low_three, low_edge, local_row, live_col, m1, m2,
    e_first, node_lo, node_hi, node, early, e1g, eb1,
):
    slots, rows, edge_width = edge.shape
    width = v.shape[1]
    sb = slot_block(slots)
    block = sb * rows
    blocks = slots // sb
    edges = slots * rows
    half = node_lo.shape[0]
    deep = half // rows // groups
    tiles = rows * width // (16 * LANES)
    slab = slab_tiles(weight_shapes(width, edge_width), len(codes)) * len(codes)
    node_lo, node_hi = [n.reshape(deep, groups, rows, width) for n in (node_lo, node_hi)]
    blk = lambda i: jnp.minimum(i, blocks - 1)
    group_at = lambda i: (0, jnp.maximum(i - blocks, 0))
    row_spec = pl.BlockSpec((block, width), lambda i: (blk(i), 0))
    slot_spec = pl.BlockSpec((sb, rows, edge_width), lambda i: (blk(i), 0, 0))
    edge_spec = pl.BlockSpec((block, edge_width), lambda i: (blk(i), 0))
    node_spec = pl.BlockSpec((deep, 1, rows, width), lambda i: (*group_at(i), 0, 0))
    far_spec = pl.BlockSpec((deep, 1, tiles, 16, LANES), lambda i: (*group_at(i), 0, 0, 0))
    slab_spec = pl.BlockSpec((slab // 2, 16, LANES), lambda i: (0, 0, 0))
    smem = pl.BlockSpec(memory_space=pltpu.SMEM)
    return pl.pallas_call(
        functools.partial(message_backward_kernel, sb, blocks, groups, codes),
        grid=(blocks + groups,),
        in_specs=[
            smem,
            smem,
            const_spec(v.shape),
            row_spec,
            row_spec,
            row_spec,
            slot_spec,
            edge_spec,
            edge_spec,
            pl.BlockSpec((1, block), lambda i: (0, blk(i))),
            const_spec(live_col.shape),
            const_spec(m1.shape),
            const_spec(m2.shape),
            const_spec(e_first.shape),
            node_spec,
            node_spec,
            const_spec(node.shape),
            const_spec(early.shape),
            const_spec(e1g.shape),
            const_spec(eb1.shape),
        ],
        out_specs=[slot_spec, far_spec, far_spec, pl.BlockSpec((rows, width), whole), slab_spec, slab_spec],
        out_shape=[
            jax.ShapeDtypeStruct((slots, rows, edge_width), F32),
            jax.ShapeDtypeStruct((deep, groups, tiles, 16, LANES), BF16),
            jax.ShapeDtypeStruct((deep, groups, tiles, 16, LANES), BF16),
            jax.ShapeDtypeStruct((rows, width), F32),
            jax.ShapeDtypeStruct((slab // 2, 16, LANES), BF16),
            jax.ShapeDtypeStruct((slab // 2, 16, LANES), BF16),
        ],
        scratch_shapes=[
            pltpu.VMEM((block, width), BF16),
            pltpu.VMEM((block, width), BF16),
            pltpu.VMEM((block, width), F32),
            pltpu.VMEM((edges * 8, LANES), F32),
            pltpu.VMEM((edges // groups * 8, LANES), F32),
            pltpu.VMEM((width, width), F32),
            pltpu.VMEM((edge_width, width), F32),
            pltpu.VMEM((width, width), F32),
            pltpu.VMEM((rows, width), F32),
            slab_scratch(slab),
        ],
        compiler_params=pltpu.CompilerParams(vmem_limit_bytes=VMEM),
        name="message_backward",
        cost_estimate=pl.CostEstimate(
            flops=2 * edges * width * (2 * width + 3 * edge_width + half // groups),
            bytes_accessed=edges * width * 6 + edges * edge_width * 10,
            transcendentals=0,
        ),
    )(
        base, order, v, a1, s1, s2, edge, low_three, low_edge, local_row, live_col, m1, m2, e_first,
        node_lo, node_hi, node, early, e1g, eb1,
    )


def node_kernel(pieces, g_u1, own, m1, *refs):
    far, grad_out = refs[:pieces], refs[pieces]
    rows, width = own.shape
    height = rows // 16
    tiles = height * (width // LANES)
    sums = far[0][:tiles].astype(F32)
    for ref in far[1:]:
        sums = sums + ref[:tiles].astype(F32)
    far_sum = jnp.concatenate(
        [sums[j * height : (j + 1) * height].reshape(rows, LANES) for j in range(width // LANES)],
        axis=1,
    )
    far_first = m1.shape[0] - width
    grad_out[...] = (
        g_u1[...]
        + fine(dot_back, own[...], m1[:width, :])
        + fine(dot_back, far_sum, m1[far_first:, :])
    )


def node_last(g_u1, own, m1, far):
    return small_call(
        functools.partial(node_kernel, len(far)),
        (g_u1, own, m1, *far), [(own.shape, F32)], "node_gradient",
        flops=8 * own.size * own.shape[1], moved=2 * MIB,
    )[0]


def weights_out_kernel(
    codes, base, first, second,
    m1g, b1, m2g, b2, m3g, e1g, e2g, e3g, b3, g1, g2, fb2, eb1, eb2, eb3, g3, slab,
):
    order_in(slab, base[0], codes, first, second)
    width, edge_width = m3g.shape[0], e2g.shape[0]
    shapes = weight_shapes(width, edge_width)
    starts = [all_tiles(shapes[:at]) for at in range(len(shapes))]
    m3g[...] = unpack(slab, starts[0], width, width)
    e1g[:, :width] = unpack(slab, starts[1], edge_width, width)
    middle = unpack(slab, starts[12], edge_width, edge_width)
    far = unpack(slab, starts[2], edge_width, width)
    over = edge_width % LANES
    base_col = width + edge_width - over
    e1g[:, width:base_col] = middle[:, : edge_width - over]
    far = pltpu.roll(jnp.concatenate([far, jnp.zeros((edge_width, LANES), F32)], axis=1), over, 1)
    lane = lax.broadcasted_iota(jnp.int32, (edge_width, LANES), 1)
    e1g[:, base_col : base_col + LANES] = jnp.where(
        lane < over, middle[:, edge_width - over : edge_width - over + LANES], far[:, :LANES]
    )
    rest = e1g.shape[1] - base_col - LANES
    e1g[:, base_col + LANES :] = far[:, LANES : LANES + rest]
    e2g[...] = unpack(slab, starts[3], edge_width, edge_width)[:, :edge_width]
    e3g[...] = unpack(slab, starts[4], edge_width, edge_width)[:, :edge_width]
    bias = unpack(slab, starts[5], 16, width)
    for row, out in enumerate((g1, g2, fb2, b3)):
        out[...] = bias[row : row + 1]
    bias = unpack(slab, starts[6], 16, edge_width)
    for row, out in enumerate((eb2, eb3, g3)):
        out[...] = bias[row : row + 1, :edge_width]
    m1g[:width, :] = unpack(slab, starts[7], width, width)
    m2g[...] = unpack(slab, starts[8], width, width)
    m1g[width : width + edge_width, :] = unpack(slab, starts[9], edge_width, width)
    bias = unpack(slab, starts[10], 16, width)
    b1[...] = bias[0:1]
    b2[...] = bias[1:2]
    eb1[...] = unpack(slab, starts[13], 16, edge_width)[:1, :edge_width]
    m1g[width + edge_width :, :] = unpack(slab, starts[11], width, width)


def weights_out(codes, base, halves_in, width, edge_width):
    shapes = [(2 * width + edge_width, width), (1, width), (width, width), (1, width)]
    shapes += [(width, width), (edge_width, 2 * width + edge_width)]
    shapes += [(edge_width, edge_width)] * 2 + [(1, width)] * 4 + [(1, edge_width)] * 4
    tiles = slab_tiles(weight_shapes(width, edge_width), len(codes)) * len(codes)
    return small_call(
        functools.partial(weights_out_kernel, codes),
        (base, *halves_in), [(s, F32) for s in shapes], "weight_gradients",
        [slab_scratch(tiles)], moved=10 * MIB, scalars=1,
    )


def exchange(value, mask, devices):
    return lax.ppermute(value, AXES, [(d, d ^ mask) for d in range(devices)])


def mask_groups(masks):
    return [masks[i : min(i + 2, len(masks) - 1)] for i in range(0, len(masks) - 1, 2)] + [masks[-1:]]


def order_codes(groups):
    masks = [mask for group in groups for mask in group]
    return [
        sum(mask for bit, mask in enumerate(masks) if place >> bit & 1)
        for place in range(1 << len(masks))
    ]


def combined(group, code):
    return sum(mask for bit, mask in enumerate(group) if code >> bit & 1)


def sent_around(value, group, devices):
    return [value] + [
        exchange(value, combined(group, code), devices) for code in range(1, 1 << len(group))
    ]


def shared_out(total, group, devices):
    parts = 1 << len(group)
    rows = total.shape[0] // parts
    return [total[:rows]] + [
        exchange(total[code * rows : (code + 1) * rows].astype(BF16), combined(group, code), devices)
        for code in range(1, parts)
    ]


def add_up(terms):
    total = terms[0].astype(F32)
    for term in terms[1:]:
        total = total + term.astype(F32)
    return total


def tied(*values):
    return lax.optimization_barrier(values)


def split_three(value):
    rows = []
    for _ in range(3):
        high = lax.reduce_precision(value, 8, 7)
        rows.append(high.astype(BF16))
        value = value - high
    return jnp.concatenate(rows + [jnp.zeros((13, value.shape[1]), BF16)], axis=0)


def per_device(
    node_in,
    edge_in,
    neighbours,
    live_counts,
    message_first,
    message_first_bias,
    message_second,
    message_second_bias,
    message_third,
    message_third_bias,
    norm_one,
    feed_first,
    feed_first_bias,
    feed_second,
    feed_second_bias,
    norm_two,
    edge_first,
    edge_first_bias,
    edge_second,
    edge_second_bias,
    edge_third,
    edge_third_bias,
    norm_three,
    node_cotangent,
    edge_cotangent,
):
    rows, slots = neighbours.shape
    width = node_in.shape[1]
    edge_width = edge_in.shape[2]
    edges = rows * slots
    hid_count = lax.axis_size("hid")
    res_count = lax.axis_size("res")
    devices = res_count * hid_count
    bits = devices.bit_length() - 1
    masks = [1 << b for b in range(bits - 1, -1, -1)]
    groups = mask_groups(masks)
    codes = order_codes(groups)
    me = lax.axis_index("res") * hid_count + lax.axis_index("hid")
    base = me.reshape(1)
    row = lambda vector: vector.reshape(1, -1)

    names = neighbours.T.reshape(edges)
    apart = (names // rows) ^ me
    place = jnp.zeros_like(names)
    for bit, mask in enumerate(masks):
        place = place | jnp.where((apart & mask) != 0, 1 << bit, 0)
    idx_row = (place * rows + names % rows).reshape(1, edges)
    res_count = devices // hid_count
    local_row = (place // res_count * rows + names % rows).reshape(1, edges)
    edge_order = group_order(place % res_count, res_count)
    live_col = jnp.broadcast_to(live_counts[:, None], (rows, LANES))
    edge = edge_in.transpose(1, 0, 2)
    cot = edge_cotangent.transpose(1, 0, 2)
    e_first = edge_first.T
    e_far = e_first[:, width + edge_width :]
    f1x = jnp.concatenate([feed_first, split_three(row(feed_first_bias))], axis=0)
    f2x = feed_second

    stack = lambda pieces: jnp.concatenate(pieces, axis=0)
    *outer, near = groups

    held = stack(sent_around(node_in, outer[0], devices))
    held, idx_row, local_row, live_col, e_far = tied(held, idx_row, local_row, live_col, e_far)
    for group in outer[1:]:
        held = stack(sent_around(held, group, devices))
    held, f1x, f2x, edge_order = tied(held, f1x, f2x, edge_order)
    node_lo, node_hi = sent_around(held, near, devices)

    f1, f2 = [f1x], [f2x]
    hid_masks = [m for m in masks if m < hid_count]
    for mask in hid_masks[:-1]:
        f1, f2 = [pieces + [exchange(p, mask, devices) for p in pieces] for pieces in (f1, f2)]

    a1, s1, s2, total = message_forward(
        node_lo, node_hi, node_in, edge, idx_row, live_col, message_first,
        row(message_first_bias), message_second, row(message_second_bias),
    )
    total, f1, f2 = tied(total, f1, f2)
    f1, f2 = [
        pieces + [exchange(p, hid_masks[-1], devices) for p in pieces] for pieces in (f1, f2)
    ]
    h1b, n1, sc1, n2, sc2, slope, h2b, far_part, own_part = residue_forward(
        node_in, total, message_third, row(message_third_bias), row(norm_one),
        row(feed_second_bias), row(norm_two), e_first, e_far, row(edge_first_bias), f1, f2,
    )

    held = stack(sent_around(far_part, outer[0], devices))
    for group in outer[1:]:
        held = stack(sent_around(held, group, devices))
    q_lo, q_hi = sent_around(held, near, devices)

    edge_out, act_one, act_two, low_three, low_two, low_one, hi, lo, own_sum, edge_gain = edge_branch(
        q_lo, q_hi, own_part, edge, cot, idx_row, live_col, e_first,
        edge_second, row(edge_second_bias), edge_third, row(edge_third_bias), row(norm_three),
    )

    terms = [lo, exchange(hi, near[0], devices)]
    made = None
    for group in reversed(outer):
        terms = shared_out(add_up(terms), group, devices)
        if made is None:
            made = edge_weights((act_two, act_one), (low_three, low_two), rows)
            terms, made = tied(terms, made)
    e3g, e2g, eb3, eb2 = made
    g_u1, v, both, early = residue_backward(
        (
            node_cotangent, own_sum, e_first, e_far, h1b, h2b, n1, sc1, n2, sc2, slope, row(norm_one),
            row(norm_two), message_third, total, e2g, e3g, eb2, eb3, edge_gain,
        ),
        terms, f1, f2,
    )

    both, low_here = tied(both, low_one)
    b_held = stack(sent_around(both, outer[0], devices))
    e1g, eb1 = edge_weights((low_here,), (edge,), rows)
    v, b_held, e1g, eb1 = tied(v, b_held, e1g, eb1)
    for group in outer[1:]:
        b_held = stack(sent_around(b_held, group, devices))
    edge_grad, far_keep, far_send, own, keep, send = message_backward(
        res_count, codes, base, edge_order, v, a1, s1, s2, edge, low_three, low_one, local_row, live_col,
        message_first, message_second, e_first, node_lo, node_hi, node_in, early, e1g, eb1,
    )
    keep, send, far_keep, far_send, b_held = tied(keep, send, far_keep, far_send, b_held)

    first, *others = reversed(outer)
    terms = [keep, exchange(send, near[0], devices)]
    total, b_held, far_send = tied(add_up(terms), b_held, far_send)
    terms = shared_out(total, first, devices)
    far_keep, far_send = [far.reshape(-1, 16, LANES) for far in (far_keep, far_send)]
    far_terms = [far_keep, exchange(far_send, near[0], devices)]
    b_near = sent_around(b_held, near, devices)
    total, b_first = tied(add_up(far_terms), b_near[0])
    far_terms = shared_out(total, first, devices)
    feed = feed_gradients((b_first, b_near[1]), feed_first, row(feed_first_bias), feed_second)
    terms, (f1g, f2g, fb1g) = tied(terms, feed)
    for group in others:
        terms = shared_out(add_up(terms), group, devices)
    held, *far_terms = tied(add_up(terms).astype(BF16), *far_terms)

    for at, group in enumerate(outer):
        around = sent_around(held, group, devices)
        if at < len(others):
            far_terms = shared_out(add_up(far_terms), others[at], devices)
        if at + 1 == len(outer):
            around, node_gradient = tied(around, node_last(g_u1, own, message_first, far_terms))
        held = stack(around)
        if at < len(others):
            held, *far_terms = tied(held, *far_terms)
    m1g, b1, m2g, b2, m3g, e1g, e2g, e3g, b3, g1, g2, fb2, eb1, eb2, eb3, g3 = weights_out(
        codes, base, sent_around(held, near, devices), width, edge_width
    )
    flat = lambda vector: vector.reshape(-1)
    return (
        h2b,
        edge_out.transpose(1, 0, 2),
        node_gradient,
        edge_grad.transpose(1, 0, 2),
        m1g,
        flat(b1),
        m2g,
        flat(b2),
        m3g,
        flat(b3),
        flat(g1),
        f1g,
        flat(fb1g),
        f2g,
        flat(fb2),
        flat(g2),
        e1g.T,
        flat(eb1),
        e2g,
        flat(eb2),
        e3g,
        flat(eb3),
        flat(g3),
    )


def solution(mesh):
    nodes, edges, shared = P(AXES, None), P(AXES, None, None), P()
    return jax.shard_map(
        per_device,
        mesh=mesh,
        in_specs=(nodes, edges, nodes, P(AXES))
        + (shared,) * 7
        + (P(None, "hid"), P("hid"), P("hid", None))
        + (shared,) * 9
        + (nodes, edges),
        out_specs=(nodes, edges, nodes, edges)
        + (shared,) * 7
        + (P(None, "hid"), P("hid"), P("hid", None))
        + (shared,) * 9,
        check_vma=False,
    )
```

```python
import functools

import jax
import jax.numpy as jnp
from jax import lax
from jax.experimental import pallas as pl
from jax.experimental.pallas import tpu as pltpu
from jax.sharding import PartitionSpec as P

EPS = 1e-05
AXES = ("res", "hid")
F32 = jnp.float32
BF16 = jnp.bfloat16
TANH_SCALE = 0.7978845608028654
TANH_CUBE = 0.044715
LANES = 128
CHUNK = 2048
MIB = 1024 * 1024
VMEM = 58 * MIB


def dot(left, right):
    return lax.dot_general(left, right, (((1,), (0,)), ((), ())), preferred_element_type=F32)


def dot_rows(left, right):
    return lax.dot_general(left, right, (((0,), (0,)), ((), ())), preferred_element_type=F32)


def dot_back(left, right):
    return lax.dot_general(left, right, (((1,), (1,)), ((), ())), preferred_element_type=F32)


def halves(value):
    high = value.astype(BF16)
    return high, (value - high.astype(F32)).astype(BF16)


def fine(product, value, weights):
    high, low = halves(value)
    return product(high, weights) + product(low, weights)


def gelu_parts(x):
    square = x * x
    t = jnp.tanh(x * (TANH_SCALE + (TANH_SCALE * TANH_CUBE) * square))
    gate = 0.5 + 0.5 * t
    act = x * gate
    slope = gate + act * (1.0 - gate) * (2 * TANH_SCALE + (6 * TANH_SCALE * TANH_CUBE) * square)
    return act, slope


def index_columns(idx_row):
    parts = [
        jnp.broadcast_to(idx_row[:, first : first + LANES], (LANES, LANES)).T
        for first in range(0, idx_row.shape[1], LANES)
    ]
    return jnp.concatenate(parts, axis=0)


def one_hot_columns(idx, start, count):
    one, zero = jnp.ones((), BF16), jnp.zeros((), BF16)
    idx = idx.astype(jnp.int16)
    lane = lax.broadcasted_iota(jnp.int32, idx.shape, 1).astype(jnp.int16)
    parts = [
        jnp.where(idx == lane + jnp.int16(start + first), one, zero)
        for first in range(0, count, LANES)
    ]
    return jnp.concatenate(parts, axis=1)


def pick_rows(idx, table_refs):
    total, start = None, 0
    for ref in table_refs:
        rows = ref.shape[0]
        step = min(rows, CHUNK)
        for first in range(0, rows, step):
            part = dot(one_hot_columns(idx, start + first, step), ref[first : first + step, :])
            total = part if total is None else total + part
        start += rows
    return total


def one_hot_rows(idx_row, start, count):
    shape = (count, idx_row.shape[1])
    row = (lax.broadcasted_iota(jnp.int32, shape, 0) + start).astype(jnp.int16)
    names = jnp.broadcast_to(idx_row, shape).astype(jnp.int16)
    return jnp.where(names == row, jnp.ones((), BF16), jnp.zeros((), BF16))


def group_rows(order, first, count, rows_ref, moved, width):
    for e in range(count):
        at = pl.multiple_of(order[0, first + e] * 8, 8)
        moved[e * 8 : e * 8 + 8, :] = rows_ref[pl.ds(at, 8), :]

    def column(at):
        return moved[pl.ds(at, count, stride=8), :]

    tiles = pl.cdiv(width, LANES)
    parts = [column(at)[:, : min(LANES, width - at * LANES)] for at in range(tiles)]
    return jnp.concatenate(parts, axis=1).astype(BF16), column(tiles)


def group_sums(rows, local, residues):
    lane = lax.broadcasted_iota(jnp.int32, local.shape, 1).astype(F32)
    picks = [
        jnp.where(local == lane + float(first), 1.0, 0.0).astype(BF16)
        for first in range(0, residues, LANES)
    ]
    return dot_rows(jnp.concatenate(picks, axis=1), rows)


def order_kernel(groups, count, names, out):
    rows = names.shape[0]
    row = lax.broadcasted_iota(jnp.int32, (LANES, LANES), 0)
    column = lax.broadcasted_iota(jnp.int32, (LANES, LANES), 1)
    upto = jnp.where(row <= column, 1.0, 0.0).astype(BF16)
    ones = jnp.ones((LANES, LANES), BF16)
    above = lax.broadcasted_iota(jnp.int32, (rows, rows), 0)
    before = jnp.where(lax.broadcasted_iota(jnp.int32, (rows, rows), 1) < above, 1.0, 0.0).astype(BF16)
    place = jnp.full(names.shape, float(2 * LANES * LANES), F32)
    for group in range(groups):
        here = names[...] == group
        low = jnp.where(here, 1.0, 0.0).astype(BF16)
        rank = dot(low, upto) + dot(before, dot(low, ones).astype(BF16))
        place = jnp.where(here, rank + float(group * count - 1), place)
    high = total = None
    for at in range(rows):
        where = jnp.broadcast_to(place[at : at + 1, :], (LANES, LANES)).T.astype(jnp.int32)
        left = jnp.where(where // LANES == column, 1.0, 0.0)
        right = jnp.where(where % LANES == column, 1.0, 0.0)
        part = dot_rows(left.astype(BF16), (right * float(at)).astype(BF16))
        high = part if high is None else high + part
        part = dot_rows(left.astype(BF16), (right * row.astype(F32)).astype(BF16))
        total = part if total is None else total + part
    number = high * float(LANES) + total
    out[...] = number[: out.shape[0], : out.shape[1]].astype(jnp.int32)


def group_order(names, groups):
    edges = names.shape[0]
    rows = pl.cdiv(pl.cdiv(edges, LANES), 8) * 8
    padded = jnp.pad(names, (0, rows * LANES - edges), constant_values=groups)
    out = small_call(
        functools.partial(order_kernel, groups, edges // groups),
        (padded.reshape(rows, LANES),), [((edges // LANES, LANES), jnp.int32)], "group_order",
    )[0]
    return out.reshape(1, edges)


def spread(column, width):
    return jnp.concatenate([column] * (width // LANES), axis=1)


def norm(value):
    centre = value - jnp.mean(value, -1, keepdims=True)
    scale = lax.rsqrt(jnp.mean(centre * centre, -1, keepdims=True) + EPS)
    return centre * scale, scale


def norm_back(inner, normed, scale):
    mean_first = jnp.mean(inner, -1, keepdims=True)
    mean_second = jnp.mean(inner * normed, -1, keepdims=True)
    return scale * (inner - mean_first - normed * mean_second)


def column_sum(value):
    return jnp.sum(value, axis=0, keepdims=True)


def whole(*_):
    return (0, 0)


def const_spec(shape):
    return pl.BlockSpec(shape, lambda *_: (0,) * len(shape), pipeline_mode=pl.Buffered(1))


def small_call(kernel, args, shapes, name, scratch=(), flops=0, moved=0, exps=0, scalars=0):
    return pl.pallas_call(
        kernel,
        grid=(1,),
        in_specs=[pl.BlockSpec(memory_space=pltpu.SMEM)] * scalars
        + [const_spec(a.shape) for a in args[scalars:]],
        out_specs=[pl.BlockSpec(s, lambda *_, n=len(s): (0,) * n) for s, _ in shapes],
        out_shape=[jax.ShapeDtypeStruct(*s) for s in shapes],
        scratch_shapes=list(scratch),
        compiler_params=pltpu.CompilerParams(vmem_limit_bytes=VMEM),
        name=name,
        cost_estimate=pl.CostEstimate(flops=flops, bytes_accessed=moved, transcendentals=exps),
    )(*args)


def tile_count(shape):
    return pl.cdiv(shape[0], 16) * pl.cdiv(shape[1], LANES)


def all_tiles(shapes):
    return sum(tile_count(s) for s in shapes)


def pack(slab, values, at=0):
    for value in values:
        rows, columns = value.shape
        count = rows // 16
        for first in range(0, columns, LANES):
            take = min(LANES, columns - first)
            tile = value[:, first : first + take].astype(BF16).reshape(count, 16, take)
            slab[at : at + count, :, :take] = tile
            at += count


def unpack(slab, at, rows, columns):
    count = rows // 16
    parts = [
        slab[at + i * count : at + (i + 1) * count].reshape(rows, LANES).astype(F32)
        for i in range(pl.cdiv(columns, LANES))
    ]
    return jnp.concatenate(parts, axis=1)


def order_out(slab, base, codes, keep, send):
    size = slab.shape[0] // len(codes)
    half = len(codes) // 2
    for place, code in enumerate(codes):
        out = keep if place < half else send
        at = (place % half) * size
        out[at : at + size] = slab[pl.ds((base ^ code) * size, size)]


def half_shapes(tiles):
    return [((tiles // 2, 16, LANES), BF16)] * 2


def slab_scratch(tiles):
    return pltpu.VMEM((tiles, 16, LANES), BF16)


def slab_tiles(shapes, chunks):
    return pl.cdiv(all_tiles(shapes), chunks)


def order_in(slab, base, codes, first, second):
    size = slab.shape[0] // len(codes)
    half = len(codes) // 2
    for place, code in enumerate(codes):
        source = first if place < half else second
        at = (place % half) * size
        slab[pl.ds((base ^ code) * size, size)] = source[at : at + size]


def padded_rows(parts, width):
    return jnp.concatenate(parts + [jnp.zeros((16 - len(parts), width), F32)], axis=0)


def slot_block(slots):
    for size in (10, 12, 8, 6, 5, 4, 3, 2):
        if slots % size == 0:
            return size
    return 1


def far_table(node_lo, node_hi, weights, put):
    tile = min(512, node_lo.shape[0])
    for source, start in ((node_lo, 0), (node_hi, node_lo.shape[0])):
        def body(i, carry, source=source, start=start):
            at = pl.multiple_of(i * tile, tile)
            put(start + at, dot(source[pl.ds(at, tile), :], weights))
            return carry
        lax.fori_loop(0, source.shape[0] // tile, body, 0)


def message_forward_kernel(
    sb, by_rows, node_lo, node_hi, node_own, edge, idx_row, names, live_col, m1, b1, m2, b2,
    a1_out, s1_out, s2_out, sum_out, table, far, near, lhs, z,
):
    step = pl.program_id(0)
    width = node_own.shape[1]
    edge_width = edge.shape[2]
    rows = edge.shape[1]
    block = sb * rows
    lanes = width // LANES

    @pl.when(step == 0)
    def _():
        weights = m1[width + edge_width :, :]
        if by_rows:
            def put(first, value):
                for at in range(8):
                    column = at % lanes * LANES
                    table[pl.ds(first * 8 + at, value.shape[0], stride=8), :] = value[
                        :, column : column + LANES
                    ]
        else:
            def put(first, value):
                table[pl.ds(first, value.shape[0]), :] = value.astype(BF16)
        far_table(node_lo, node_hi, weights, put)
        near[:edge_width, :] = m1[width : width + edge_width, :]
        near[edge_width:, :] = jnp.zeros_like(near[edge_width:, :])
        near[edge_width : edge_width + rows, :] = (
            dot(node_own[...], m1[:width, :]) + b1[...]
        ).astype(BF16)
        shape = (rows, near.shape[0] - edge_width)
        eye = lax.broadcasted_iota(jnp.int32, shape, 0) == lax.broadcasted_iota(jnp.int32, shape, 1)
        for at in range(0, block, rows):
            lhs[at : at + rows, edge_width:] = jnp.where(eye, 1.0, 0.0).astype(BF16)
        sum_out[...] = jnp.zeros_like(sum_out)

    lhs[:, :edge_width] = edge[...].reshape(block, edge_width)
    z[...] = dot(lhs[...], near[...])
    if not by_rows:
        z[...] += pick_rows(index_columns(idx_row[...]), (table,))
    upper = lax.broadcasted_iota(jnp.int32, (8, LANES), 0) < lanes

    def fetch(at):
        for e in range(at, at + 16, 2):
            pair = [
                table[pl.ds(pl.multiple_of(names[0, step * block + e + i] * 8, 8), 8), :]
                for i in range(2)
            ]
            far[e * lanes : e * lanes + 8, :] = jnp.where(upper, *pair)

    def fetched(at):
        return jnp.concatenate(
            [far[pl.ds(at * lanes + j, 16, stride=lanes), :] for j in range(lanes)], axis=1
        )

    if by_rows:
        fetch(0)
    for at in range(0, block, 16):
        value = z[at : at + 16, :]
        if by_rows:
            if at + 16 < block:
                fetch(at + 16)
            value = value + fetched(at)
        act, slope = gelu_parts(value)
        a1_out[at : at + 16, :] = act.astype(BF16)
        s1_out[at : at + 16, :] = slope.astype(BF16)
    z[...] = dot(a1_out[...], m2[...])
    bias = b2[...]
    for row in range(0, rows, 16):
        count = live_col[row : row + 16, :]
        inverse = 1.0 / count.astype(F32)
        total = sum_out[row : row + 16, :]
        for s in range(sb):
            at = s * rows + row
            act, slope = gelu_parts(z[at : at + 16, :] + bias)
            s2_out[at : at + 16, :] = slope.astype(BF16)
            share = jnp.where(count > step * sb + s, inverse, 0.0)
            total = total + act.astype(BF16).astype(F32) * spread(share, width)
        sum_out[row : row + 16, :] = total


def message_forward(node_lo, node_hi, node_own, edge, idx_row, live_col, m1, b1, m2, b2):
    slots, rows, edge_width = edge.shape
    width = node_own.shape[1]
    residues = 2 * node_lo.shape[0]
    by_rows = residues <= 4096 and width == 4 * LANES
    sb = slot_block(slots) if by_rows else 4
    block = sb * rows
    edges = slots * rows
    near = pl.cdiv(edge_width + rows, LANES) * LANES
    row_spec = pl.BlockSpec((block, width), lambda i: (i, 0))
    return pl.pallas_call(
        functools.partial(message_forward_kernel, sb, by_rows),
        grid=(slots // sb,),
        in_specs=[
            const_spec(node_lo.shape),
            const_spec(node_hi.shape),
            const_spec(node_own.shape),
            pl.BlockSpec((sb, rows, edge_width), lambda i: (i, 0, 0)),
            pl.BlockSpec((1, block), lambda i: (0, i)),
            pl.BlockSpec(memory_space=pltpu.SMEM),
            const_spec(live_col.shape),
            const_spec(m1.shape),
            const_spec(b1.shape),
            const_spec(m2.shape),
            const_spec(b2.shape),
        ],
        out_specs=[row_spec, row_spec, row_spec, pl.BlockSpec((rows, width), whole)],
        out_shape=[jax.ShapeDtypeStruct((edges, width), BF16)] * 3
        + [jax.ShapeDtypeStruct((rows, width), F32)],
        scratch_shapes=[
            pltpu.VMEM((residues * 8, LANES), F32) if by_rows else pltpu.VMEM((residues, width), BF16),
            pltpu.VMEM((block * 4 if by_rows else 8, LANES), F32),
            pltpu.VMEM((near, width), BF16),
            pltpu.VMEM((block, near), BF16),
            pltpu.VMEM((block, width), F32),
        ],
        compiler_params=pltpu.CompilerParams(vmem_limit_bytes=VMEM),
        name="message_forward",
        cost_estimate=pl.CostEstimate(
            flops=2 * edges * width * (residues + edge_width + width),
            bytes_accessed=edges * width * 6 + edges * edge_width * 2 + edges * LANES * 4,
            transcendentals=2 * edges * width,
        ),
    )(node_lo, node_hi, node_own, edge, idx_row, idx_row, live_col, m1, b1, m2, b2)


def residue_forward_kernel(parts, node, total, m3, b3, g1, fb2, g2, e_first, e_far, eb, *refs):
    f1, f2 = refs[:parts], refs[parts : 2 * parts]
    h1b_out, n1_out, sc1_out, n2_out, sc2_out, slope_out, h2b_out, far_out, own_out = refs[2 * parts :]
    width, hidden = node.shape[1], f1[0].shape[1]
    u1 = node[...].astype(F32) + fine(dot, total[...], m3[...]) + b3[...]
    n1, sc1 = norm(u1)
    h1 = n1 * g1[...]
    h1b = h1.astype(BF16)
    h1b_out[...] = h1b
    n1_out[...] = n1
    sc1_out[...] = jnp.broadcast_to(sc1, sc1_out.shape)
    y2 = None
    for p in range(parts):
        bias = f1[p][width : width + 16, :].astype(F32)
        bias = bias[0:1] + bias[1:2] + bias[2:3]
        act, slope = gelu_parts(dot(h1b, f1[p][:width, :]) + bias)
        slope_out[:, p * hidden : (p + 1) * hidden] = slope
        part = dot(act.astype(BF16), f2[p][...])
        y2 = part if y2 is None else y2 + part
    n2, sc2 = norm(h1 + (y2 + fb2[...]))
    h2b = (n2 * g2[...]).astype(BF16)
    n2_out[...] = n2
    sc2_out[...] = jnp.broadcast_to(sc2, sc2_out.shape)
    h2b_out[...] = h2b
    far_out[...] = dot_back(h2b, e_far[...]).astype(BF16)
    own_out[...] = dot_back(h2b, e_first[:, :width]) + eb[...]


def residue_forward(node, total, m3, b3, g1, fb2, g2, e_first, e_far, eb, f1, f2):
    rows, width = node.shape
    edge_width = e_first.shape[0]
    hidden = len(f1) * f1[0].shape[1]
    shapes = [
        ((rows, width), BF16),
        ((rows, width), F32),
        ((rows, LANES), F32),
        ((rows, width), F32),
        ((rows, LANES), F32),
        ((rows, hidden), F32),
        ((rows, width), BF16),
        ((rows, edge_width), BF16),
        ((rows, edge_width), F32),
    ]
    return small_call(
        functools.partial(residue_forward_kernel, len(f1)),
        (node, total, m3, b3, g1, fb2, g2, e_first, e_far, eb, *f1, *f2),
        shapes, "residue_forward", flops=4 * rows * width * hidden, moved=5 * MIB,
        exps=rows * hidden,
    )


def edge_kernel(
    sb, blocks, hi_chunks, by_rows, far_lo, far_hi, own, edge, cot, idx, idx_row, names, live_col,
    e_first, e2, eb2, e3, eb3, g3,
    edge_out, act_one_out, act_two_out, low_three_out, low_two_out, low_one_out, hi_out, lo_out, own_out, gain_out,
    low_first, gs, table, far, z, slope_ref,
):
    step = pl.program_id(0)
    rows, width = own.shape
    node_width = (e_first.shape[1] - width) // 2
    e_mid = e_first.at[:, node_width : node_width + width]
    tiles = pl.cdiv(width, LANES)
    per = 8 // tiles
    size = 32

    @pl.when(step == 0)
    def _():
        own_out[...] = jnp.zeros_like(own_out)
        gs[...] = jnp.zeros_like(gs)
        half = far_lo.shape[0]
        if by_rows:
            for source, start in ((far_lo, 0), (far_hi, half)):
                for first in range(0, half, 512):
                    value = source[first : first + 512, :].astype(F32)
                    for at in range(8):
                        column = at % tiles * LANES
                        take = min(LANES, width - column)
                        table[pl.ds((start + first) * 8 + at, value.shape[0], stride=8), :take] = value[
                            :, column : column + take
                        ]

    @pl.when(step < blocks)
    def _():
        block = sb * rows
        flat = edge[...].reshape(block, width)
        z[...] = dot_back(flat, e_mid[...])
        if not by_rows:
            z[...] += pick_rows(index_columns(idx[...]), (far_lo, far_hi))
        sub = lax.broadcasted_iota(jnp.int32, (8, LANES), 0)

        def fetch(at):
            for e in range(at, at + size, per):
                got = [
                    table[pl.ds(pl.multiple_of(names[0, step * block + e + i] * 8, 8), 8), :]
                    for i in range(per)
                ]
                value = got[-1]
                for i in range(per - 2, -1, -1):
                    value = jnp.where(sub < (i + 1) * tiles, got[i], value)
                far[e * tiles : e * tiles + 8, :] = value

        def fetched(at):
            parts = [
                far[pl.ds(at * tiles + j, size, stride=tiles), :][:, : min(LANES, width - j * LANES)]
                for j in range(tiles)
            ]
            return jnp.concatenate(parts, axis=1)

        if by_rows:
            fetch(0)
        for at in range(0, block, size):
            value = z[at : at + size, :] + own[at % rows : at % rows + size, :]
            if by_rows:
                if at + size < block:
                    fetch(at + size)
                value = value + fetched(at)
            act, slope = gelu_parts(value)
            act_one_out[at : at + size, :] = act.astype(BF16)
            slope_ref[at : at + size, :] = slope
        act_one = act_one_out[...]
        act_two, slope_two = gelu_parts(dot(act_one, e2[...]) + eb2[...])
        act_two = act_two.astype(BF16)
        act_two_out[...] = act_two
        w_three = dot(act_two, e3[...]) + eb3[...]
        normed, scale = norm(flat.astype(F32) + w_three)
        count = spread(live_col[...], pl.cdiv(width, LANES) * LANES)[:, :width]
        live = jnp.concatenate(
            [jnp.where(count > step * sb + s, 1.0, 0.0) for s in range(sb)], axis=0
        )
        edge_out[...] = (normed * g3[...] * live).astype(BF16).reshape(sb, rows, width)
        grad = cot[...].reshape(block, width).astype(F32) * live
        gs[...] += jnp.sum((grad * normed).reshape(sb, rows, width), axis=0)
        low_three = norm_back(grad * g3[...], normed, scale).astype(BF16)
        low_three_out[...] = low_three
        low_two = (dot_back(low_three, e3[...]) * slope_two).astype(BF16)
        low_two_out[...] = low_two
        low_one = (dot_back(low_two, e2[...]) * slope_ref[...]).astype(BF16)
        low_one_out[...] = low_one
        own_out[...] += jnp.sum(low_one.astype(F32).reshape(sb, rows, width), axis=0)
        low_first[pl.ds(pl.multiple_of(step * block, block), block), :] = low_one

    chunk = hi_out.shape[0]

    @pl.when((step >= blocks) & (step < blocks + hi_chunks))
    def _():
        start = (step - blocks + hi_chunks) * chunk
        hi_out[...] = dot(one_hot_rows(idx_row[...], start, chunk), low_first[...]).astype(BF16)

    @pl.when(step >= blocks + hi_chunks)
    def _():
        start = (step - blocks - hi_chunks) * chunk
        lo_out[...] = dot(one_hot_rows(idx_row[...], start, chunk), low_first[...])

    @pl.when(step == blocks + 2 * hi_chunks - 1)
    def _():
        gain_out[...] = column_sum(gs[...])


def edge_branch(far_lo, far_hi, own, edge, cot, idx_row, live_col, e_first, e2, eb2, e3, eb3, g3):
    slots, rows, width = edge.shape
    sb = slot_block(slots)
    edges = slots * rows
    block = sb * rows
    blocks = slots // sb
    half = far_lo.shape[0]
    chunk = min(512, half)
    hi_chunks = half // chunk
    by_rows = half <= 2048 and 8 % pl.cdiv(width, LANES) == 0
    blk = lambda i: jnp.minimum(i, blocks - 1)
    hi_at = lambda i: (jnp.clip(i - blocks, 0, hi_chunks - 1), 0)
    lo_at = lambda i: (jnp.clip(i - blocks - hi_chunks, 0, hi_chunks - 1), 0)
    slot_spec = pl.BlockSpec((sb, rows, width), lambda i: (blk(i), 0, 0))
    row_spec = pl.BlockSpec((block, width), lambda i: (blk(i), 0))
    return pl.pallas_call(
        functools.partial(edge_kernel, sb, blocks, hi_chunks, by_rows),
        grid=(blocks + 2 * hi_chunks,),
        in_specs=[
            const_spec(far_lo.shape),
            const_spec(far_hi.shape),
            const_spec(own.shape),
            slot_spec,
            slot_spec,
            pl.BlockSpec((1, block), lambda i: (0, blk(i))),
            const_spec(idx_row.shape),
            pl.BlockSpec(memory_space=pltpu.SMEM),
            const_spec(live_col.shape),
            const_spec(e_first.shape),
            const_spec(e2.shape),
            const_spec(eb2.shape),
            const_spec(e3.shape),
            const_spec(eb3.shape),
            const_spec(g3.shape),
        ],
        out_specs=[slot_spec]
        + [row_spec] * 5
        + [
            pl.BlockSpec((chunk, width), hi_at),
            pl.BlockSpec((chunk, width), lo_at),
            pl.BlockSpec((rows, width), whole),
            pl.BlockSpec((1, width), whole),
        ],
        out_shape=[jax.ShapeDtypeStruct((slots, rows, width), BF16)]
        + [jax.ShapeDtypeStruct((edges, width), BF16)] * 5
        + [
            jax.ShapeDtypeStruct((half, width), BF16),
            jax.ShapeDtypeStruct((half, width), F32),
            jax.ShapeDtypeStruct((rows, width), F32),
            jax.ShapeDtypeStruct((1, width), F32),
        ],
        scratch_shapes=[
            pltpu.VMEM((edges, width), BF16),
            pltpu.VMEM((rows, width), F32),
            pltpu.VMEM((half * 16 if by_rows else 8, LANES), F32),
            pltpu.VMEM((block * 8, LANES), F32),
            pltpu.VMEM((block, width), F32),
            pltpu.VMEM((block, width), F32),
        ],
        compiler_params=pltpu.CompilerParams(vmem_limit_bytes=VMEM),
        name="edge_branch",
        cost_estimate=pl.CostEstimate(
            flops=2 * edges * width * (4 * half + 5 * width),
            bytes_accessed=edges * width * 16,
            transcendentals=2 * edges * width,
        ),
    )(far_lo, far_hi, own, edge, cot, idx_row, idx_row, idx_row, live_col, e_first, e2, eb2, e3, eb3, g3)


def edge_weights_kernel(blocks, pairs, *refs):
    step = pl.program_id(0)
    lefts, rights = refs[:pairs], refs[pairs : 2 * pairs]
    grads, biases, sums = refs[2 * pairs : 3 * pairs], refs[3 * pairs : 4 * pairs], refs[-1]
    rows = sums.shape[1]

    @pl.when(step == 0)
    def _():
        for ref in (*grads, sums):
            ref[...] = jnp.zeros_like(ref)

    for at in range(pairs):
        left, right = [r[...].reshape(-1, r.shape[-1]) for r in (lefts[at], rights[at])]
        grads[at][...] += dot_rows(left, right)
        low = left if lefts[at].ndim < rights[at].ndim else right
        sums[at] += jnp.sum(low.astype(F32).reshape(-1, rows, low.shape[1]), axis=0)

    @pl.when(step == blocks - 1)
    def _():
        for at in range(pairs):
            biases[at][...] = column_sum(sums[at])


def edge_weights(lefts, rights, rows):
    pairs = len(lefts)
    edges, width = lefts[0].shape
    slots = edges // rows
    sb = slot_block(slots)

    def spec(array):
        if array.ndim == 3:
            return pl.BlockSpec((sb, rows, width), lambda i: (i, 0, 0))
        return pl.BlockSpec((sb * rows, width), lambda i: (i, 0))

    shapes = [(width, width)] * pairs + [(1, width)] * pairs
    return pl.pallas_call(
        functools.partial(edge_weights_kernel, slots // sb, pairs),
        grid=(slots // sb,),
        in_specs=[spec(array) for array in (*lefts, *rights)],
        out_specs=[pl.BlockSpec(s, whole) for s in shapes],
        out_shape=[jax.ShapeDtypeStruct(s, F32) for s in shapes],
        scratch_shapes=[pltpu.VMEM((pairs, rows, width), F32)],
        compiler_params=pltpu.CompilerParams(vmem_limit_bytes=VMEM),
        name="edge_weights",
        cost_estimate=pl.CostEstimate(
            flops=2 * pairs * edges * width * width,
            bytes_accessed=pairs * edges * width * 4,
            transcendentals=0,
        ),
    )(*lefts, *rights)


def early_shapes(width, edge_width):
    return [
        (width, width),
        (edge_width, width),
        (edge_width, width),
        (edge_width, edge_width),
        (edge_width, edge_width),
        (16, width),
        (16, edge_width),
    ]


def residue_backward_kernel(
    parts, pieces, node_cot, own_sum, e_first, e_far, h1b, h2b, n1, sc1, n2, sc2, slope, g1, g2, m3,
    total, e2g, e3g, eb2, eb3, edge_gain, *refs,
):
    far = refs[:pieces]
    f1 = refs[pieces : pieces + parts]
    f2 = refs[pieces + parts : pieces + 2 * parts]
    gu1_out, v_out, both_out, slab = refs[pieces + 2 * parts :]
    width, hidden = h2b.shape[1], f1[0].shape[1]
    far_sum = far[0][: far[1].shape[0], :]
    for ref in far[1:]:
        far_sum = far_sum + ref[...].astype(F32)
    own = own_sum[...]
    g_h2 = (
        node_cot[...].astype(F32)
        + fine(dot, own, e_first[:, :width])
        + fine(dot, far_sum, e_far[...])
    )
    gain_two = column_sum(g_h2 * n2[...])
    g_u2 = norm_back(g_h2 * g2[...], n2[...], sc2[:, :1])
    gy2 = g_u2.astype(BF16)
    both_out[:, :width] = h1b[...]
    both_out[:, width:] = gy2
    g_h1 = g_u2
    for p in range(parts):
        gy1 = dot_back(gy2, f2[p][...]) * slope[:, p * hidden : (p + 1) * hidden]
        g_h1 = g_h1 + dot_back(gy1.astype(BF16), f1[p][:width, :])
    gain_one = column_sum(g_h1 * n1[...])
    g_u1 = norm_back(g_h1 * g1[...], n1[...], sc1[:, :1])
    gu1_out[...] = g_u1
    v_out[...] = fine(dot_back, g_u1, m3[...])
    bias = [gain_one, gain_two, column_sum(gy2.astype(F32)), column_sum(g_u1)]
    slab[...] = jnp.zeros_like(slab)
    pack(
        slab,
        [
            dot_rows(total[...].astype(BF16), g_u1.astype(BF16)),
            dot_rows(own.astype(BF16), h2b[...]),
            dot_rows(far_sum.astype(BF16), h2b[...]),
            e2g[...],
            e3g[...],
            padded_rows(bias, width),
            padded_rows([eb2[...], eb3[...], edge_gain[...]], own.shape[1]),
        ],
    )


def residue_backward(args, far, f1, f2):
    node_cot, e_first, slope = args[0], args[2], args[10]
    rows, width = node_cot.shape
    shapes = [
        ((rows, width), F32),
        ((rows, width), F32),
        ((rows, 2 * width), BF16),
        ((all_tiles(early_shapes(width, e_first.shape[0])), 16, LANES), BF16),
    ]
    return small_call(
        functools.partial(residue_backward_kernel, len(f1), len(far)),
        (*args, *far, *f1, *f2),
        shapes, "residue_backward",
        flops=4 * rows * width * slope.shape[1], moved=8 * MIB,
    )


def feed_kernel(first, second, f1, fb1, f2, f1g, f2g, fb1g):
    width = f1.shape[0]

    @pl.when(pl.program_id(0) == 0)
    def _():
        for ref in (f1g, f2g, fb1g):
            ref[...] = jnp.zeros_like(ref)

    for both in (first, second):
        h1b, gy2 = both[:, :width], both[:, width:]
        act, slope = gelu_parts(dot(h1b, f1[...]) + fb1[...])
        gy1 = (dot_back(gy2, f2[...]) * slope).astype(BF16)
        f1g[...] += dot_rows(h1b, gy1)
        f2g[...] += dot_rows(act.astype(BF16), gy2)
        fb1g[...] += column_sum(gy1.astype(F32))


def feed_gradients(both, f1, fb1, f2):
    width, hidden = f1.shape
    half = both[0].shape[0]
    chunk = min(512, half)
    shapes = [(width, hidden), (hidden, width), (1, hidden)]
    return pl.pallas_call(
        feed_kernel,
        grid=(half // chunk,),
        in_specs=[pl.BlockSpec((chunk, 2 * width), lambda i: (i, 0))] * 2
        + [const_spec(a.shape) for a in (f1, fb1, f2)],
        out_specs=[pl.BlockSpec(s, whole) for s in shapes],
        out_shape=[jax.ShapeDtypeStruct(s, F32) for s in shapes],
        compiler_params=pltpu.CompilerParams(vmem_limit_bytes=VMEM),
        name="feed_gradients",
        cost_estimate=pl.CostEstimate(
            flops=16 * half * width * hidden,
            bytes_accessed=8 * half * width,
            transcendentals=2 * half * hidden,
        ),
    )(*both, f1, fb1, f2)


def late_shapes(width, edge_width):
    return [
        (width, width),
        (width, width),
        (edge_width, width),
        (16, width),
        (width, width),
        (edge_width, edge_width),
        (16, edge_width),
    ]


def weight_shapes(width, edge_width):
    return early_shapes(width, edge_width) + late_shapes(width, edge_width)


def message_backward_kernel(
    sb, blocks, groups, codes, base, order, v, a1, s1, s2, edge, low_three, low_edge, local_row, live_col,
    m1, m2, e_first, node_lo, node_hi, node, early, e1g, eb1,
    edge_grad, far_keep, far_send, own, keep, send,
    low_two, low_one, grad, rows_ref, moved, m2g, m1eg, m1fg, b2s, slab,
):
    step = pl.program_id(0)
    rows, width = v.shape
    edge_width = edge.shape[2]
    block = sb * rows
    tiles = width // LANES
    size = 16

    @pl.when(step == 0)
    def _():
        for ref in (own, m2g, m1eg, m1fg, b2s):
            ref[...] = jnp.zeros_like(ref)

    @pl.when(step < blocks)
    def _():
        for row in range(0, rows, size):
            count = live_col[row : row + size, :]
            inverse = 1.0 / count.astype(F32)
            value = v[row : row + size, :]
            total = b2s[row : row + size, :]
            for s in range(sb):
                at = s * rows + row
                share = jnp.where(count > step * sb + s, inverse, 0.0)
                low = (value * spread(share, width) * s2[at : at + size, :].astype(F32)).astype(BF16)
                low_two[at : at + size, :] = low
                total = total + low.astype(F32)
            b2s[row : row + size, :] = total
        grad[...] = dot_back(low_two[...], m2[...])
        m2g[...] += dot_rows(a1[...], low_two[...])
        first = pl.multiple_of(step * (block * 8), 8)
        rows_ref[pl.ds(first + tiles, block, stride=8), :] = index_columns(local_row[...]).astype(F32)
        for row in range(0, rows, size):
            total = own[row : row + size, :]
            for s in range(sb):
                at = s * rows + row
                low = (grad[at : at + size, :] * s1[at : at + size, :].astype(F32)).astype(BF16)
                low_one[at : at + size, :] = low
                low = low.astype(F32)
                total = total + low
                for j in range(tiles):
                    rows_ref[pl.ds(first + at * 8 + j, size, stride=8), :] = low[
                        :, j * LANES : (j + 1) * LANES
                    ]
            own[row : row + size, :] = total
        m1eg[...] += dot_rows(edge[...].reshape(block, edge_width), low_one[...])
        total = (
            low_three[...].astype(F32)
            + dot(low_edge[...], e_first[:, width : width + edge_width])
            + dot_back(low_one[...], m1[width : width + edge_width, :])
        )
        edge_grad[...] = total.reshape(sb, rows, edge_width)

    @pl.when(step >= blocks)
    def _():
        deep = far_keep.shape[0]
        count = block * blocks // groups
        values, local = group_rows(order, (step - blocks) * count, count, rows_ref, moved, width)
        sums = group_sums(values, local, 2 * deep * rows).astype(BF16)
        near = jnp.concatenate(
            [ref[at, 0] for ref in (node_lo, node_hi) for at in range(deep)], axis=0
        )
        m1fg[...] += dot_rows(near, sums)
        height = rows // 16
        for at in range(2 * deep):
            out = (far_keep if at < deep else far_send).at[at % deep, 0]
            for j in range(tiles):
                tile = sums[at * rows : (at + 1) * rows, j * LANES : (j + 1) * LANES]
                out[j * height : (j + 1) * height] = tile.reshape(height, 16, LANES)

    @pl.when(step == blocks + groups - 1)
    def _():
        count = early.shape[0]
        slab[:count] = early[...]
        slab[count:] = jnp.zeros_like(slab[count:])
        pack(
            slab,
            [
                dot_rows(node[...], own[...].astype(BF16)),
                m2g[...],
                m1eg[...],
                padded_rows([column_sum(own[...]), column_sum(b2s[...])], width),
                m1fg[...],
                e1g[...],
                padded_rows([eb1[...]], edge_width),
            ],
            count,
        )
        order_out(slab, base[0], codes, keep, send)


def message_backward(
    groups, codes, base, order, v, a1, s1, s2, edge, low_three, low_edge, local_row, live_col, m1, m2,
    e_first, node_lo, node_hi, node, early, e1g, eb1,
):
    slots, rows, edge_width = edge.shape
    width = v.shape[1]
    sb = slot_block(slots)
    block = sb * rows
    blocks = slots // sb
    edges = slots * rows
    half = node_lo.shape[0]
    deep = half // rows // groups
    tiles = rows * width // (16 * LANES)
    slab = slab_tiles(weight_shapes(width, edge_width), len(codes)) * len(codes)
    node_lo, node_hi = [n.reshape(deep, groups, rows, width) for n in (node_lo, node_hi)]
    blk = lambda i: jnp.minimum(i, blocks - 1)
    group_at = lambda i: (0, jnp.maximum(i - blocks, 0))
    row_spec = pl.BlockSpec((block, width), lambda i: (blk(i), 0))
    slot_spec = pl.BlockSpec((sb, rows, edge_width), lambda i: (blk(i), 0, 0))
    edge_spec = pl.BlockSpec((block, edge_width), lambda i: (blk(i), 0))
    node_spec = pl.BlockSpec((deep, 1, rows, width), lambda i: (*group_at(i), 0, 0))
    far_spec = pl.BlockSpec((deep, 1, tiles, 16, LANES), lambda i: (*group_at(i), 0, 0, 0))
    slab_spec = pl.BlockSpec((slab // 2, 16, LANES), lambda i: (0, 0, 0))
    smem = pl.BlockSpec(memory_space=pltpu.SMEM)
    return pl.pallas_call(
        functools.partial(message_backward_kernel, sb, blocks, groups, codes),
        grid=(blocks + groups,),
        in_specs=[
            smem,
            smem,
            const_spec(v.shape),
            row_spec,
            row_spec,
            row_spec,
            slot_spec,
            edge_spec,
            edge_spec,
            pl.BlockSpec((1, block), lambda i: (0, blk(i))),
            const_spec(live_col.shape),
            const_spec(m1.shape),
            const_spec(m2.shape),
            const_spec(e_first.shape),
            node_spec,
            node_spec,
            const_spec(node.shape),
            const_spec(early.shape),
            const_spec(e1g.shape),
            const_spec(eb1.shape),
        ],
        out_specs=[slot_spec, far_spec, far_spec, pl.BlockSpec((rows, width), whole), slab_spec, slab_spec],
        out_shape=[
            jax.ShapeDtypeStruct((slots, rows, edge_width), F32),
            jax.ShapeDtypeStruct((deep, groups, tiles, 16, LANES), BF16),
            jax.ShapeDtypeStruct((deep, groups, tiles, 16, LANES), BF16),
            jax.ShapeDtypeStruct((rows, width), F32),
            jax.ShapeDtypeStruct((slab // 2, 16, LANES), BF16),
            jax.ShapeDtypeStruct((slab // 2, 16, LANES), BF16),
        ],
        scratch_shapes=[
            pltpu.VMEM((block, width), BF16),
            pltpu.VMEM((block, width), BF16),
            pltpu.VMEM((block, width), F32),
            pltpu.VMEM((edges * 8, LANES), F32),
            pltpu.VMEM((edges // groups * 8, LANES), F32),
            pltpu.VMEM((width, width), F32),
            pltpu.VMEM((edge_width, width), F32),
            pltpu.VMEM((width, width), F32),
            pltpu.VMEM((rows, width), F32),
            slab_scratch(slab),
        ],
        compiler_params=pltpu.CompilerParams(vmem_limit_bytes=VMEM),
        name="message_backward",
        cost_estimate=pl.CostEstimate(
            flops=2 * edges * width * (2 * width + 3 * edge_width + half // groups),
            bytes_accessed=edges * width * 6 + edges * edge_width * 10,
            transcendentals=0,
        ),
    )(
        base, order, v, a1, s1, s2, edge, low_three, low_edge, local_row, live_col, m1, m2, e_first,
        node_lo, node_hi, node, early, e1g, eb1,
    )


def node_kernel(pieces, g_u1, own, m1, *refs):
    far, grad_out = refs[:pieces], refs[pieces]
    rows, width = own.shape
    height = rows // 16
    tiles = height * (width // LANES)
    sums = far[0][:tiles].astype(F32)
    for ref in far[1:]:
        sums = sums + ref[:tiles].astype(F32)
    far_sum = jnp.concatenate(
        [sums[j * height : (j + 1) * height].reshape(rows, LANES) for j in range(width // LANES)],
        axis=1,
    )
    far_first = m1.shape[0] - width
    grad_out[...] = (
        g_u1[...]
        + fine(dot_back, own[...], m1[:width, :])
        + fine(dot_back, far_sum, m1[far_first:, :])
    )


def node_last(g_u1, own, m1, far):
    return small_call(
        functools.partial(node_kernel, len(far)),
        (g_u1, own, m1, *far), [(own.shape, F32)], "node_gradient",
        flops=8 * own.size * own.shape[1], moved=2 * MIB,
    )[0]


def weights_out_kernel(
    codes, base, first, second,
    m1g, b1, m2g, b2, m3g, e1g, e2g, e3g, b3, g1, g2, fb2, eb1, eb2, eb3, g3, slab,
):
    order_in(slab, base[0], codes, first, second)
    width, edge_width = m3g.shape[0], e2g.shape[0]
    shapes = weight_shapes(width, edge_width)
    starts = [all_tiles(shapes[:at]) for at in range(len(shapes))]
    m3g[...] = unpack(slab, starts[0], width, width)
    e1g[:, :width] = unpack(slab, starts[1], edge_width, width)
    middle = unpack(slab, starts[12], edge_width, edge_width)
    far = unpack(slab, starts[2], edge_width, width)
    over = edge_width % LANES
    base_col = width + edge_width - over
    e1g[:, width:base_col] = middle[:, : edge_width - over]
    far = pltpu.roll(jnp.concatenate([far, jnp.zeros((edge_width, LANES), F32)], axis=1), over, 1)
    lane = lax.broadcasted_iota(jnp.int32, (edge_width, LANES), 1)
    e1g[:, base_col : base_col + LANES] = jnp.where(
        lane < over, middle[:, edge_width - over : edge_width - over + LANES], far[:, :LANES]
    )
    rest = e1g.shape[1] - base_col - LANES
    e1g[:, base_col + LANES :] = far[:, LANES : LANES + rest]
    e2g[...] = unpack(slab, starts[3], edge_width, edge_width)[:, :edge_width]
    e3g[...] = unpack(slab, starts[4], edge_width, edge_width)[:, :edge_width]
    bias = unpack(slab, starts[5], 16, width)
    for row, out in enumerate((g1, g2, fb2, b3)):
        out[...] = bias[row : row + 1]
    bias = unpack(slab, starts[6], 16, edge_width)
    for row, out in enumerate((eb2, eb3, g3)):
        out[...] = bias[row : row + 1, :edge_width]
    m1g[:width, :] = unpack(slab, starts[7], width, width)
    m2g[...] = unpack(slab, starts[8], width, width)
    m1g[width : width + edge_width, :] = unpack(slab, starts[9], edge_width, width)
    bias = unpack(slab, starts[10], 16, width)
    b1[...] = bias[0:1]
    b2[...] = bias[1:2]
    eb1[...] = unpack(slab, starts[13], 16, edge_width)[:1, :edge_width]
    m1g[width + edge_width :, :] = unpack(slab, starts[11], width, width)


def weights_out(codes, base, halves_in, width, edge_width):
    shapes = [(2 * width + edge_width, width), (1, width), (width, width), (1, width)]
    shapes += [(width, width), (edge_width, 2 * width + edge_width)]
    shapes += [(edge_width, edge_width)] * 2 + [(1, width)] * 4 + [(1, edge_width)] * 4
    tiles = slab_tiles(weight_shapes(width, edge_width), len(codes)) * len(codes)
    return small_call(
        functools.partial(weights_out_kernel, codes),
        (base, *halves_in), [(s, F32) for s in shapes], "weight_gradients",
        [slab_scratch(tiles)], moved=10 * MIB, scalars=1,
    )


def exchange(value, mask, devices):
    return lax.ppermute(value, AXES, [(d, d ^ mask) for d in range(devices)])


def mask_groups(masks):
    return [masks[i : min(i + 2, len(masks) - 1)] for i in range(0, len(masks) - 1, 2)] + [masks[-1:]]


def order_codes(groups):
    masks = [mask for group in groups for mask in group]
    return [
        sum(mask for bit, mask in enumerate(masks) if place >> bit & 1)
        for place in range(1 << len(masks))
    ]


def combined(group, code):
    return sum(mask for bit, mask in enumerate(group) if code >> bit & 1)


def sent_around(value, group, devices):
    return [value] + [
        exchange(value, combined(group, code), devices) for code in range(1, 1 << len(group))
    ]


def shared_out(total, group, devices):
    parts = 1 << len(group)
    rows = total.shape[0] // parts
    return [total] + [
        exchange(total[code * rows : (code + 1) * rows].astype(BF16), combined(group, code), devices)
        for code in range(1, parts)
    ]


def add_up(terms):
    total = terms[0][: terms[1].shape[0]].astype(F32)
    for term in terms[1:]:
        total = total + term.astype(F32)
    return total


def tied(*values):
    return lax.optimization_barrier(values)


def split_three(value):
    rows = []
    for _ in range(3):
        high = lax.reduce_precision(value, 8, 7)
        rows.append(high.astype(BF16))
        value = value - high
    return jnp.concatenate(rows + [jnp.zeros((13, value.shape[1]), BF16)], axis=0)


def per_device(
    node_in,
    edge_in,
    neighbours,
    live_counts,
    message_first,
    message_first_bias,
    message_second,
    message_second_bias,
    message_third,
    message_third_bias,
    norm_one,
    feed_first,
    feed_first_bias,
    feed_second,
    feed_second_bias,
    norm_two,
    edge_first,
    edge_first_bias,
    edge_second,
    edge_second_bias,
    edge_third,
    edge_third_bias,
    norm_three,
    node_cotangent,
    edge_cotangent,
):
    rows, slots = neighbours.shape
    width = node_in.shape[1]
    edge_width = edge_in.shape[2]
    edges = rows * slots
    hid_count = lax.axis_size("hid")
    res_count = lax.axis_size("res")
    devices = res_count * hid_count
    bits = devices.bit_length() - 1
    masks = [1 << b for b in range(bits - 1, -1, -1)]
    groups = mask_groups(masks)
    codes = order_codes(groups)
    me = lax.axis_index("res") * hid_count + lax.axis_index("hid")
    base = me.reshape(1)
    row = lambda vector: vector.reshape(1, -1)

    names = neighbours.T.reshape(edges)
    apart = (names // rows) ^ me
    place = jnp.zeros_like(names)
    for bit, mask in enumerate(masks):
        place = place | jnp.where((apart & mask) != 0, 1 << bit, 0)
    idx_row = (place * rows + names % rows).reshape(1, edges)
    res_count = devices // hid_count
    local_row = (place // res_count * rows + names % rows).reshape(1, edges)
    edge_order = group_order(place % res_count, res_count)
    live_col = jnp.broadcast_to(live_counts[:, None], (rows, LANES))
    edge = edge_in.transpose(1, 0, 2)
    cot = edge_cotangent.transpose(1, 0, 2)
    e_first = edge_first.T
    e_far = e_first[:, width + edge_width :]
    f1x = jnp.concatenate([feed_first, split_three(row(feed_first_bias))], axis=0)
    f2x = feed_second

    stack = lambda pieces: jnp.concatenate(pieces, axis=0)
    *outer, near = groups

    held = stack(sent_around(node_in, outer[0], devices))
    held, idx_row, local_row = tied(held, idx_row, local_row)
    for group in outer[1:]:
        held = stack(sent_around(held, group, devices))
    held, f1x, f2x, edge_order, live_col = tied(held, f1x, f2x, edge_order, live_col)
    node_lo, node_hi = sent_around(held, near, devices)

    f1, f2 = [f1x], [f2x]
    hid_masks = [m for m in masks if m < hid_count]
    for mask in hid_masks[:-1]:
        f1, f2 = [pieces + [exchange(p, mask, devices) for p in pieces] for pieces in (f1, f2)]

    a1, s1, s2, total = message_forward(
        node_lo, node_hi, node_in, edge, idx_row, live_col, message_first,
        row(message_first_bias), message_second, row(message_second_bias),
    )
    total, f1, f2, e_far = tied(total, f1, f2, e_far)
    f1, f2 = [
        pieces + [exchange(p, hid_masks[-1], devices) for p in pieces] for pieces in (f1, f2)
    ]
    h1b, n1, sc1, n2, sc2, slope, h2b, far_part, own_part = residue_forward(
        node_in, total, message_third, row(message_third_bias), row(norm_one),
        row(feed_second_bias), row(norm_two), e_first, e_far, row(edge_first_bias), f1, f2,
    )

    held = stack(sent_around(far_part, outer[0], devices))
    for group in outer[1:]:
        held = stack(sent_around(held, group, devices))
    q_lo, q_hi = sent_around(held, near, devices)

    edge_out, act_one, act_two, low_three, low_two, low_one, hi, lo, own_sum, edge_gain = edge_branch(
        q_lo, q_hi, own_part, edge, cot, idx_row, live_col, e_first,
        edge_second, row(edge_second_bias), edge_third, row(edge_third_bias), row(norm_three),
    )

    terms = [lo, exchange(hi, near[0], devices)]
    made = None
    for group in reversed(outer):
        terms = shared_out(add_up(terms), group, devices)
        if made is None:
            made = edge_weights((act_two, act_one), (low_three, low_two), rows)
            terms, made = tied(terms, made)
    e3g, e2g, eb3, eb2 = made
    g_u1, v, both, early = residue_backward(
        (
            node_cotangent, own_sum, e_first, e_far, h1b, h2b, n1, sc1, n2, sc2, slope, row(norm_one),
            row(norm_two), message_third, total, e2g, e3g, eb2, eb3, edge_gain,
        ),
        terms, f1, f2,
    )

    both, low_here = tied(both, low_one)
    b_held = stack(sent_around(both, outer[0], devices))
    e1g, eb1 = edge_weights((low_here,), (edge,), rows)
    v, b_held, e1g, eb1 = tied(v, b_held, e1g, eb1)
    for group in outer[1:]:
        b_held = stack(sent_around(b_held, group, devices))
    edge_grad, far_keep, far_send, own, keep, send = message_backward(
        res_count, codes, base, edge_order, v, a1, s1, s2, edge, low_three, low_one, local_row, live_col,
        message_first, message_second, e_first, node_lo, node_hi, node_in, early, e1g, eb1,
    )
    keep, send, far_keep, far_send, b_held = tied(keep, send, far_keep, far_send, b_held)

    first, *others = reversed(outer)
    terms = [keep, exchange(send, near[0], devices)]
    total, b_held, far_send = tied(add_up(terms), b_held, far_send)
    terms = shared_out(total, first, devices)
    far_keep, far_send = [far.reshape(-1, 16, LANES) for far in (far_keep, far_send)]
    far_terms = [far_keep, exchange(far_send, near[0], devices)]
    b_near = sent_around(b_held, near, devices)
    total, b_first = tied(add_up(far_terms), b_near[0])
    far_terms = shared_out(total, first, devices)
    feed = feed_gradients((b_first, b_near[1]), feed_first, row(feed_first_bias), feed_second)
    terms, (f1g, f2g, fb1g) = tied(terms, feed)
    for group in others:
        terms = shared_out(add_up(terms), group, devices)
    held, *far_terms[:3] = tied(add_up(terms).astype(BF16), *far_terms[:3])

    for at, group in enumerate(outer):
        around = sent_around(held, group, devices)
        if at + 1 == len(outer):
            around, node_gradient = tied(around, node_last(g_u1, own, message_first, far_terms))
        held = stack(around)
        if at < len(others):
            held, *far_terms = tied(held, *far_terms)
            far_terms = shared_out(add_up(far_terms), others[at], devices)
    m1g, b1, m2g, b2, m3g, e1g, e2g, e3g, b3, g1, g2, fb2, eb1, eb2, eb3, g3 = weights_out(
        codes, base, sent_around(held, near, devices), width, edge_width
    )
    flat = lambda vector: vector.reshape(-1)
    return (
        h2b,
        edge_out.transpose(1, 0, 2),
        node_gradient,
        edge_grad.transpose(1, 0, 2),
        m1g,
        flat(b1),
        m2g,
        flat(b2),
        m3g,
        flat(b3),
        flat(g1),
        f1g,
        flat(fb1g),
        f2g,
        flat(fb2),
        flat(g2),
        e1g.T,
        flat(eb1),
        e2g,
        flat(eb2),
        e3g,
        flat(eb3),
        flat(g3),
    )


def solution(mesh):
    nodes, edges, shared = P(AXES, None), P(AXES, None, None), P()
    return jax.shard_map(
        per_device,
        mesh=mesh,
        in_specs=(nodes, edges, nodes, P(AXES))
        + (shared,) * 7
        + (P(None, "hid"), P("hid"), P("hid", None))
        + (shared,) * 9
        + (nodes, edges),
        out_specs=(nodes, edges, nodes, edges)
        + (shared,) * 7
        + (P(None, "hid"), P("hid"), P("hid", None))
        + (shared,) * 9,
        check_vma=False,
    )
```

```python
import functools

import jax
import jax.numpy as jnp
from jax import lax
from jax.experimental import pallas as pl
from jax.experimental.pallas import tpu as pltpu
from jax.sharding import PartitionSpec as P

EPS = 1e-05
AXES = ("res", "hid")
F32 = jnp.float32
BF16 = jnp.bfloat16
TANH_SCALE = 0.7978845608028654
TANH_CUBE = 0.044715
LANES = 128
CHUNK = 2048
MIB = 1024 * 1024
VMEM = 58 * MIB


def dot(left, right):
    return lax.dot_general(left, right, (((1,), (0,)), ((), ())), preferred_element_type=F32)


def dot_rows(left, right):
    return lax.dot_general(left, right, (((0,), (0,)), ((), ())), preferred_element_type=F32)


def dot_back(left, right):
    return lax.dot_general(left, right, (((1,), (1,)), ((), ())), preferred_element_type=F32)


def halves(value):
    high = value.astype(BF16)
    return high, (value - high.astype(F32)).astype(BF16)


def fine(product, value, weights):
    high, low = halves(value)
    return product(high, weights) + product(low, weights)


def gelu_parts(x):
    square = x * x
    t = jnp.tanh(x * (TANH_SCALE + (TANH_SCALE * TANH_CUBE) * square))
    gate = 0.5 + 0.5 * t
    act = x * gate
    slope = gate + act * (1.0 - gate) * (2 * TANH_SCALE + (6 * TANH_SCALE * TANH_CUBE) * square)
    return act, slope


def index_columns(idx_row):
    parts = [
        jnp.broadcast_to(idx_row[:, first : first + LANES], (LANES, LANES)).T
        for first in range(0, idx_row.shape[1], LANES)
    ]
    return jnp.concatenate(parts, axis=0)


def one_hot_columns(idx, start, count):
    one, zero = jnp.ones((), BF16), jnp.zeros((), BF16)
    idx = idx.astype(jnp.int16)
    lane = lax.broadcasted_iota(jnp.int32, idx.shape, 1).astype(jnp.int16)
    parts = [
        jnp.where(idx == lane + jnp.int16(start + first), one, zero)
        for first in range(0, count, LANES)
    ]
    return jnp.concatenate(parts, axis=1)


def pick_rows(idx, table_refs):
    total, start = None, 0
    for ref in table_refs:
        rows = ref.shape[0]
        step = min(rows, CHUNK)
        for first in range(0, rows, step):
            part = dot(one_hot_columns(idx, start + first, step), ref[first : first + step, :])
            total = part if total is None else total + part
        start += rows
    return total


def one_hot_rows(idx_row, start, count):
    shape = (count, idx_row.shape[1])
    row = (lax.broadcasted_iota(jnp.int32, shape, 0) + start).astype(jnp.int16)
    names = jnp.broadcast_to(idx_row, shape).astype(jnp.int16)
    return jnp.where(names == row, jnp.ones((), BF16), jnp.zeros((), BF16))


def group_rows(order, first, count, rows_ref, moved, width):
    for e in range(count):
        at = pl.multiple_of(order[0, first + e] * 8, 8)
        moved[e * 8 : e * 8 + 8, :] = rows_ref[pl.ds(at, 8), :]

    def column(at):
        return moved[pl.ds(at, count, stride=8), :]

    tiles = pl.cdiv(width, LANES)
    parts = [column(at)[:, : min(LANES, width - at * LANES)] for at in range(tiles)]
    return jnp.concatenate(parts, axis=1).astype(BF16), column(tiles)


def group_sums(rows, local, residues):
    lane = lax.broadcasted_iota(jnp.int32, local.shape, 1).astype(F32)
    picks = [
        jnp.where(local == lane + float(first), 1.0, 0.0).astype(BF16)
        for first in range(0, residues, LANES)
    ]
    return dot_rows(jnp.concatenate(picks, axis=1), rows)


def order_kernel(groups, count, names, out):
    rows = names.shape[0]
    row = lax.broadcasted_iota(jnp.int32, (LANES, LANES), 0)
    column = lax.broadcasted_iota(jnp.int32, (LANES, LANES), 1)
    upto = jnp.where(row <= column, 1.0, 0.0).astype(BF16)
    ones = jnp.ones((LANES, LANES), BF16)
    above = lax.broadcasted_iota(jnp.int32, (rows, rows), 0)
    before = jnp.where(lax.broadcasted_iota(jnp.int32, (rows, rows), 1) < above, 1.0, 0.0).astype(BF16)
    place = jnp.full(names.shape, float(2 * LANES * LANES), F32)
    for group in range(groups):
        here = names[...] == group
        low = jnp.where(here, 1.0, 0.0).astype(BF16)
        rank = dot(low, upto) + dot(before, dot(low, ones).astype(BF16))
        place = jnp.where(here, rank + float(group * count - 1), place)
    high = total = None
    for at in range(rows):
        where = jnp.broadcast_to(place[at : at + 1, :], (LANES, LANES)).T.astype(jnp.int32)
        left = jnp.where(where // LANES == column, 1.0, 0.0)
        right = jnp.where(where % LANES == column, 1.0, 0.0)
        part = dot_rows(left.astype(BF16), (right * float(at)).astype(BF16))
        high = part if high is None else high + part
        part = dot_rows(left.astype(BF16), (right * row.astype(F32)).astype(BF16))
        total = part if total is None else total + part
    number = high * float(LANES) + total
    out[...] = number[: out.shape[0], : out.shape[1]].astype(jnp.int32)


def group_order(names, groups):
    edges = names.shape[0]
    rows = pl.cdiv(pl.cdiv(edges, LANES), 8) * 8
    padded = jnp.pad(names, (0, rows * LANES - edges), constant_values=groups)
    out = small_call(
        functools.partial(order_kernel, groups, edges // groups),
        (padded.reshape(rows, LANES),), [((edges // LANES, LANES), jnp.int32)], "group_order",
    )[0]
    return out.reshape(1, edges)


def spread(column, width):
    return jnp.concatenate([column] * (width // LANES), axis=1)


def norm(value):
    centre = value - jnp.mean(value, -1, keepdims=True)
    scale = lax.rsqrt(jnp.mean(centre * centre, -1, keepdims=True) + EPS)
    return centre * scale, scale


def norm_back(inner, normed, scale):
    mean_first = jnp.mean(inner, -1, keepdims=True)
    mean_second = jnp.mean(inner * normed, -1, keepdims=True)
    return scale * (inner - mean_first - normed * mean_second)


def column_sum(value):
    return jnp.sum(value, axis=0, keepdims=True)


def whole(*_):
    return (0, 0)


def const_spec(shape):
    return pl.BlockSpec(shape, lambda *_: (0,) * len(shape), pipeline_mode=pl.Buffered(1))


def small_call(kernel, args, shapes, name, scratch=(), flops=0, moved=0, exps=0, scalars=0):
    return pl.pallas_call(
        kernel,
        grid=(1,),
        in_specs=[pl.BlockSpec(memory_space=pltpu.SMEM)] * scalars
        + [const_spec(a.shape) for a in args[scalars:]],
        out_specs=[pl.BlockSpec(s, lambda *_, n=len(s): (0,) * n) for s, _ in shapes],
        out_shape=[jax.ShapeDtypeStruct(*s) for s in shapes],
        scratch_shapes=list(scratch),
        compiler_params=pltpu.CompilerParams(vmem_limit_bytes=VMEM),
        name=name,
        cost_estimate=pl.CostEstimate(flops=flops, bytes_accessed=moved, transcendentals=exps),
    )(*args)


def tile_count(shape):
    return pl.cdiv(shape[0], 16) * pl.cdiv(shape[1], LANES)


def all_tiles(shapes):
    return sum(tile_count(s) for s in shapes)


def pack(slab, values, at=0):
    for value in values:
        rows, columns = value.shape
        count = rows // 16
        for first in range(0, columns, LANES):
            take = min(LANES, columns - first)
            tile = value[:, first : first + take].astype(BF16).reshape(count, 16, take)
            slab[at : at + count, :, :take] = tile
            at += count


def unpack(slab, at, rows, columns):
    count = rows // 16
    parts = [
        slab[at + i * count : at + (i + 1) * count].reshape(rows, LANES).astype(F32)
        for i in range(pl.cdiv(columns, LANES))
    ]
    return jnp.concatenate(parts, axis=1)


def order_out(slab, base, codes, keep, send):
    size = slab.shape[0] // len(codes)
    half = len(codes) // 2
    for place, code in enumerate(codes):
        out = keep if place < half else send
        at = (place % half) * size
        out[at : at + size] = slab[pl.ds((base ^ code) * size, size)]


def half_shapes(tiles):
    return [((tiles // 2, 16, LANES), BF16)] * 2


def slab_scratch(tiles):
    return pltpu.VMEM((tiles, 16, LANES), BF16)


def slab_tiles(shapes, chunks):
    return pl.cdiv(all_tiles(shapes), chunks)


def order_in(slab, base, codes, first, second):
    size = slab.shape[0] // len(codes)
    half = len(codes) // 2
    for place, code in enumerate(codes):
        source = first if place < half else second
        at = (place % half) * size
        slab[pl.ds((base ^ code) * size, size)] = source[at : at + size]


def padded_rows(parts, width):
    return jnp.concatenate(parts + [jnp.zeros((16 - len(parts), width), F32)], axis=0)


def slot_block(slots):
    for size in (10, 12, 8, 6, 5, 4, 3, 2):
        if slots % size == 0:
            return size
    return 1


def far_table(node_lo, node_hi, weights, put):
    tile = min(512, node_lo.shape[0])
    for source, start in ((node_lo, 0), (node_hi, node_lo.shape[0])):
        def body(i, carry, source=source, start=start):
            at = pl.multiple_of(i * tile, tile)
            put(start + at, dot(source[pl.ds(at, tile), :], weights))
            return carry
        lax.fori_loop(0, source.shape[0] // tile, body, 0)


def message_forward_kernel(
    sb, by_rows, node_lo, node_hi, node_own, edge, idx_row, names, live_col, m1, b1, m2, b2,
    a1_out, s1_out, s2_out, sum_out, table, far, near, lhs, z,
):
    step = pl.program_id(0)
    width = node_own.shape[1]
    edge_width = edge.shape[2]
    rows = edge.shape[1]
    block = sb * rows
    lanes = width // LANES

    @pl.when(step == 0)
    def _():
        weights = m1[width + edge_width :, :]
        if by_rows:
            def put(first, value):
                for at in range(8):
                    column = at % lanes * LANES
                    table[pl.ds(first * 8 + at, value.shape[0], stride=8), :] = value[
                        :, column : column + LANES
                    ]
        else:
            def put(first, value):
                table[pl.ds(first, value.shape[0]), :] = value.astype(BF16)
        far_table(node_lo, node_hi, weights, put)
        near[:edge_width, :] = m1[width : width + edge_width, :]
        near[edge_width:, :] = jnp.zeros_like(near[edge_width:, :])
        near[edge_width : edge_width + rows, :] = (
            dot(node_own[...], m1[:width, :]) + b1[...]
        ).astype(BF16)
        shape = (rows, near.shape[0] - edge_width)
        eye = lax.broadcasted_iota(jnp.int32, shape, 0) == lax.broadcasted_iota(jnp.int32, shape, 1)
        for at in range(0, block, rows):
            lhs[at : at + rows, edge_width:] = jnp.where(eye, 1.0, 0.0).astype(BF16)
        sum_out[...] = jnp.zeros_like(sum_out)

    lhs[:, :edge_width] = edge[...].reshape(block, edge_width)
    z[...] = dot(lhs[...], near[...])
    if not by_rows:
        z[...] += pick_rows(index_columns(idx_row[...]), (table,))
    upper = lax.broadcasted_iota(jnp.int32, (8, LANES), 0) < lanes

    def fetch(at):
        for e in range(at, at + 16, 2):
            pair = [
                table[pl.ds(pl.multiple_of(names[0, step * block + e + i] * 8, 8), 8), :]
                for i in range(2)
            ]
            far[e * lanes : e * lanes + 8, :] = jnp.where(upper, *pair)

    def fetched(at):
        return jnp.concatenate(
            [far[pl.ds(at * lanes + j, 16, stride=lanes), :] for j in range(lanes)], axis=1
        )

    if by_rows:
        fetch(0)
    for at in range(0, block, 16):
        value = z[at : at + 16, :]
        if by_rows:
            if at + 16 < block:
                fetch(at + 16)
            value = value + fetched(at)
        act, slope = gelu_parts(value)
        a1_out[at : at + 16, :] = act.astype(BF16)
        s1_out[at : at + 16, :] = slope.astype(BF16)
    z[...] = dot(a1_out[...], m2[...])
    bias = b2[...]
    for row in range(0, rows, 16):
        count = live_col[row : row + 16, :]
        inverse = 1.0 / count.astype(F32)
        total = sum_out[row : row + 16, :]
        for s in range(sb):
            at = s * rows + row
            act, slope = gelu_parts(z[at : at + 16, :] + bias)
            s2_out[at : at + 16, :] = slope.astype(BF16)
            share = jnp.where(count > step * sb + s, inverse, 0.0)
            total = total + act.astype(BF16).astype(F32) * spread(share, width)
        sum_out[row : row + 16, :] = total


def message_forward(node_lo, node_hi, node_own, edge, idx_row, live_col, m1, b1, m2, b2):
    slots, rows, edge_width = edge.shape
    width = node_own.shape[1]
    residues = 2 * node_lo.shape[0]
    by_rows = residues <= 4096 and width == 4 * LANES
    sb = slot_block(slots) if by_rows else 4
    block = sb * rows
    edges = slots * rows
    near = pl.cdiv(edge_width + rows, LANES) * LANES
    row_spec = pl.BlockSpec((block, width), lambda i: (i, 0))
    return pl.pallas_call(
        functools.partial(message_forward_kernel, sb, by_rows),
        grid=(slots // sb,),
        in_specs=[
            const_spec(node_lo.shape),
            const_spec(node_hi.shape),
            const_spec(node_own.shape),
            pl.BlockSpec((sb, rows, edge_width), lambda i: (i, 0, 0)),
            pl.BlockSpec((1, block), lambda i: (0, i)),
            pl.BlockSpec(memory_space=pltpu.SMEM),
            const_spec(live_col.shape),
            const_spec(m1.shape),
            const_spec(b1.shape),
            const_spec(m2.shape),
            const_spec(b2.shape),
        ],
        out_specs=[row_spec, row_spec, row_spec, pl.BlockSpec((rows, width), whole)],
        out_shape=[jax.ShapeDtypeStruct((edges, width), BF16)] * 3
        + [jax.ShapeDtypeStruct((rows, width), F32)],
        scratch_shapes=[
            pltpu.VMEM((residues * 8, LANES), F32) if by_rows else pltpu.VMEM((residues, width), BF16),
            pltpu.VMEM((block * 4 if by_rows else 8, LANES), F32),
            pltpu.VMEM((near, width), BF16),
            pltpu.VMEM((block, near), BF16),
            pltpu.VMEM((block, width), F32),
        ],
        compiler_params=pltpu.CompilerParams(vmem_limit_bytes=VMEM),
        name="message_forward",
        cost_estimate=pl.CostEstimate(
            flops=2 * edges * width * (residues + edge_width + width),
            bytes_accessed=edges * width * 6 + edges * edge_width * 2 + edges * LANES * 4,
            transcendentals=2 * edges * width,
        ),
    )(node_lo, node_hi, node_own, edge, idx_row, idx_row, live_col, m1, b1, m2, b2)


def joined(refs, at):
    return jnp.concatenate([refs[2 * at][...], refs[2 * at + 1][...]], axis=0)


def residue_forward_kernel(parts, node, total, m3, b3, g1, fb2, g2, e_first, e_far, eb, *refs):
    f1, f2 = refs[:parts], refs[parts : 3 * parts]
    h1b_out, n1_out, sc1_out, n2_out, sc2_out, slope_out, h2b_out, far_out, own_out = refs[3 * parts :]
    width, hidden = node.shape[1], f1[0].shape[1]
    u1 = node[...].astype(F32) + fine(dot, total[...], m3[...]) + b3[...]
    n1, sc1 = norm(u1)
    h1 = n1 * g1[...]
    h1b = h1.astype(BF16)
    h1b_out[...] = h1b
    n1_out[...] = n1
    sc1_out[...] = jnp.broadcast_to(sc1, sc1_out.shape)
    y2 = None
    for p in range(parts):
        bias = f1[p][width : width + 16, :].astype(F32)
        bias = bias[0:1] + bias[1:2] + bias[2:3]
        act, slope = gelu_parts(dot(h1b, f1[p][:width, :]) + bias)
        slope_out[:, p * hidden : (p + 1) * hidden] = slope
        part = dot(act.astype(BF16), joined(f2, p))
        y2 = part if y2 is None else y2 + part
    n2, sc2 = norm(h1 + (y2 + fb2[...]))
    h2b = (n2 * g2[...]).astype(BF16)
    n2_out[...] = n2
    sc2_out[...] = jnp.broadcast_to(sc2, sc2_out.shape)
    h2b_out[...] = h2b
    far_out[...] = dot_back(h2b, e_far[...]).astype(BF16)
    own_out[...] = dot_back(h2b, e_first[:, :width]) + eb[...]


def residue_forward(node, total, m3, b3, g1, fb2, g2, e_first, e_far, eb, f1, f2):
    rows, width = node.shape
    edge_width = e_first.shape[0]
    hidden = len(f1) * f1[0].shape[1]
    shapes = [
        ((rows, width), BF16),
        ((rows, width), F32),
        ((rows, LANES), F32),
        ((rows, width), F32),
        ((rows, LANES), F32),
        ((rows, hidden), F32),
        ((rows, width), BF16),
        ((rows, edge_width), BF16),
        ((rows, edge_width), F32),
    ]
    return small_call(
        functools.partial(residue_forward_kernel, len(f1)),
        (node, total, m3, b3, g1, fb2, g2, e_first, e_far, eb, *f1, *f2),
        shapes, "residue_forward", flops=4 * rows * width * hidden, moved=5 * MIB,
        exps=rows * hidden,
    )


def edge_kernel(
    sb, blocks, hi_chunks, by_rows, far_lo, far_hi, own, edge, cot, idx, idx_row, names, live_col,
    e_first, e2, eb2, e3, eb3, g3,
    edge_out, act_one_out, act_two_out, low_three_out, low_two_out, low_one_out, hi_out, lo_out, own_out, gain_out,
    low_first, gs, table, far, z, slope_ref,
):
    step = pl.program_id(0)
    rows, width = own.shape
    node_width = (e_first.shape[1] - width) // 2
    e_mid = e_first.at[:, node_width : node_width + width]
    tiles = pl.cdiv(width, LANES)
    per = 8 // tiles
    size = 32

    @pl.when(step == 0)
    def _():
        own_out[...] = jnp.zeros_like(own_out)
        gs[...] = jnp.zeros_like(gs)
        half = far_lo.shape[0]
        if by_rows:
            for source, start in ((far_lo, 0), (far_hi, half)):
                for first in range(0, half, 512):
                    value = source[first : first + 512, :].astype(F32)
                    for at in range(8):
                        column = at % tiles * LANES
                        take = min(LANES, width - column)
                        table[pl.ds((start + first) * 8 + at, value.shape[0], stride=8), :take] = value[
                            :, column : column + take
                        ]

    @pl.when(step < blocks)
    def _():
        block = sb * rows
        flat = edge[...].reshape(block, width)
        z[...] = dot_back(flat, e_mid[...])
        if not by_rows:
            z[...] += pick_rows(index_columns(idx[...]), (far_lo, far_hi))
        sub = lax.broadcasted_iota(jnp.int32, (8, LANES), 0)

        def fetch(at):
            for e in range(at, at + size, per):
                got = [
                    table[pl.ds(pl.multiple_of(names[0, step * block + e + i] * 8, 8), 8), :]
                    for i in range(per)
                ]
                value = got[-1]
                for i in range(per - 2, -1, -1):
                    value = jnp.where(sub < (i + 1) * tiles, got[i], value)
                far[e * tiles : e * tiles + 8, :] = value

        def fetched(at):
            parts = [
                far[pl.ds(at * tiles + j, size, stride=tiles), :][:, : min(LANES, width - j * LANES)]
                for j in range(tiles)
            ]
            return jnp.concatenate(parts, axis=1)

        if by_rows:
            fetch(0)
        for at in range(0, block, size):
            value = z[at : at + size, :] + own[at % rows : at % rows + size, :]
            if by_rows:
                if at + size < block:
                    fetch(at + size)
                value = value + fetched(at)
            act, slope = gelu_parts(value)
            act_one_out[at : at + size, :] = act.astype(BF16)
            slope_ref[at : at + size, :] = slope
        act_one = act_one_out[...]
        act_two, slope_two = gelu_parts(dot(act_one, e2[...]) + eb2[...])
        act_two = act_two.astype(BF16)
        act_two_out[...] = act_two
        w_three = dot(act_two, e3[...]) + eb3[...]
        normed, scale = norm(flat.astype(F32) + w_three)
        count = spread(live_col[...], pl.cdiv(width, LANES) * LANES)[:, :width]
        live = jnp.concatenate(
            [jnp.where(count > step * sb + s, 1.0, 0.0) for s in range(sb)], axis=0
        )
        edge_out[...] = (normed * g3[...] * live).astype(BF16).reshape(sb, rows, width)
        grad = cot[...].reshape(block, width).astype(F32) * live
        gs[...] += jnp.sum((grad * normed).reshape(sb, rows, width), axis=0)
        low_three = norm_back(grad * g3[...], normed, scale).astype(BF16)
        low_three_out[...] = low_three
        low_two = (dot_back(low_three, e3[...]) * slope_two).astype(BF16)
        low_two_out[...] = low_two
        low_one = (dot_back(low_two, e2[...]) * slope_ref[...]).astype(BF16)
        low_one_out[...] = low_one
        own_out[...] += jnp.sum(low_one.astype(F32).reshape(sb, rows, width), axis=0)
        low_first[pl.ds(pl.multiple_of(step * block, block), block), :] = low_one

    chunk = hi_out.shape[0]

    @pl.when((step >= blocks) & (step < blocks + hi_chunks))
    def _():
        start = (step - blocks + hi_chunks) * chunk
        hi_out[...] = dot(one_hot_rows(idx_row[...], start, chunk), low_first[...]).astype(BF16)

    @pl.when(step >= blocks + hi_chunks)
    def _():
        start = (step - blocks - hi_chunks) * chunk
        lo_out[...] = dot(one_hot_rows(idx_row[...], start, chunk), low_first[...])

    @pl.when(step == blocks + 2 * hi_chunks - 1)
    def _():
        gain_out[...] = column_sum(gs[...])


def edge_branch(far_lo, far_hi, own, edge, cot, idx_row, live_col, e_first, e2, eb2, e3, eb3, g3):
    slots, rows, width = edge.shape
    sb = slot_block(slots)
    edges = slots * rows
    block = sb * rows
    blocks = slots // sb
    half = far_lo.shape[0]
    chunk = min(512, half)
    hi_chunks = half // chunk
    by_rows = half <= 2048 and 8 % pl.cdiv(width, LANES) == 0
    blk = lambda i: jnp.minimum(i, blocks - 1)
    hi_at = lambda i: (jnp.clip(i - blocks, 0, hi_chunks - 1), 0)
    lo_at = lambda i: (jnp.clip(i - blocks - hi_chunks, 0, hi_chunks - 1), 0)
    slot_spec = pl.BlockSpec((sb, rows, width), lambda i: (blk(i), 0, 0))
    row_spec = pl.BlockSpec((block, width), lambda i: (blk(i), 0))
    return pl.pallas_call(
        functools.partial(edge_kernel, sb, blocks, hi_chunks, by_rows),
        grid=(blocks + 2 * hi_chunks,),
        in_specs=[
            const_spec(far_lo.shape),
            const_spec(far_hi.shape),
            const_spec(own.shape),
            slot_spec,
            slot_spec,
            pl.BlockSpec((1, block), lambda i: (0, blk(i))),
            const_spec(idx_row.shape),
            pl.BlockSpec(memory_space=pltpu.SMEM),
            const_spec(live_col.shape),
            const_spec(e_first.shape),
            const_spec(e2.shape),
            const_spec(eb2.shape),
            const_spec(e3.shape),
            const_spec(eb3.shape),
            const_spec(g3.shape),
        ],
        out_specs=[slot_spec]
        + [row_spec] * 5
        + [
            pl.BlockSpec((chunk, width), hi_at),
            pl.BlockSpec((chunk, width), lo_at),
            pl.BlockSpec((rows, width), whole),
            pl.BlockSpec((1, width), whole),
        ],
        out_shape=[jax.ShapeDtypeStruct((slots, rows, width), BF16)]
        + [jax.ShapeDtypeStruct((edges, width), BF16)] * 5
        + [
            jax.ShapeDtypeStruct((half, width), BF16),
            jax.ShapeDtypeStruct((half, width), F32),
            jax.ShapeDtypeStruct((rows, width), F32),
            jax.ShapeDtypeStruct((1, width), F32),
        ],
        scratch_shapes=[
            pltpu.VMEM((edges, width), BF16),
            pltpu.VMEM((rows, width), F32),
            pltpu.VMEM((half * 16 if by_rows else 8, LANES), F32),
            pltpu.VMEM((block * 8, LANES), F32),
            pltpu.VMEM((block, width), F32),
            pltpu.VMEM((block, width), F32),
        ],
        compiler_params=pltpu.CompilerParams(vmem_limit_bytes=VMEM),
        name="edge_branch",
        cost_estimate=pl.CostEstimate(
            flops=2 * edges * width * (4 * half + 5 * width),
            bytes_accessed=edges * width * 16,
            transcendentals=2 * edges * width,
        ),
    )(far_lo, far_hi, own, edge, cot, idx_row, idx_row, idx_row, live_col, e_first, e2, eb2, e3, eb3, g3)


def edge_weights_kernel(blocks, pairs, *refs):
    step = pl.program_id(0)
    lefts, rights = refs[:pairs], refs[pairs : 2 * pairs]
    grads, biases, sums = refs[2 * pairs : 3 * pairs], refs[3 * pairs : 4 * pairs], refs[-1]
    rows = sums.shape[1]

    @pl.when(step == 0)
    def _():
        for ref in (*grads, sums):
            ref[...] = jnp.zeros_like(ref)

    for at in range(pairs):
        left, right = [r[...].reshape(-1, r.shape[-1]) for r in (lefts[at], rights[at])]
        grads[at][...] += dot_rows(left, right)
        low = left if lefts[at].ndim < rights[at].ndim else right
        sums[at] += jnp.sum(low.astype(F32).reshape(-1, rows, low.shape[1]), axis=0)

    @pl.when(step == blocks - 1)
    def _():
        for at in range(pairs):
            biases[at][...] = column_sum(sums[at])


def edge_weights(lefts, rights, rows):
    pairs = len(lefts)
    edges, width = lefts[0].shape
    slots = edges // rows
    sb = slot_block(slots)

    def spec(array):
        if array.ndim == 3:
            return pl.BlockSpec((sb, rows, width), lambda i: (i, 0, 0))
        return pl.BlockSpec((sb * rows, width), lambda i: (i, 0))

    shapes = [(width, width)] * pairs + [(1, width)] * pairs
    return pl.pallas_call(
        functools.partial(edge_weights_kernel, slots // sb, pairs),
        grid=(slots // sb,),
        in_specs=[spec(array) for array in (*lefts, *rights)],
        out_specs=[pl.BlockSpec(s, whole) for s in shapes],
        out_shape=[jax.ShapeDtypeStruct(s, F32) for s in shapes],
        scratch_shapes=[pltpu.VMEM((pairs, rows, width), F32)],
        compiler_params=pltpu.CompilerParams(vmem_limit_bytes=VMEM),
        name="edge_weights",
        cost_estimate=pl.CostEstimate(
            flops=2 * pairs * edges * width * width,
            bytes_accessed=pairs * edges * width * 4,
            transcendentals=0,
        ),
    )(*lefts, *rights)


def early_shapes(width, edge_width):
    return [
        (width, width),
        (edge_width, width),
        (edge_width, width),
        (edge_width, edge_width),
        (edge_width, edge_width),
        (16, width),
        (16, edge_width),
    ]


def residue_backward_kernel(
    parts, pieces, node_cot, own_sum, e_first, e_far, h1b, h2b, n1, sc1, n2, sc2, slope, g1, g2, m3,
    total, e2g, e3g, eb2, eb3, edge_gain, *refs,
):
    far = refs[:pieces]
    f1 = refs[pieces : pieces + parts]
    f2 = refs[pieces + parts : pieces + 3 * parts]
    gu1_out, v_out, both_out, slab = refs[pieces + 3 * parts :]
    width, hidden = h2b.shape[1], f1[0].shape[1]
    far_sum = far[0][: far[1].shape[0], :]
    for ref in far[1:]:
        far_sum = far_sum + ref[...].astype(F32)
    own = own_sum[...]
    g_h2 = (
        node_cot[...].astype(F32)
        + fine(dot, own, e_first[:, :width])
        + fine(dot, far_sum, e_far[...])
    )
    gain_two = column_sum(g_h2 * n2[...])
    g_u2 = norm_back(g_h2 * g2[...], n2[...], sc2[:, :1])
    gy2 = g_u2.astype(BF16)
    both_out[:, :width] = h1b[...]
    both_out[:, width:] = gy2
    g_h1 = g_u2
    for p in range(parts):
        gy1 = dot_back(gy2, joined(f2, p)) * slope[:, p * hidden : (p + 1) * hidden]
        g_h1 = g_h1 + dot_back(gy1.astype(BF16), f1[p][:width, :])
    gain_one = column_sum(g_h1 * n1[...])
    g_u1 = norm_back(g_h1 * g1[...], n1[...], sc1[:, :1])
    gu1_out[...] = g_u1
    v_out[...] = fine(dot_back, g_u1, m3[...])
    bias = [gain_one, gain_two, column_sum(gy2.astype(F32)), column_sum(g_u1)]
    slab[...] = jnp.zeros_like(slab)
    pack(
        slab,
        [
            dot_rows(total[...].astype(BF16), g_u1.astype(BF16)),
            dot_rows(own.astype(BF16), h2b[...]),
            dot_rows(far_sum.astype(BF16), h2b[...]),
            e2g[...],
            e3g[...],
            padded_rows(bias, width),
            padded_rows([eb2[...], eb3[...], edge_gain[...]], own.shape[1]),
        ],
    )


def residue_backward(args, far, f1, f2):
    node_cot, e_first, slope = args[0], args[2], args[10]
    rows, width = node_cot.shape
    shapes = [
        ((rows, width), F32),
        ((rows, width), F32),
        ((rows, 2 * width), BF16),
        ((all_tiles(early_shapes(width, e_first.shape[0])), 16, LANES), BF16),
    ]
    return small_call(
        functools.partial(residue_backward_kernel, len(f1), len(far)),
        (*args, *far, *f1, *f2),
        shapes, "residue_backward",
        flops=4 * rows * width * slope.shape[1], moved=8 * MIB,
    )


def feed_kernel(first, second, f1, fb1, f2, f1g, f2g, fb1g):
    width = f1.shape[0]

    @pl.when(pl.program_id(0) == 0)
    def _():
        for ref in (f1g, f2g, fb1g):
            ref[...] = jnp.zeros_like(ref)

    for both in (first, second):
        h1b, gy2 = both[:, :width], both[:, width:]
        act, slope = gelu_parts(dot(h1b, f1[...]) + fb1[...])
        gy1 = (dot_back(gy2, f2[...]) * slope).astype(BF16)
        f1g[...] += dot_rows(h1b, gy1)
        f2g[...] += dot_rows(act.astype(BF16), gy2)
        fb1g[...] += column_sum(gy1.astype(F32))


def feed_gradients(both, f1, fb1, f2):
    width, hidden = f1.shape
    half = both[0].shape[0]
    chunk = min(512, half)
    shapes = [(width, hidden), (hidden, width), (1, hidden)]
    return pl.pallas_call(
        feed_kernel,
        grid=(half // chunk,),
        in_specs=[pl.BlockSpec((chunk, 2 * width), lambda i: (i, 0))] * 2
        + [const_spec(a.shape) for a in (f1, fb1, f2)],
        out_specs=[pl.BlockSpec(s, whole) for s in shapes],
        out_shape=[jax.ShapeDtypeStruct(s, F32) for s in shapes],
        compiler_params=pltpu.CompilerParams(vmem_limit_bytes=VMEM),
        name="feed_gradients",
        cost_estimate=pl.CostEstimate(
            flops=16 * half * width * hidden,
            bytes_accessed=8 * half * width,
            transcendentals=2 * half * hidden,
        ),
    )(*both, f1, fb1, f2)


def late_shapes(width, edge_width):
    return [
        (width, width),
        (width, width),
        (edge_width, width),
        (16, width),
        (width, width),
        (edge_width, edge_width),
        (16, edge_width),
    ]


def weight_shapes(width, edge_width):
    return early_shapes(width, edge_width) + late_shapes(width, edge_width)


def message_backward_kernel(
    sb, blocks, groups, at_once, codes, base, order, v, a1, s1, s2, edge, low_three, low_edge, local_row, live_col,
    m1, m2, e_first, node_lo, node_hi, node, early, e1g, eb1,
    edge_grad, far_keep, far_send, own, keep, send,
    low_two, low_one, grad, rows_ref, moved, m2g, m1eg, m1fg, b2s, slab,
):
    step = pl.program_id(0)
    rows, width = v.shape
    edge_width = edge.shape[2]
    block = sb * rows
    tiles = width // LANES
    size = 16

    @pl.when(step == 0)
    def _():
        for ref in (own, m2g, m1eg, m1fg, b2s):
            ref[...] = jnp.zeros_like(ref)

    @pl.when(step < blocks)
    def _():
        for row in range(0, rows, size):
            count = live_col[row : row + size, :]
            inverse = 1.0 / count.astype(F32)
            value = v[row : row + size, :]
            total = b2s[row : row + size, :]
            for s in range(sb):
                at = s * rows + row
                share = jnp.where(count > step * sb + s, inverse, 0.0)
                low = (value * spread(share, width) * s2[at : at + size, :].astype(F32)).astype(BF16)
                low_two[at : at + size, :] = low
                total = total + low.astype(F32)
            b2s[row : row + size, :] = total
        grad[...] = dot_back(low_two[...], m2[...])
        m2g[...] += dot_rows(a1[...], low_two[...])
        first = pl.multiple_of(step * (block * 8), 8)
        rows_ref[pl.ds(first + tiles, block, stride=8), :] = index_columns(local_row[...]).astype(F32)
        for row in range(0, rows, size):
            total = own[row : row + size, :]
            for s in range(sb):
                at = s * rows + row
                low = (grad[at : at + size, :] * s1[at : at + size, :].astype(F32)).astype(BF16)
                low_one[at : at + size, :] = low
                low = low.astype(F32)
                total = total + low
                for j in range(tiles):
                    rows_ref[pl.ds(first + at * 8 + j, size, stride=8), :] = low[
                        :, j * LANES : (j + 1) * LANES
                    ]
            own[row : row + size, :] = total
        m1eg[...] += dot_rows(edge[...].reshape(block, edge_width), low_one[...])
        total = (
            low_three[...].astype(F32)
            + dot(low_edge[...], e_first[:, width : width + edge_width])
            + dot_back(low_one[...], m1[width : width + edge_width, :])
        )
        edge_grad[...] = total.reshape(sb, rows, edge_width)

    @pl.when(step >= blocks)
    def _():
        deep = far_keep.shape[0]
        count = block * blocks // groups
        height = rows // 16
        picked = [
            group_rows(
                order, ((step - blocks) * at_once + i) * count, count, rows_ref, moved.at[i], width
            )
            for i in range(at_once)
        ]
        for i, (values, local) in enumerate(picked):
            sums = group_sums(values, local, 2 * deep * rows).astype(BF16)
            near = jnp.concatenate(
                [ref[at, i] for ref in (node_lo, node_hi) for at in range(deep)], axis=0
            )
            m1fg[...] += dot_rows(near, sums)
            for at in range(2 * deep):
                out = (far_keep if at < deep else far_send).at[at % deep, i]
                for j in range(tiles):
                    tile = sums[at * rows : (at + 1) * rows, j * LANES : (j + 1) * LANES]
                    out[j * height : (j + 1) * height] = tile.reshape(height, 16, LANES)

    @pl.when(step == blocks + groups // at_once - 1)
    def _():
        count = early.shape[0]
        slab[:count] = early[...]
        slab[count:] = jnp.zeros_like(slab[count:])
        pack(
            slab,
            [
                dot_rows(node[...], own[...].astype(BF16)),
                m2g[...],
                m1eg[...],
                padded_rows([column_sum(own[...]), column_sum(b2s[...])], width),
                m1fg[...],
                e1g[...],
                padded_rows([eb1[...]], edge_width),
            ],
            count,
        )
        order_out(slab, base[0], codes, keep, send)


def message_backward(
    groups, codes, base, order, v, a1, s1, s2, edge, low_three, low_edge, local_row, live_col, m1, m2,
    e_first, node_lo, node_hi, node, early, e1g, eb1,
):
    slots, rows, edge_width = edge.shape
    width = v.shape[1]
    sb = slot_block(slots)
    block = sb * rows
    blocks = slots // sb
    edges = slots * rows
    half = node_lo.shape[0]
    deep = half // rows // groups
    at_once = 2 if groups % 2 == 0 else 1
    tiles = rows * width // (16 * LANES)
    slab = slab_tiles(weight_shapes(width, edge_width), len(codes)) * len(codes)
    node_lo, node_hi = [n.reshape(deep, groups, rows, width) for n in (node_lo, node_hi)]
    blk = lambda i: jnp.minimum(i, blocks - 1)
    group_at = lambda i: (0, jnp.maximum(i - blocks, 0))
    row_spec = pl.BlockSpec((block, width), lambda i: (blk(i), 0))
    slot_spec = pl.BlockSpec((sb, rows, edge_width), lambda i: (blk(i), 0, 0))
    edge_spec = pl.BlockSpec((block, edge_width), lambda i: (blk(i), 0))
    node_spec = pl.BlockSpec((deep, at_once, rows, width), lambda i: (*group_at(i), 0, 0))
    far_spec = pl.BlockSpec((deep, at_once, tiles, 16, LANES), lambda i: (*group_at(i), 0, 0, 0))
    slab_spec = pl.BlockSpec((slab // 2, 16, LANES), lambda i: (0, 0, 0))
    smem = pl.BlockSpec(memory_space=pltpu.SMEM)
    return pl.pallas_call(
        functools.partial(message_backward_kernel, sb, blocks, groups, at_once, codes),
        grid=(blocks + groups // at_once,),
        in_specs=[
            smem,
            smem,
            const_spec(v.shape),
            row_spec,
            row_spec,
            row_spec,
            slot_spec,
            edge_spec,
            edge_spec,
            pl.BlockSpec((1, block), lambda i: (0, blk(i))),
            const_spec(live_col.shape),
            const_spec(m1.shape),
            const_spec(m2.shape),
            const_spec(e_first.shape),
            node_spec,
            node_spec,
            const_spec(node.shape),
            const_spec(early.shape),
            const_spec(e1g.shape),
            const_spec(eb1.shape),
        ],
        out_specs=[slot_spec, far_spec, far_spec, pl.BlockSpec((rows, width), whole), slab_spec, slab_spec],
        out_shape=[
            jax.ShapeDtypeStruct((slots, rows, edge_width), F32),
            jax.ShapeDtypeStruct((deep, groups, tiles, 16, LANES), BF16),
            jax.ShapeDtypeStruct((deep, groups, tiles, 16, LANES), BF16),
            jax.ShapeDtypeStruct((rows, width), F32),
            jax.ShapeDtypeStruct((slab // 2, 16, LANES), BF16),
            jax.ShapeDtypeStruct((slab // 2, 16, LANES), BF16),
        ],
        scratch_shapes=[
            pltpu.VMEM((block, width), BF16),
            pltpu.VMEM((block, width), BF16),
            pltpu.VMEM((block, width), F32),
            pltpu.VMEM((edges * 8, LANES), F32),
            pltpu.VMEM((at_once, edges // groups * 8, LANES), F32),
            pltpu.VMEM((width, width), F32),
            pltpu.VMEM((edge_width, width), F32),
            pltpu.VMEM((width, width), F32),
            pltpu.VMEM((rows, width), F32),
            slab_scratch(slab),
        ],
        compiler_params=pltpu.CompilerParams(vmem_limit_bytes=VMEM),
        name="message_backward",
        cost_estimate=pl.CostEstimate(
            flops=2 * edges * width * (2 * width + 3 * edge_width + half // groups),
            bytes_accessed=edges * width * 6 + edges * edge_width * 10,
            transcendentals=0,
        ),
    )(
        base, order, v, a1, s1, s2, edge, low_three, low_edge, local_row, live_col, m1, m2, e_first,
        node_lo, node_hi, node, early, e1g, eb1,
    )


def node_kernel(pieces, g_u1, own, m1, *refs):
    far, grad_out = refs[:pieces], refs[pieces]
    rows, width = own.shape
    height = rows // 16
    tiles = height * (width // LANES)
    sums = far[0][:tiles].astype(F32)
    for ref in far[1:]:
        sums = sums + ref[:tiles].astype(F32)
    far_sum = jnp.concatenate(
        [sums[j * height : (j + 1) * height].reshape(rows, LANES) for j in range(width // LANES)],
        axis=1,
    )
    far_first = m1.shape[0] - width
    grad_out[...] = (
        g_u1[...]
        + fine(dot_back, own[...], m1[:width, :])
        + fine(dot_back, far_sum, m1[far_first:, :])
    )


def node_last(g_u1, own, m1, far):
    return small_call(
        functools.partial(node_kernel, len(far)),
        (g_u1, own, m1, *far), [(own.shape, F32)], "node_gradient",
        flops=8 * own.size * own.shape[1], moved=2 * MIB,
    )[0]


def weights_out_kernel(
    codes, base, first, second,
    m1g, b1, m2g, b2, m3g, e1g, e2g, e3g, b3, g1, g2, fb2, eb1, eb2, eb3, g3, slab,
):
    order_in(slab, base[0], codes, first, second)
    width, edge_width = m3g.shape[0], e2g.shape[0]
    shapes = weight_shapes(width, edge_width)
    starts = [all_tiles(shapes[:at]) for at in range(len(shapes))]
    m3g[...] = unpack(slab, starts[0], width, width)
    e1g[:, :width] = unpack(slab, starts[1], edge_width, width)
    middle = unpack(slab, starts[12], edge_width, edge_width)
    far = unpack(slab, starts[2], edge_width, width)
    over = edge_width % LANES
    base_col = width + edge_width - over
    e1g[:, width:base_col] = middle[:, : edge_width - over]
    far = pltpu.roll(jnp.concatenate([far, jnp.zeros((edge_width, LANES), F32)], axis=1), over, 1)
    lane = lax.broadcasted_iota(jnp.int32, (edge_width, LANES), 1)
    e1g[:, base_col : base_col + LANES] = jnp.where(
        lane < over, middle[:, edge_width - over : edge_width - over + LANES], far[:, :LANES]
    )
    rest = e1g.shape[1] - base_col - LANES
    e1g[:, base_col + LANES :] = far[:, LANES : LANES + rest]
    e2g[...] = unpack(slab, starts[3], edge_width, edge_width)[:, :edge_width]
    e3g[...] = unpack(slab, starts[4], edge_width, edge_width)[:, :edge_width]
    bias = unpack(slab, starts[5], 16, width)
    for row, out in enumerate((g1, g2, fb2, b3)):
        out[...] = bias[row : row + 1]
    bias = unpack(slab, starts[6], 16, edge_width)
    for row, out in enumerate((eb2, eb3, g3)):
        out[...] = bias[row : row + 1, :edge_width]
    m1g[:width, :] = unpack(slab, starts[7], width, width)
    m2g[...] = unpack(slab, starts[8], width, width)
    m1g[width : width + edge_width, :] = unpack(slab, starts[9], edge_width, width)
    bias = unpack(slab, starts[10], 16, width)
    b1[...] = bias[0:1]
    b2[...] = bias[1:2]
    eb1[...] = unpack(slab, starts[13], 16, edge_width)[:1, :edge_width]
    m1g[width + edge_width :, :] = unpack(slab, starts[11], width, width)


def weights_out(codes, base, halves_in, width, edge_width):
    shapes = [(2 * width + edge_width, width), (1, width), (width, width), (1, width)]
    shapes += [(width, width), (edge_width, 2 * width + edge_width)]
    shapes += [(edge_width, edge_width)] * 2 + [(1, width)] * 4 + [(1, edge_width)] * 4
    tiles = slab_tiles(weight_shapes(width, edge_width), len(codes)) * len(codes)
    return small_call(
        functools.partial(weights_out_kernel, codes),
        (base, *halves_in), [(s, F32) for s in shapes], "weight_gradients",
        [slab_scratch(tiles)], moved=10 * MIB, scalars=1,
    )


def exchange(value, mask, devices):
    return lax.ppermute(value, AXES, [(d, d ^ mask) for d in range(devices)])


def mask_groups(masks):
    return [masks[i : min(i + 2, len(masks) - 1)] for i in range(0, len(masks) - 1, 2)] + [masks[-1:]]


def order_codes(groups):
    masks = [mask for group in groups for mask in group]
    return [
        sum(mask for bit, mask in enumerate(masks) if place >> bit & 1)
        for place in range(1 << len(masks))
    ]


def combined(group, code):
    return sum(mask for bit, mask in enumerate(group) if code >> bit & 1)


def sent_around(value, group, devices):
    return [value] + [
        exchange(value, combined(group, code), devices) for code in range(1, 1 << len(group))
    ]


def shared_out(total, group, devices):
    parts = 1 << len(group)
    rows = total.shape[0] // parts
    return [total] + [
        exchange(total[code * rows : (code + 1) * rows].astype(BF16), combined(group, code), devices)
        for code in range(1, parts)
    ]


def add_up(terms):
    total = terms[0][: terms[1].shape[0]].astype(F32)
    for term in terms[1:]:
        total = total + term.astype(F32)
    return total


def tied(*values):
    return lax.optimization_barrier(values)


def split_three(value):
    rows = []
    for _ in range(3):
        high = lax.reduce_precision(value, 8, 7)
        rows.append(high.astype(BF16))
        value = value - high
    return jnp.concatenate(rows + [jnp.zeros((13, value.shape[1]), BF16)], axis=0)


def per_device(
    node_in,
    edge_in,
    neighbours,
    live_counts,
    message_first,
    message_first_bias,
    message_second,
    message_second_bias,
    message_third,
    message_third_bias,
    norm_one,
    feed_first,
    feed_first_bias,
    feed_second,
    feed_second_bias,
    norm_two,
    edge_first,
    edge_first_bias,
    edge_second,
    edge_second_bias,
    edge_third,
    edge_third_bias,
    norm_three,
    node_cotangent,
    edge_cotangent,
):
    rows, slots = neighbours.shape
    width = node_in.shape[1]
    edge_width = edge_in.shape[2]
    edges = rows * slots
    hid_count = lax.axis_size("hid")
    res_count = lax.axis_size("res")
    devices = res_count * hid_count
    bits = devices.bit_length() - 1
    masks = [1 << b for b in range(bits - 1, -1, -1)]
    groups = mask_groups(masks)
    codes = order_codes(groups)
    me = lax.axis_index("res") * hid_count + lax.axis_index("hid")
    base = me.reshape(1)
    row = lambda vector: vector.reshape(1, -1)

    names = neighbours.T.reshape(edges)
    apart = (names // rows) ^ me
    place = jnp.zeros_like(names)
    for bit, mask in enumerate(masks):
        place = place | jnp.where((apart & mask) != 0, 1 << bit, 0)
    idx_row = (place * rows + names % rows).reshape(1, edges)
    res_count = devices // hid_count
    local_row = (place // res_count * rows + names % rows).reshape(1, edges)
    edge_order = group_order(place % res_count, res_count)
    live_col = jnp.broadcast_to(live_counts[:, None], (rows, LANES))
    edge = edge_in.transpose(1, 0, 2)
    cot = edge_cotangent.transpose(1, 0, 2)
    e_first = edge_first.T
    e_far = e_first[:, width + edge_width :]
    f1x = jnp.concatenate([feed_first, split_three(row(feed_first_bias))], axis=0)
    cut = feed_second.shape[0] // 2
    hid_masks = [m for m in masks if m < hid_count]

    def across(pieces):
        for mask in hid_masks[:-1]:
            pieces = pieces + [exchange(p, mask, devices) for p in pieces]
        return pieces

    def over(pieces):
        return pieces + [exchange(p, hid_masks[-1], devices) for p in pieces]

    f2a = across([feed_second[:cut]])

    stack = lambda pieces: jnp.concatenate(pieces, axis=0)
    *outer, near = groups

    held = stack(sent_around(node_in, outer[0], devices))
    held, idx_row, local_row, f2a = tied(held, idx_row, local_row, f2a)
    for group in outer[1:]:
        held = stack(sent_around(held, group, devices))
    f2b = feed_second[cut:]
    held, f1x, f2a, f2b, edge_order, live_col = tied(held, f1x, f2a, f2b, edge_order, live_col)
    node_lo, node_hi = sent_around(held, near, devices)

    f2a = over(f2a)
    f1, f2b = across([f1x]), across([f2b])

    a1, s1, s2, total = message_forward(
        node_lo, node_hi, node_in, edge, idx_row, live_col, message_first,
        row(message_first_bias), message_second, row(message_second_bias),
    )
    total, f1, f2a, f2b, e_far = tied(total, f1, f2a, f2b, e_far)
    f1, f2b = over(f1), over(f2b)
    f2 = [half for pair in zip(f2a, f2b) for half in pair]
    h1b, n1, sc1, n2, sc2, slope, h2b, far_part, own_part = residue_forward(
        node_in, total, message_third, row(message_third_bias), row(norm_one),
        row(feed_second_bias), row(norm_two), e_first, e_far, row(edge_first_bias), f1, f2,
    )

    held = stack(sent_around(far_part, outer[0], devices))
    for group in outer[1:]:
        held = stack(sent_around(held, group, devices))
    q_lo, q_hi = sent_around(held, near, devices)

    edge_out, act_one, act_two, low_three, low_two, low_one, hi, lo, own_sum, edge_gain = edge_branch(
        q_lo, q_hi, own_part, edge, cot, idx_row, live_col, e_first,
        edge_second, row(edge_second_bias), edge_third, row(edge_third_bias), row(norm_three),
    )

    terms = [lo, exchange(hi, near[0], devices)]
    pairs, made = [(act_two, low_three), (act_one, low_two)], []
    for group in reversed(outer):
        total_far = add_up(terms)
        if pairs:
            left, right = pairs.pop(0)
            total_far, left = tied(total_far, left)
        terms = shared_out(total_far, group, devices)
        if len(made) < 2:
            terms, got = tied(terms, edge_weights((left,), (right,), rows))
            made.append(got)
    (e3g, eb3), (e2g, eb2) = made
    g_u1, v, both, early = residue_backward(
        (
            node_cotangent, own_sum, e_first, e_far, h1b, h2b, n1, sc1, n2, sc2, slope, row(norm_one),
            row(norm_two), message_third, total, e2g, e3g, eb2, eb3, edge_gain,
        ),
        terms, f1, f2,
    )

    both, low_here = tied(both, low_one)
    b_held = stack(sent_around(both, outer[0], devices))
    e1g, eb1 = edge_weights((low_here,), (edge,), rows)
    v, b_held, e1g, eb1 = tied(v, b_held, e1g, eb1)
    for group in outer[1:]:
        b_held = stack(sent_around(b_held, group, devices))
    edge_grad, far_keep, far_send, own, keep, send = message_backward(
        res_count, codes, base, edge_order, v, a1, s1, s2, edge, low_three, low_one, local_row, live_col,
        message_first, message_second, e_first, node_lo, node_hi, node_in, early, e1g, eb1,
    )
    keep, send, far_keep, far_send, b_held = tied(keep, send, far_keep, far_send, b_held)

    first, *others = reversed(outer)
    terms = [keep, exchange(send, near[0], devices)]
    total, b_held, far_send = tied(add_up(terms), b_held, far_send)
    terms = shared_out(total, first, devices)
    far_keep, far_send = [far.reshape(-1, 16, LANES) for far in (far_keep, far_send)]
    far_terms = [far_keep, exchange(far_send, near[0], devices)]
    b_near = sent_around(b_held, near, devices)
    total, b_first = tied(add_up(far_terms), b_near[0])
    far_terms = shared_out(total, first, devices)
    feed = feed_gradients((b_first, b_near[1]), feed_first, row(feed_first_bias), feed_second)
    terms, (f1g, f2g, fb1g) = tied(terms, feed)
    for group in others:
        terms = shared_out(add_up(terms), group, devices)
    held, *far_terms[:3] = tied(add_up(terms).astype(BF16), *far_terms[:3])

    for at, group in enumerate(outer):
        around = sent_around(held, group, devices)
        if at + 1 == len(outer):
            around, node_gradient = tied(around, node_last(g_u1, own, message_first, far_terms))
        held = stack(around)
        if at < len(others):
            held, *far_terms = tied(held, *far_terms)
            far_terms = shared_out(add_up(far_terms), others[at], devices)
    m1g, b1, m2g, b2, m3g, e1g, e2g, e3g, b3, g1, g2, fb2, eb1, eb2, eb3, g3 = weights_out(
        codes, base, sent_around(held, near, devices), width, edge_width
    )
    flat = lambda vector: vector.reshape(-1)
    return (
        h2b,
        edge_out.transpose(1, 0, 2),
        node_gradient,
        edge_grad.transpose(1, 0, 2),
        m1g,
        flat(b1),
        m2g,
        flat(b2),
        m3g,
        flat(b3),
        flat(g1),
        f1g,
        flat(fb1g),
        f2g,
        flat(fb2),
        flat(g2),
        e1g.T,
        flat(eb1),
        e2g,
        flat(eb2),
        e3g,
        flat(eb3),
        flat(g3),
    )


def solution(mesh):
    nodes, edges, shared = P(AXES, None), P(AXES, None, None), P()
    return jax.shard_map(
        per_device,
        mesh=mesh,
        in_specs=(nodes, edges, nodes, P(AXES))
        + (shared,) * 7
        + (P(None, "hid"), P("hid"), P("hid", None))
        + (shared,) * 9
        + (nodes, edges),
        out_specs=(nodes, edges, nodes, edges)
        + (shared,) * 7
        + (P(None, "hid"), P("hid"), P("hid", None))
        + (shared,) * 9,
        check_vma=False,
    )
```

```python
import functools

import jax
import jax.numpy as jnp
from jax import lax
from jax.experimental import pallas as pl
from jax.experimental.pallas import tpu as pltpu
from jax.sharding import PartitionSpec as P

EPS = 1e-05
AXES = ("res", "hid")
F32 = jnp.float32
BF16 = jnp.bfloat16
TANH_SCALE = 0.7978845608028654
TANH_CUBE = 0.044715
LANES = 128
CHUNK = 2048
MIB = 1024 * 1024
VMEM = 58 * MIB


def dot(left, right):
    return lax.dot_general(left, right, (((1,), (0,)), ((), ())), preferred_element_type=F32)


def dot_rows(left, right):
    return lax.dot_general(left, right, (((0,), (0,)), ((), ())), preferred_element_type=F32)


def dot_back(left, right):
    return lax.dot_general(left, right, (((1,), (1,)), ((), ())), preferred_element_type=F32)


def halves(value):
    high = value.astype(BF16)
    return high, (value - high.astype(F32)).astype(BF16)


def fine(product, value, weights):
    high, low = halves(value)
    return product(high, weights) + product(low, weights)


def gelu_parts(x):
    square = x * x
    t = jnp.tanh(x * (TANH_SCALE + (TANH_SCALE * TANH_CUBE) * square))
    gate = 0.5 + 0.5 * t
    act = x * gate
    slope = gate + act * (1.0 - gate) * (2 * TANH_SCALE + (6 * TANH_SCALE * TANH_CUBE) * square)
    return act, slope


def index_columns(idx_row):
    parts = [
        jnp.broadcast_to(idx_row[:, first : first + LANES], (LANES, LANES)).T
        for first in range(0, idx_row.shape[1], LANES)
    ]
    return jnp.concatenate(parts, axis=0)


def one_hot_columns(idx, start, count):
    one, zero = jnp.ones((), BF16), jnp.zeros((), BF16)
    idx = idx.astype(jnp.int16)
    lane = lax.broadcasted_iota(jnp.int32, idx.shape, 1).astype(jnp.int16)
    parts = [
        jnp.where(idx == lane + jnp.int16(start + first), one, zero)
        for first in range(0, count, LANES)
    ]
    return jnp.concatenate(parts, axis=1)


def pick_rows(idx, table_refs):
    total, start = None, 0
    for ref in table_refs:
        rows = ref.shape[0]
        step = min(rows, CHUNK)
        for first in range(0, rows, step):
            part = dot(one_hot_columns(idx, start + first, step), ref[first : first + step, :])
            total = part if total is None else total + part
        start += rows
    return total


def one_hot_rows(idx_row, start, count):
    shape = (count, idx_row.shape[1])
    row = (lax.broadcasted_iota(jnp.int32, shape, 0) + start).astype(jnp.int16)
    names = jnp.broadcast_to(idx_row, shape).astype(jnp.int16)
    return jnp.where(names == row, jnp.ones((), BF16), jnp.zeros((), BF16))


def group_rows(order, first, count, rows_ref, moved, width):
    for e in range(count):
        at = pl.multiple_of(order[0, first + e] * 8, 8)
        moved[e * 8 : e * 8 + 8, :] = rows_ref[pl.ds(at, 8), :]

    def column(at):
        return moved[pl.ds(at, count, stride=8), :]

    tiles = pl.cdiv(width, LANES)
    parts = [column(at)[:, : min(LANES, width - at * LANES)] for at in range(tiles)]
    return jnp.concatenate(parts, axis=1).astype(BF16), column(tiles)


def group_sums(rows, local, residues):
    lane = lax.broadcasted_iota(jnp.int32, local.shape, 1).astype(F32)
    picks = [
        jnp.where(local == lane + float(first), 1.0, 0.0).astype(BF16)
        for first in range(0, residues, LANES)
    ]
    return dot_rows(jnp.concatenate(picks, axis=1), rows)


def order_kernel(groups, count, names, out):
    rows = names.shape[0]
    row = lax.broadcasted_iota(jnp.int32, (LANES, LANES), 0)
    column = lax.broadcasted_iota(jnp.int32, (LANES, LANES), 1)
    upto = jnp.where(row <= column, 1.0, 0.0).astype(BF16)
    ones = jnp.ones((LANES, LANES), BF16)
    above = lax.broadcasted_iota(jnp.int32, (rows, rows), 0)
    before = jnp.where(lax.broadcasted_iota(jnp.int32, (rows, rows), 1) < above, 1.0, 0.0).astype(BF16)
    place = jnp.full(names.shape, float(2 * LANES * LANES), F32)
    for group in range(groups):
        here = names[...] == group
        low = jnp.where(here, 1.0, 0.0).astype(BF16)
        rank = dot(low, upto) + dot(before, dot(low, ones).astype(BF16))
        place = jnp.where(here, rank + float(group * count - 1), place)
    high = total = None
    for at in range(rows):
        where = jnp.broadcast_to(place[at : at + 1, :], (LANES, LANES)).T.astype(jnp.int32)
        left = jnp.where(where // LANES == column, 1.0, 0.0)
        right = jnp.where(where % LANES == column, 1.0, 0.0)
        part = dot_rows(left.astype(BF16), (right * float(at)).astype(BF16))
        high = part if high is None else high + part
        part = dot_rows(left.astype(BF16), (right * row.astype(F32)).astype(BF16))
        total = part if total is None else total + part
    number = high * float(LANES) + total
    out[...] = number[: out.shape[0], : out.shape[1]].astype(jnp.int32)


def group_order(names, groups):
    edges = names.shape[0]
    rows = pl.cdiv(pl.cdiv(edges, LANES), 8) * 8
    padded = jnp.pad(names, (0, rows * LANES - edges), constant_values=groups)
    out = small_call(
        functools.partial(order_kernel, groups, edges // groups),
        (padded.reshape(rows, LANES),), [((edges // LANES, LANES), jnp.int32)], "group_order",
    )[0]
    return out.reshape(1, edges)


def spread(column, width):
    return jnp.concatenate([column] * (width // LANES), axis=1)


def norm(value):
    centre = value - jnp.mean(value, -1, keepdims=True)
    scale = lax.rsqrt(jnp.mean(centre * centre, -1, keepdims=True) + EPS)
    return centre * scale, scale


def norm_back(inner, normed, scale):
    mean_first = jnp.mean(inner, -1, keepdims=True)
    mean_second = jnp.mean(inner * normed, -1, keepdims=True)
    return scale * (inner - mean_first - normed * mean_second)


def column_sum(value):
    return jnp.sum(value, axis=0, keepdims=True)


def whole(*_):
    return (0, 0)


def const_spec(shape):
    return pl.BlockSpec(shape, lambda *_: (0,) * len(shape), pipeline_mode=pl.Buffered(1))


def small_call(kernel, args, shapes, name, scratch=(), flops=0, moved=0, exps=0, scalars=0):
    return pl.pallas_call(
        kernel,
        grid=(1,),
        in_specs=[pl.BlockSpec(memory_space=pltpu.SMEM)] * scalars
        + [const_spec(a.shape) for a in args[scalars:]],
        out_specs=[pl.BlockSpec(s, lambda *_, n=len(s): (0,) * n) for s, _ in shapes],
        out_shape=[jax.ShapeDtypeStruct(*s) for s in shapes],
        scratch_shapes=list(scratch),
        compiler_params=pltpu.CompilerParams(vmem_limit_bytes=VMEM),
        name=name,
        cost_estimate=pl.CostEstimate(flops=flops, bytes_accessed=moved, transcendentals=exps),
    )(*args)


def tile_count(shape):
    return pl.cdiv(shape[0], 16) * pl.cdiv(shape[1], LANES)


def all_tiles(shapes):
    return sum(tile_count(s) for s in shapes)


def pack(slab, values, at=0):
    for value in values:
        rows, columns = value.shape
        count = rows // 16
        for first in range(0, columns, LANES):
            take = min(LANES, columns - first)
            tile = value[:, first : first + take].astype(BF16).reshape(count, 16, take)
            slab[at : at + count, :, :take] = tile
            at += count


def unpack(slab, at, rows, columns):
    count = rows // 16
    parts = [
        slab[at + i * count : at + (i + 1) * count].reshape(rows, LANES).astype(F32)
        for i in range(pl.cdiv(columns, LANES))
    ]
    return jnp.concatenate(parts, axis=1)


def order_out(slab, base, codes, keep, send):
    size = slab.shape[0] // len(codes)
    half = len(codes) // 2
    for place, code in enumerate(codes):
        out = keep if place < half else send
        at = (place % half) * size
        out[at : at + size] = slab[pl.ds((base ^ code) * size, size)]


def half_shapes(tiles):
    return [((tiles // 2, 16, LANES), BF16)] * 2


def slab_scratch(tiles):
    return pltpu.VMEM((tiles, 16, LANES), BF16)


def slab_tiles(shapes, chunks):
    return pl.cdiv(all_tiles(shapes), chunks)


def order_in(slab, base, codes, first, second):
    size = slab.shape[0] // len(codes)
    half = len(codes) // 2
    for place, code in enumerate(codes):
        source = first if place < half else second
        at = (place % half) * size
        slab[pl.ds((base ^ code) * size, size)] = source[at : at + size]


def padded_rows(parts, width):
    return jnp.concatenate(parts + [jnp.zeros((16 - len(parts), width), F32)], axis=0)


def slot_block(slots):
    for size in (10, 12, 8, 6, 5, 4, 3, 2):
        if slots % size == 0:
            return size
    return 1


def far_table(node_lo, node_hi, weights, put):
    tile = min(512, node_lo.shape[0])
    for source, start in ((node_lo, 0), (node_hi, node_lo.shape[0])):
        def body(i, carry, source=source, start=start):
            at = pl.multiple_of(i * tile, tile)
            put(start + at, dot(source[pl.ds(at, tile), :], weights))
            return carry
        lax.fori_loop(0, source.shape[0] // tile, body, 0)


def message_forward_kernel(
    sb, by_rows, node_lo, node_hi, node_own, edge, idx_row, names, live_col, m1, b1, m2, b2,
    a1_out, s1_out, s2_out, sum_out, table, far, near, lhs, z,
):
    step = pl.program_id(0)
    width = node_own.shape[1]
    edge_width = edge.shape[2]
    rows = edge.shape[1]
    block = sb * rows
    lanes = width // LANES

    @pl.when(step == 0)
    def _():
        weights = m1[width + edge_width :, :]
        if by_rows:
            def put(first, value):
                for at in range(8):
                    column = at % lanes * LANES
                    table[pl.ds(first * 8 + at, value.shape[0], stride=8), :] = value[
                        :, column : column + LANES
                    ]
        else:
            def put(first, value):
                table[pl.ds(first, value.shape[0]), :] = value.astype(BF16)
        far_table(node_lo, node_hi, weights, put)
        near[:edge_width, :] = m1[width : width + edge_width, :]
        near[edge_width:, :] = jnp.zeros_like(near[edge_width:, :])
        near[edge_width : edge_width + rows, :] = (
            dot(node_own[...], m1[:width, :]) + b1[...]
        ).astype(BF16)
        shape = (rows, near.shape[0] - edge_width)
        eye = lax.broadcasted_iota(jnp.int32, shape, 0) == lax.broadcasted_iota(jnp.int32, shape, 1)
        for at in range(0, block, rows):
            lhs[at : at + rows, edge_width:] = jnp.where(eye, 1.0, 0.0).astype(BF16)
        sum_out[...] = jnp.zeros_like(sum_out)

    lhs[:, :edge_width] = edge[...].reshape(block, edge_width)
    z[...] = dot(lhs[...], near[...])
    if not by_rows:
        z[...] += pick_rows(index_columns(idx_row[...]), (table,))
    upper = lax.broadcasted_iota(jnp.int32, (8, LANES), 0) < lanes

    def fetch(at):
        for e in range(at, at + 16, 2):
            pair = [
                table[pl.ds(pl.multiple_of(names[0, step * block + e + i] * 8, 8), 8), :]
                for i in range(2)
            ]
            far[e * lanes : e * lanes + 8, :] = jnp.where(upper, *pair)

    def fetched(at):
        return jnp.concatenate(
            [far[pl.ds(at * lanes + j, 16, stride=lanes), :] for j in range(lanes)], axis=1
        )

    if by_rows:
        fetch(0)
    for at in range(0, block, 16):
        value = z[at : at + 16, :]
        if by_rows:
            if at + 16 < block:
                fetch(at + 16)
            value = value + fetched(at)
        act, slope = gelu_parts(value)
        a1_out[at : at + 16, :] = act.astype(BF16)
        s1_out[at : at + 16, :] = slope.astype(BF16)
    z[...] = dot(a1_out[...], m2[...])
    bias = b2[...]
    for row in range(0, rows, 16):
        count = live_col[row : row + 16, :]
        inverse = 1.0 / count.astype(F32)
        total = sum_out[row : row + 16, :]
        for s in range(sb):
            at = s * rows + row
            act, slope = gelu_parts(z[at : at + 16, :] + bias)
            s2_out[at : at + 16, :] = slope.astype(BF16)
            share = jnp.where(count > step * sb + s, inverse, 0.0)
            total = total + act.astype(BF16).astype(F32) * spread(share, width)
        sum_out[row : row + 16, :] = total


def message_forward(node_lo, node_hi, node_own, edge, idx_row, live_col, m1, b1, m2, b2):
    slots, rows, edge_width = edge.shape
    width = node_own.shape[1]
    residues = 2 * node_lo.shape[0]
    by_rows = residues <= 4096 and width == 4 * LANES
    sb = slot_block(slots) if by_rows else 4
    block = sb * rows
    edges = slots * rows
    near = pl.cdiv(edge_width + rows, LANES) * LANES
    row_spec = pl.BlockSpec((block, width), lambda i: (i, 0))
    return pl.pallas_call(
        functools.partial(message_forward_kernel, sb, by_rows),
        grid=(slots // sb,),
        in_specs=[
            const_spec(node_lo.shape),
            const_spec(node_hi.shape),
            const_spec(node_own.shape),
            pl.BlockSpec((sb, rows, edge_width), lambda i: (i, 0, 0)),
            pl.BlockSpec((1, block), lambda i: (0, i)),
            pl.BlockSpec(memory_space=pltpu.SMEM),
            const_spec(live_col.shape),
            const_spec(m1.shape),
            const_spec(b1.shape),
            const_spec(m2.shape),
            const_spec(b2.shape),
        ],
        out_specs=[row_spec, row_spec, row_spec, pl.BlockSpec((rows, width), whole)],
        out_shape=[jax.ShapeDtypeStruct((edges, width), BF16)] * 3
        + [jax.ShapeDtypeStruct((rows, width), F32)],
        scratch_shapes=[
            pltpu.VMEM((residues * 8, LANES), F32) if by_rows else pltpu.VMEM((residues, width), BF16),
            pltpu.VMEM((block * 4 if by_rows else 8, LANES), F32),
            pltpu.VMEM((near, width), BF16),
            pltpu.VMEM((block, near), BF16),
            pltpu.VMEM((block, width), F32),
        ],
        compiler_params=pltpu.CompilerParams(vmem_limit_bytes=VMEM),
        name="message_forward",
        cost_estimate=pl.CostEstimate(
            flops=2 * edges * width * (residues + edge_width + width),
            bytes_accessed=edges * width * 6 + edges * edge_width * 2 + edges * LANES * 4,
            transcendentals=2 * edges * width,
        ),
    )(node_lo, node_hi, node_own, edge, idx_row, idx_row, live_col, m1, b1, m2, b2)


def joined(refs, at):
    return jnp.concatenate([refs[2 * at][...], refs[2 * at + 1][...]], axis=0)


def residue_forward_kernel(parts, node, total, m3, b3, g1, fb2, g2, e_first, e_far, eb, *refs):
    f1, f2 = refs[:parts], refs[parts : 3 * parts]
    h1b_out, n1_out, sc1_out, n2_out, sc2_out, slope_out, h2b_out, far_out, own_out = refs[3 * parts :]
    width, hidden = node.shape[1], f1[0].shape[1]
    u1 = node[...].astype(F32) + fine(dot, total[...], m3[...]) + b3[...]
    n1, sc1 = norm(u1)
    h1 = n1 * g1[...]
    h1b = h1.astype(BF16)
    h1b_out[...] = h1b
    n1_out[...] = n1
    sc1_out[...] = jnp.broadcast_to(sc1, sc1_out.shape)
    y2 = None
    for p in range(parts):
        bias = f1[p][width : width + 16, :].astype(F32)
        bias = bias[0:1] + bias[1:2] + bias[2:3]
        act, slope = gelu_parts(dot(h1b, f1[p][:width, :]) + bias)
        slope_out[:, p * hidden : (p + 1) * hidden] = slope
        part = dot(act.astype(BF16), joined(f2, p))
        y2 = part if y2 is None else y2 + part
    n2, sc2 = norm(h1 + (y2 + fb2[...]))
    h2b = (n2 * g2[...]).astype(BF16)
    n2_out[...] = n2
    sc2_out[...] = jnp.broadcast_to(sc2, sc2_out.shape)
    h2b_out[...] = h2b
    far_out[...] = dot_back(h2b, e_far[...]).astype(BF16)
    own_out[...] = dot_back(h2b, e_first[:, :width]) + eb[...]


def residue_forward(node, total, m3, b3, g1, fb2, g2, e_first, e_far, eb, f1, f2):
    rows, width = node.shape
    edge_width = e_first.shape[0]
    hidden = len(f1) * f1[0].shape[1]
    shapes = [
        ((rows, width), BF16),
        ((rows, width), F32),
        ((rows, LANES), F32),
        ((rows, width), F32),
        ((rows, LANES), F32),
        ((rows, hidden), F32),
        ((rows, width), BF16),
        ((rows, edge_width), BF16),
        ((rows, edge_width), F32),
    ]
    return small_call(
        functools.partial(residue_forward_kernel, len(f1)),
        (node, total, m3, b3, g1, fb2, g2, e_first, e_far, eb, *f1, *f2),
        shapes, "residue_forward", flops=4 * rows * width * hidden, moved=5 * MIB,
        exps=rows * hidden,
    )


def edge_kernel(
    sb, blocks, hi_chunks, by_rows, far_lo, far_hi, own, edge, cot, idx, idx_row, names, live_col,
    e_first, e2, eb2, e3, eb3, g3,
    edge_out, act_one_out, act_two_out, low_three_out, low_two_out, low_one_out, hi_out, lo_out, own_out, gain_out,
    low_first, gs, table, far, z, slope_ref,
):
    step = pl.program_id(0)
    rows, width = own.shape
    node_width = (e_first.shape[1] - width) // 2
    e_mid = e_first.at[:, node_width : node_width + width]
    tiles = pl.cdiv(width, LANES)
    per = 8 // tiles
    size = 32

    @pl.when(step == 0)
    def _():
        own_out[...] = jnp.zeros_like(own_out)
        gs[...] = jnp.zeros_like(gs)
        half = far_lo.shape[0]
        if by_rows:
            for source, start in ((far_lo, 0), (far_hi, half)):
                for first in range(0, half, 512):
                    value = source[first : first + 512, :].astype(F32)
                    for at in range(8):
                        column = at % tiles * LANES
                        take = min(LANES, width - column)
                        table[pl.ds((start + first) * 8 + at, value.shape[0], stride=8), :take] = value[
                            :, column : column + take
                        ]

    @pl.when(step < blocks)
    def _():
        block = sb * rows
        flat = edge[...].reshape(block, width)
        z[...] = dot_back(flat, e_mid[...])
        if not by_rows:
            z[...] += pick_rows(index_columns(idx[...]), (far_lo, far_hi))
        sub = lax.broadcasted_iota(jnp.int32, (8, LANES), 0)

        def fetch(at):
            for e in range(at, at + size, per):
                got = [
                    table[pl.ds(pl.multiple_of(names[0, step * block + e + i] * 8, 8), 8), :]
                    for i in range(per)
                ]
                value = got[-1]
                for i in range(per - 2, -1, -1):
                    value = jnp.where(sub < (i + 1) * tiles, got[i], value)
                far[e * tiles : e * tiles + 8, :] = value

        def fetched(at):
            parts = [
                far[pl.ds(at * tiles + j, size, stride=tiles), :][:, : min(LANES, width - j * LANES)]
                for j in range(tiles)
            ]
            return jnp.concatenate(parts, axis=1)

        if by_rows:
            fetch(0)
        for at in range(0, block, size):
            value = z[at : at + size, :] + own[at % rows : at % rows + size, :]
            if by_rows:
                if at + size < block:
                    fetch(at + size)
                value = value + fetched(at)
            act, slope = gelu_parts(value)
            act_one_out[at : at + size, :] = act.astype(BF16)
            slope_ref[at : at + size, :] = slope
        act_one = act_one_out[...]
        act_two, slope_two = gelu_parts(dot(act_one, e2[...]) + eb2[...])
        act_two = act_two.astype(BF16)
        act_two_out[...] = act_two
        w_three = dot(act_two, e3[...]) + eb3[...]
        normed, scale = norm(flat.astype(F32) + w_three)
        count = spread(live_col[...], pl.cdiv(width, LANES) * LANES)[:, :width]
        live = jnp.concatenate(
            [jnp.where(count > step * sb + s, 1.0, 0.0) for s in range(sb)], axis=0
        )
        edge_out[...] = (normed * g3[...] * live).astype(BF16).reshape(sb, rows, width)
        grad = cot[...].reshape(block, width).astype(F32) * live
        gs[...] += jnp.sum((grad * normed).reshape(sb, rows, width), axis=0)
        low_three = norm_back(grad * g3[...], normed, scale).astype(BF16)
        low_three_out[...] = low_three
        low_two = (dot_back(low_three, e3[...]) * slope_two).astype(BF16)
        low_two_out[...] = low_two
        low_one = (dot_back(low_two, e2[...]) * slope_ref[...]).astype(BF16)
        low_one_out[...] = low_one
        own_out[...] += jnp.sum(low_one.astype(F32).reshape(sb, rows, width), axis=0)
        low_first[pl.ds(pl.multiple_of(step * block, block), block), :] = low_one

    chunk = hi_out.shape[0]

    @pl.when((step >= blocks) & (step < blocks + hi_chunks))
    def _():
        start = (step - blocks + hi_chunks) * chunk
        hi_out[...] = dot(one_hot_rows(idx_row[...], start, chunk), low_first[...]).astype(BF16)

    @pl.when(step >= blocks + hi_chunks)
    def _():
        start = (step - blocks - hi_chunks) * chunk
        lo_out[...] = dot(one_hot_rows(idx_row[...], start, chunk), low_first[...])

    @pl.when(step == blocks + 2 * hi_chunks - 1)
    def _():
        gain_out[...] = column_sum(gs[...])


def edge_branch(far_lo, far_hi, own, edge, cot, idx_row, live_col, e_first, e2, eb2, e3, eb3, g3):
    slots, rows, width = edge.shape
    sb = slot_block(slots)
    edges = slots * rows
    block = sb * rows
    blocks = slots // sb
    half = far_lo.shape[0]
    chunk = min(512, half)
    hi_chunks = half // chunk
    by_rows = half <= 2048 and 8 % pl.cdiv(width, LANES) == 0
    blk = lambda i: jnp.minimum(i, blocks - 1)
    hi_at = lambda i: (jnp.clip(i - blocks, 0, hi_chunks - 1), 0)
    lo_at = lambda i: (jnp.clip(i - blocks - hi_chunks, 0, hi_chunks - 1), 0)
    slot_spec = pl.BlockSpec((sb, rows, width), lambda i: (blk(i), 0, 0))
    row_spec = pl.BlockSpec((block, width), lambda i: (blk(i), 0))
    return pl.pallas_call(
        functools.partial(edge_kernel, sb, blocks, hi_chunks, by_rows),
        grid=(blocks + 2 * hi_chunks,),
        in_specs=[
            const_spec(far_lo.shape),
            const_spec(far_hi.shape),
            const_spec(own.shape),
            slot_spec,
            slot_spec,
            pl.BlockSpec((1, block), lambda i: (0, blk(i))),
            const_spec(idx_row.shape),
            pl.BlockSpec(memory_space=pltpu.SMEM),
            const_spec(live_col.shape),
            const_spec(e_first.shape),
            const_spec(e2.shape),
            const_spec(eb2.shape),
            const_spec(e3.shape),
            const_spec(eb3.shape),
            const_spec(g3.shape),
        ],
        out_specs=[slot_spec]
        + [row_spec] * 5
        + [
            pl.BlockSpec((chunk, width), hi_at),
            pl.BlockSpec((chunk, width), lo_at),
            pl.BlockSpec((rows, width), whole),
            pl.BlockSpec((1, width), whole),
        ],
        out_shape=[jax.ShapeDtypeStruct((slots, rows, width), BF16)]
        + [jax.ShapeDtypeStruct((edges, width), BF16)] * 5
        + [
            jax.ShapeDtypeStruct((half, width), BF16),
            jax.ShapeDtypeStruct((half, width), F32),
            jax.ShapeDtypeStruct((rows, width), F32),
            jax.ShapeDtypeStruct((1, width), F32),
        ],
        scratch_shapes=[
            pltpu.VMEM((edges, width), BF16),
            pltpu.VMEM((rows, width), F32),
            pltpu.VMEM((half * 16 if by_rows else 8, LANES), F32),
            pltpu.VMEM((block * 8, LANES), F32),
            pltpu.VMEM((block, width), F32),
            pltpu.VMEM((block, width), F32),
        ],
        compiler_params=pltpu.CompilerParams(vmem_limit_bytes=VMEM),
        name="edge_branch",
        cost_estimate=pl.CostEstimate(
            flops=2 * edges * width * (4 * half + 5 * width),
            bytes_accessed=edges * width * 16,
            transcendentals=2 * edges * width,
        ),
    )(far_lo, far_hi, own, edge, cot, idx_row, idx_row, idx_row, live_col, e_first, e2, eb2, e3, eb3, g3)


def edge_weights_kernel(blocks, pairs, *refs):
    step = pl.program_id(0)
    lefts, rights = refs[:pairs], refs[pairs : 2 * pairs]
    grads, biases, sums = refs[2 * pairs : 3 * pairs], refs[3 * pairs : 4 * pairs], refs[-1]
    rows = sums.shape[1]

    @pl.when(step == 0)
    def _():
        for ref in (*grads, sums):
            ref[...] = jnp.zeros_like(ref)

    for at in range(pairs):
        left, right = [r[...].reshape(-1, r.shape[-1]) for r in (lefts[at], rights[at])]
        grads[at][...] += dot_rows(left, right)
        low = left if lefts[at].ndim < rights[at].ndim else right
        sums[at] += jnp.sum(low.astype(F32).reshape(-1, rows, low.shape[1]), axis=0)

    @pl.when(step == blocks - 1)
    def _():
        for at in range(pairs):
            biases[at][...] = column_sum(sums[at])


def edge_weights(lefts, rights, rows):
    pairs = len(lefts)
    edges, width = lefts[0].shape
    slots = edges // rows
    sb = slot_block(slots)

    def spec(array):
        if array.ndim == 3:
            return pl.BlockSpec((sb, rows, width), lambda i: (i, 0, 0))
        return pl.BlockSpec((sb * rows, width), lambda i: (i, 0))

    shapes = [(width, width)] * pairs + [(1, width)] * pairs
    return pl.pallas_call(
        functools.partial(edge_weights_kernel, slots // sb, pairs),
        grid=(slots // sb,),
        in_specs=[spec(array) for array in (*lefts, *rights)],
        out_specs=[pl.BlockSpec(s, whole) for s in shapes],
        out_shape=[jax.ShapeDtypeStruct(s, F32) for s in shapes],
        scratch_shapes=[pltpu.VMEM((pairs, rows, width), F32)],
        compiler_params=pltpu.CompilerParams(vmem_limit_bytes=VMEM),
        name="edge_weights",
        cost_estimate=pl.CostEstimate(
            flops=2 * pairs * edges * width * width,
            bytes_accessed=pairs * edges * width * 4,
            transcendentals=0,
        ),
    )(*lefts, *rights)


def early_shapes(width, edge_width):
    return [
        (width, width),
        (edge_width, width),
        (edge_width, width),
        (16, width),
        (16, edge_width),
    ]


def residue_backward_kernel(
    parts, pieces, node_cot, own_sum, e_first, e_far, h1b, h2b, n1, sc1, n2, sc2, slope, g1, g2, m3,
    total, edge_gain, *refs,
):
    far = refs[:pieces]
    f1 = refs[pieces : pieces + parts]
    f2 = refs[pieces + parts : pieces + 3 * parts]
    gu1_out, v_out, both_out, slab = refs[pieces + 3 * parts :]
    width, hidden = h2b.shape[1], f1[0].shape[1]
    far_sum = far[0][: far[1].shape[0], :]
    for ref in far[1:]:
        far_sum = far_sum + ref[...].astype(F32)
    own = own_sum[...]
    g_h2 = (
        node_cot[...].astype(F32)
        + fine(dot, own, e_first[:, :width])
        + fine(dot, far_sum, e_far[...])
    )
    gain_two = column_sum(g_h2 * n2[...])
    g_u2 = norm_back(g_h2 * g2[...], n2[...], sc2[:, :1])
    gy2 = g_u2.astype(BF16)
    both_out[:, :width] = h1b[...]
    both_out[:, width:] = gy2
    g_h1 = g_u2
    for p in range(parts):
        gy1 = dot_back(gy2, joined(f2, p)) * slope[:, p * hidden : (p + 1) * hidden]
        g_h1 = g_h1 + dot_back(gy1.astype(BF16), f1[p][:width, :])
    gain_one = column_sum(g_h1 * n1[...])
    g_u1 = norm_back(g_h1 * g1[...], n1[...], sc1[:, :1])
    gu1_out[...] = g_u1
    v_out[...] = fine(dot_back, g_u1, m3[...])
    bias = [gain_one, gain_two, column_sum(gy2.astype(F32)), column_sum(g_u1)]
    slab[...] = jnp.zeros_like(slab)
    pack(
        slab,
        [
            dot_rows(total[...].astype(BF16), g_u1.astype(BF16)),
            dot_rows(own.astype(BF16), h2b[...]),
            dot_rows(far_sum.astype(BF16), h2b[...]),
            padded_rows(bias, width),
            padded_rows([edge_gain[...]], own.shape[1]),
        ],
    )


def residue_backward(args, far, f1, f2):
    node_cot, e_first, slope = args[0], args[2], args[10]
    rows, width = node_cot.shape
    shapes = [
        ((rows, width), F32),
        ((rows, width), F32),
        ((rows, 2 * width), BF16),
        ((all_tiles(early_shapes(width, e_first.shape[0])), 16, LANES), BF16),
    ]
    return small_call(
        functools.partial(residue_backward_kernel, len(f1), len(far)),
        (*args, *far, *f1, *f2),
        shapes, "residue_backward",
        flops=4 * rows * width * slope.shape[1], moved=8 * MIB,
    )


def feed_kernel(first, second, f1, fb1, f2, f1g, f2g, fb1g):
    width = f1.shape[0]

    @pl.when(pl.program_id(0) == 0)
    def _():
        for ref in (f1g, f2g, fb1g):
            ref[...] = jnp.zeros_like(ref)

    for both in (first, second):
        h1b, gy2 = both[:, :width], both[:, width:]
        act, slope = gelu_parts(dot(h1b, f1[...]) + fb1[...])
        gy1 = (dot_back(gy2, f2[...]) * slope).astype(BF16)
        f1g[...] += dot_rows(h1b, gy1)
        f2g[...] += dot_rows(act.astype(BF16), gy2)
        fb1g[...] += column_sum(gy1.astype(F32))


def feed_gradients(both, f1, fb1, f2):
    width, hidden = f1.shape
    half = both[0].shape[0]
    chunk = min(512, half)
    shapes = [(width, hidden), (hidden, width), (1, hidden)]
    return pl.pallas_call(
        feed_kernel,
        grid=(half // chunk,),
        in_specs=[pl.BlockSpec((chunk, 2 * width), lambda i: (i, 0))] * 2
        + [const_spec(a.shape) for a in (f1, fb1, f2)],
        out_specs=[pl.BlockSpec(s, whole) for s in shapes],
        out_shape=[jax.ShapeDtypeStruct(s, F32) for s in shapes],
        compiler_params=pltpu.CompilerParams(vmem_limit_bytes=VMEM),
        name="feed_gradients",
        cost_estimate=pl.CostEstimate(
            flops=16 * half * width * hidden,
            bytes_accessed=8 * half * width,
            transcendentals=2 * half * hidden,
        ),
    )(*both, f1, fb1, f2)


def late_shapes(width, edge_width):
    return [
        (width, width),
        (width, width),
        (edge_width, width),
        (16, width),
        (width, width),
        (edge_width, edge_width),
        (edge_width, edge_width),
        (edge_width, edge_width),
        (16, edge_width),
    ]


def weight_shapes(width, edge_width):
    return early_shapes(width, edge_width) + late_shapes(width, edge_width)


def message_backward_kernel(
    sb, blocks, groups, at_once, codes, base, order, v, a1, s1, s2, edge, low_three, low_edge, local_row, live_col,
    m1, m2, e_first, node_lo, node_hi, node, early,
    e1g, e2g, e3g, eb1, eb2, eb3,
    edge_grad, far_keep, far_send, own, keep, send,
    low_two, low_one, grad, rows_ref, moved, m2g, m1eg, m1fg, b2s, slab,
):
    step = pl.program_id(0)
    rows, width = v.shape
    edge_width = edge.shape[2]
    block = sb * rows
    tiles = width // LANES
    size = 16

    @pl.when(step == 0)
    def _():
        for ref in (own, m2g, m1eg, m1fg, b2s):
            ref[...] = jnp.zeros_like(ref)

    @pl.when(step < blocks)
    def _():
        for row in range(0, rows, size):
            count = live_col[row : row + size, :]
            inverse = 1.0 / count.astype(F32)
            value = v[row : row + size, :]
            total = b2s[row : row + size, :]
            for s in range(sb):
                at = s * rows + row
                share = jnp.where(count > step * sb + s, inverse, 0.0)
                low = (value * spread(share, width) * s2[at : at + size, :].astype(F32)).astype(BF16)
                low_two[at : at + size, :] = low
                total = total + low.astype(F32)
            b2s[row : row + size, :] = total
        grad[...] = dot_back(low_two[...], m2[...])
        m2g[...] += dot_rows(a1[...], low_two[...])
        first = pl.multiple_of(step * (block * 8), 8)
        rows_ref[pl.ds(first + tiles, block, stride=8), :] = index_columns(local_row[...]).astype(F32)
        for row in range(0, rows, size):
            total = own[row : row + size, :]
            for s in range(sb):
                at = s * rows + row
                low = (grad[at : at + size, :] * s1[at : at + size, :].astype(F32)).astype(BF16)
                low_one[at : at + size, :] = low
                low = low.astype(F32)
                total = total + low
                for j in range(tiles):
                    rows_ref[pl.ds(first + at * 8 + j, size, stride=8), :] = low[
                        :, j * LANES : (j + 1) * LANES
                    ]
            own[row : row + size, :] = total
        m1eg[...] += dot_rows(edge[...].reshape(block, edge_width), low_one[...])
        total = (
            low_three[...].astype(F32)
            + dot(low_edge[...], e_first[:, width : width + edge_width])
            + dot_back(low_one[...], m1[width : width + edge_width, :])
        )
        edge_grad[...] = total.reshape(sb, rows, edge_width)

    @pl.when(step >= blocks)
    def _():
        deep = far_keep.shape[0]
        count = block * blocks // groups
        height = rows // 16
        picked = [
            group_rows(
                order, ((step - blocks) * at_once + i) * count, count, rows_ref, moved.at[i], width
            )
            for i in range(at_once)
        ]
        for i, (values, local) in enumerate(picked):
            sums = group_sums(values, local, 2 * deep * rows).astype(BF16)
            near = jnp.concatenate(
                [ref[at, i] for ref in (node_lo, node_hi) for at in range(deep)], axis=0
            )
            m1fg[...] += dot_rows(near, sums)
            for at in range(2 * deep):
                out = (far_keep if at < deep else far_send).at[at % deep, i]
                for j in range(tiles):
                    tile = sums[at * rows : (at + 1) * rows, j * LANES : (j + 1) * LANES]
                    out[j * height : (j + 1) * height] = tile.reshape(height, 16, LANES)

    @pl.when(step == blocks + groups // at_once - 1)
    def _():
        count = early.shape[0]
        slab[:count] = early[...]
        slab[count:] = jnp.zeros_like(slab[count:])
        pack(
            slab,
            [
                dot_rows(node[...], own[...].astype(BF16)),
                m2g[...],
                m1eg[...],
                padded_rows([column_sum(own[...]), column_sum(b2s[...])], width),
                m1fg[...],
                e1g[...],
                e2g[...],
                e3g[...],
                padded_rows([eb1[...], eb2[...], eb3[...]], edge_width),
            ],
            count,
        )
        order_out(slab, base[0], codes, keep, send)


def message_backward(
    groups, codes, base, order, v, a1, s1, s2, edge, low_three, low_edge, local_row, live_col, m1, m2,
    e_first, node_lo, node_hi, node, early, edge_grads,
):
    slots, rows, edge_width = edge.shape
    width = v.shape[1]
    sb = slot_block(slots)
    block = sb * rows
    blocks = slots // sb
    edges = slots * rows
    half = node_lo.shape[0]
    deep = half // rows // groups
    at_once = 2 if groups % 2 == 0 else 1
    tiles = rows * width // (16 * LANES)
    slab = slab_tiles(weight_shapes(width, edge_width), len(codes)) * len(codes)
    node_lo, node_hi = [n.reshape(deep, groups, rows, width) for n in (node_lo, node_hi)]
    blk = lambda i: jnp.minimum(i, blocks - 1)
    group_at = lambda i: (0, jnp.maximum(i - blocks, 0))
    row_spec = pl.BlockSpec((block, width), lambda i: (blk(i), 0))
    slot_spec = pl.BlockSpec((sb, rows, edge_width), lambda i: (blk(i), 0, 0))
    edge_spec = pl.BlockSpec((block, edge_width), lambda i: (blk(i), 0))
    node_spec = pl.BlockSpec((deep, at_once, rows, width), lambda i: (*group_at(i), 0, 0))
    far_spec = pl.BlockSpec((deep, at_once, tiles, 16, LANES), lambda i: (*group_at(i), 0, 0, 0))
    slab_spec = pl.BlockSpec((slab // 2, 16, LANES), lambda i: (0, 0, 0))
    smem = pl.BlockSpec(memory_space=pltpu.SMEM)
    return pl.pallas_call(
        functools.partial(message_backward_kernel, sb, blocks, groups, at_once, codes),
        grid=(blocks + groups // at_once,),
        in_specs=[
            smem,
            smem,
            const_spec(v.shape),
            row_spec,
            row_spec,
            row_spec,
            slot_spec,
            edge_spec,
            edge_spec,
            pl.BlockSpec((1, block), lambda i: (0, blk(i))),
            const_spec(live_col.shape),
            const_spec(m1.shape),
            const_spec(m2.shape),
            const_spec(e_first.shape),
            node_spec,
            node_spec,
            const_spec(node.shape),
            const_spec(early.shape),
        ]
        + [const_spec(a.shape) for a in edge_grads],
        out_specs=[slot_spec, far_spec, far_spec, pl.BlockSpec((rows, width), whole), slab_spec, slab_spec],
        out_shape=[
            jax.ShapeDtypeStruct((slots, rows, edge_width), F32),
            jax.ShapeDtypeStruct((deep, groups, tiles, 16, LANES), BF16),
            jax.ShapeDtypeStruct((deep, groups, tiles, 16, LANES), BF16),
            jax.ShapeDtypeStruct((rows, width), F32),
            jax.ShapeDtypeStruct((slab // 2, 16, LANES), BF16),
            jax.ShapeDtypeStruct((slab // 2, 16, LANES), BF16),
        ],
        scratch_shapes=[
            pltpu.VMEM((block, width), BF16),
            pltpu.VMEM((block, width), BF16),
            pltpu.VMEM((block, width), F32),
            pltpu.VMEM((edges * 8, LANES), F32),
            pltpu.VMEM((at_once, edges // groups * 8, LANES), F32),
            pltpu.VMEM((width, width), F32),
            pltpu.VMEM((edge_width, width), F32),
            pltpu.VMEM((width, width), F32),
            pltpu.VMEM((rows, width), F32),
            slab_scratch(slab),
        ],
        compiler_params=pltpu.CompilerParams(vmem_limit_bytes=VMEM),
        name="message_backward",
        cost_estimate=pl.CostEstimate(
            flops=2 * edges * width * (2 * width + 3 * edge_width + half // groups),
            bytes_accessed=edges * width * 6 + edges * edge_width * 10,
            transcendentals=0,
        ),
    )(
        base, order, v, a1, s1, s2, edge, low_three, low_edge, local_row, live_col, m1, m2, e_first,
        node_lo, node_hi, node, early, *edge_grads,
    )


def node_kernel(pieces, g_u1, own, m1, *refs):
    far, grad_out = refs[:pieces], refs[pieces]
    rows, width = own.shape
    height = rows // 16
    tiles = height * (width // LANES)
    sums = far[0][:tiles].astype(F32)
    for ref in far[1:]:
        sums = sums + ref[:tiles].astype(F32)
    far_sum = jnp.concatenate(
        [sums[j * height : (j + 1) * height].reshape(rows, LANES) for j in range(width // LANES)],
        axis=1,
    )
    far_first = m1.shape[0] - width
    grad_out[...] = (
        g_u1[...]
        + fine(dot_back, own[...], m1[:width, :])
        + fine(dot_back, far_sum, m1[far_first:, :])
    )


def node_last(g_u1, own, m1, far):
    return small_call(
        functools.partial(node_kernel, len(far)),
        (g_u1, own, m1, *far), [(own.shape, F32)], "node_gradient",
        flops=8 * own.size * own.shape[1], moved=2 * MIB,
    )[0]


def weights_out_kernel(
    codes, base, first, second,
    m1g, b1, m2g, b2, m3g, e1g, e2g, e3g, b3, g1, g2, fb2, eb1, eb2, eb3, g3, slab,
):
    order_in(slab, base[0], codes, first, second)
    width, edge_width = m3g.shape[0], e2g.shape[0]
    shapes = weight_shapes(width, edge_width)
    starts = [all_tiles(shapes[:at]) for at in range(len(shapes))]
    m3g[...] = unpack(slab, starts[0], width, width)
    e1g[:, :width] = unpack(slab, starts[1], edge_width, width)
    middle = unpack(slab, starts[10], edge_width, edge_width)
    far = unpack(slab, starts[2], edge_width, width)
    over = edge_width % LANES
    base_col = width + edge_width - over
    e1g[:, width:base_col] = middle[:, : edge_width - over]
    far = pltpu.roll(jnp.concatenate([far, jnp.zeros((edge_width, LANES), F32)], axis=1), over, 1)
    lane = lax.broadcasted_iota(jnp.int32, (edge_width, LANES), 1)
    e1g[:, base_col : base_col + LANES] = jnp.where(
        lane < over, middle[:, edge_width - over : edge_width - over + LANES], far[:, :LANES]
    )
    rest = e1g.shape[1] - base_col - LANES
    e1g[:, base_col + LANES :] = far[:, LANES : LANES + rest]
    bias = unpack(slab, starts[3], 16, width)
    for row, out in enumerate((g1, g2, fb2, b3)):
        out[...] = bias[row : row + 1]
    g3[...] = unpack(slab, starts[4], 16, edge_width)[:1, :edge_width]
    m1g[:width, :] = unpack(slab, starts[5], width, width)
    m2g[...] = unpack(slab, starts[6], width, width)
    m1g[width : width + edge_width, :] = unpack(slab, starts[7], edge_width, width)
    bias = unpack(slab, starts[8], 16, width)
    b1[...] = bias[0:1]
    b2[...] = bias[1:2]
    m1g[width + edge_width :, :] = unpack(slab, starts[9], width, width)
    e2g[...] = unpack(slab, starts[11], edge_width, edge_width)[:, :edge_width]
    e3g[...] = unpack(slab, starts[12], edge_width, edge_width)[:, :edge_width]
    bias = unpack(slab, starts[13], 16, edge_width)
    for row, out in enumerate((eb1, eb2, eb3)):
        out[...] = bias[row : row + 1, :edge_width]


def weights_out(codes, base, halves_in, width, edge_width):
    shapes = [(2 * width + edge_width, width), (1, width), (width, width), (1, width)]
    shapes += [(width, width), (edge_width, 2 * width + edge_width)]
    shapes += [(edge_width, edge_width)] * 2 + [(1, width)] * 4 + [(1, edge_width)] * 4
    tiles = slab_tiles(weight_shapes(width, edge_width), len(codes)) * len(codes)
    return small_call(
        functools.partial(weights_out_kernel, codes),
        (base, *halves_in), [(s, F32) for s in shapes], "weight_gradients",
        [slab_scratch(tiles)], moved=10 * MIB, scalars=1,
    )


def exchange(value, mask, devices):
    return lax.ppermute(value, AXES, [(d, d ^ mask) for d in range(devices)])


def mask_groups(masks):
    return [masks[i : min(i + 2, len(masks) - 1)] for i in range(0, len(masks) - 1, 2)] + [masks[-1:]]


def order_codes(groups):
    masks = [mask for group in groups for mask in group]
    return [
        sum(mask for bit, mask in enumerate(masks) if place >> bit & 1)
        for place in range(1 << len(masks))
    ]


def combined(group, code):
    return sum(mask for bit, mask in enumerate(group) if code >> bit & 1)


def sent_around(value, group, devices):
    return [value] + [
        exchange(value, combined(group, code), devices) for code in range(1, 1 << len(group))
    ]


def shared_out(total, group, devices):
    parts = 1 << len(group)
    rows = total.shape[0] // parts
    return [total] + [
        exchange(total[code * rows : (code + 1) * rows].astype(BF16), combined(group, code), devices)
        for code in range(1, parts)
    ]


def add_up(terms):
    total = terms[0][: terms[1].shape[0]].astype(F32)
    for term in terms[1:]:
        total = total + term.astype(F32)
    return total


def tied(*values):
    return lax.optimization_barrier(values)


def split_three(value):
    rows = []
    for _ in range(3):
        high = lax.reduce_precision(value, 8, 7)
        rows.append(high.astype(BF16))
        value = value - high
    return jnp.concatenate(rows + [jnp.zeros((13, value.shape[1]), BF16)], axis=0)


def per_device(
    node_in,
    edge_in,
    neighbours,
    live_counts,
    message_first,
    message_first_bias,
    message_second,
    message_second_bias,
    message_third,
    message_third_bias,
    norm_one,
    feed_first,
    feed_first_bias,
    feed_second,
    feed_second_bias,
    norm_two,
    edge_first,
    edge_first_bias,
    edge_second,
    edge_second_bias,
    edge_third,
    edge_third_bias,
    norm_three,
    node_cotangent,
    edge_cotangent,
):
    rows, slots = neighbours.shape
    width = node_in.shape[1]
    edge_width = edge_in.shape[2]
    edges = rows * slots
    hid_count = lax.axis_size("hid")
    res_count = lax.axis_size("res")
    devices = res_count * hid_count
    bits = devices.bit_length() - 1
    masks = [1 << b for b in range(bits - 1, -1, -1)]
    groups = mask_groups(masks)
    codes = order_codes(groups)
    me = lax.axis_index("res") * hid_count + lax.axis_index("hid")
    base = me.reshape(1)
    row = lambda vector: vector.reshape(1, -1)

    names = neighbours.T.reshape(edges)
    apart = (names // rows) ^ me
    place = jnp.zeros_like(names)
    for bit, mask in enumerate(masks):
        place = place | jnp.where((apart & mask) != 0, 1 << bit, 0)
    idx_row = (place * rows + names % rows).reshape(1, edges)
    res_count = devices // hid_count
    local_row = (place // res_count * rows + names % rows).reshape(1, edges)
    edge_order = group_order(place % res_count, res_count)
    live_col = jnp.broadcast_to(live_counts[:, None], (rows, LANES))
    edge = edge_in.transpose(1, 0, 2)
    cot = edge_cotangent.transpose(1, 0, 2)
    e_first = edge_first.T
    e_far = e_first[:, width + edge_width :]
    f1x = jnp.concatenate([feed_first, split_three(row(feed_first_bias))], axis=0)
    cut = feed_second.shape[0] // 2
    hid_masks = [m for m in masks if m < hid_count]

    def across(pieces):
        for mask in hid_masks[:-1]:
            pieces = pieces + [exchange(p, mask, devices) for p in pieces]
        return pieces

    def over(pieces):
        return pieces + [exchange(p, hid_masks[-1], devices) for p in pieces]

    f2a = across([feed_second[:cut]])

    stack = lambda pieces: jnp.concatenate(pieces, axis=0)
    *outer, near = groups

    held = stack(sent_around(node_in, outer[0], devices))
    held, idx_row, local_row, f2a = tied(held, idx_row, local_row, f2a)
    for group in outer[1:]:
        held = stack(sent_around(held, group, devices))
    f2b = feed_second[cut:]
    held, f1x, f2a, f2b, edge_order, live_col = tied(held, f1x, f2a, f2b, edge_order, live_col)
    node_lo, node_hi = sent_around(held, near, devices)

    f2a = over(f2a)
    f1, f2b = across([f1x]), across([f2b])

    a1, s1, s2, total = message_forward(
        node_lo, node_hi, node_in, edge, idx_row, live_col, message_first,
        row(message_first_bias), message_second, row(message_second_bias),
    )
    total, f1, f2a, f2b, e_far = tied(total, f1, f2a, f2b, e_far)
    f1, f2b = over(f1), over(f2b)
    f2 = [half for pair in zip(f2a, f2b) for half in pair]
    h1b, n1, sc1, n2, sc2, slope, h2b, far_part, own_part = residue_forward(
        node_in, total, message_third, row(message_third_bias), row(norm_one),
        row(feed_second_bias), row(norm_two), e_first, e_far, row(edge_first_bias), f1, f2,
    )

    held = stack(sent_around(far_part, outer[0], devices))
    for group in outer[1:]:
        held = stack(sent_around(held, group, devices))
    q_lo, q_hi = sent_around(held, near, devices)

    edge_out, act_one, act_two, low_three, low_two, low_one, hi, lo, own_sum, edge_gain = edge_branch(
        q_lo, q_hi, own_part, edge, cot, idx_row, live_col, e_first,
        edge_second, row(edge_second_bias), edge_third, row(edge_third_bias), row(norm_three),
    )

    terms = [lo, exchange(hi, near[0], devices)]
    for group in reversed(outer):
        terms = shared_out(add_up(terms), group, devices)
    g_u1, v, both, early = residue_backward(
        (
            node_cotangent, own_sum, e_first, e_far, h1b, h2b, n1, sc1, n2, sc2, slope, row(norm_one),
            row(norm_two), message_third, total, edge_gain,
        ),
        terms, f1, f2,
    )

    both, low_here = tied(both, low_one)
    b_held = stack(sent_around(both, outer[0], devices))
    edge_grads = edge_weights((low_here, act_one, act_two), (edge, low_two, low_three), rows)
    v, b_held, edge_grads = tied(v, b_held, edge_grads)
    for group in outer[1:]:
        b_held = stack(sent_around(b_held, group, devices))
    edge_grad, far_keep, far_send, own, keep, send = message_backward(
        res_count, codes, base, edge_order, v, a1, s1, s2, edge, low_three, low_one, local_row, live_col,
        message_first, message_second, e_first, node_lo, node_hi, node_in, early, edge_grads,
    )
    keep, send, far_keep, far_send, b_held = tied(keep, send, far_keep, far_send, b_held)

    first, *others = reversed(outer)
    terms = [keep, exchange(send, near[0], devices)]
    total, b_held, far_send = tied(add_up(terms), b_held, far_send)
    terms = shared_out(total, first, devices)
    far_keep, far_send = [far.reshape(-1, 16, LANES) for far in (far_keep, far_send)]
    far_terms = [far_keep, exchange(far_send, near[0], devices)]
    b_near = sent_around(b_held, near, devices)
    total, b_first = tied(add_up(far_terms), b_near[0])
    far_terms = shared_out(total, first, devices)
    feed = feed_gradients((b_first, b_near[1]), feed_first, row(feed_first_bias), feed_second)
    terms, (f1g, f2g, fb1g) = tied(terms, feed)
    for group in others:
        terms = shared_out(add_up(terms), group, devices)
    held, *far_terms[:3] = tied(add_up(terms).astype(BF16), *far_terms[:3])

    for at, group in enumerate(outer):
        around = sent_around(held, group, devices)
        if at + 1 == len(outer):
            around, node_gradient = tied(around, node_last(g_u1, own, message_first, far_terms))
        held = stack(around)
        if at < len(others):
            held, *far_terms = tied(held, *far_terms)
            far_terms = shared_out(add_up(far_terms), others[at], devices)
    m1g, b1, m2g, b2, m3g, e1g, e2g, e3g, b3, g1, g2, fb2, eb1, eb2, eb3, g3 = weights_out(
        codes, base, sent_around(held, near, devices), width, edge_width
    )
    flat = lambda vector: vector.reshape(-1)
    return (
        h2b,
        edge_out.transpose(1, 0, 2),
        node_gradient,
        edge_grad.transpose(1, 0, 2),
        m1g,
        flat(b1),
        m2g,
        flat(b2),
        m3g,
        flat(b3),
        flat(g1),
        f1g,
        flat(fb1g),
        f2g,
        flat(fb2),
        flat(g2),
        e1g.T,
        flat(eb1),
        e2g,
        flat(eb2),
        e3g,
        flat(eb3),
        flat(g3),
    )


def solution(mesh):
    nodes, edges, shared = P(AXES, None), P(AXES, None, None), P()
    return jax.shard_map(
        per_device,
        mesh=mesh,
        in_specs=(nodes, edges, nodes, P(AXES))
        + (shared,) * 7
        + (P(None, "hid"), P("hid"), P("hid", None))
        + (shared,) * 9
        + (nodes, edges),
        out_specs=(nodes, edges, nodes, edges)
        + (shared,) * 7
        + (P(None, "hid"), P("hid"), P("hid", None))
        + (shared,) * 9,
        check_vma=False,
    )
```

```python
import functools

import jax
import jax.numpy as jnp
from jax import lax
from jax.experimental import pallas as pl
from jax.experimental.pallas import tpu as pltpu
from jax.sharding import PartitionSpec as P

EPS = 1e-05
AXES = ("res", "hid")
F32 = jnp.float32
BF16 = jnp.bfloat16
TANH_SCALE = 0.7978845608028654
TANH_CUBE = 0.044715
LANES = 128
CHUNK = 2048
MIB = 1024 * 1024
VMEM = 58 * MIB


def dot(left, right):
    return lax.dot_general(left, right, (((1,), (0,)), ((), ())), preferred_element_type=F32)


def dot_rows(left, right):
    return lax.dot_general(left, right, (((0,), (0,)), ((), ())), preferred_element_type=F32)


def dot_back(left, right):
    return lax.dot_general(left, right, (((1,), (1,)), ((), ())), preferred_element_type=F32)


def halves(value):
    high = value.astype(BF16)
    return high, (value - high.astype(F32)).astype(BF16)


def fine(product, value, weights):
    high, low = halves(value)
    return product(high, weights) + product(low, weights)


def gelu_parts(x):
    square = x * x
    t = jnp.tanh(x * (TANH_SCALE + (TANH_SCALE * TANH_CUBE) * square))
    gate = 0.5 + 0.5 * t
    act = x * gate
    slope = gate + act * (1.0 - gate) * (2 * TANH_SCALE + (6 * TANH_SCALE * TANH_CUBE) * square)
    return act, slope


def index_columns(idx_row):
    parts = [
        jnp.broadcast_to(idx_row[:, first : first + LANES], (LANES, LANES)).T
        for first in range(0, idx_row.shape[1], LANES)
    ]
    return jnp.concatenate(parts, axis=0)


def one_hot_columns(idx, start, count):
    one, zero = jnp.ones((), BF16), jnp.zeros((), BF16)
    idx = idx.astype(jnp.int16)
    lane = lax.broadcasted_iota(jnp.int32, idx.shape, 1).astype(jnp.int16)
    parts = [
        jnp.where(idx == lane + jnp.int16(start + first), one, zero)
        for first in range(0, count, LANES)
    ]
    return jnp.concatenate(parts, axis=1)


def pick_rows(idx, table_refs):
    total, start = None, 0
    for ref in table_refs:
        rows = ref.shape[0]
        step = min(rows, CHUNK)
        for first in range(0, rows, step):
            part = dot(one_hot_columns(idx, start + first, step), ref[first : first + step, :])
            total = part if total is None else total + part
        start += rows
    return total


def one_hot_rows(idx_row, start, count):
    shape = (count, idx_row.shape[1])
    row = (lax.broadcasted_iota(jnp.int32, shape, 0) + start).astype(jnp.int16)
    names = jnp.broadcast_to(idx_row, shape).astype(jnp.int16)
    return jnp.where(names == row, jnp.ones((), BF16), jnp.zeros((), BF16))


def group_rows(order, first, count, rows_ref, moved, width):
    for e in range(count):
        at = pl.multiple_of(order[0, first + e] * 8, 8)
        moved[e * 8 : e * 8 + 8, :] = rows_ref[pl.ds(at, 8), :]

    def column(at):
        return moved[pl.ds(at, count, stride=8), :]

    tiles = pl.cdiv(width, LANES)
    parts = [column(at)[:, : min(LANES, width - at * LANES)] for at in range(tiles)]
    return jnp.concatenate(parts, axis=1).astype(BF16), column(tiles)


def group_sums(rows, local, residues):
    lane = lax.broadcasted_iota(jnp.int32, local.shape, 1).astype(F32)
    picks = [
        jnp.where(local == lane + float(first), 1.0, 0.0).astype(BF16)
        for first in range(0, residues, LANES)
    ]
    return dot_rows(jnp.concatenate(picks, axis=1), rows)


def order_kernel(groups, count, names, out):
    rows = names.shape[0]
    row = lax.broadcasted_iota(jnp.int32, (LANES, LANES), 0)
    column = lax.broadcasted_iota(jnp.int32, (LANES, LANES), 1)
    upto = jnp.where(row <= column, 1.0, 0.0).astype(BF16)
    ones = jnp.ones((LANES, LANES), BF16)
    above = lax.broadcasted_iota(jnp.int32, (rows, rows), 0)
    before = jnp.where(lax.broadcasted_iota(jnp.int32, (rows, rows), 1) < above, 1.0, 0.0).astype(BF16)
    place = jnp.full(names.shape, float(2 * LANES * LANES), F32)
    for group in range(groups):
        here = names[...] == group
        low = jnp.where(here, 1.0, 0.0).astype(BF16)
        rank = dot(low, upto) + dot(before, dot(low, ones).astype(BF16))
        place = jnp.where(here, rank + float(group * count - 1), place)
    high = total = None
    for at in range(rows):
        where = jnp.broadcast_to(place[at : at + 1, :], (LANES, LANES)).T.astype(jnp.int32)
        left = jnp.where(where // LANES == column, 1.0, 0.0)
        right = jnp.where(where % LANES == column, 1.0, 0.0)
        part = dot_rows(left.astype(BF16), (right * float(at)).astype(BF16))
        high = part if high is None else high + part
        part = dot_rows(left.astype(BF16), (right * row.astype(F32)).astype(BF16))
        total = part if total is None else total + part
    number = high * float(LANES) + total
    out[...] = number[: out.shape[0], : out.shape[1]].astype(jnp.int32)


def group_order(names, groups):
    edges = names.shape[0]
    rows = pl.cdiv(pl.cdiv(edges, LANES), 8) * 8
    padded = jnp.pad(names, (0, rows * LANES - edges), constant_values=groups)
    out = small_call(
        functools.partial(order_kernel, groups, edges // groups),
        (padded.reshape(rows, LANES),), [((edges // LANES, LANES), jnp.int32)], "group_order",
    )[0]
    return out.reshape(1, edges)


def spread(column, width):
    return jnp.concatenate([column] * (width // LANES), axis=1)


def norm(value):
    centre = value - jnp.mean(value, -1, keepdims=True)
    scale = lax.rsqrt(jnp.mean(centre * centre, -1, keepdims=True) + EPS)
    return centre * scale, scale


def norm_back(inner, normed, scale):
    mean_first = jnp.mean(inner, -1, keepdims=True)
    mean_second = jnp.mean(inner * normed, -1, keepdims=True)
    return scale * (inner - mean_first - normed * mean_second)


def column_sum(value):
    return jnp.sum(value, axis=0, keepdims=True)


def whole(*_):
    return (0, 0)


def const_spec(shape):
    return pl.BlockSpec(shape, lambda *_: (0,) * len(shape), pipeline_mode=pl.Buffered(1))


def small_call(kernel, args, shapes, name, scratch=(), flops=0, moved=0, exps=0, scalars=0):
    return pl.pallas_call(
        kernel,
        grid=(1,),
        in_specs=[pl.BlockSpec(memory_space=pltpu.SMEM)] * scalars
        + [const_spec(a.shape) for a in args[scalars:]],
        out_specs=[pl.BlockSpec(s, lambda *_, n=len(s): (0,) * n) for s, _ in shapes],
        out_shape=[jax.ShapeDtypeStruct(*s) for s in shapes],
        scratch_shapes=list(scratch),
        compiler_params=pltpu.CompilerParams(vmem_limit_bytes=VMEM),
        name=name,
        cost_estimate=pl.CostEstimate(flops=flops, bytes_accessed=moved, transcendentals=exps),
    )(*args)


def tile_count(shape):
    return pl.cdiv(shape[0], 16) * pl.cdiv(shape[1], LANES)


def all_tiles(shapes):
    return sum(tile_count(s) for s in shapes)


def pack(slab, values, at=0):
    for value in values:
        rows, columns = value.shape
        count = rows // 16
        for first in range(0, columns, LANES):
            take = min(LANES, columns - first)
            tile = value[:, first : first + take].astype(BF16).reshape(count, 16, take)
            slab[at : at + count, :, :take] = tile
            at += count


def unpack(slab, at, rows, columns):
    count = rows // 16
    parts = [
        slab[at + i * count : at + (i + 1) * count].reshape(rows, LANES).astype(F32)
        for i in range(pl.cdiv(columns, LANES))
    ]
    return jnp.concatenate(parts, axis=1)


def order_out(slab, base, codes, keep, send):
    size = slab.shape[0] // len(codes)
    half = len(codes) // 2
    for place, code in enumerate(codes):
        out = keep if place < half else send
        at = (place % half) * size
        out[at : at + size] = slab[pl.ds((base ^ code) * size, size)]


def half_shapes(tiles):
    return [((tiles // 2, 16, LANES), BF16)] * 2


def slab_scratch(tiles):
    return pltpu.VMEM((tiles, 16, LANES), BF16)


def slab_tiles(shapes, chunks):
    return pl.cdiv(all_tiles(shapes), chunks)


def order_in(slab, base, codes, first, second):
    size = slab.shape[0] // len(codes)
    half = len(codes) // 2
    for place, code in enumerate(codes):
        source = first if place < half else second
        at = (place % half) * size
        slab[pl.ds((base ^ code) * size, size)] = source[at : at + size]


def padded_rows(parts, width):
    return jnp.concatenate(parts + [jnp.zeros((16 - len(parts), width), F32)], axis=0)


def slot_block(slots):
    for size in (12, 10, 8, 6, 5, 4, 3, 2):
        if slots % size == 0:
            return size
    return 1


def far_table(node_lo, node_hi, weights, put):
    tile = min(512, node_lo.shape[0])
    for source, start in ((node_lo, 0), (node_hi, node_lo.shape[0])):
        def body(i, carry, source=source, start=start):
            at = pl.multiple_of(i * tile, tile)
            put(start + at, dot(source[pl.ds(at, tile), :], weights))
            return carry
        lax.fori_loop(0, source.shape[0] // tile, body, 0)


def message_forward_kernel(
    sb, by_rows, node_lo, node_hi, node_own, edge, idx_row, names, live_col, m1, b1, m2, b2,
    a1_out, s1_out, s2_out, sum_out, table, far, near, lhs, z,
):
    step = pl.program_id(0)
    width = node_own.shape[1]
    edge_width = edge.shape[2]
    rows = edge.shape[1]
    block = sb * rows
    lanes = width // LANES

    @pl.when(step == 0)
    def _():
        weights = m1[width + edge_width :, :]
        if by_rows:
            def put(first, value):
                for at in range(8):
                    column = at % lanes * LANES
                    table[pl.ds(first * 8 + at, value.shape[0], stride=8), :] = value[
                        :, column : column + LANES
                    ]
        else:
            def put(first, value):
                table[pl.ds(first, value.shape[0]), :] = value.astype(BF16)
        far_table(node_lo, node_hi, weights, put)
        near[:edge_width, :] = m1[width : width + edge_width, :]
        near[edge_width:, :] = jnp.zeros_like(near[edge_width:, :])
        near[edge_width : edge_width + rows, :] = (
            dot(node_own[...], m1[:width, :]) + b1[...]
        ).astype(BF16)
        shape = (rows, near.shape[0] - edge_width)
        eye = lax.broadcasted_iota(jnp.int32, shape, 0) == lax.broadcasted_iota(jnp.int32, shape, 1)
        for at in range(0, block, rows):
            lhs[at : at + rows, edge_width:] = jnp.where(eye, 1.0, 0.0).astype(BF16)
        sum_out[...] = jnp.zeros_like(sum_out)

    lhs[:, :edge_width] = edge[...].reshape(block, edge_width)
    z[...] = dot(lhs[...], near[...])
    if not by_rows:
        z[...] += pick_rows(index_columns(idx_row[...]), (table,))
    upper = lax.broadcasted_iota(jnp.int32, (8, LANES), 0) < lanes

    def fetch(at):
        for e in range(at, at + 16, 2):
            pair = [
                table[pl.ds(pl.multiple_of(names[0, step * block + e + i] * 8, 8), 8), :]
                for i in range(2)
            ]
            far[e * lanes : e * lanes + 8, :] = jnp.where(upper, *pair)

    def fetched(at):
        return jnp.concatenate(
            [far[pl.ds(at * lanes + j, 16, stride=lanes), :] for j in range(lanes)], axis=1
        )

    if by_rows:
        fetch(0)
    for at in range(0, block, 16):
        value = z[at : at + 16, :]
        if by_rows:
            if at + 16 < block:
                fetch(at + 16)
            value = value + fetched(at)
        act, slope = gelu_parts(value)
        a1_out[at : at + 16, :] = act.astype(BF16)
        s1_out[at : at + 16, :] = slope.astype(BF16)
    z[...] = dot(a1_out[...], m2[...])
    bias = b2[...]
    for row in range(0, rows, 16):
        count = live_col[row : row + 16, :]
        inverse = 1.0 / count.astype(F32)
        total = sum_out[row : row + 16, :]
        for s in range(sb):
            at = s * rows + row
            act, slope = gelu_parts(z[at : at + 16, :] + bias)
            s2_out[at : at + 16, :] = slope.astype(BF16)
            share = jnp.where(count > step * sb + s, inverse, 0.0)
            total = total + act.astype(BF16).astype(F32) * spread(share, width)
        sum_out[row : row + 16, :] = total


def message_forward(node_lo, node_hi, node_own, edge, idx_row, live_col, m1, b1, m2, b2):
    slots, rows, edge_width = edge.shape
    width = node_own.shape[1]
    residues = 2 * node_lo.shape[0]
    by_rows = residues <= 4096 and width == 4 * LANES
    sb = slot_block(slots) if by_rows else 4
    block = sb * rows
    edges = slots * rows
    near = pl.cdiv(edge_width + rows, LANES) * LANES
    row_spec = pl.BlockSpec((block, width), lambda i: (i, 0))
    return pl.pallas_call(
        functools.partial(message_forward_kernel, sb, by_rows),
        grid=(slots // sb,),
        in_specs=[
            const_spec(node_lo.shape),
            const_spec(node_hi.shape),
            const_spec(node_own.shape),
            pl.BlockSpec((sb, rows, edge_width), lambda i: (i, 0, 0)),
            pl.BlockSpec((1, block), lambda i: (0, i)),
            pl.BlockSpec(memory_space=pltpu.SMEM),
            const_spec(live_col.shape),
            const_spec(m1.shape),
            const_spec(b1.shape),
            const_spec(m2.shape),
            const_spec(b2.shape),
        ],
        out_specs=[row_spec, row_spec, row_spec, pl.BlockSpec((rows, width), whole)],
        out_shape=[jax.ShapeDtypeStruct((edges, width), BF16)] * 3
        + [jax.ShapeDtypeStruct((rows, width), F32)],
        scratch_shapes=[
            pltpu.VMEM((residues * 8, LANES), F32) if by_rows else pltpu.VMEM((residues, width), BF16),
            pltpu.VMEM((block * 4 if by_rows else 8, LANES), F32),
            pltpu.VMEM((near, width), BF16),
            pltpu.VMEM((block, near), BF16),
            pltpu.VMEM((block, width), F32),
        ],
        compiler_params=pltpu.CompilerParams(vmem_limit_bytes=VMEM),
        name="message_forward",
        cost_estimate=pl.CostEstimate(
            flops=2 * edges * width * (residues + edge_width + width),
            bytes_accessed=edges * width * 6 + edges * edge_width * 2 + edges * LANES * 4,
            transcendentals=2 * edges * width,
        ),
    )(node_lo, node_hi, node_own, edge, idx_row, idx_row, live_col, m1, b1, m2, b2)


def joined(refs, at):
    return jnp.concatenate([refs[2 * at][...], refs[2 * at + 1][...]], axis=0)


def residue_forward_kernel(parts, node, total, m3, b3, g1, fb2, g2, e_first, e_far, eb, *refs):
    f1, f2 = refs[:parts], refs[parts : 3 * parts]
    h1b_out, n1_out, sc1_out, n2_out, sc2_out, slope_out, h2b_out, far_out, own_out = refs[3 * parts :]
    width, hidden = node.shape[1], f1[0].shape[1]
    u1 = node[...].astype(F32) + fine(dot, total[...], m3[...]) + b3[...]
    n1, sc1 = norm(u1)
    h1 = n1 * g1[...]
    h1b = h1.astype(BF16)
    h1b_out[...] = h1b
    n1_out[...] = n1
    sc1_out[...] = jnp.broadcast_to(sc1, sc1_out.shape)
    y2 = None
    for p in range(parts):
        bias = f1[p][width : width + 16, :].astype(F32)
        bias = bias[0:1] + bias[1:2] + bias[2:3]
        act, slope = gelu_parts(dot(h1b, f1[p][:width, :]) + bias)
        slope_out[:, p * hidden : (p + 1) * hidden] = slope
        part = dot(act.astype(BF16), joined(f2, p))
        y2 = part if y2 is None else y2 + part
    n2, sc2 = norm(h1 + (y2 + fb2[...]))
    h2b = (n2 * g2[...]).astype(BF16)
    n2_out[...] = n2
    sc2_out[...] = jnp.broadcast_to(sc2, sc2_out.shape)
    h2b_out[...] = h2b
    far_out[...] = dot_back(h2b, e_far[...]).astype(BF16)
    own_out[...] = dot_back(h2b, e_first[:, :width]) + eb[...]


def residue_forward(node, total, m3, b3, g1, fb2, g2, e_first, e_far, eb, f1, f2):
    rows, width = node.shape
    edge_width = e_first.shape[0]
    hidden = len(f1) * f1[0].shape[1]
    shapes = [
        ((rows, width), BF16),
        ((rows, width), F32),
        ((rows, LANES), F32),
        ((rows, width), F32),
        ((rows, LANES), F32),
        ((rows, hidden), F32),
        ((rows, width), BF16),
        ((rows, edge_width), BF16),
        ((rows, edge_width), F32),
    ]
    return small_call(
        functools.partial(residue_forward_kernel, len(f1)),
        (node, total, m3, b3, g1, fb2, g2, e_first, e_far, eb, *f1, *f2),
        shapes, "residue_forward", flops=4 * rows * width * hidden, moved=5 * MIB,
        exps=rows * hidden,
    )


def edge_kernel(
    sb, blocks, hi_chunks, by_rows, far_lo, far_hi, own, edge, cot, idx, idx_row, names, live_col,
    e_first, e2, eb2, e3, eb3, g3,
    edge_out, act_one_out, act_two_out, low_three_out, low_two_out, low_one_out, hi_out, lo_out, own_out, gain_out,
    low_first, gs, table, far, z, slope_ref,
):
    step = pl.program_id(0)
    rows, width = own.shape
    node_width = (e_first.shape[1] - width) // 2
    e_mid = e_first.at[:, node_width : node_width + width]
    tiles = pl.cdiv(width, LANES)
    per = 8 // tiles
    size = 32

    @pl.when(step == 0)
    def _():
        own_out[...] = jnp.zeros_like(own_out)
        gs[...] = jnp.zeros_like(gs)
        half = far_lo.shape[0]
        if by_rows:
            for source, start in ((far_lo, 0), (far_hi, half)):
                for first in range(0, half, 512):
                    value = source[first : first + 512, :].astype(F32)
                    for at in range(8):
                        column = at % tiles * LANES
                        take = min(LANES, width - column)
                        table[pl.ds((start + first) * 8 + at, value.shape[0], stride=8), :take] = value[
                            :, column : column + take
                        ]

    @pl.when(step < blocks)
    def _():
        block = sb * rows
        flat = edge[...].reshape(block, width)
        z[...] = dot_back(flat, e_mid[...])
        if not by_rows:
            z[...] += pick_rows(index_columns(idx[...]), (far_lo, far_hi))
        sub = lax.broadcasted_iota(jnp.int32, (8, LANES), 0)

        def fetch(at):
            for e in range(at, at + size, per):
                got = [
                    table[pl.ds(pl.multiple_of(names[0, step * block + e + i] * 8, 8), 8), :]
                    for i in range(per)
                ]
                value = got[-1]
                for i in range(per - 2, -1, -1):
                    value = jnp.where(sub < (i + 1) * tiles, got[i], value)
                far[e * tiles : e * tiles + 8, :] = value

        def fetched(at):
            parts = [
                far[pl.ds(at * tiles + j, size, stride=tiles), :][:, : min(LANES, width - j * LANES)]
                for j in range(tiles)
            ]
            return jnp.concatenate(parts, axis=1)

        if by_rows:
            fetch(0)
        for at in range(0, block, size):
            value = z[at : at + size, :] + own[at % rows : at % rows + size, :]
            if by_rows:
                if at + size < block:
                    fetch(at + size)
                value = value + fetched(at)
            act, slope = gelu_parts(value)
            act_one_out[at : at + size, :] = act.astype(BF16)
            slope_ref[at : at + size, :] = slope
        act_one = act_one_out[...]
        act_two, slope_two = gelu_parts(dot(act_one, e2[...]) + eb2[...])
        act_two = act_two.astype(BF16)
        act_two_out[...] = act_two
        w_three = dot(act_two, e3[...]) + eb3[...]
        normed, scale = norm(flat.astype(F32) + w_three)
        count = spread(live_col[...], pl.cdiv(width, LANES) * LANES)[:, :width]
        live = jnp.concatenate(
            [jnp.where(count > step * sb + s, 1.0, 0.0) for s in range(sb)], axis=0
        )
        edge_out[...] = (normed * g3[...] * live).astype(BF16).reshape(sb, rows, width)
        grad = cot[...].reshape(block, width).astype(F32) * live
        gs[...] += jnp.sum((grad * normed).reshape(sb, rows, width), axis=0)
        low_three = norm_back(grad * g3[...], normed, scale).astype(BF16)
        low_three_out[...] = low_three
        low_two = (dot_back(low_three, e3[...]) * slope_two).astype(BF16)
        low_two_out[...] = low_two
        low_one = (dot_back(low_two, e2[...]) * slope_ref[...]).astype(BF16)
        low_one_out[...] = low_one
        own_out[...] += jnp.sum(low_one.astype(F32).reshape(sb, rows, width), axis=0)
        low_first[pl.ds(pl.multiple_of(step * block, block), block), :] = low_one

    chunk = hi_out.shape[0]

    @pl.when((step >= blocks) & (step < blocks + hi_chunks))
    def _():
        start = (step - blocks + hi_chunks) * chunk
        hi_out[...] = dot(one_hot_rows(idx_row[...], start, chunk), low_first[...]).astype(BF16)

    @pl.when(step >= blocks + hi_chunks)
    def _():
        start = (step - blocks - hi_chunks) * chunk
        lo_out[...] = dot(one_hot_rows(idx_row[...], start, chunk), low_first[...])

    @pl.when(step == blocks + 2 * hi_chunks - 1)
    def _():
        gain_out[...] = column_sum(gs[...])


def edge_branch(far_lo, far_hi, own, edge, cot, idx_row, live_col, e_first, e2, eb2, e3, eb3, g3):
    slots, rows, width = edge.shape
    sb = slot_block(slots)
    edges = slots * rows
    block = sb * rows
    blocks = slots // sb
    half = far_lo.shape[0]
    chunk = min(512, half)
    hi_chunks = half // chunk
    by_rows = half <= 2048 and 8 % pl.cdiv(width, LANES) == 0
    blk = lambda i: jnp.minimum(i, blocks - 1)
    hi_at = lambda i: (jnp.clip(i - blocks, 0, hi_chunks - 1), 0)
    lo_at = lambda i: (jnp.clip(i - blocks - hi_chunks, 0, hi_chunks - 1), 0)
    slot_spec = pl.BlockSpec((sb, rows, width), lambda i: (blk(i), 0, 0))
    row_spec = pl.BlockSpec((block, width), lambda i: (blk(i), 0))
    return pl.pallas_call(
        functools.partial(edge_kernel, sb, blocks, hi_chunks, by_rows),
        grid=(blocks + 2 * hi_chunks,),
        in_specs=[
            const_spec(far_lo.shape),
            const_spec(far_hi.shape),
            const_spec(own.shape),
            slot_spec,
            slot_spec,
            pl.BlockSpec((1, block), lambda i: (0, blk(i))),
            const_spec(idx_row.shape),
            pl.BlockSpec(memory_space=pltpu.SMEM),
            const_spec(live_col.shape),
            const_spec(e_first.shape),
            const_spec(e2.shape),
            const_spec(eb2.shape),
            const_spec(e3.shape),
            const_spec(eb3.shape),
            const_spec(g3.shape),
        ],
        out_specs=[slot_spec]
        + [row_spec] * 5
        + [
            pl.BlockSpec((chunk, width), hi_at),
            pl.BlockSpec((chunk, width), lo_at),
            pl.BlockSpec((rows, width), whole),
            pl.BlockSpec((1, width), whole),
        ],
        out_shape=[jax.ShapeDtypeStruct((slots, rows, width), BF16)]
        + [jax.ShapeDtypeStruct((edges, width), BF16)] * 5
        + [
            jax.ShapeDtypeStruct((half, width), BF16),
            jax.ShapeDtypeStruct((half, width), F32),
            jax.ShapeDtypeStruct((rows, width), F32),
            jax.ShapeDtypeStruct((1, width), F32),
        ],
        scratch_shapes=[
            pltpu.VMEM((edges, width), BF16),
            pltpu.VMEM((rows, width), F32),
            pltpu.VMEM((half * 16 if by_rows else 8, LANES), F32),
            pltpu.VMEM((block * 8, LANES), F32),
            pltpu.VMEM((block, width), F32),
            pltpu.VMEM((block, width), F32),
        ],
        compiler_params=pltpu.CompilerParams(vmem_limit_bytes=VMEM),
        name="edge_branch",
        cost_estimate=pl.CostEstimate(
            flops=2 * edges * width * (4 * half + 5 * width),
            bytes_accessed=edges * width * 16,
            transcendentals=2 * edges * width,
        ),
    )(far_lo, far_hi, own, edge, cot, idx_row, idx_row, idx_row, live_col, e_first, e2, eb2, e3, eb3, g3)


def edge_weights_kernel(blocks, pairs, *refs):
    step = pl.program_id(0)
    lefts, rights = refs[:pairs], refs[pairs : 2 * pairs]
    grads, biases, sums = refs[2 * pairs : 3 * pairs], refs[3 * pairs : 4 * pairs], refs[-1]
    rows = sums.shape[1]

    @pl.when(step == 0)
    def _():
        for ref in (*grads, sums):
            ref[...] = jnp.zeros_like(ref)

    for at in range(pairs):
        left, right = [r[...].reshape(-1, r.shape[-1]) for r in (lefts[at], rights[at])]
        grads[at][...] += dot_rows(left, right)
        low = left if lefts[at].ndim < rights[at].ndim else right
        sums[at] += jnp.sum(low.astype(F32).reshape(-1, rows, low.shape[1]), axis=0)

    @pl.when(step == blocks - 1)
    def _():
        for at in range(pairs):
            biases[at][...] = column_sum(sums[at])


def edge_weights(lefts, rights, rows):
    pairs = len(lefts)
    edges, width = lefts[0].shape
    slots = edges // rows
    sb = slot_block(slots)

    def spec(array):
        if array.ndim == 3:
            return pl.BlockSpec((sb, rows, width), lambda i: (i, 0, 0))
        return pl.BlockSpec((sb * rows, width), lambda i: (i, 0))

    shapes = [(width, width)] * pairs + [(1, width)] * pairs
    return pl.pallas_call(
        functools.partial(edge_weights_kernel, slots // sb, pairs),
        grid=(slots // sb,),
        in_specs=[spec(array) for array in (*lefts, *rights)],
        out_specs=[pl.BlockSpec(s, whole) for s in shapes],
        out_shape=[jax.ShapeDtypeStruct(s, F32) for s in shapes],
        scratch_shapes=[pltpu.VMEM((pairs, rows, width), F32)],
        compiler_params=pltpu.CompilerParams(vmem_limit_bytes=VMEM),
        name="edge_weights",
        cost_estimate=pl.CostEstimate(
            flops=2 * pairs * edges * width * width,
            bytes_accessed=pairs * edges * width * 4,
            transcendentals=0,
        ),
    )(*lefts, *rights)


def early_shapes(width, edge_width):
    return [
        (width, width),
        (edge_width, width),
        (edge_width, width),
        (16, width),
        (16, edge_width),
    ]


def residue_backward_kernel(
    parts, pieces, node_cot, own_sum, e_first, e_far, h1b, h2b, n1, sc1, n2, sc2, slope, g1, g2, m3,
    total, edge_gain, *refs,
):
    far = refs[:pieces]
    f1 = refs[pieces : pieces + parts]
    f2 = refs[pieces + parts : pieces + 3 * parts]
    gu1_out, v_out, both_out, slab = refs[pieces + 3 * parts :]
    width, hidden = h2b.shape[1], f1[0].shape[1]
    far_sum = far[0][: far[1].shape[0], :]
    for ref in far[1:]:
        far_sum = far_sum + ref[...].astype(F32)
    own = own_sum[...]
    g_h2 = (
        node_cot[...].astype(F32)
        + fine(dot, own, e_first[:, :width])
        + fine(dot, far_sum, e_far[...])
    )
    gain_two = column_sum(g_h2 * n2[...])
    g_u2 = norm_back(g_h2 * g2[...], n2[...], sc2[:, :1])
    gy2 = g_u2.astype(BF16)
    both_out[:, :width] = h1b[...]
    both_out[:, width:] = gy2
    g_h1 = g_u2
    for p in range(parts):
        gy1 = dot_back(gy2, joined(f2, p)) * slope[:, p * hidden : (p + 1) * hidden]
        g_h1 = g_h1 + dot_back(gy1.astype(BF16), f1[p][:width, :])
    gain_one = column_sum(g_h1 * n1[...])
    g_u1 = norm_back(g_h1 * g1[...], n1[...], sc1[:, :1])
    gu1_out[...] = g_u1
    v_out[...] = fine(dot_back, g_u1, m3[...])
    bias = [gain_one, gain_two, column_sum(gy2.astype(F32)), column_sum(g_u1)]
    slab[...] = jnp.zeros_like(slab)
    pack(
        slab,
        [
            dot_rows(total[...].astype(BF16), g_u1.astype(BF16)),
            dot_rows(own.astype(BF16), h2b[...]),
            dot_rows(far_sum.astype(BF16), h2b[...]),
            padded_rows(bias, width),
            padded_rows([edge_gain[...]], own.shape[1]),
        ],
    )


def residue_backward(args, far, f1, f2):
    node_cot, e_first, slope = args[0], args[2], args[10]
    rows, width = node_cot.shape
    shapes = [
        ((rows, width), F32),
        ((rows, width), F32),
        ((rows, 2 * width), BF16),
        ((all_tiles(early_shapes(width, e_first.shape[0])), 16, LANES), BF16),
    ]
    return small_call(
        functools.partial(residue_backward_kernel, len(f1), len(far)),
        (*args, *far, *f1, *f2),
        shapes, "residue_backward",
        flops=4 * rows * width * slope.shape[1], moved=8 * MIB,
    )


def feed_kernel(first, second, f1, fb1, f2, f1g, f2g, fb1g):
    width = f1.shape[0]

    @pl.when(pl.program_id(0) == 0)
    def _():
        for ref in (f1g, f2g, fb1g):
            ref[...] = jnp.zeros_like(ref)

    for both in (first, second):
        h1b, gy2 = both[:, :width], both[:, width:]
        act, slope = gelu_parts(dot(h1b, f1[...]) + fb1[...])
        gy1 = (dot_back(gy2, f2[...]) * slope).astype(BF16)
        f1g[...] += dot_rows(h1b, gy1)
        f2g[...] += dot_rows(act.astype(BF16), gy2)
        fb1g[...] += column_sum(gy1.astype(F32))


def feed_gradients(both, f1, fb1, f2):
    width, hidden = f1.shape
    half = both[0].shape[0]
    chunk = min(512, half)
    shapes = [(width, hidden), (hidden, width), (1, hidden)]
    return pl.pallas_call(
        feed_kernel,
        grid=(half // chunk,),
        in_specs=[pl.BlockSpec((chunk, 2 * width), lambda i: (i, 0))] * 2
        + [const_spec(a.shape) for a in (f1, fb1, f2)],
        out_specs=[pl.BlockSpec(s, whole) for s in shapes],
        out_shape=[jax.ShapeDtypeStruct(s, F32) for s in shapes],
        compiler_params=pltpu.CompilerParams(vmem_limit_bytes=VMEM),
        name="feed_gradients",
        cost_estimate=pl.CostEstimate(
            flops=16 * half * width * hidden,
            bytes_accessed=8 * half * width,
            transcendentals=2 * half * hidden,
        ),
    )(*both, f1, fb1, f2)


def late_shapes(width, edge_width):
    return [
        (width, width),
        (width, width),
        (edge_width, width),
        (16, width),
        (width, width),
        (edge_width, edge_width),
        (edge_width, edge_width),
        (edge_width, edge_width),
        (16, edge_width),
    ]


def weight_shapes(width, edge_width):
    return early_shapes(width, edge_width) + late_shapes(width, edge_width)


def message_backward_kernel(
    sb, blocks, groups, at_once, codes, base, order, v, a1, s1, s2, edge, low_three, low_edge, local_row, live_col,
    m1, m2, e_first, node_lo, node_hi, node, early,
    e1g, e2g, e3g, eb1, eb2, eb3,
    edge_grad, far_keep, far_send, own, keep, send,
    low_two, low_one, grad, rows_ref, moved, m2g, m1eg, m1fg, b2s, slab,
):
    step = pl.program_id(0)
    rows, width = v.shape
    edge_width = edge.shape[2]
    block = sb * rows
    tiles = width // LANES
    size = 16

    @pl.when(step == 0)
    def _():
        for ref in (own, m2g, m1eg, m1fg, b2s):
            ref[...] = jnp.zeros_like(ref)

    @pl.when(step < blocks)
    def _():
        for row in range(0, rows, size):
            count = live_col[row : row + size, :]
            inverse = 1.0 / count.astype(F32)
            value = v[row : row + size, :]
            total = b2s[row : row + size, :]
            for s in range(sb):
                at = s * rows + row
                share = jnp.where(count > step * sb + s, inverse, 0.0)
                low = (value * spread(share, width) * s2[at : at + size, :].astype(F32)).astype(BF16)
                low_two[at : at + size, :] = low
                total = total + low.astype(F32)
            b2s[row : row + size, :] = total
        grad[...] = dot_back(low_two[...], m2[...])
        m2g[...] += dot_rows(a1[...], low_two[...])
        first = pl.multiple_of(step * (block * 8), 8)
        rows_ref[pl.ds(first + tiles, block, stride=8), :] = index_columns(local_row[...]).astype(F32)
        for row in range(0, rows, size):
            total = own[row : row + size, :]
            for s in range(sb):
                at = s * rows + row
                low = (grad[at : at + size, :] * s1[at : at + size, :].astype(F32)).astype(BF16)
                low_one[at : at + size, :] = low
                low = low.astype(F32)
                total = total + low
                for j in range(tiles):
                    rows_ref[pl.ds(first + at * 8 + j, size, stride=8), :] = low[
                        :, j * LANES : (j + 1) * LANES
                    ]
            own[row : row + size, :] = total
        m1eg[...] += dot_rows(edge[...].reshape(block, edge_width), low_one[...])
        total = (
            low_three[...].astype(F32)
            + dot(low_edge[...], e_first[:, width : width + edge_width])
            + dot_back(low_one[...], m1[width : width + edge_width, :])
        )
        edge_grad[...] = total.reshape(sb, rows, edge_width)

    @pl.when(step >= blocks)
    def _():
        deep = far_keep.shape[0]
        count = block * blocks // groups
        height = rows // 16
        picked = [
            group_rows(
                order, ((step - blocks) * at_once + i) * count, count, rows_ref, moved.at[i], width
            )
            for i in range(at_once)
        ]
        for i, (values, local) in enumerate(picked):
            sums = group_sums(values, local, 2 * deep * rows).astype(BF16)
            near = jnp.concatenate(
                [ref[at, i] for ref in (node_lo, node_hi) for at in range(deep)], axis=0
            )
            m1fg[...] += dot_rows(near, sums)
            for at in range(2 * deep):
                out = (far_keep if at < deep else far_send).at[at % deep, i]
                for j in range(tiles):
                    tile = sums[at * rows : (at + 1) * rows, j * LANES : (j + 1) * LANES]
                    out[j * height : (j + 1) * height] = tile.reshape(height, 16, LANES)

    @pl.when(step == blocks + groups // at_once - 1)
    def _():
        count = early.shape[0]
        slab[:count] = early[...]
        slab[count:] = jnp.zeros_like(slab[count:])
        pack(
            slab,
            [
                dot_rows(node[...], own[...].astype(BF16)),
                m2g[...],
                m1eg[...],
                padded_rows([column_sum(own[...]), column_sum(b2s[...])], width),
                m1fg[...],
                e1g[...],
                e2g[...],
                e3g[...],
                padded_rows([eb1[...], eb2[...], eb3[...]], edge_width),
            ],
            count,
        )
        order_out(slab, base[0], codes, keep, send)


def message_backward(
    groups, codes, base, order, v, a1, s1, s2, edge, low_three, low_edge, local_row, live_col, m1, m2,
    e_first, node_lo, node_hi, node, early, edge_grads,
):
    slots, rows, edge_width = edge.shape
    width = v.shape[1]
    sb = slot_block(slots)
    block = sb * rows
    blocks = slots // sb
    edges = slots * rows
    half = node_lo.shape[0]
    deep = half // rows // groups
    at_once = 4 if groups % 4 == 0 else 1
    tiles = rows * width // (16 * LANES)
    slab = slab_tiles(weight_shapes(width, edge_width), len(codes)) * len(codes)
    node_lo, node_hi = [n.reshape(deep, groups, rows, width) for n in (node_lo, node_hi)]
    blk = lambda i: jnp.minimum(i, blocks - 1)
    group_at = lambda i: (0, jnp.maximum(i - blocks, 0))
    row_spec = pl.BlockSpec((block, width), lambda i: (blk(i), 0))
    slot_spec = pl.BlockSpec((sb, rows, edge_width), lambda i: (blk(i), 0, 0))
    edge_spec = pl.BlockSpec((block, edge_width), lambda i: (blk(i), 0))
    node_spec = pl.BlockSpec((deep, at_once, rows, width), lambda i: (*group_at(i), 0, 0))
    far_spec = pl.BlockSpec((deep, at_once, tiles, 16, LANES), lambda i: (*group_at(i), 0, 0, 0))
    slab_spec = pl.BlockSpec((slab // 2, 16, LANES), lambda i: (0, 0, 0))
    smem = pl.BlockSpec(memory_space=pltpu.SMEM)
    return pl.pallas_call(
        functools.partial(message_backward_kernel, sb, blocks, groups, at_once, codes),
        grid=(blocks + groups // at_once,),
        in_specs=[
            smem,
            smem,
            const_spec(v.shape),
            row_spec,
            row_spec,
            row_spec,
            slot_spec,
            edge_spec,
            edge_spec,
            pl.BlockSpec((1, block), lambda i: (0, blk(i))),
            const_spec(live_col.shape),
            const_spec(m1.shape),
            const_spec(m2.shape),
            const_spec(e_first.shape),
            node_spec,
            node_spec,
            const_spec(node.shape),
            const_spec(early.shape),
        ]
        + [const_spec(a.shape) for a in edge_grads],
        out_specs=[slot_spec, far_spec, far_spec, pl.BlockSpec((rows, width), whole), slab_spec, slab_spec],
        out_shape=[
            jax.ShapeDtypeStruct((slots, rows, edge_width), F32),
            jax.ShapeDtypeStruct((deep, groups, tiles, 16, LANES), BF16),
            jax.ShapeDtypeStruct((deep, groups, tiles, 16, LANES), BF16),
            jax.ShapeDtypeStruct((rows, width), F32),
            jax.ShapeDtypeStruct((slab // 2, 16, LANES), BF16),
            jax.ShapeDtypeStruct((slab // 2, 16, LANES), BF16),
        ],
        scratch_shapes=[
            pltpu.VMEM((block, width), BF16),
            pltpu.VMEM((block, width), BF16),
            pltpu.VMEM((block, width), F32),
            pltpu.VMEM((edges * 8, LANES), F32),
            pltpu.VMEM((at_once, edges // groups * 8, LANES), F32),
            pltpu.VMEM((width, width), F32),
            pltpu.VMEM((edge_width, width), F32),
            pltpu.VMEM((width, width), F32),
            pltpu.VMEM((rows, width), F32),
            slab_scratch(slab),
        ],
        compiler_params=pltpu.CompilerParams(vmem_limit_bytes=VMEM),
        name="message_backward",
        cost_estimate=pl.CostEstimate(
            flops=2 * edges * width * (2 * width + 3 * edge_width + half // groups),
            bytes_accessed=edges * width * 6 + edges * edge_width * 10,
            transcendentals=0,
        ),
    )(
        base, order, v, a1, s1, s2, edge, low_three, low_edge, local_row, live_col, m1, m2, e_first,
        node_lo, node_hi, node, early, *edge_grads,
    )


def node_kernel(pieces, g_u1, own, m1, *refs):
    far, grad_out = refs[:pieces], refs[pieces]
    rows, width = own.shape
    height = rows // 16
    tiles = height * (width // LANES)
    sums = far[0][:tiles].astype(F32)
    for ref in far[1:]:
        sums = sums + ref[:tiles].astype(F32)
    far_sum = jnp.concatenate(
        [sums[j * height : (j + 1) * height].reshape(rows, LANES) for j in range(width // LANES)],
        axis=1,
    )
    far_first = m1.shape[0] - width
    grad_out[...] = (
        g_u1[...]
        + fine(dot_back, own[...], m1[:width, :])
        + fine(dot_back, far_sum, m1[far_first:, :])
    )


def node_last(g_u1, own, m1, far):
    return small_call(
        functools.partial(node_kernel, len(far)),
        (g_u1, own, m1, *far), [(own.shape, F32)], "node_gradient",
        flops=8 * own.size * own.shape[1], moved=2 * MIB,
    )[0]


def weights_out_kernel(
    codes, base, first, second,
    m1g, b1, m2g, b2, m3g, e1g, e2g, e3g, b3, g1, g2, fb2, eb1, eb2, eb3, g3, slab,
):
    order_in(slab, base[0], codes, first, second)
    width, edge_width = m3g.shape[0], e2g.shape[0]
    shapes = weight_shapes(width, edge_width)
    starts = [all_tiles(shapes[:at]) for at in range(len(shapes))]
    m3g[...] = unpack(slab, starts[0], width, width)
    e1g[:, :width] = unpack(slab, starts[1], edge_width, width)
    middle = unpack(slab, starts[10], edge_width, edge_width)
    far = unpack(slab, starts[2], edge_width, width)
    over = edge_width % LANES
    base_col = width + edge_width - over
    e1g[:, width:base_col] = middle[:, : edge_width - over]
    far = pltpu.roll(jnp.concatenate([far, jnp.zeros((edge_width, LANES), F32)], axis=1), over, 1)
    lane = lax.broadcasted_iota(jnp.int32, (edge_width, LANES), 1)
    e1g[:, base_col : base_col + LANES] = jnp.where(
        lane < over, middle[:, edge_width - over : edge_width - over + LANES], far[:, :LANES]
    )
    rest = e1g.shape[1] - base_col - LANES
    e1g[:, base_col + LANES :] = far[:, LANES : LANES + rest]
    bias = unpack(slab, starts[3], 16, width)
    for row, out in enumerate((g1, g2, fb2, b3)):
        out[...] = bias[row : row + 1]
    g3[...] = unpack(slab, starts[4], 16, edge_width)[:1, :edge_width]
    m1g[:width, :] = unpack(slab, starts[5], width, width)
    m2g[...] = unpack(slab, starts[6], width, width)
    m1g[width : width + edge_width, :] = unpack(slab, starts[7], edge_width, width)
    bias = unpack(slab, starts[8], 16, width)
    b1[...] = bias[0:1]
    b2[...] = bias[1:2]
    m1g[width + edge_width :, :] = unpack(slab, starts[9], width, width)
    e2g[...] = unpack(slab, starts[11], edge_width, edge_width)[:, :edge_width]
    e3g[...] = unpack(slab, starts[12], edge_width, edge_width)[:, :edge_width]
    bias = unpack(slab, starts[13], 16, edge_width)
    for row, out in enumerate((eb1, eb2, eb3)):
        out[...] = bias[row : row + 1, :edge_width]


def weights_out(codes, base, halves_in, width, edge_width):
    shapes = [(2 * width + edge_width, width), (1, width), (width, width), (1, width)]
    shapes += [(width, width), (edge_width, 2 * width + edge_width)]
    shapes += [(edge_width, edge_width)] * 2 + [(1, width)] * 4 + [(1, edge_width)] * 4
    tiles = slab_tiles(weight_shapes(width, edge_width), len(codes)) * len(codes)
    return small_call(
        functools.partial(weights_out_kernel, codes),
        (base, *halves_in), [(s, F32) for s in shapes], "weight_gradients",
        [slab_scratch(tiles)], moved=10 * MIB, scalars=1,
    )


def exchange(value, mask, devices):
    return lax.ppermute(value, AXES, [(d, d ^ mask) for d in range(devices)])


def mask_groups(masks):
    return [masks[i : min(i + 2, len(masks) - 1)] for i in range(0, len(masks) - 1, 2)] + [masks[-1:]]


def order_codes(groups):
    masks = [mask for group in groups for mask in group]
    return [
        sum(mask for bit, mask in enumerate(masks) if place >> bit & 1)
        for place in range(1 << len(masks))
    ]


def combined(group, code):
    return sum(mask for bit, mask in enumerate(group) if code >> bit & 1)


def sent_around(value, group, devices):
    return [value] + [
        exchange(value, combined(group, code), devices) for code in range(1, 1 << len(group))
    ]


def shared_out(total, group, devices):
    parts = 1 << len(group)
    rows = total.shape[0] // parts
    return [total] + [
        exchange(total[code * rows : (code + 1) * rows].astype(BF16), combined(group, code), devices)
        for code in range(1, parts)
    ]


def add_up(terms):
    total = terms[0][: terms[1].shape[0]].astype(F32)
    for term in terms[1:]:
        total = total + term.astype(F32)
    return total


def tied(*values):
    return lax.optimization_barrier(values)


def split_three(value):
    rows = []
    for _ in range(3):
        high = lax.reduce_precision(value, 8, 7)
        rows.append(high.astype(BF16))
        value = value - high
    return jnp.concatenate(rows + [jnp.zeros((13, value.shape[1]), BF16)], axis=0)


def per_device(
    node_in,
    edge_in,
    neighbours,
    live_counts,
    message_first,
    message_first_bias,
    message_second,
    message_second_bias,
    message_third,
    message_third_bias,
    norm_one,
    feed_first,
    feed_first_bias,
    feed_second,
    feed_second_bias,
    norm_two,
    edge_first,
    edge_first_bias,
    edge_second,
    edge_second_bias,
    edge_third,
    edge_third_bias,
    norm_three,
    node_cotangent,
    edge_cotangent,
):
    rows, slots = neighbours.shape
    width = node_in.shape[1]
    edge_width = edge_in.shape[2]
    edges = rows * slots
    hid_count = lax.axis_size("hid")
    res_count = lax.axis_size("res")
    devices = res_count * hid_count
    bits = devices.bit_length() - 1
    masks = [1 << b for b in range(bits - 1, -1, -1)]
    groups = mask_groups(masks)
    codes = order_codes(groups)
    me = lax.axis_index("res") * hid_count + lax.axis_index("hid")
    base = me.reshape(1)
    row = lambda vector: vector.reshape(1, -1)

    names = neighbours.T.reshape(edges)
    apart = (names // rows) ^ me
    place = jnp.zeros_like(names)
    for bit, mask in enumerate(masks):
        place = place | jnp.where((apart & mask) != 0, 1 << bit, 0)
    idx_row = (place * rows + names % rows).reshape(1, edges)
    res_count = devices // hid_count
    local_row = (place // res_count * rows + names % rows).reshape(1, edges)
    edge_order = group_order(place % res_count, res_count)
    live_col = jnp.broadcast_to(live_counts[:, None], (rows, LANES))
    edge = edge_in.transpose(1, 0, 2)
    cot = edge_cotangent.transpose(1, 0, 2)
    e_first = edge_first.T
    e_far = e_first[:, width + edge_width :]
    f1x = jnp.concatenate([feed_first, split_three(row(feed_first_bias))], axis=0)
    cut = feed_second.shape[0] // 2
    hid_masks = [m for m in masks if m < hid_count]

    def across(pieces):
        for mask in hid_masks[:-1]:
            pieces = pieces + [exchange(p, mask, devices) for p in pieces]
        return pieces

    def over(pieces):
        return pieces + [exchange(p, hid_masks[-1], devices) for p in pieces]

    f2a = across([feed_second[:cut]])

    stack = lambda pieces: jnp.concatenate(pieces, axis=0)
    *outer, near = groups

    held = stack(sent_around(node_in, outer[0], devices))
    held, idx_row, local_row, f2a, e_far = tied(held, idx_row, local_row, f2a, e_far)
    for group in outer[1:]:
        held = stack(sent_around(held, group, devices))
    f2b = feed_second[cut:]
    held, f1x, f2a, f2b, edge_order, live_col = tied(held, f1x, f2a, f2b, edge_order, live_col)
    node_lo, node_hi = sent_around(held, near, devices)

    f2a = over(f2a)
    f1, f2b = across([f1x]), across([f2b])

    a1, s1, s2, total = message_forward(
        node_lo, node_hi, node_in, edge, idx_row, live_col, message_first,
        row(message_first_bias), message_second, row(message_second_bias),
    )
    total, f1, f2a, f2b = tied(total, f1, f2a, f2b)
    f1, f2b = over(f1), over(f2b)
    f2 = [half for pair in zip(f2a, f2b) for half in pair]
    h1b, n1, sc1, n2, sc2, slope, h2b, far_part, own_part = residue_forward(
        node_in, total, message_third, row(message_third_bias), row(norm_one),
        row(feed_second_bias), row(norm_two), e_first, e_far, row(edge_first_bias), f1, f2,
    )

    held = stack(sent_around(far_part, outer[0], devices))
    for group in outer[1:]:
        held = stack(sent_around(held, group, devices))
    q_lo, q_hi = sent_around(held, near, devices)

    edge_out, act_one, act_two, low_three, low_two, low_one, hi, lo, own_sum, edge_gain = edge_branch(
        q_lo, q_hi, own_part, edge, cot, idx_row, live_col, e_first,
        edge_second, row(edge_second_bias), edge_third, row(edge_third_bias), row(norm_three),
    )

    terms = [lo, exchange(hi, near[0], devices)]
    for group in reversed(outer):
        terms = shared_out(add_up(terms), group, devices)
    g_u1, v, both, early = residue_backward(
        (
            node_cotangent, own_sum, e_first, e_far, h1b, h2b, n1, sc1, n2, sc2, slope, row(norm_one),
            row(norm_two), message_third, total, edge_gain,
        ),
        terms, f1, f2,
    )

    both, low_here = tied(both, low_one)
    b_held = stack(sent_around(both, outer[0], devices))
    edge_grads = edge_weights((low_here, act_one, act_two), (edge, low_two, low_three), rows)
    v, b_held, edge_grads = tied(v, b_held, edge_grads)
    for group in outer[1:]:
        b_held = stack(sent_around(b_held, group, devices))
    edge_grad, far_keep, far_send, own, keep, send = message_backward(
        res_count, codes, base, edge_order, v, a1, s1, s2, edge, low_three, low_one, local_row, live_col,
        message_first, message_second, e_first, node_lo, node_hi, node_in, early, edge_grads,
    )
    keep, send, far_keep, far_send, b_held = tied(keep, send, far_keep, far_send, b_held)

    first, *others = reversed(outer)
    terms = [keep, exchange(send, near[0], devices)]
    total, b_held, far_send = tied(add_up(terms), b_held, far_send)
    terms = shared_out(total, first, devices)
    far_keep, far_send = [far.reshape(-1, 16, LANES) for far in (far_keep, far_send)]
    far_terms = [far_keep, exchange(far_send, near[0], devices)]
    b_near = sent_around(b_held, near, devices)
    total, b_first = tied(add_up(far_terms), b_near[0])
    far_terms = shared_out(total, first, devices)
    feed = feed_gradients((b_first, b_near[1]), feed_first, row(feed_first_bias), feed_second)
    terms, (f1g, f2g, fb1g) = tied(terms, feed)
    for group in others:
        terms = shared_out(add_up(terms), group, devices)
    held, *far_terms[:3] = tied(add_up(terms).astype(BF16), *far_terms[:3])

    for at, group in enumerate(outer):
        around = sent_around(held, group, devices)
        if at + 1 == len(outer):
            around, node_gradient = tied(around, node_last(g_u1, own, message_first, far_terms))
        held = stack(around)
        if at < len(others):
            held, *far_terms = tied(held, *far_terms)
            far_terms = shared_out(add_up(far_terms), others[at], devices)
    m1g, b1, m2g, b2, m3g, e1g, e2g, e3g, b3, g1, g2, fb2, eb1, eb2, eb3, g3 = weights_out(
        codes, base, sent_around(held, near, devices), width, edge_width
    )
    flat = lambda vector: vector.reshape(-1)
    return (
        h2b,
        edge_out.transpose(1, 0, 2),
        node_gradient,
        edge_grad.transpose(1, 0, 2),
        m1g,
        flat(b1),
        m2g,
        flat(b2),
        m3g,
        flat(b3),
        flat(g1),
        f1g,
        flat(fb1g),
        f2g,
        flat(fb2),
        flat(g2),
        e1g.T,
        flat(eb1),
        e2g,
        flat(eb2),
        e3g,
        flat(eb3),
        flat(g3),
    )


def solution(mesh):
    nodes, edges, shared = P(AXES, None), P(AXES, None, None), P()
    return jax.shard_map(
        per_device,
        mesh=mesh,
        in_specs=(nodes, edges, nodes, P(AXES))
        + (shared,) * 7
        + (P(None, "hid"), P("hid"), P("hid", None))
        + (shared,) * 9
        + (nodes, edges),
        out_specs=(nodes, edges, nodes, edges)
        + (shared,) * 7
        + (P(None, "hid"), P("hid"), P("hid", None))
        + (shared,) * 9,
        check_vma=False,
    )
```
